32 devices in a mesh: seq: 16 (over z, y, x), head: 2 (over core).
Axes of the slice: x: 2, y: 2, z: 4, core: 2. Of those that a mesh axis runs over, the one named last changes fastest.
Arguments:
- hidden_in: bfloat16 [1024, 2, 1536], P('seq'), may hold values from -4 to 4
- doc_ids: int32 [1024, 2], P('seq'), may hold values from 0 to 3, as said below
- routes: int32 [1024, 2, 6], P('seq'), may hold values from 0 to 15, all different within a row; in each aligned block of 128 rows (0 to 127, 128 to 255, ..., all dimensions but the last counted through in order) at most 96 rows name the same one
- norm1_gain: float32 [1536], replicated, may hold values from 0.5 to 1.5
- w_z: bfloat16 [1536, 3072], P('seq', 'head'), may hold values from -4 to 4
- w_x: bfloat16 [1536, 3072], P('seq', 'head'), may hold values from -4 to 4
- w_bc: bfloat16 [1536, 256], P('seq'), may hold values from -4 to 4
- w_dt: bfloat16 [1536, 48], P('seq', 'head'), may hold values from -4 to 4
- conv_x: float32 [4, 3072], P(None, 'head'), may hold values from -4 to 4
- conv_bc: float32 [4, 256], replicated, may hold values from -4 to 4
- convb_x: float32 [3072], P('head'), may hold values from -4 to 4
- convb_bc: float32 [256], replicated, may hold values from -4 to 4
- dt_bias: float32 [48], P('head'), may hold values from -1 to 1
- a_log: float32 [48], P('head'), may hold values from -10 to -3.5
- d_skip: float32 [48], P('head'), may hold values from 0.5 to 2
- gnorm_gain: float32 [3072], P('head'), may hold values from 0.5 to 1.5
- w_out: bfloat16 [3072, 1536], P('head', 'seq'), may hold values from -4 to 4
- norm2_gain: float32 [1536], replicated, may hold values from 0.5 to 1.5
- router: bfloat16 [1536, 16], P('seq'), may hold values from -4 to 4
- shared_gate: bfloat16 [1536, 1024], P('seq', 'head'), may hold values from -4 to 4
- shared_up: bfloat16 [1536, 1024], P('seq', 'head'), may hold values from -4 to 4
- shared_down: bfloat16 [1024, 1536], P('head', 'seq'), may hold values from -4 to 4
- expert_gate: bfloat16 [16, 1536, 512], P('seq', None, 'head'), may hold values from -4 to 4
- expert_up: bfloat16 [16, 1536, 512], P('seq', None, 'head'), may hold values from -4 to 4
- expert_down: bfloat16 [16, 512, 1536], P('seq', 'head'), may hold values from -4 to 4
- cotangent: bfloat16 [1024, 2, 1536], P('seq'), may hold values from -4 to 4
Outputs:
- block_out: float32 [1024, 2, 1536], P('seq')
- input_grad: float32 [1024, 2, 1536], P('seq')
- norm1_gain_grad: float32 [1536], replicated
- w_z_grad: float32 [1536, 3072], P('seq', 'head')
- w_x_grad: float32 [1536, 3072], P('seq', 'head')
- w_bc_grad: float32 [1536, 256], P('seq')
- w_dt_grad: float32 [1536, 48], P('seq', 'head')
- conv_x_grad: float32 [4, 3072], P(None, 'head')
- conv_bc_grad: float32 [4, 256], replicated
- convb_x_grad: float32 [3072], P('head')
- convb_bc_grad: float32 [256], replicated
- dt_bias_grad: float32 [48], P('head')
- a_log_grad: float32 [48], P('head')
- d_skip_grad: float32 [48], P('head')
- gnorm_gain_grad: float32 [3072], P('head')
- w_out_grad: float32 [3072, 1536], P('head', 'seq')
- norm2_gain_grad: float32 [1536], replicated
- router_grad: float32 [1536, 16], P('seq')
- shared_gate_grad: float32 [1536, 1024], P('seq', 'head')
- shared_up_grad: float32 [1536, 1024], P('seq', 'head')
- shared_down_grad: float32 [1024, 1536], P('head', 'seq')
- expert_gate_grad: float32 [16, 1536, 512], P('seq', None, 'head')
- expert_up_grad: float32 [16, 1536, 512], P('seq', None, 'head')
- expert_down_grad: float32 [16, 512, 1536], P('seq', 'head')
The draws below stay inside these ranges and needn't reach their ends.
Inputs may be any that keep to these rules, and one draw needn't show every extreme that they name: `doc_ids`: document numbers along each sequence start at 0 and rise by one at the first position of each document. One sequence, drawn from the seed, is a single document; every other one holds 4 documents. `routes`: each token names 6 different experts. Among the 128 tokens of one index of seq (position-major storage order) no expert is named by more than 96 tokens, a bound that some block reaches.
All inputs are finite; a program needn't handle non-finite values.
Results may differ from the reference program's by a relative error of at most 0.024.
The reference program's roundings to bfloat16 on the way count: a program that leaves them out, or rounds other values in their place, can miss the bound.
Values may be sent and summed in bfloat16 or wider, within the bound.
A program may use at most 384 MiB of HBM per device.

```python
import math
import jax
import jax.numpy as jnp
import numpy as np
from jax import lax

D = 1536
HEADS = 48
HDIM = 64
STATE = 128
KER = 4
FFE = 512
SHARED = 1024
TOPK = 6
SEQS = 2
SPAN = 64
DOCS = 4
INNER = 3072
EXPERTS = 16
LENGTH = 1024
TOK_DEV = 128
CAP = 96
N_SEQ = 16
N_HEAD = 2


def normal_fill(key, shape, scale):
    values = jnp.clip(jax.random.normal(key, shape, jnp.float32), -4.0, 4.0)
    return values * scale


def draw_doc_ids(key, part):
    key = jax.random.fold_in(key, 11)
    key_whole, key_place = jax.random.split(key)
    whole_seq = jax.random.randint(key_whole, (), 0, SEQS)
    scores = jax.random.randint(key_place, (SEQS, LENGTH - 1), 0, 2 ** 16) * LENGTH + jnp.arange(LENGTH - 1, dtype=jnp.int32)[None, :]
    picked = jnp.argsort(scores, axis=1)[:, :DOCS - 1] + 1
    seq_rows = jnp.broadcast_to(jnp.arange(SEQS, dtype=jnp.int32)[:, None], picked.shape)
    starts = jnp.zeros((SEQS, LENGTH), jnp.int32).at[seq_rows, picked].set(1)
    starts = jnp.where(jnp.arange(SEQS, dtype=jnp.int32)[:, None] == whole_seq, 0, starts)
    return jnp.cumsum(starts, axis=1).astype(jnp.int32).T


def draw_hidden_in(key, part):
    key = jax.random.fold_in(key, 21)
    return normal_fill(key, (LENGTH, SEQS, D), 1.0).astype(jnp.bfloat16)


def draw_cotangent(key, part):
    key = jax.random.fold_in(key, 22)
    return normal_fill(key, (LENGTH, SEQS, D), 1.0).astype(jnp.bfloat16)


def draw_w_z(key, part):
    key = jax.random.fold_in(key, 23)
    return normal_fill(key, (D, INNER), D ** (-0.5)).astype(jnp.bfloat16)


def draw_w_x(key, part):
    key = jax.random.fold_in(key, 24)
    return normal_fill(key, (D, INNER), D ** (-0.5)).astype(jnp.bfloat16)


def draw_w_bc(key, part):
    key = jax.random.fold_in(key, 25)
    return normal_fill(key, (D, 2 * STATE), D ** (-0.5)).astype(jnp.bfloat16)


def draw_w_dt(key, part):
    key = jax.random.fold_in(key, 26)
    return normal_fill(key, (D, HEADS), D ** (-0.5)).astype(jnp.bfloat16)


def draw_conv_x(key, part):
    key = jax.random.fold_in(key, 27)
    return normal_fill(key, (KER, INNER), KER ** (-0.5))


def draw_conv_bc(key, part):
    key = jax.random.fold_in(key, 28)
    return normal_fill(key, (KER, 2 * STATE), KER ** (-0.5))


def draw_convb_x(key, part):
    key = jax.random.fold_in(key, 29)
    return normal_fill(key, (INNER,), 0.3)


def draw_convb_bc(key, part):
    key = jax.random.fold_in(key, 30)
    return normal_fill(key, (2 * STATE,), 0.3)


def draw_w_out(key, part):
    key = jax.random.fold_in(key, 31)
    return normal_fill(key, (INNER, D), INNER ** (-0.5)).astype(jnp.bfloat16)


def draw_router(key, part):
    key = jax.random.fold_in(key, 32)
    return normal_fill(key, (D, EXPERTS), (4 * D) ** (-0.5)).astype(jnp.bfloat16)


def draw_shared_gate(key, part):
    key = jax.random.fold_in(key, 33)
    return normal_fill(key, (D, SHARED), D ** (-0.5)).astype(jnp.bfloat16)


def draw_shared_up(key, part):
    key = jax.random.fold_in(key, 34)
    return normal_fill(key, (D, SHARED), D ** (-0.5)).astype(jnp.bfloat16)


def draw_shared_down(key, part):
    key = jax.random.fold_in(key, 35)
    return normal_fill(key, (SHARED, D), (SHARED // 4) ** (-0.5)).astype(jnp.bfloat16)


def draw_expert_gate(key, part):
    key = jax.random.fold_in(key, 36)
    return normal_fill(key, (EXPERTS, D, FFE), D ** (-0.5)).astype(jnp.bfloat16)


def draw_expert_up(key, part):
    key = jax.random.fold_in(key, 37)
    return normal_fill(key, (EXPERTS, D, FFE), D ** (-0.5)).astype(jnp.bfloat16)


def draw_expert_down(key, part):
    key = jax.random.fold_in(key, 38)
    return normal_fill(key, (EXPERTS, FFE, D), (FFE // 16) ** (-0.5)).astype(jnp.bfloat16)


def block_levels(stream_key, shape, cuts, least, largest):
    gain, own = 1.0, jax.random.fold_in(stream_key, 6)
    for position, blocks in cuts:
        draws = jnp.exp(jax.random.uniform(jax.random.fold_in(own, position), (blocks,), jnp.float32, least / len(cuts), largest / len(cuts)))
        gain = gain * jnp.repeat(draws, shape[position] // blocks).reshape([-1 if axis == position else 1 for axis in range(len(shape))])
    return gain


def assign_block(rng, own, number, rows, amount, top, most, slope):
    order = jax.random.permutation(rng, amount)
    heavy_load, common = portions_of(amount, rows * top, most, slope, True), portions_of(amount, rows * top, most, slope, False)
    places = jnp.arange(amount)

    def named(lengths, offset_by):
        used = int((lengths > 0).sum())
        fixed = max(1, used // 4)
        moved = fixed + (places - fixed + offset_by * (used - fixed)) % max(1, amount - fixed)
        return jnp.zeros((amount,), jnp.int32).at[order[jnp.where(places < fixed, places, moved)]].set(jnp.asarray(lengths, jnp.int32))

    lengths = jnp.where(number % 4 == 0, named(heavy_load, number // 4), named(common, number - number // 4 - 1))
    mixed = jax.random.permutation(jax.random.fold_in(own, 3), amount)
    source_of, sink = mixed[0:amount // 2 * 2:2], mixed[1:amount // 2 * 2:2]
    margin = jnp.minimum(lengths[source_of] - 1, most - lengths[sink]) // 2
    margin = jnp.where((source_of == order[0]) | (sink == order[0]) | (lengths[sink] == 0), 0, jnp.maximum(margin, 0))
    moved = jax.random.randint(jax.random.fold_in(own, 4), (amount // 2,), 0, 1 << 20) % (margin + 1)
    lengths = lengths.at[source_of].add(-moved).at[sink].add(moved)
    labels = jnp.searchsorted(jnp.cumsum(lengths), jnp.arange(rows * top), side="right").astype(jnp.int32)
    table = labels.reshape(top, rows).T
    table = table[jax.random.permutation(jax.random.fold_in(own, 1), rows)]
    offset_by = jax.random.randint(jax.random.fold_in(own, 2), (rows, 1), 0, top)
    return jnp.take_along_axis(table, (jnp.arange(top)[None, :] + offset_by) % top, axis=1)


def portions_of(number_of, total, bound, lean, full):
    portions = [(1 << 20) // math.isqrt(standing ** lean) + 1 for standing in range(1, number_of + 1)]
    largest = bound if full else min(bound, max(-(-total // number_of), total * portions[0] // sum(portions)))
    least = 1 if total - largest >= number_of - 1 else 0
    holding, surplus = [largest] + [least] * (number_of - 1), total - largest - least * (number_of - 1)
    while surplus > 0:
        movable = [i for i in range(1, number_of) if holding[i] < largest] or [i for i in range(1, number_of) if holding[i] < bound]
        pool, budget = sum([portions[i] for i in movable]), surplus
        for i in movable:
            extra = min(bound - holding[i], max(1, budget * portions[i] // pool), surplus)
            holding[i] = holding[i] + extra
            surplus = surplus - extra
    return np.array(holding)


def setup_inputs(seed: int = 0) -> dict:
    splits = jax.random.split(jax.random.key(seed), 27)
    hidden_in = draw_hidden_in(jax.random.fold_in(splits[26], 71), 0)
    doc_ids = draw_doc_ids(jax.random.fold_in(splits[26], 71), 0)
    routes_keys = jax.random.split(jax.random.fold_in(splits[2], 1), LENGTH * SEQS // TOK_DEV)
    routes_turns = jax.random.permutation(jax.random.fold_in(splits[2], 3), LENGTH * SEQS // TOK_DEV)
    routes = jax.vmap(lambda own, number: assign_block(jax.random.fold_in(splits[2], 2), own, number, TOK_DEV, EXPERTS, TOPK, CAP, 1))(routes_keys, routes_turns).reshape((LENGTH, SEQS, TOPK))
    norm1_gain = jnp.clip(1.0 + 0.1 * jax.random.normal(splits[3], (D,), jnp.float32), 0.5, 1.5)
    w_z = draw_w_z(jax.random.fold_in(splits[26], 71), 0)
    w_x = draw_w_x(jax.random.fold_in(splits[26], 71), 0)
    w_bc = draw_w_bc(jax.random.fold_in(splits[26], 71), 0)
    w_dt = draw_w_dt(jax.random.fold_in(splits[26], 71), 0)
    conv_x = draw_conv_x(jax.random.fold_in(splits[26], 71), 0)
    conv_bc = draw_conv_bc(jax.random.fold_in(splits[26], 71), 0)
    convb_x = draw_convb_x(jax.random.fold_in(splits[26], 71), 0)
    convb_bc = draw_convb_bc(jax.random.fold_in(splits[26], 71), 0)
    dt_bias = jnp.clip(jax.random.uniform(splits[12], (HEADS,), jnp.float32, -1.0, 1.0) * block_levels(splits[12], (HEADS,), ((0, 2),), -0.4, 0.0), -1.0, 1.0)
    a_log = jnp.clip(-10.0 + 6.5 * jax.random.uniform(splits[13], (HEADS,), jnp.float32) ** block_levels(splits[13], (HEADS,), ((0, 2),), -0.2, 0.2), -10.0, -3.5)
    d_skip = jnp.clip(0.5 + 1.5 * jax.random.uniform(splits[14], (HEADS,), jnp.float32) ** block_levels(splits[14], (HEADS,), ((0, 2),), -0.2, 0.2), 0.5, 2.0)
    gnorm_gain = jnp.clip(1.0 + 0.1 * jax.random.normal(splits[15], (INNER,), jnp.float32), 0.5, 1.5)
    w_out = draw_w_out(jax.random.fold_in(splits[26], 71), 0)
    norm2_gain = jnp.clip(1.0 + 0.1 * jax.random.normal(splits[17], (D,), jnp.float32), 0.5, 1.5)
    router = draw_router(jax.random.fold_in(splits[26], 71), 0)
    shared_gate = draw_shared_gate(jax.random.fold_in(splits[26], 71), 0)
    shared_up = draw_shared_up(jax.random.fold_in(splits[26], 71), 0)
    shared_down = draw_shared_down(jax.random.fold_in(splits[26], 71), 0)
    expert_gate = draw_expert_gate(jax.random.fold_in(splits[26], 71), 0)
    expert_up = draw_expert_up(jax.random.fold_in(splits[26], 71), 0)
    expert_down = draw_expert_down(jax.random.fold_in(splits[26], 71), 0)
    cotangent = draw_cotangent(jax.random.fold_in(splits[26], 71), 0)
    return dict(hidden_in=hidden_in, doc_ids=doc_ids, routes=routes, norm1_gain=norm1_gain, w_z=w_z, w_x=w_x, w_bc=w_bc, w_dt=w_dt, conv_x=conv_x, conv_bc=conv_bc, convb_x=convb_x, convb_bc=convb_bc, dt_bias=dt_bias, a_log=a_log, d_skip=d_skip, gnorm_gain=gnorm_gain, w_out=w_out, norm2_gain=norm2_gain, router=router, shared_gate=shared_gate, shared_up=shared_up, shared_down=shared_down, expert_gate=expert_gate, expert_up=expert_up, expert_down=expert_down, cotangent=cotangent)


EPS = 1e-05
HIGH = lax.Precision.HIGHEST

@jax.custom_vjp
def low(v):
    return lax.optimization_barrier(v.astype(jnp.bfloat16)).astype(jnp.float32)

@jax.custom_vjp
def low_back(v):
    return v

def low_keep(v):
    return (low(v), None)

def low_pass(kept, grad):
    return (grad,)

def back_keep(v):
    return (v, None)

def back_low(kept, grad):
    return (low(grad),)
low.defvjp(low_keep, low_pass)
low_back.defvjp(back_keep, back_low)

def rms_scale(values):
    return lax.rsqrt(lax.optimization_barrier(jnp.mean(values * values, axis=-1, keepdims=True)) + EPS)

def project(left_side, right_side):
    return jnp.einsum('...d,de->...e', left_side, right_side, precision=HIGH)

def conv_apply(conv_ext, docs_ext, weight, conv_bias):
    length_here = conv_ext.shape[0] - (KER - 1)
    running = conv_bias
    for offset in range(KER):
        same_doc = (docs_ext[offset:offset + length_here] == docs_ext[KER - 1:]).astype(jnp.float32)
        running = running + weight[offset] * conv_ext[offset:offset + length_here] * same_doc[..., None]
    return jax.nn.silu(running)

def group_parts(x_heads, step_size, b_state, decay_rate, doc_ids, prev_doc):
    log_decay = jnp.cumsum(step_size * decay_rate, axis=0)
    end_keep = (doc_ids == doc_ids[-1:]).astype(jnp.float32)
    weight = jnp.exp(log_decay[-1:] - log_decay) * end_keep[..., None] * step_size
    s_local = jnp.einsum('tsh,tshp,tsn->shpn', weight, x_heads, b_state, precision=HIGH)
    a_total = jnp.exp(log_decay[-1]) * (doc_ids[-1] == prev_doc).astype(jnp.float32)[:, None]
    return (s_local, a_total)

def group_output(x_heads, step_size, b_state, c_state, decay_rate, doc_ids, prev_doc, s_in):
    length_here = x_heads.shape[0]
    log_decay = jnp.cumsum(step_size * decay_rate, axis=0)
    causal = jnp.arange(length_here)[:, None] >= jnp.arange(length_here)[None, :]
    pair_mask = (causal[:, :, None] & (doc_ids[:, None, :] == doc_ids[None, :, :])).astype(jnp.float32)
    gap_decay = log_decay[:, None] - log_decay[None, :]
    decay_table = jnp.exp(jnp.where(pair_mask[..., None] > 0, gap_decay, 0.0)) * pair_mask[..., None]
    cross_dot = jnp.einsum('tsn,usn->tus', c_state, b_state, precision=HIGH)
    y_intra = jnp.einsum('tush,ush,ushp->tshp', decay_table * cross_dot[..., None], step_size, x_heads, precision=HIGH)
    enters = jnp.exp(log_decay) * (doc_ids == prev_doc[None, :]).astype(jnp.float32)[..., None]
    y_inter = jnp.einsum('tsn,shpn->tshp', c_state, s_in, precision=HIGH) * enters[..., None]
    return y_intra + y_inter

def scan_ssm(x_heads, step_size, b_state, c_state, decay_rate, doc_ids, prev_doc):
    group_count = LENGTH // SPAN

    def to_groups(values):
        return values.reshape((group_count, SPAN) + values.shape[1:])
    first_prev = to_groups(prev_doc)[:, 0]

    @jax.checkpoint
    def group_step(carry_state, group_data):
        x_group, step_group, b_group, c_group, doc_group, prev_group = group_data
        y_group = group_output(x_group, step_group, b_group, c_group, decay_rate, doc_group, prev_group, carry_state)
        s_local, a_total = group_parts(x_group, step_group, b_group, decay_rate, doc_group, prev_group)
        return (a_total[..., None, None] * carry_state + s_local, y_group)
    zero_state = jnp.zeros((SEQS, HEADS, HDIM, STATE), jnp.float32)
    _, y_groups = lax.scan(group_step, zero_state, (to_groups(x_heads), to_groups(step_size), to_groups(b_state), to_groups(c_state), to_groups(doc_ids), first_prev))
    return y_groups.reshape(x_heads.shape)

def reference(hidden_in, doc_ids, routes, norm1_gain, w_z, w_x, w_bc, w_dt, conv_x, conv_bc, convb_x, convb_bc, dt_bias, a_log, d_skip, gnorm_gain, w_out, norm2_gain, router, shared_gate, shared_up, shared_down, expert_gate, expert_up, expert_down, cotangent):
    token_count = LENGTH * SEQS
    slot_total = token_count * TOPK
    rows_most = N_SEQ * CAP
    half_width = FFE // N_HEAD
    prev_doc = jnp.concatenate([doc_ids[:1], doc_ids[:-1]], 0)
    docs_ext = jnp.concatenate([jnp.full((KER - 1, SEQS), -1, jnp.int32), doc_ids], 0)
    route_flat = routes.reshape(slot_total)
    expert_ids = jnp.arange(EXPERTS, dtype=jnp.int32)
    route_hits = (route_flat[:, None] == expert_ids[None, :]).astype(jnp.int32)
    slot_rank = lax.optimization_barrier(jnp.sum(jnp.cumsum(route_hits, axis=0) * route_hits, axis=1)) - 1
    target = route_flat * rows_most + slot_rank
    entry_table = jnp.zeros((EXPERTS * rows_most,), jnp.int32).at[target].set(jnp.arange(slot_total, dtype=jnp.int32) + 1)
    entry_live = entry_table > 0
    entry_slot = jnp.maximum(entry_table - 1, 0)
    entry_token = entry_slot // TOPK
    drop_index = jnp.where(entry_live, entry_slot, slot_total)

    def forward_apply(block_input, first_norm_gain, gate_projection_weight, input_projection_weight, bstate_projection_weight, step_projection_weight, conv_kernel_input, conv_kernel_bstate, input_conv_shift, bstate_conv_shift, step_shift_value, log_decay_rate, skip_path_gain, gated_norm_gain, output_projection_weight, second_norm_gain, router_weight_matrix, shared_gate_weight, shared_up_weight, shared_down_weight, expert_gate_weight, expert_up_weight, expert_down_weight):
        normed_one = low(block_input * rms_scale(block_input) * first_norm_gain)
        gate_z = low_back(project(normed_one, gate_projection_weight))
        proj_x = low_back(project(normed_one, input_projection_weight))
        proj_bc = low_back(project(normed_one, bstate_projection_weight))
        dt_pre = low_back(project(normed_one, step_projection_weight)) + step_shift_value
        conv_in = jnp.concatenate([proj_x, proj_bc], -1)
        conv_ext = jnp.concatenate([jnp.zeros((KER - 1, SEQS, conv_in.shape[-1]), jnp.float32), conv_in], 0)
        conv_out = conv_apply(conv_ext, docs_ext, jnp.concatenate([conv_kernel_input, conv_kernel_bstate], -1), jnp.concatenate([input_conv_shift, bstate_conv_shift], -1))
        x_heads = conv_out[..., :INNER].reshape(LENGTH, SEQS, HEADS, HDIM)
        b_state = conv_out[..., INNER:INNER + STATE]
        c_state = conv_out[..., INNER + STATE:]
        step_size = jax.nn.softplus(dt_pre)
        decay_rate = -jnp.exp(log_decay_rate)
        y_heads = scan_ssm(x_heads, step_size, b_state, c_state, decay_rate, doc_ids, prev_doc) + skip_path_gain[:, None] * x_heads
        y_flat = y_heads.reshape(LENGTH, SEQS, INNER)
        gated = y_flat * jax.nn.silu(gate_z)
        mixed_out = low(gated * rms_scale(gated) * gated_norm_gain)
        residual = block_input + low_back(project(mixed_out, output_projection_weight))
        normed_two = low(residual * rms_scale(residual) * second_norm_gain)
        logits = low_back(project(normed_two, router_weight_matrix))
        gate_probs = jax.nn.softmax(jnp.take_along_axis(logits, routes, axis=-1), axis=-1)
        share_act = low(jax.nn.silu(low_back(project(normed_two, shared_gate_weight))) * low_back(project(normed_two, shared_up_weight)))
        share_out = low_back(project(share_act, shared_down_weight))
        every_row_block = normed_two.reshape(token_count, D)[entry_token] * entry_live[:, None].astype(jnp.float32)
        every_row_block = every_row_block.reshape(EXPERTS, rows_most, D)

        def expert_row_block(inputs):
            input_row_block, gate_w, up_w, down_w = inputs
            summed = jnp.zeros_like(input_row_block)
            for half_index in range(N_HEAD):
                columns = slice(half_index * half_width, (half_index + 1) * half_width)
                rows_half = low_back(input_row_block)
                hid_gate = low_back(project(rows_half, gate_w[:, columns]))
                hid_up = low_back(project(rows_half, up_w[:, columns]))
                hid_act = low(jax.nn.silu(hid_gate) * hid_up)
                summed = summed + low(project(hid_act, down_w[columns]))
            return low_back(summed)
        expert_result = lax.map(jax.checkpoint(expert_row_block), (every_row_block, expert_gate_weight, expert_up_weight, expert_down_weight))
        slot_out = jnp.zeros((slot_total + 1, D), jnp.float32).at[drop_index].add(expert_result.reshape(-1, D))[:slot_total]
        routed = lax.optimization_barrier(jnp.sum(gate_probs[..., None] * slot_out.reshape(LENGTH, SEQS, TOPK, D), axis=-2))
        return residual + routed + share_out
    block_out, pullback = jax.vjp(forward_apply, hidden_in.astype(jnp.float32), norm1_gain, w_z.astype(jnp.float32), w_x.astype(jnp.float32), w_bc.astype(jnp.float32), w_dt.astype(jnp.float32), conv_x, conv_bc, convb_x, convb_bc, dt_bias, a_log, d_skip, gnorm_gain, w_out.astype(jnp.float32), norm2_gain, router.astype(jnp.float32), shared_gate.astype(jnp.float32), shared_up.astype(jnp.float32), shared_down.astype(jnp.float32), expert_gate.astype(jnp.float32), expert_up.astype(jnp.float32), expert_down.astype(jnp.float32))
    gradients = pullback(cotangent.astype(jnp.float32))
    return (block_out, gradients[0], gradients[1], gradients[2], gradients[3], gradients[4], gradients[5], gradients[6], gradients[7], gradients[8], gradients[9], gradients[10], gradients[11], gradients[12], gradients[13], gradients[14], gradients[15], gradients[16], gradients[17], gradients[18], gradients[19], gradients[20], gradients[21], gradients[22])
```

```python
import functools

import jax
import jax.numpy as jnp
from jax import lax
from jax.experimental import pallas as pl
from jax.experimental.pallas import tpu as pltpu
from jax.sharding import PartitionSpec as P

KER = 4
INNER = 3072


EPS = 1e-05
HIGH = lax.Precision.HIGHEST


def passed_along(array, axis, by):
    length = lax.axis_size(axis)
    pairs = [(i, i + by) for i in range(length) if 0 <= i + by < length]
    return lax.ppermute(array, axis, pairs)


def entering(array, axis, combine, identity, reverse):
    length, here = (lax.axis_size(axis), lax.axis_index(axis))
    everything = jax.tree.map(
        lambda part, kind: lax.all_gather(part.astype(kind), axis),
        array,
        jax.tree.map(lambda a: jnp.bfloat16 if a.dtype == jnp.float32 else a.dtype, array),
    )
    start = jax.tree.map(
        lambda part, zero: jnp.broadcast_to(jnp.asarray(zero, part.dtype), part.shape),
        array,
        identity,
    )

    def hop(k, before):
        at = length - 1 - k if reverse else k
        reached = at > here if reverse else at < here
        new = combine(
            before, jax.tree.map(lambda part, own: part[at].astype(own.dtype), everything, array)
        )
        return jax.tree.map(lambda a, b: jnp.where(reached, a, b), new, before)

    return lax.fori_loop(0, length, hop, start)


def shortened(array):

    def short(part):
        return part.astype(jnp.bfloat16) if part.dtype == jnp.float32 else part

    return jax.tree.map(short, array)


def conv_apply(conv_ext, docs_ext, weight, conv_bias):
    length_here = conv_ext.shape[0] - (KER - 1)
    running = conv_bias
    for offset in range(KER):
        same_doc = (docs_ext[offset : offset + length_here] == docs_ext[KER - 1 :]).astype(
            jnp.float32
        )
        running = (
            running + weight[offset] * conv_ext[offset : offset + length_here] * same_doc[..., None]
        )
    return jax.nn.silu(running)


def group_parts(x_heads, step_size, b_state, decay_rate, doc_ids, prev_doc):
    log_decay = jnp.cumsum(step_size * decay_rate, axis=0)
    end_keep = (doc_ids == doc_ids[-1:]).astype(jnp.float32)
    weight = jnp.exp(log_decay[-1:] - log_decay) * end_keep[..., None] * step_size
    s_local = jnp.einsum("tsh,tshp,tsn->shpn", weight, x_heads, b_state, precision=HIGH)
    a_total = jnp.exp(log_decay[-1]) * (doc_ids[-1] == prev_doc).astype(jnp.float32)[:, None]
    return (s_local, a_total)


def group_output(x_heads, step_size, b_state, c_state, decay_rate, doc_ids, prev_doc, s_in):
    length_here = x_heads.shape[0]
    log_decay = jnp.cumsum(step_size * decay_rate, axis=0)
    causal = jnp.arange(length_here)[:, None] >= jnp.arange(length_here)[None, :]
    pair_mask = (causal[:, :, None] & (doc_ids[:, None, :] == doc_ids[None, :, :])).astype(
        jnp.float32
    )
    gap_decay = log_decay[:, None] - log_decay[None, :]
    decay_table = (
        jnp.exp(jnp.where(pair_mask[..., None] > 0, gap_decay, 0.0)) * pair_mask[..., None]
    )
    cross_dot = jnp.einsum("tsn,usn->tus", c_state, b_state, precision=HIGH)
    y_intra = jnp.einsum(
        "tush,ush,ushp->tshp",
        decay_table * cross_dot[..., None],
        step_size,
        x_heads,
        precision=HIGH,
    )
    enters = jnp.exp(log_decay) * (doc_ids == prev_doc[None, :]).astype(jnp.float32)[..., None]
    y_inter = jnp.einsum("tsn,shpn->tshp", c_state, s_in, precision=HIGH) * enters[..., None]
    return y_intra + y_inter


def ssm_local(x_heads, step_size, b_state, c_state, decay_rate, s_in, doc_ids, prev_doc):
    y_core = group_output(x_heads, step_size, b_state, c_state, decay_rate, doc_ids, prev_doc, s_in)
    s_local, a_total = group_parts(x_heads, step_size, b_state, decay_rate, doc_ids, prev_doc)
    return (y_core, a_total[..., None, None] * s_in + s_local)


def carry_combine(earlier, later_part):
    return (earlier[0] * later_part[0], later_part[0][..., None, None] * earlier[1] + later_part[1])


def head_total(partial_sum):
    return lax.psum(partial_sum, "head")


def flat_dot(left_side, right_side):
    lead_dims = left_side.shape[:-1]
    product = jnp.dot(
        left_side.reshape(-1, left_side.shape[-1]), right_side, preferred_element_type=jnp.float32
    )
    return product.reshape(lead_dims + (right_side.shape[-1],))


def flat_dot_t(left_side, right_side):
    lead_dims = left_side.shape[:-1]
    product = lax.dot_general(
        left_side.reshape(-1, left_side.shape[-1]),
        right_side,
        (((1,), (1,)), ((), ())),
        preferred_element_type=jnp.float32,
    )
    return product.reshape(lead_dims + (right_side.shape[0],))


def outer_sum(left_side, right_side):
    return lax.dot_general(
        left_side.reshape(-1, left_side.shape[-1]),
        right_side.reshape(-1, right_side.shape[-1]),
        (((0,), (0,)), ((), ())),
        preferred_element_type=jnp.float32,
    )


def silu_slope(values, sigmoid_of):
    return sigmoid_of * (1.0 + values * (1.0 - sigmoid_of))


def norm_back(grad_normed, values, scale_of, gain):
    scaled_grad = grad_normed * gain
    gain_grad = jnp.sum((grad_normed * values * scale_of).reshape(-1, values.shape[-1]), axis=0)
    cube = scale_of * scale_of * scale_of
    value_grad = scale_of * scaled_grad - values * cube * jnp.mean(
        scaled_grad * values, axis=-1, keepdims=True
    )
    return (value_grad, gain_grad)


def on_device(
    hidden_in,
    doc_ids,
    routes,
    norm1_gain,
    w_z,
    w_x,
    w_bc,
    w_dt,
    conv_x,
    conv_bc,
    convb_x,
    convb_bc,
    dt_bias,
    a_log,
    d_skip,
    gnorm_gain,
    w_out,
    norm2_gain,
    router,
    shared_gate,
    shared_up,
    shared_down,
    expert_gate,
    expert_up,
    expert_down,
    cotangent,
):
    block_len, seq_here, width = hidden_in.shape
    top_count = routes.shape[-1]
    heads_here = dt_bias.shape[0]
    inner_here = convb_x.shape[0]
    head_size = inner_here // heads_here
    state_size = convb_bc.shape[0] // 2
    seq_count = lax.axis_size("seq")
    local_experts = expert_gate.shape[0]
    experts_all = local_experts * seq_count
    tok_here = block_len * seq_here
    capacity = 2 * tok_here * top_count // experts_all
    edge_len = KER - 1
    x_float = hidden_in.astype(jnp.float32)
    scale_one = lax.rsqrt(jnp.mean(x_float * x_float, axis=-1, keepdims=True) + EPS)
    normed_one = (x_float * scale_one * norm1_gain).astype(jnp.bfloat16)
    gathered = (
        lax.all_gather(w_z, "seq", axis=0, tiled=True),
        lax.all_gather(w_x, "seq", axis=0, tiled=True),
        lax.all_gather(w_dt, "seq", axis=0, tiled=True),
        lax.all_gather(w_bc, "seq", axis=0, tiled=True),
        lax.all_gather(router, "seq", axis=0, tiled=True),
        lax.all_gather(shared_gate, "seq", axis=0, tiled=True),
        lax.all_gather(shared_up, "seq", axis=0, tiled=True),
        lax.all_gather(w_out, "seq", axis=1, tiled=True),
        lax.all_gather(shared_down, "seq", axis=1, tiled=True),
    )
    full_z, full_x, full_dt, full_bc, full_router, full_sgate, full_sup, full_out, full_sdown = (
        gathered
    )
    gate_z = flat_dot(normed_one, full_z)
    proj_x = flat_dot(normed_one, full_x)
    proj_bc = flat_dot(normed_one, full_bc)
    dt_pre = flat_dot(normed_one, full_dt) + dt_bias
    conv_in = jnp.concatenate([proj_x, proj_bc], axis=-1)
    tail_in, tail_doc = (
        passed_along(conv_in[block_len - edge_len :].astype(jnp.bfloat16), "seq", 1).astype(
            jnp.float32
        ),
        passed_along(
            doc_ids[block_len - edge_len :].astype(jnp.float32).astype(jnp.bfloat16), "seq", 1
        ).astype(jnp.float32),
    )
    conv_ext = jnp.concatenate([tail_in, conv_in], 0)
    docs_ext = jnp.concatenate([tail_doc.astype(jnp.int32), doc_ids], 0)
    conv_weight = jnp.concatenate([conv_x, conv_bc], -1)
    conv_shift = jnp.concatenate([convb_x, convb_bc], -1)
    conv_out = conv_apply(conv_ext, docs_ext, conv_weight, conv_shift)
    x_heads = conv_out[..., :inner_here].reshape(block_len, seq_here, heads_here, head_size)
    b_state = conv_out[..., inner_here : inner_here + state_size]
    c_state = conv_out[..., inner_here + state_size :]
    step_size = jax.nn.softplus(dt_pre)
    decay_rate = -jnp.exp(a_log)
    prev_doc = docs_ext[edge_len - 1]
    s_local, a_total = group_parts(x_heads, step_size, b_state, decay_rate, doc_ids, prev_doc)
    ones_start = jnp.ones_like(a_total)
    zeros_start = jnp.zeros_like(s_local)
    a_before, s_before = entering(
        (a_total, s_local), "seq", carry_combine, (ones_start, zeros_start), False
    )
    y_core = group_output(
        x_heads, step_size, b_state, c_state, decay_rate, doc_ids, prev_doc, s_before
    )
    y_heads = y_core + d_skip[:, None] * x_heads
    y_flat = y_heads.reshape(block_len, seq_here, inner_here)
    gate_sig = jax.nn.sigmoid(gate_z)
    gated = y_flat * gate_z * gate_sig
    square_sum = head_total(jnp.sum(gated * gated, axis=-1, keepdims=True))
    scale_gated = lax.rsqrt(square_sum / INNER + EPS)
    mixed_out = (gated * scale_gated * gnorm_gain).astype(jnp.bfloat16)
    residual = x_float + head_total(flat_dot(mixed_out, full_out))
    scale_two = lax.rsqrt(jnp.mean(residual * residual, axis=-1, keepdims=True) + EPS)
    normed_two = (residual * scale_two * norm2_gain).astype(jnp.bfloat16)
    logits = flat_dot(normed_two, full_router)
    gate_probs = jax.nn.softmax(jnp.take_along_axis(logits, routes, axis=-1), axis=-1)
    share_gate = flat_dot(normed_two, full_sgate)
    share_up = flat_dot(normed_two, full_sup)
    share_sig = jax.nn.sigmoid(share_gate)
    share_act = (share_gate * share_sig * share_up).astype(jnp.bfloat16)
    share_part = flat_dot(share_act, full_sdown)
    slot_total = tok_here * top_count
    route_flat = routes.reshape(slot_total)
    expert_ids = jnp.arange(experts_all, dtype=jnp.int32)
    route_hits = (route_flat[:, None] == expert_ids[None, :]).astype(jnp.int32)
    slot_rank = jnp.sum(jnp.cumsum(route_hits, axis=0) * route_hits, axis=1) - 1
    target = route_flat * capacity + slot_rank
    entry_table = (
        jnp.zeros((experts_all * capacity,), jnp.int32)
        .at[target]
        .set(jnp.arange(slot_total, dtype=jnp.int32) + 1)
    )
    entry_live = entry_table > 0
    entry_slot = jnp.maximum(entry_table - 1, 0)
    entry_token = entry_slot // top_count
    tokens_flat = normed_two.reshape(tok_here, width)
    send_rows = jnp.where(
        entry_live[:, None], tokens_flat[entry_token], jnp.zeros((), jnp.bfloat16)
    ).reshape(experts_all, capacity, width)
    received = lax.all_to_all(send_rows, "seq", split_axis=0, concat_axis=0, tiled=True)
    input_row_block = received.reshape(seq_count, local_experts, received.shape[1], width)
    hid_gate = jnp.einsum(
        "jecd,edf->jecf", input_row_block, expert_gate, preferred_element_type=jnp.float32
    )
    hid_up = jnp.einsum(
        "jecd,edf->jecf", input_row_block, expert_up, preferred_element_type=jnp.float32
    )
    hid_act = (hid_gate * jax.nn.sigmoid(hid_gate) * hid_up).astype(jnp.bfloat16)
    half_out = jnp.einsum(
        "jecf,efd->jecd", hid_act, expert_down, preferred_element_type=jnp.float32
    ).astype(jnp.bfloat16)
    returned_rows = lax.all_to_all(
        half_out.reshape(received.shape), "seq", split_axis=0, concat_axis=0, tiled=True
    )
    kept_shape = (seq_count * local_experts, received.shape[1], hid_gate.shape[-1])
    returned_rows, rows_kept, gate_kept, up_kept = (
        returned_rows,
        received,
        hid_gate.reshape(kept_shape),
        hid_up.reshape(kept_shape),
    )
    slot_rows = returned_rows.reshape(-1, width)[target].reshape(tok_here, top_count, width)
    probs_flat = gate_probs.reshape(tok_here, top_count)
    routed_part = share_part.reshape(tok_here, width)
    for slot_index in range(top_count):
        routed_part = routed_part + probs_flat[:, slot_index, None] * slot_rows[
            :, slot_index
        ].astype(jnp.float32)
    moe_out = head_total(routed_part.reshape(block_len, seq_here, width))
    block_out = residual + moe_out
    gathered = (
        lax.all_gather(w_z, "seq", axis=0, tiled=True),
        lax.all_gather(w_x, "seq", axis=0, tiled=True),
        lax.all_gather(w_dt, "seq", axis=0, tiled=True),
        lax.all_gather(w_bc, "seq", axis=0, tiled=True),
        lax.all_gather(router, "seq", axis=0, tiled=True),
        lax.all_gather(shared_gate, "seq", axis=0, tiled=True),
        lax.all_gather(shared_up, "seq", axis=0, tiled=True),
        lax.all_gather(w_out, "seq", axis=1, tiled=True),
        lax.all_gather(shared_down, "seq", axis=1, tiled=True),
    )
    full_z, full_x, full_dt, full_bc, full_router, full_sgate, full_sup, full_out, full_sdown = (
        gathered
    )
    grad_out = cotangent.astype(jnp.float32)
    grad_flat = grad_out.reshape(tok_here, width)
    entry_prob = jnp.where(entry_live, gate_probs.reshape(-1)[entry_slot], 0.0)
    send_grads = (
        (entry_prob[:, None] * grad_flat[entry_token])
        .astype(jnp.bfloat16)
        .reshape(experts_all, capacity, width)
    )
    recv_grads = lax.all_to_all(send_grads, "seq", split_axis=0, concat_axis=0, tiled=True)
    grads_in = recv_grads.reshape(seq_count, local_experts, capacity, width)
    input_row_block = rows_kept.reshape(seq_count, local_experts, capacity, width)
    hid_gate = gate_kept.reshape(seq_count, local_experts, capacity, -1)
    hid_up = up_kept.reshape(seq_count, local_experts, capacity, -1)
    hid_sig = jax.nn.sigmoid(hid_gate)
    hid_act = (hid_gate * hid_sig * hid_up).astype(jnp.bfloat16)
    d_act = jnp.einsum("jecd,efd->jecf", grads_in, expert_down, preferred_element_type=jnp.float32)
    hidden_up_gradient = (d_act * hid_gate * hid_sig).astype(jnp.bfloat16)
    d_hid_gate = (d_act * hid_up * silu_slope(hid_gate, hid_sig)).astype(jnp.bfloat16)
    grad_edown = jnp.einsum("jecf,jecd->efd", hid_act, grads_in, preferred_element_type=jnp.float32)
    grad_egate = jnp.einsum(
        "uqpy,uqpn->qyn", input_row_block, d_hid_gate, preferred_element_type=jnp.float32
    )
    expert_up_gradient = jnp.einsum(
        "uqpy,uqpn->qyn", input_row_block, hidden_up_gradient, preferred_element_type=jnp.float32
    )
    d_rows = jnp.einsum(
        "jecf,edf->jecd", d_hid_gate, expert_gate, preferred_element_type=jnp.float32
    )
    d_rows = (
        d_rows
        + jnp.einsum(
            "jecf,edf->jecd", hidden_up_gradient, expert_up, preferred_element_type=jnp.float32
        )
    ).astype(jnp.bfloat16)
    back_rows = lax.all_to_all(
        d_rows.reshape(recv_grads.shape), "seq", split_axis=0, concat_axis=0, tiled=True
    )
    d_share_act = flat_dot_t(cotangent, full_sdown)
    d_share_up = (d_share_act * share_gate * share_sig).astype(jnp.bfloat16)
    d_share_gate = (d_share_act * share_up * silu_slope(share_gate, share_sig)).astype(jnp.bfloat16)
    grad_sdown = outer_sum(share_act, cotangent)
    grad_sgate = outer_sum(normed_two, d_share_gate)
    grad_sup = outer_sum(normed_two, d_share_up)
    d_normed_two = (
        flat_dot_t(d_share_gate, full_sgate) + flat_dot_t(d_share_up, full_sup)
    ).reshape(tok_here, width)
    prob_grad = jnp.stack(
        [
            jnp.sum(grad_flat * slot_rows[:, slot_index].astype(jnp.float32), axis=-1)
            for slot_index in range(top_count)
        ],
        axis=-1,
    )
    back_slots = back_rows.reshape(-1, width)[target].reshape(tok_here, top_count, width)
    for slot_index in range(top_count):
        d_normed_two = d_normed_two + back_slots[:, slot_index].astype(jnp.float32)
    d_normed_two, prob_grad = head_total(
        (
            d_normed_two.reshape(block_len, seq_here, width),
            prob_grad.reshape(block_len, seq_here, top_count),
        )
    )
    d_chosen = gate_probs * (prob_grad - jnp.sum(gate_probs * prob_grad, axis=-1, keepdims=True))
    d_logits = jnp.sum(
        d_chosen[..., None] * (routes[..., None] == expert_ids).astype(jnp.float32), axis=-2
    ).astype(jnp.bfloat16)
    grad_router = outer_sum(normed_two, d_logits)
    d_normed_two = d_normed_two + flat_dot_t(d_logits, full_router)
    d_resid_norm, grad_norm2 = norm_back(d_normed_two, residual, scale_two, norm2_gain)
    d_resid = grad_out + d_resid_norm
    d_resid_low = d_resid.astype(jnp.bfloat16)
    d_mixed = flat_dot_t(d_resid_low, full_out)
    grad_out_w = outer_sum(mixed_out, d_resid_low)
    gain_scaled = d_mixed * gnorm_gain
    grad_gnorm = jnp.sum((d_mixed * gated * scale_gated).reshape(-1, inner_here), axis=0)
    cross_sum = head_total(jnp.sum(gain_scaled * gated, axis=-1, keepdims=True))
    d_gated = (
        scale_gated * gain_scaled
        - gated * scale_gated * scale_gated * scale_gated * cross_sum / INNER
    )
    d_y = d_gated * gate_z * gate_sig
    d_gate_z = (d_gated * y_flat * silu_slope(gate_z, gate_sig)).astype(jnp.bfloat16)
    d_y_heads = d_y.reshape(x_heads.shape)
    grad_skip = jnp.sum(d_y_heads * x_heads, axis=(0, 1, 3))
    log_decay = jnp.cumsum(step_size * decay_rate, axis=0)
    enters = jnp.exp(log_decay) * (doc_ids == prev_doc[None, :]).astype(jnp.float32)[..., None]
    g_local = jnp.einsum("tsh,tshp,tsn->shpn", enters, d_y_heads, c_state, precision=HIGH)
    a_after, state_grad = entering(
        (a_total, g_local), "seq", carry_combine, (ones_start, zeros_start), True
    )

    def local_scan(x_part, step_part, b_part, c_part, rate_part, state_part):
        return ssm_local(
            x_part, step_part, b_part, c_part, rate_part, state_part, doc_ids, prev_doc
        )

    _, scan_back = jax.vjp(local_scan, x_heads, step_size, b_state, c_state, decay_rate, s_before)
    d_xh, d_step, d_bstate, d_cstate, d_rate, _ = scan_back((d_y_heads, state_grad))
    d_xh = d_xh + d_skip[:, None] * d_y_heads
    d_bc = head_total(jnp.concatenate([d_bstate, d_cstate], axis=-1))
    d_dt_pre = d_step * jax.nn.sigmoid(dt_pre)
    grad_dtb = jnp.sum(d_dt_pre, axis=(0, 1))
    grad_alog = d_rate * decay_rate
    d_conv_out = jnp.concatenate([d_xh.reshape(block_len, seq_here, inner_here), d_bc], axis=-1)

    def local_conv(ext_part, weight_part, shift_part):
        return conv_apply(ext_part, docs_ext, weight_part, shift_part)

    _, conv_back = jax.vjp(local_conv, conv_ext, conv_weight, conv_shift)
    d_ext, grad_cweight, grad_cshift = conv_back(d_conv_out)
    from_next = passed_along(shortened(d_ext[:edge_len]), "seq", -1)
    d_conv_in = d_ext[edge_len:] + jnp.concatenate(
        [jnp.zeros((block_len - edge_len,) + from_next.shape[1:], jnp.float32), from_next], 0
    )
    d_proj_x = d_conv_in[..., :inner_here].astype(jnp.bfloat16)
    d_proj_bc = d_conv_in[..., inner_here:].astype(jnp.bfloat16)
    d_dt_low = d_dt_pre.astype(jnp.bfloat16)
    grad_wz = outer_sum(normed_one, d_gate_z)
    grad_wx = outer_sum(normed_one, d_proj_x)
    grad_wbc = outer_sum(normed_one, d_proj_bc)
    grad_wdt = outer_sum(normed_one, d_dt_low)
    head_first = jnp.where(lax.axis_index("head") == 0, 1.0, 0.0)
    d_normed_one = (
        flat_dot_t(d_gate_z, full_z) + flat_dot_t(d_proj_x, full_x) + flat_dot_t(d_dt_low, full_dt)
    )
    d_normed_one = head_total(d_normed_one + head_first * flat_dot_t(d_proj_bc, full_bc))
    d_x_norm, grad_norm1 = norm_back(d_normed_one, x_float, scale_one, norm1_gain)
    input_grad = d_resid + d_x_norm
    reduced = (
        lax.psum_scatter(grad_wz, "seq", scatter_dimension=0, tiled=True),
        lax.psum_scatter(grad_wx, "seq", scatter_dimension=0, tiled=True),
        lax.psum_scatter(grad_wdt, "seq", scatter_dimension=0, tiled=True),
        lax.psum_scatter(grad_wbc, "seq", scatter_dimension=0, tiled=True),
        lax.psum_scatter(grad_router, "seq", scatter_dimension=0, tiled=True),
        lax.psum_scatter(grad_sgate, "seq", scatter_dimension=0, tiled=True),
        lax.psum_scatter(grad_sup, "seq", scatter_dimension=0, tiled=True),
        lax.psum_scatter(grad_out_w, "seq", scatter_dimension=1, tiled=True),
        lax.psum_scatter(grad_sdown, "seq", scatter_dimension=1, tiled=True),
    )
    red_z, red_x, red_dt, red_bc, red_router, red_sgate, red_sup, red_out, red_sdown = reduced
    small_sums = lax.psum(
        (
            grad_norm1,
            grad_norm2,
            grad_cweight,
            grad_cshift,
            grad_dtb,
            grad_alog,
            grad_skip,
            grad_gnorm,
        ),
        "seq",
    )
    sum_norm1, sum_norm2, sum_cweight, sum_cshift, sum_dtb, sum_alog, sum_skip, sum_gnorm = (
        small_sums
    )
    return (
        block_out,
        input_grad,
        sum_norm1,
        red_z,
        red_x,
        red_bc,
        red_dt,
        sum_cweight[:, :inner_here],
        sum_cweight[:, inner_here:],
        sum_cshift[:inner_here],
        sum_cshift[inner_here:],
        sum_dtb,
        sum_alog,
        sum_skip,
        sum_gnorm,
        red_out,
        sum_norm2,
        red_router,
        red_sgate,
        red_sup,
        red_sdown,
        grad_egate,
        expert_up_gradient,
        grad_edown,
    )


MESH = pl.DeviceIdType.MESH
VMEM = pltpu.VMEM


def peers():
    here, side = lax.axis_index("seq"), lax.axis_index("head")
    x, y, z = lax.rem(here, 2), lax.rem(here // 2, 2), here // 4
    col = x + 2 * y
    return here, side, z, col, (1 - x) + 2 * y, x + 2 * (1 - y), 3 - col


def layers(z):
    lo, hi = lax.rem(z, 2), z // 2
    return [2 * (1 - hi if k & 2 else hi) + (1 - lo if k & 1 else lo) for k in range(4)]


def greet(devices):
    barrier = pltpu.get_barrier_semaphore()
    for device in devices:
        pl.semaphore_signal(barrier, inc=1, device_id=device, device_id_type=MESH)
    pl.semaphore_wait(barrier, len(devices))


class Mail:
    def __init__(self, send, base=0):
        self.send, self.sent, self.base = send, [], base

    def put(self, src, dst, sem, to):
        copy = pltpu.make_async_remote_copy(
            src_ref=src,
            dst_ref=dst,
            send_sem=self.send.at[self.base + len(self.sent)],
            recv_sem=sem,
            device_id=to,
            device_id_type=MESH,
        )
        copy.start()
        self.sent.append(copy)

    def arrived(self, dst, sem):
        pltpu.make_async_remote_copy(
            src_ref=dst,
            dst_ref=dst,
            send_sem=self.send.at[0],
            recv_sem=sem,
            device_id=(0, 0),
            device_id_type=MESH,
        ).wait_recv()

    def finish(self):
        for copy in self.sent:
            copy.wait_send()


def rows_at(ref, start, size, step):
    return ref.at[pl.ds(pl.multiple_of(start, step), size)]


def gather_steps(mail, own_ref, out_ref, recv, recv_half, rows, half):
    here, side, z, col, cx, cy, cd = peers()
    zs = layers(z)
    base = 4 * z

    def block(place):
        return rows_at(out_ref, place * rows, rows, 16)

    def part(place, which):
        size = rows - half if which else half
        return rows_at(out_ref, place * rows + which * half, size, 16)

    mail.put(own_ref, block(here), recv.at[3], (base + cx, side))
    mail.put(own_ref, block(here), recv.at[7], (base + cy, side))
    for k in (1, 2, 3):
        mail.put(own_ref, block(here), recv.at[k - 1], (4 * zs[k] + col, side))
    yield
    for k in range(4):
        if k:
            at = 4 * zs[k] + col
            mail.arrived(block(at), recv.at[k - 1])
            mail.put(block(at), block(at), recv.at[3 + k], (base + cx, side))
            mail.put(block(at), block(at), recv.at[7 + k], (base + cy, side))
            yield
        at = 4 * zs[k] + cx
        mail.arrived(block(at), recv.at[3 + k])
        mail.put(part(at, 0), part(at, 0), recv_half.at[k], (base + cy, side))
        at = 4 * zs[k] + cy
        mail.arrived(block(at), recv.at[7 + k])
        mail.put(part(at, 1), part(at, 1), recv_half.at[4 + k], (base + cx, side))
        yield
    for k in range(4):
        at = 4 * zs[k] + cd
        mail.arrived(part(at, 0), recv_half.at[k])
        mail.arrived(part(at, 1), recv_half.at[4 + k])
        yield


def near(side):
    here, side, z, col, cx, cy, cd = peers()
    zs = layers(z)
    return [(4 * z + cx, side), (4 * z + cy, side)] + [(4 * zs[k] + col, side) for k in (1, 2, 3)]


def note_puts(mail, src_of, notes_out, recv_n):
    here, side = peers()[:2]
    for k in range(1, 16):
        to = lax.rem(here + k, 16)
        mail.put(src_of(to), notes_out.at[here], recv_n.at[here], (to, side))


def note_waits(mail, notes_out, recv_n):
    here = peers()[0]
    for k in range(1, 16):
        place = lax.rem(here + k, 16)
        mail.arrived(notes_out.at[place], recv_n.at[place])


def gather_kernel(rows, own_ref, note_ref, out_ref, notes_out, send, recv, recv_half, recv_n, local):
    here, side = peers()[:2]
    greet(same_side(side, here))
    mine = pltpu.make_async_copy(own_ref, rows_at(out_ref, here * rows, rows, 16), local)
    mine.start()
    mail = Mail(send)
    steps = gather_steps(mail, own_ref, out_ref, recv, recv_half, rows, rows // 2)
    next(steps)
    notes_out[here] = note_ref[...]
    note_puts(mail, lambda to: note_ref, notes_out, recv_n)
    for _ in steps:
        pass
    note_waits(mail, notes_out, recv_n)
    mine.wait()
    mail.finish()


def gather_rows(block, note, number):
    rows, width = block.shape
    vmem = pl.BlockSpec(memory_space=VMEM)
    return pl.pallas_call(
        functools.partial(gather_kernel, rows),
        out_shape=(
            jax.ShapeDtypeStruct((16 * rows, width), block.dtype),
            jax.ShapeDtypeStruct((16,) + note.shape, note.dtype),
        ),
        in_specs=[vmem, vmem],
        out_specs=(vmem, vmem),
        scratch_shapes=[
            pltpu.SemaphoreType.DMA((34,)),
            pltpu.SemaphoreType.DMA((11,)),
            pltpu.SemaphoreType.DMA((8,)),
            pltpu.SemaphoreType.DMA((16,)),
            pltpu.SemaphoreType.DMA,
        ],
        compiler_params=pltpu.CompilerParams(
            collective_id=number, has_side_effects=True, vmem_limit_bytes=48 << 20
        ),
        name=f"gather_{number}",
    )(block, note)


def reduce_steps(mail, part_ref, out_ref, got, sums, recv, rows):
    here, side, z, col, cx, cy, cd = peers()
    zs = layers(z)
    base = 4 * z
    half = rows // 2
    got_a, got_b, got_x, got_y, got_z = got
    sum_x, sum_y, sum_z = sums
    to_x, to_y = (base + cx, side), (base + cy, side)
    f32 = jnp.float32

    def half_of(place, which):
        return rows_at(part_ref, place * rows + which * half, half, half)

    def far(k):
        at = 4 * zs[k] + cd
        mail.put(half_of(at, 0), got_a.at[k], recv.at[k], to_y)
        mail.put(half_of(at, 1), got_b.at[k], recv.at[4 + k], to_x)

    def plain(k):
        mail.put(half_of(4 * zs[k] + cx, 1), got_x.at[k, pl.ds(half, half)], recv.at[12 + k], to_x)
        mail.put(half_of(4 * zs[k] + cy, 0), got_y.at[k, pl.ds(0, half)], recv.at[16 + k], to_y)

    def joined(k):
        mail.arrived(got_a.at[k], recv.at[k])
        total = half_of(4 * zs[k] + cx, 0)[...].astype(f32) + got_a[k].astype(f32)
        sum_x[k] = total.astype(sum_x.dtype)
        mail.put(sum_x.at[k], got_x.at[k, pl.ds(0, half)], recv.at[8 + k], to_x)
        mail.arrived(got_b.at[k], recv.at[4 + k])
        total = half_of(4 * zs[k] + cy, 1)[...].astype(f32) + got_b[k].astype(f32)
        sum_y[k] = total.astype(sum_y.dtype)
        mail.put(sum_y.at[k], got_y.at[k, pl.ds(half, half)], recv.at[20 + k], to_y)

    def column(k):
        mail.arrived(got_x.at[k, pl.ds(half, half)], recv.at[12 + k])
        mail.arrived(got_y.at[k, pl.ds(0, half)], recv.at[16 + k])
        mail.arrived(got_x.at[k, pl.ds(0, half)], recv.at[8 + k])
        mail.arrived(got_y.at[k, pl.ds(half, half)], recv.at[20 + k])
        own = part_ref[pl.ds(pl.multiple_of((4 * zs[k] + col) * rows, rows), rows)].astype(f32)
        total = own + got_x[k].astype(f32) + got_y[k].astype(f32)
        if k:
            sum_z[k - 1] = total.astype(sum_z.dtype)
            mail.put(sum_z.at[k - 1], got_z.at[k - 1], recv.at[23 + k], (4 * zs[k] + col, side))
        else:
            out_ref[...] = total

    far(3)
    plain(3)
    yield
    far(2)
    plain(2)
    yield
    joined(3)
    yield
    far(1)
    plain(1)
    yield
    joined(2)
    yield
    column(3)
    yield
    far(0)
    plain(0)
    yield
    joined(1)
    yield
    column(2)
    yield
    joined(0)
    yield
    column(1)
    yield
    column(0)
    yield
    for k in (3, 2, 1):
        mail.arrived(got_z.at[k - 1], recv.at[23 + k])
        out_ref[...] += got_z[k - 1].astype(f32)


def reduce_scratch(rows, width, kind):
    half = rows // 2
    shapes = [(4, half), (4, half), (4, rows), (4, rows), (3, rows), (4, half), (4, half), (3, rows)]
    return [VMEM(shape + (width,), kind) for shape in shapes]


def reduce_kernel(rows, part_ref, note_ref, out_ref, notes_out, *refs):
    got, sums, (send, recv, recv_n) = refs[:5], refs[5:8], refs[8:]
    here, side = peers()[:2]
    greet(same_side(side, here))
    mail = Mail(send)
    steps = reduce_steps(mail, part_ref, out_ref, got, sums, recv, rows)
    next(steps)
    notes_out[here] = note_ref[here]
    note_puts(mail, lambda to: note_ref.at[to], notes_out, recv_n)
    for _ in steps:
        pass
    note_waits(mail, notes_out, recv_n)
    mail.finish()


def reduce_rows(parts, notes, number):
    rows, width = parts.shape[0] // 16, parts.shape[1]
    vmem = pl.BlockSpec(memory_space=VMEM)
    return pl.pallas_call(
        functools.partial(reduce_kernel, rows),
        out_shape=(
            jax.ShapeDtypeStruct((rows, width), jnp.float32),
            jax.ShapeDtypeStruct(notes.shape, notes.dtype),
        ),
        in_specs=[vmem, vmem],
        out_specs=(vmem, vmem),
        scratch_shapes=reduce_scratch(rows, width, parts.dtype)
        + [
            pltpu.SemaphoreType.DMA((42,)),
            pltpu.SemaphoreType.DMA((27,)),
            pltpu.SemaphoreType.DMA((16,)),
        ],
        compiler_params=pltpu.CompilerParams(
            collective_id=number, has_side_effects=True, vmem_limit_bytes=48 << 20
        ),
        name=f"reduce_{number}",
    )(parts, notes)


def same_side(side, here):
    return [(lax.rem(here + k, 16), side) for k in range(1, 16)]


def enter_kernel(
    rows,
    own_ref,
    blocks_ref,
    small_ref,
    gate_ref,
    up_ref,
    down_ref,
    all_ref,
    extra_ref,
    cols_ref,
    small_other,
    gate_other,
    up_other,
    down_other,
    send,
    recv,
    recv_half,
    recv_w,
    recv_e,
    recv_s,
    local,
):
    here, side = peers()[:2]
    places = 16
    sibling = (here, 1 - side)
    greet(same_side(side, here) + [sibling])
    depth = blocks_ref.shape[1]
    extra = rows - 64
    half_here = here // 8
    mail = Mail(send)
    mine = pltpu.make_async_copy(own_ref, rows_at(all_ref, here * rows, rows, 16), local.at[0])
    mine.start()

    def strip(place):
        return rows_at(cols_ref, place * depth, depth, 16)

    steps = gather_steps(mail, own_ref, all_ref, recv, recv_half, rows, rows // 32 * 16)
    next(steps)
    mail.put(small_ref, small_other, recv_s.at[0], sibling)
    away = []
    for k in range(1, 8):
        to = 8 * side + lax.rem(here + k, 8)
        away.append(to)
    first = 8 * side + lax.rem(here, 8)
    is_mine = side == half_here
    for k in range(1, 8):
        to = 8 * side + lax.rem(here + k, 8)
        mail.put(blocks_ref.at[to - 8 * side], strip(here), recv_w.at[here], (to, side))

    @pl.when(is_mine)
    def _():
        pltpu.make_async_copy(blocks_ref.at[here - 8 * side], strip(here), local.at[1]).start()

    @pl.when(jnp.logical_not(is_mine))
    def _():
        pltpu.make_async_remote_copy(
            src_ref=blocks_ref.at[first - 8 * side],
            dst_ref=strip(here),
            send_sem=local.at[1],
            recv_sem=recv_w.at[here],
            device_id=(first, side),
            device_id_type=MESH,
        ).start()

    mail.put(gate_ref, gate_other, recv_s.at[1], sibling)
    mail.put(up_ref, up_other, recv_s.at[2], sibling)
    mail.put(down_ref, down_other, recv_s.at[3], sibling)
    for _ in steps:
        pass
    mine.wait()
    for place in range(places):
        src = all_ref.at[pl.ds(place * rows + 64, extra)]
        mail.put(src, extra_ref.at[pl.ds(place * extra, extra)], recv_e.at[place], sibling)

    def forward(place, sem):
        return pltpu.make_async_remote_copy(
            src_ref=strip(place),
            dst_ref=strip(place),
            send_sem=local.at[2 + sem],
            recv_sem=recv_w.at[place],
            device_id=sibling,
            device_id_type=MESH,
        )

    @pl.when(is_mine)
    def _():
        pltpu.make_async_copy(blocks_ref.at[here - 8 * side], strip(here), local.at[1]).wait()
        forward(here, 0).start()

    @pl.when(jnp.logical_not(is_mine))
    def _():
        forward(here, 0).wait_recv()
        pltpu.make_async_remote_copy(
            src_ref=blocks_ref.at[first - 8 * side],
            dst_ref=strip(here),
            send_sem=local.at[1],
            recv_sem=recv_w.at[here],
            device_id=(first, side),
            device_id_type=MESH,
        ).wait_send()

    for k in range(1, places):
        place = lax.rem(here + k, places)
        forward(place, k).wait_recv()

        @pl.when(is_mine)
        def _():
            forward(place, k).start()

    @pl.when(is_mine)
    def _():
        for k in range(places):
            forward(lax.rem(here + k, places), k).wait_send()

    mail.arrived(small_other, recv_s.at[0])
    mail.arrived(gate_other, recv_s.at[1])
    mail.arrived(up_other, recv_s.at[2])
    mail.arrived(down_other, recv_s.at[3])
    for place in range(places):
        mail.arrived(extra_ref.at[pl.ds(place * extra, extra)], recv_e.at[place])
    mail.finish()


def enter(own, blocks, small, gate, up, down, number):
    rows, width = own.shape
    extra = rows - 64
    depth, cols = blocks.shape[1:]
    shape = jax.ShapeDtypeStruct
    hbm = pl.BlockSpec(memory_space=pl.ANY)
    vmem = pl.BlockSpec(memory_space=VMEM)
    return pl.pallas_call(
        functools.partial(enter_kernel, rows),
        out_shape=(
            shape((16 * rows, width), own.dtype),
            shape((16 * extra, width), own.dtype),
            shape((16 * depth, cols), blocks.dtype),
            shape(small.shape, small.dtype),
            shape(gate.shape, gate.dtype),
            shape(up.shape, up.dtype),
            shape(down.shape, down.dtype),
        ),
        in_specs=[vmem, vmem, vmem, hbm, hbm, hbm],
        out_specs=(vmem, vmem, vmem, vmem, hbm, hbm, hbm),
        scratch_shapes=[
            pltpu.SemaphoreType.DMA((46,)),
            pltpu.SemaphoreType.DMA((11,)),
            pltpu.SemaphoreType.DMA((8,)),
            pltpu.SemaphoreType.DMA((16,)),
            pltpu.SemaphoreType.DMA((16,)),
            pltpu.SemaphoreType.DMA((4,)),
            pltpu.SemaphoreType.DMA((18,)),
        ],
        compiler_params=pltpu.CompilerParams(
            collective_id=number, has_side_effects=True, vmem_limit_bytes=48 << 20
        ),
        name="enter",
    )(own, blocks, small, gate, up, down)


def leave_kernel(
    main_ref,
    bcr_ref,
    small_ref,
    main_out,
    bcr_out,
    small_out,
    got_main,
    got_bcr,
    send_main,
    send_bcr,
    bcr_parts,
    bcr_mine,
    bcr_sib,
    small_sum,
    small_got,
    send,
    recv_sib,
    recv_main,
    recv_bcr,
    recv_small,
    cond,
    local,
):
    here, side = peers()[:2]
    sibling = (here, 1 - side)
    half_here = here // 8
    is_main = side == half_here
    f32 = jnp.float32
    greet(same_side(side, here) + [sibling])
    mail = Mail(send)
    depth = main_ref.shape[1]
    mail.put(small_ref, small_got, recv_sib.at[1], sibling)

    def give_main():
        return pltpu.make_async_remote_copy(
            src_ref=main_ref,
            dst_ref=got_main,
            send_sem=cond.at[0],
            recv_sem=recv_sib.at[0],
            device_id=sibling,
            device_id_type=MESH,
        )

    def give_bcr():
        return pltpu.make_async_remote_copy(
            src_ref=bcr_ref,
            dst_ref=got_bcr,
            send_sem=cond.at[0],
            recv_sem=recv_sib.at[0],
            device_id=sibling,
            device_id_type=MESH,
        )

    def send_on(total, out, sem, slot, k):
        to = lax.rem(here + k, 16)
        return pltpu.make_async_remote_copy(
            src_ref=total.at[to],
            dst_ref=out.at[slot],
            send_sem=cond.at[k],
            recv_sem=sem.at[slot],
            device_id=(to, side),
            device_id_type=MESH,
        )

    slot = lax.rem(here, 8)

    @pl.when(is_main)
    def _():
        give_bcr().start()

    @pl.when(jnp.logical_not(is_main))
    def _():
        give_main().start()

    mail.arrived(small_got, recv_sib.at[1])
    small_sum[...] = small_ref[...] + small_got[...]
    small_out[here] = small_sum[...]
    for k in range(1, 16):
        to = lax.rem(here + k, 16)
        mail.put(small_sum, small_out.at[here], recv_small.at[here], (to, side))

    @pl.when(is_main)
    def _():
        give_main().wait_recv()
        for k in range(1, 16):
            to = lax.rem(here + k, 16)
            total = main_ref[to].astype(f32) + got_main[to].astype(f32)
            send_main[to] = total.astype(send_main.dtype)
            send_on(send_main, main_out, recv_main, slot, k).start()
        total = main_ref[here].astype(f32) + got_main[here].astype(f32)
        main_out[slot] = total.astype(main_out.dtype)

    @pl.when(jnp.logical_not(is_main))
    def _():
        give_bcr().wait_recv()
        for k in range(1, 16):
            to = lax.rem(here + k, 16)
            total = bcr_ref[to].astype(f32) + got_bcr[to].astype(f32)
            send_bcr[to] = total.astype(send_bcr.dtype)
            send_on(send_bcr, bcr_parts, recv_bcr, slot, k).start()
        total = bcr_ref[here].astype(f32) + got_bcr[here].astype(f32)
        bcr_parts[slot] = total.astype(bcr_parts.dtype)

    for j in range(8):
        from_main = 8 * side + j
        from_bcr = 8 * (1 - side) + j

        @pl.when(from_bcr != here)
        def _():
            mail.arrived(bcr_parts.at[j], recv_bcr.at[j])

    total = bcr_parts[0].astype(f32)
    for j in range(1, 8):
        total = total + bcr_parts[j].astype(f32)
    bcr_mine[...] = total
    mail.put(bcr_mine, bcr_sib, recv_sib.at[2], sibling)
    for j in range(8):
        from_main = 8 * side + j

        @pl.when(from_main != here)
        def _():
            mail.arrived(main_out.at[j], recv_main.at[j])

    for k in range(1, 16):
        place = lax.rem(here + k, 16)
        mail.arrived(small_out.at[place], recv_small.at[place])
    mail.arrived(bcr_sib, recv_sib.at[2])
    bcr_out[...] = bcr_mine[...] + bcr_sib[...]

    @pl.when(is_main)
    def _():
        give_bcr().wait_send()
        for k in range(1, 16):
            send_on(send_main, main_out, recv_main, slot, k).wait_send()

    @pl.when(jnp.logical_not(is_main))
    def _():
        give_main().wait_send()
        for k in range(1, 16):
            send_on(send_bcr, bcr_parts, recv_bcr, slot, k).wait_send()

    mail.finish()


def leave(main, bcr, small, number):
    shape = jax.ShapeDtypeStruct
    vmem = pl.BlockSpec(memory_space=VMEM)
    low = jnp.bfloat16
    return pl.pallas_call(
        leave_kernel,
        out_shape=(
            shape((8,) + main.shape[1:], low),
            shape(bcr.shape[1:], jnp.float32),
            shape((16,) + small.shape, jnp.float32),
        ),
        in_specs=[vmem] * 3,
        out_specs=(vmem, vmem, vmem),
        scratch_shapes=[
            VMEM(main.shape, low),
            VMEM(bcr.shape, low),
            VMEM(main.shape, low),
            VMEM(bcr.shape, low),
            VMEM((8,) + bcr.shape[1:], low),
            VMEM(bcr.shape[1:], jnp.float32),
            VMEM(bcr.shape[1:], jnp.float32),
            VMEM(small.shape, jnp.float32),
            VMEM(small.shape, jnp.float32),
            pltpu.SemaphoreType.DMA((17,)),
            pltpu.SemaphoreType.DMA((3,)),
            pltpu.SemaphoreType.DMA((8,)),
            pltpu.SemaphoreType.DMA((8,)),
            pltpu.SemaphoreType.DMA((16,)),
            pltpu.SemaphoreType.DMA((16,)),
            pltpu.SemaphoreType.DMA,
        ],
        compiler_params=pltpu.CompilerParams(
            collective_id=number, has_side_effects=True, vmem_limit_bytes=56 << 20
        ),
        name="leave",
    )(main, bcr, small)


def swap_kernel(count, *refs):
    own, other, (send, recv) = refs[:count], refs[count : 2 * count], refs[2 * count :]
    here, side = peers()[:2]
    greet([(here, 1 - side)])
    mail = Mail(send)
    for i in range(count):
        mail.put(own[i], other[i], recv.at[i], (here, 1 - side))
    for i in range(count):
        mail.arrived(other[i], recv.at[i])
    mail.finish()


def swap(arrays, number):
    count = len(arrays)
    hbm = pl.BlockSpec(memory_space=pl.ANY)
    return pl.pallas_call(
        functools.partial(swap_kernel, count),
        out_shape=tuple(jax.ShapeDtypeStruct(a.shape, a.dtype) for a in arrays),
        in_specs=[hbm] * count,
        out_specs=(hbm,) * count,
        scratch_shapes=[
            pltpu.SemaphoreType.DMA((count,)),
            pltpu.SemaphoreType.DMA((count,)),
        ],
        compiler_params=pltpu.CompilerParams(collective_id=number, has_side_effects=True),
        name=f"swap_{number}",
    )(*arrays)


def chunked(array, chunk):
    return array.reshape((array.shape[0] // chunk, chunk) + array.shape[1:])


def scan_core(x_heads, step_size, b_state, c_state, decay_rate, doc_ids, chunk):
    length = doc_ids.shape[0]
    prev_all = jnp.concatenate([doc_ids[:1], doc_ids[:-1]], 0)
    docs, prev = chunked(doc_ids, chunk), chunked(prev_all, chunk)[:, :1]
    x_c, step_c = chunked(x_heads, chunk), chunked(step_size, chunk)
    b_c, c_c = chunked(b_state, chunk), chunked(c_state, chunk)
    logs = jnp.cumsum(step_c * decay_rate, axis=1)
    causal = jnp.arange(chunk)[:, None] >= jnp.arange(chunk)[None, :]
    pair = causal[None] & (docs[:, :, None] == docs[:, None, :])
    logs_h = logs.transpose(0, 2, 1)
    gap = logs_h[:, :, :, None] - logs_h[:, :, None, :]
    table = jnp.exp(jnp.where(pair[:, None], gap, 0.0)) * pair[:, None].astype(jnp.float32)
    cross = jnp.einsum("gtn,gun->gtu", c_c, b_c, precision=HIGH)
    weights = table * cross[:, None] * step_c.transpose(0, 2, 1)[:, :, None, :]
    intra = jnp.einsum("ghtu,guhp->gthp", weights, x_c, precision=HIGH)
    enters = jnp.exp(logs) * (docs == prev).astype(jnp.float32)[..., None]
    end_keep = (docs == docs[:, -1:]).astype(jnp.float32)
    tail = jnp.exp(logs[:, -1:] - logs) * end_keep[..., None] * step_c
    local = jnp.einsum("gth,gthp,gtn->ghpn", tail, x_c, b_c, precision=HIGH)
    keep = enters[:, -1]
    state = jnp.zeros_like(local[0])
    before = []
    for group in range(length // chunk):
        before.append(state)
        state = keep[group][:, None, None] * state + local[group]
    before = jnp.stack(before)
    inter = jnp.einsum("gtn,ghpn->gthp", c_c, before, precision=HIGH) * enters[..., None]
    return (intra + inter).reshape(x_heads.shape)


def by_heads(
    hidden_in,
    doc_ids,
    routes,
    norm1_gain,
    w_z,
    w_x,
    w_bc,
    w_dt,
    conv_x,
    conv_bc,
    convb_x,
    convb_bc,
    dt_bias,
    a_log,
    d_skip,
    gnorm_gain,
    w_out,
    norm2_gain,
    router,
    shared_gate,
    shared_up,
    shared_down,
    expert_gate,
    expert_up,
    expert_down,
    cotangent,
):
    places = lax.axis_size("seq")
    here, side = lax.axis_index("seq"), lax.axis_index("head")
    block_len, _, width = hidden_in.shape
    length = block_len * places
    heads_all = 2 * dt_bias.shape[0]
    heads = heads_all // places
    inner = 2 * convb_x.shape[0]
    chans = inner // places
    head_size = chans // heads
    state = convb_bc.shape[0] // 2
    shared_all = 2 * shared_gate.shape[1]
    shared = shared_all // places
    experts = router.shape[1]
    top_count = routes.shape[-1]
    hidden = 2 * expert_gate.shape[2]

    half_here, slot = here // 8, lax.rem(here, 8)
    low, f32 = jnp.bfloat16, jnp.float32

    def mine_of(own, other):
        return jnp.where(side == half_here, own, other)

    def ordered(own, other, axis):
        pair = jnp.where(side == 0, jnp.stack([own, other], axis), jnp.stack([other, own], axis))
        return pair

    def padded(array, rows):
        flat = array.reshape(-1)
        return jnp.pad(flat, (0, rows * width - flat.shape[0])).reshape(rows, width)

    x_own = lax.dynamic_index_in_dim(hidden_in, side, 1, False).astype(f32)
    g_own = lax.dynamic_index_in_dim(cotangent, side, 1, False)
    scale_one = lax.rsqrt(jnp.mean(x_own * x_own, axis=-1, keepdims=True) + EPS)
    n1_own = (x_own * scale_one * norm1_gain).astype(low)
    ids = jnp.concatenate([doc_ids[:, :, None], routes], 2)
    ids = lax.dynamic_index_in_dim(ids, side, 1, False)
    bc_half = lax.dynamic_slice_in_dim(w_bc, side * state, state, 1)
    own_rows = jnp.concatenate(
        [
            n1_own,
            bc_half.reshape(8, width),
            router.reshape(1, width),
            padded(w_dt, 2),
            padded(ids.astype(low), 1),
            jnp.zeros((4, width), low),
        ],
        0,
    )
    blocks = jnp.concatenate(
        [
            part.reshape(part.shape[0], 8, part.shape[1] // 8)
            for part in (w_z, w_x, shared_gate, shared_up, w_out.T, shared_down.T)
        ],
        2,
    ).transpose(1, 0, 2)
    small = jnp.concatenate(
        [
            conv_x,
            convb_x[None],
            gnorm_gain[None],
            jnp.pad(jnp.concatenate([dt_bias, a_log, d_skip]), (0, width - 72))[None],
            jnp.zeros((1, width), f32),
        ],
        0,
    )
    eg, eu, ed = expert_gate[0], expert_up[0], expert_down[0]
    all_rows, extra_sib, cols, small_sib, eg_o, eu_o, ed_o = enter(
        own_rows, blocks, small, eg, eu, ed, 1
    )
    all_rows = all_rows.reshape(places, 80, width)
    extra_sib = extra_sib.reshape(places, 16, width)
    n1 = all_rows[:, :block_len].reshape(length, width)
    extra_own = all_rows[:, block_len:]
    wbc = ordered(
        extra_own[:, :8].reshape(width, state), extra_sib[:, :8].reshape(width, state), 1
    ).reshape(width, 2 * state)
    wrouter = extra_own[:, 8].reshape(width, experts)
    wdt = mine_of(extra_own[:, 9:11], extra_sib[:, 9:11]).reshape(places, 2 * width)
    wdt = wdt[:, : w_dt.shape[0] * w_dt.shape[1]].reshape(width, w_dt.shape[1])
    wdt = lax.dynamic_slice_in_dim(wdt, slot * heads, heads, 1)
    ids = extra_own[:, 11, : block_len * 7].reshape(length, 7).astype(jnp.int32)
    docs, picks = ids[:, 0], ids[:, 1:]
    small = mine_of(small, small_sib)
    wide_small = lax.dynamic_slice_in_dim(small, slot * chans, chans, 1)
    taps = jnp.concatenate([wide_small[:KER], conv_bc], 1)
    shift = jnp.concatenate([wide_small[KER], convb_bc], 0)
    gn_gain = wide_small[KER + 1]
    head_params = small[KER + 2, :72].reshape(3, 24)
    head_params = lax.dynamic_slice_in_dim(head_params, slot * heads, heads, 1)
    bias_dt, rate_log, skip = head_params[0], head_params[1], head_params[2]
    wz, wx, sg, su = cols[:, :192], cols[:, 192:384], cols[:, 384:448], cols[:, 448:512]
    wout_t, sd_t = cols[:, 512:704], cols[:, 704:768]

    def note(values):
        return jnp.pad(values.reshape(1, block_len), ((0, 7), (0, 128 - block_len)))

    def notes(values):
        return jnp.pad(
            values.reshape(places, 1, block_len), ((0, 0), (0, 7), (0, 128 - block_len))
        )

    def noted(array):
        return array[:, 0, :block_len]

    win = jnp.concatenate([wz, wx, wbc, wdt], 1)
    proj = flat_dot(n1, win)
    gate_z = proj[:, :chans]
    conv_in = proj[:, chans : 2 * chans + 2 * state]
    dt_pre = proj[:, 2 * chans + 2 * state :] + bias_dt
    conv_ext = jnp.concatenate([jnp.zeros((KER - 1, conv_in.shape[1]), jnp.float32), conv_in], 0)
    docs_ext = jnp.concatenate([jnp.full((KER - 1,), -1, jnp.int32), docs], 0)

    def local_conv(ext_part, weight_part, shift_part):
        return conv_apply(ext_part, docs_ext, weight_part, shift_part)

    conv_out, conv_back = jax.vjp(local_conv, conv_ext, taps, shift)
    x_heads = conv_out[:, :chans].reshape(length, heads, head_size)
    b_state = conv_out[:, chans : chans + state]
    c_state = conv_out[:, chans + state :]
    step_size = jax.nn.softplus(dt_pre)
    decay_rate = -jnp.exp(rate_log)

    def local_scan(x_part, step_part, b_part, c_part, rate_part):
        return scan_core(x_part, step_part, b_part, c_part, rate_part, docs, 128)

    core, scan_back = jax.vjp(local_scan, x_heads, step_size, b_state, c_state, decay_rate)
    y_flat = (core + skip[:, None] * x_heads).reshape(length, chans)
    gate_sig = jax.nn.sigmoid(gate_z)
    gated = y_flat * gate_z * gate_sig
    gained = (gated * gn_gain).astype(jnp.bfloat16)
    out_part = flat_dot_t(gained, wout_t)
    out_sum, squares = reduce_rows(out_part.astype(low), notes(jnp.sum(gated * gated, axis=-1)), 2)
    scale_own = lax.rsqrt(jnp.sum(noted(squares), axis=0) / inner + EPS)[:, None]
    out_own = scale_own * out_sum
    residual = x_own + out_own

    scale_two = lax.rsqrt(jnp.mean(residual * residual, axis=-1, keepdims=True) + EPS)
    n2_own = (residual * scale_two * norm2_gain).astype(jnp.bfloat16)
    n2, scale_gated = gather_rows(n2_own, note(scale_own), 3)
    scale_gated = noted(scale_gated).reshape(length, 1)
    g_all, _ = gather_rows(g_own, note(scale_own), 4)
    wup = jnp.concatenate([eg, eg_o, sg, eu, eu_o, su], 1)
    wdown = jnp.concatenate([ed, ed_o, sd_t.T], 0)
    wide = hidden + shared
    logits = flat_dot(n2, wrouter)
    named = jnp.sum((picks[:, :, None] == jnp.arange(experts)).astype(jnp.float32), axis=1)
    top = jnp.max(jnp.where(named > 0, logits, -jnp.inf), axis=-1, keepdims=True)
    raised = jnp.exp(jnp.where(named > 0, logits - top, 0.0)) * named
    probs = raised / jnp.sum(raised, axis=-1, keepdims=True)
    prob = lax.dynamic_slice_in_dim(probs, here, 1, 1)
    col_prob = jnp.concatenate(
        [jnp.broadcast_to(prob, (length, hidden)), jnp.ones((length, shared), jnp.float32)], 1
    )
    hid = flat_dot(n2, wup)
    h_gate, h_up = hid[:, :wide], hid[:, wide:]
    h_sig = jax.nn.sigmoid(h_gate)
    act = h_gate * h_sig * h_up
    act_low = (act * col_prob).astype(jnp.bfloat16)
    moe_part = flat_dot(act_low, wdown)
    block_sum, _ = reduce_rows(moe_part.astype(low), notes(jnp.zeros((length,), f32)), 5)
    block_own = residual + block_sum

    d_act = flat_dot_t(g_all, wdown)
    prob_grad = jnp.sum((act * d_act)[:, :hidden], axis=-1)
    d_act = d_act * col_prob
    d_up = d_act * h_gate * h_sig
    d_gate = d_act * h_up * silu_slope(h_gate, h_sig)
    d_hid = jnp.concatenate([d_gate, d_up], 1).astype(jnp.bfloat16)
    grad_down = outer_sum(act_low, g_all)
    grad_up = outer_sum(n2, d_hid)
    dn2_part = flat_dot_t(d_hid, wup)
    dn2, prob_grads = reduce_rows(dn2_part.astype(low), notes(prob_grad), 6)
    prob_grads = noted(prob_grads).T
    probs_own = lax.dynamic_slice_in_dim(probs, here * block_len, block_len, 0)
    d_logits = (
        probs_own * (prob_grads - jnp.sum(probs_own * prob_grads, axis=-1, keepdims=True))
    ).astype(jnp.bfloat16)
    grad_router = outer_sum(n2_own, d_logits)
    dn2 = dn2 + flat_dot_t(d_logits, wrouter)
    d_norm, grad_norm2 = norm_back(dn2, residual, scale_two, norm2_gain)
    d_res = g_own.astype(jnp.float32) + d_norm
    d_res_low = d_res.astype(jnp.bfloat16)

    cross_own = jnp.sum(d_res_low.astype(jnp.float32) * out_own, axis=-1, keepdims=True) / scale_own
    d_res_all, cross = gather_rows(d_res_low, note(cross_own), 7)
    cross = noted(cross).reshape(length, 1)
    d_mixed = flat_dot(d_res_all, wout_t)
    mixed_out = (gated * scale_gated * gn_gain).astype(jnp.bfloat16)
    grad_out_t = outer_sum(d_res_all, mixed_out)
    grad_gnorm = jnp.sum(d_mixed * gated * scale_gated, axis=0)
    d_gated = scale_gated * gn_gain * d_mixed - gated * (
        scale_gated * scale_gated * scale_gated * cross / inner
    )
    d_y = d_gated * gate_z * gate_sig
    d_z = (d_gated * y_flat * silu_slope(gate_z, gate_sig)).astype(jnp.bfloat16)
    d_y_heads = d_y.reshape(x_heads.shape)
    grad_skip = jnp.sum(d_y_heads * x_heads, axis=(0, 2))
    d_xh, d_step, d_b, d_c, d_rate = scan_back(d_y_heads)
    d_xh = d_xh + skip[:, None] * d_y_heads
    d_dt = d_step * jax.nn.sigmoid(dt_pre)
    grad_dtb = jnp.sum(d_dt, axis=0)
    grad_alog = d_rate * decay_rate
    d_conv = jnp.concatenate([d_xh.reshape(length, chans), d_b, d_c], 1)
    d_ext, grad_taps, grad_shift = conv_back(d_conv)
    d_in = jnp.concatenate(
        [d_z, d_ext[KER - 1 :].astype(jnp.bfloat16), d_dt.astype(jnp.bfloat16)], 1
    )
    grad_in = outer_sum(n1, d_in)
    dn1, _ = reduce_rows(flat_dot_t(d_in, win).astype(low), notes(jnp.zeros((length,), f32)), 8)
    d_x, grad_norm1 = norm_back(dn1, x_own, scale_one, norm1_gain)
    input_own = d_res + d_x

    grads = jnp.concatenate(
        [
            grad_in[:, : 2 * chans],
            grad_up[:, hidden:wide],
            grad_up[:, wide + hidden :],
            grad_out_t,
            grad_down[hidden:].T,
        ],
        1,
    ).astype(low)
    main = grads.reshape(places, 96, 768)
    bcr = jnp.concatenate(
        [
            grad_in[:, 2 * chans : 2 * chans + 2 * state].reshape(places, 96, 256),
            grad_router.reshape(places, 6, 256),
            jnp.zeros((places, 10, 256), f32),
        ],
        1,
    ).astype(low)
    grad_wdt = grad_in[:, 2 * chans + 2 * state :]
    singles = jnp.concatenate(
        [
            grad_norm1,
            grad_norm2,
            grad_taps[:, chans:].reshape(-1),
            grad_shift[chans:],
            grad_taps[:, :chans].reshape(-1),
            grad_shift[:chans],
            grad_gnorm,
            grad_dtb,
            grad_alog,
            grad_skip,
            grad_wdt.reshape(-1),
        ]
    )
    singles = jnp.pad(singles, (0, 88 * 128 - singles.shape[0])).reshape(88, 128)
    main, bcr, singles = leave(main, bcr, singles, 9)
    singles = singles.reshape(places, -1)
    sums = jnp.sum(singles[:, :4352], axis=0)
    sums = jnp.split(sums, [1536, 3072, 4096])
    lists = lax.dynamic_slice_in_dim(singles, 8 * side, 8, 0)[:, 4352:]
    lists = jnp.split(lists, [768, 960, 1152, 1155, 1158, 1161, 1161 + 4608], axis=1)

    def joined(part):
        return part.transpose(1, 0, 2).reshape(part.shape[1], -1)

    main = main.astype(f32)
    bc_sum = bcr[:96]
    router_sum = bcr[96:102].reshape(96, experts)
    wdt_sum = joined(lists[6].reshape(8, width, heads))
    wdt_sum = lax.dynamic_slice_in_dim(wdt_sum, here * 96, 96, 0)
    other = swap(
        (
            block_own,
            input_own,
            grad_up[:, 256:512].astype(low),
            grad_up[:, wide + 256 : wide + 512].astype(low),
            grad_down[256:512].astype(low),
        ),
        10,
    )
    return (
        ordered(block_own, other[0], 1),
        ordered(input_own, other[1], 1),
        sums[0],
        joined(main[:, :, :192]),
        joined(main[:, :, 192:384]),
        bc_sum,
        wdt_sum,
        joined(lists[0].reshape(8, KER, chans)),
        sums[2].reshape(KER, 2 * state),
        lists[1].reshape(-1),
        sums[3],
        lists[3].reshape(-1),
        lists[4].reshape(-1),
        lists[5].reshape(-1),
        lists[2].reshape(-1),
        joined(main[:, :, 512:704]).T,
        sums[1],
        router_sum,
        joined(main[:, :, 384:448]),
        joined(main[:, :, 448:512]),
        joined(main[:, :, 704:768]).T,
        (grad_up[:, :256] + other[2].astype(f32))[None],
        (grad_up[:, wide : wide + 256] + other[3].astype(f32))[None],
        (grad_down[:256] + other[4].astype(f32))[None],
    )


def solution(mesh):
    places = mesh.shape["seq"]
    whole_heads = places == 16 and mesh.shape["head"] == 2
    placed = (
        P("seq", None, None),
        P("seq", None),
        P("seq", None, None),
        P(),
        P("seq", "head"),
        P("seq", "head"),
        P("seq", None),
        P("seq", "head"),
        P(None, "head"),
        P(),
        P("head"),
        P(),
        P("head"),
        P("head"),
        P("head"),
        P("head"),
        P("head", "seq"),
        P(),
        P("seq", None),
        P("seq", "head"),
        P("seq", "head"),
        P("head", "seq"),
        P("seq", None, "head"),
        P("seq", None, "head"),
        P("seq", "head", None),
        P("seq", None, None),
    )
    return jax.shard_map(
        by_heads if whole_heads else on_device,
        mesh=mesh,
        in_specs=placed,
        out_specs=(
            P("seq", None, None),
            P("seq", None, None),
            P(),
            P("seq", "head"),
            P("seq", "head"),
            P("seq", None),
            P("seq", "head"),
            P(None, "head"),
            P(),
            P("head"),
            P(),
            P("head"),
            P("head"),
            P("head"),
            P("head"),
            P("head", "seq"),
            P(),
            P("seq", None),
            P("seq", "head"),
            P("seq", "head"),
            P("head", "seq"),
            P("seq", None, "head"),
            P("seq", None, "head"),
            P("seq", "head", None),
        ),
        check_vma=False,
    )
```

```python
import functools

import jax
import jax.numpy as jnp
from jax import lax
from jax.experimental import pallas as pl
from jax.experimental.pallas import tpu as pltpu
from jax.sharding import PartitionSpec as P

KER = 4
INNER = 3072


EPS = 1e-05
HIGH = lax.Precision.HIGHEST


def passed_along(array, axis, by):
    length = lax.axis_size(axis)
    pairs = [(i, i + by) for i in range(length) if 0 <= i + by < length]
    return lax.ppermute(array, axis, pairs)


def entering(array, axis, combine, identity, reverse):
    length, here = (lax.axis_size(axis), lax.axis_index(axis))
    everything = jax.tree.map(
        lambda part, kind: lax.all_gather(part.astype(kind), axis),
        array,
        jax.tree.map(lambda a: jnp.bfloat16 if a.dtype == jnp.float32 else a.dtype, array),
    )
    start = jax.tree.map(
        lambda part, zero: jnp.broadcast_to(jnp.asarray(zero, part.dtype), part.shape),
        array,
        identity,
    )

    def hop(k, before):
        at = length - 1 - k if reverse else k
        reached = at > here if reverse else at < here
        new = combine(
            before, jax.tree.map(lambda part, own: part[at].astype(own.dtype), everything, array)
        )
        return jax.tree.map(lambda a, b: jnp.where(reached, a, b), new, before)

    return lax.fori_loop(0, length, hop, start)


def shortened(array):

    def short(part):
        return part.astype(jnp.bfloat16) if part.dtype == jnp.float32 else part

    return jax.tree.map(short, array)


def conv_apply(conv_ext, docs_ext, weight, conv_bias):
    length_here = conv_ext.shape[0] - (KER - 1)
    running = conv_bias
    for offset in range(KER):
        same_doc = (docs_ext[offset : offset + length_here] == docs_ext[KER - 1 :]).astype(
            jnp.float32
        )
        running = (
            running + weight[offset] * conv_ext[offset : offset + length_here] * same_doc[..., None]
        )
    return jax.nn.silu(running)


def group_parts(x_heads, step_size, b_state, decay_rate, doc_ids, prev_doc):
    log_decay = jnp.cumsum(step_size * decay_rate, axis=0)
    end_keep = (doc_ids == doc_ids[-1:]).astype(jnp.float32)
    weight = jnp.exp(log_decay[-1:] - log_decay) * end_keep[..., None] * step_size
    s_local = jnp.einsum("tsh,tshp,tsn->shpn", weight, x_heads, b_state, precision=HIGH)
    a_total = jnp.exp(log_decay[-1]) * (doc_ids[-1] == prev_doc).astype(jnp.float32)[:, None]
    return (s_local, a_total)


def group_output(x_heads, step_size, b_state, c_state, decay_rate, doc_ids, prev_doc, s_in):
    length_here = x_heads.shape[0]
    log_decay = jnp.cumsum(step_size * decay_rate, axis=0)
    causal = jnp.arange(length_here)[:, None] >= jnp.arange(length_here)[None, :]
    pair_mask = (causal[:, :, None] & (doc_ids[:, None, :] == doc_ids[None, :, :])).astype(
        jnp.float32
    )
    gap_decay = log_decay[:, None] - log_decay[None, :]
    decay_table = (
        jnp.exp(jnp.where(pair_mask[..., None] > 0, gap_decay, 0.0)) * pair_mask[..., None]
    )
    cross_dot = jnp.einsum("tsn,usn->tus", c_state, b_state, precision=HIGH)
    y_intra = jnp.einsum(
        "tush,ush,ushp->tshp",
        decay_table * cross_dot[..., None],
        step_size,
        x_heads,
        precision=HIGH,
    )
    enters = jnp.exp(log_decay) * (doc_ids == prev_doc[None, :]).astype(jnp.float32)[..., None]
    y_inter = jnp.einsum("tsn,shpn->tshp", c_state, s_in, precision=HIGH) * enters[..., None]
    return y_intra + y_inter


def ssm_local(x_heads, step_size, b_state, c_state, decay_rate, s_in, doc_ids, prev_doc):
    y_core = group_output(x_heads, step_size, b_state, c_state, decay_rate, doc_ids, prev_doc, s_in)
    s_local, a_total = group_parts(x_heads, step_size, b_state, decay_rate, doc_ids, prev_doc)
    return (y_core, a_total[..., None, None] * s_in + s_local)


def carry_combine(earlier, later_part):
    return (earlier[0] * later_part[0], later_part[0][..., None, None] * earlier[1] + later_part[1])


def head_total(partial_sum):
    return lax.psum(partial_sum, "head")


def flat_dot(left_side, right_side):
    lead_dims = left_side.shape[:-1]
    product = jnp.dot(
        left_side.reshape(-1, left_side.shape[-1]), right_side, preferred_element_type=jnp.float32
    )
    return product.reshape(lead_dims + (right_side.shape[-1],))


def flat_dot_t(left_side, right_side):
    lead_dims = left_side.shape[:-1]
    product = lax.dot_general(
        left_side.reshape(-1, left_side.shape[-1]),
        right_side,
        (((1,), (1,)), ((), ())),
        preferred_element_type=jnp.float32,
    )
    return product.reshape(lead_dims + (right_side.shape[0],))


def outer_sum(left_side, right_side):
    return lax.dot_general(
        left_side.reshape(-1, left_side.shape[-1]),
        right_side.reshape(-1, right_side.shape[-1]),
        (((0,), (0,)), ((), ())),
        preferred_element_type=jnp.float32,
    )


def silu_slope(values, sigmoid_of):
    return sigmoid_of * (1.0 + values * (1.0 - sigmoid_of))


def norm_back(grad_normed, values, scale_of, gain):
    scaled_grad = grad_normed * gain
    gain_grad = jnp.sum((grad_normed * values * scale_of).reshape(-1, values.shape[-1]), axis=0)
    cube = scale_of * scale_of * scale_of
    value_grad = scale_of * scaled_grad - values * cube * jnp.mean(
        scaled_grad * values, axis=-1, keepdims=True
    )
    return (value_grad, gain_grad)


def on_device(
    hidden_in,
    doc_ids,
    routes,
    norm1_gain,
    w_z,
    w_x,
    w_bc,
    w_dt,
    conv_x,
    conv_bc,
    convb_x,
    convb_bc,
    dt_bias,
    a_log,
    d_skip,
    gnorm_gain,
    w_out,
    norm2_gain,
    router,
    shared_gate,
    shared_up,
    shared_down,
    expert_gate,
    expert_up,
    expert_down,
    cotangent,
):
    block_len, seq_here, width = hidden_in.shape
    top_count = routes.shape[-1]
    heads_here = dt_bias.shape[0]
    inner_here = convb_x.shape[0]
    head_size = inner_here // heads_here
    state_size = convb_bc.shape[0] // 2
    seq_count = lax.axis_size("seq")
    local_experts = expert_gate.shape[0]
    experts_all = local_experts * seq_count
    tok_here = block_len * seq_here
    capacity = 2 * tok_here * top_count // experts_all
    edge_len = KER - 1
    x_float = hidden_in.astype(jnp.float32)
    scale_one = lax.rsqrt(jnp.mean(x_float * x_float, axis=-1, keepdims=True) + EPS)
    normed_one = (x_float * scale_one * norm1_gain).astype(jnp.bfloat16)
    gathered = (
        lax.all_gather(w_z, "seq", axis=0, tiled=True),
        lax.all_gather(w_x, "seq", axis=0, tiled=True),
        lax.all_gather(w_dt, "seq", axis=0, tiled=True),
        lax.all_gather(w_bc, "seq", axis=0, tiled=True),
        lax.all_gather(router, "seq", axis=0, tiled=True),
        lax.all_gather(shared_gate, "seq", axis=0, tiled=True),
        lax.all_gather(shared_up, "seq", axis=0, tiled=True),
        lax.all_gather(w_out, "seq", axis=1, tiled=True),
        lax.all_gather(shared_down, "seq", axis=1, tiled=True),
    )
    full_z, full_x, full_dt, full_bc, full_router, full_sgate, full_sup, full_out, full_sdown = (
        gathered
    )
    gate_z = flat_dot(normed_one, full_z)
    proj_x = flat_dot(normed_one, full_x)
    proj_bc = flat_dot(normed_one, full_bc)
    dt_pre = flat_dot(normed_one, full_dt) + dt_bias
    conv_in = jnp.concatenate([proj_x, proj_bc], axis=-1)
    tail_in, tail_doc = (
        passed_along(conv_in[block_len - edge_len :].astype(jnp.bfloat16), "seq", 1).astype(
            jnp.float32
        ),
        passed_along(
            doc_ids[block_len - edge_len :].astype(jnp.float32).astype(jnp.bfloat16), "seq", 1
        ).astype(jnp.float32),
    )
    conv_ext = jnp.concatenate([tail_in, conv_in], 0)
    docs_ext = jnp.concatenate([tail_doc.astype(jnp.int32), doc_ids], 0)
    conv_weight = jnp.concatenate([conv_x, conv_bc], -1)
    conv_shift = jnp.concatenate([convb_x, convb_bc], -1)
    conv_out = conv_apply(conv_ext, docs_ext, conv_weight, conv_shift)
    x_heads = conv_out[..., :inner_here].reshape(block_len, seq_here, heads_here, head_size)
    b_state = conv_out[..., inner_here : inner_here + state_size]
    c_state = conv_out[..., inner_here + state_size :]
    step_size = jax.nn.softplus(dt_pre)
    decay_rate = -jnp.exp(a_log)
    prev_doc = docs_ext[edge_len - 1]
    s_local, a_total = group_parts(x_heads, step_size, b_state, decay_rate, doc_ids, prev_doc)
    ones_start = jnp.ones_like(a_total)
    zeros_start = jnp.zeros_like(s_local)
    a_before, s_before = entering(
        (a_total, s_local), "seq", carry_combine, (ones_start, zeros_start), False
    )
    y_core = group_output(
        x_heads, step_size, b_state, c_state, decay_rate, doc_ids, prev_doc, s_before
    )
    y_heads = y_core + d_skip[:, None] * x_heads
    y_flat = y_heads.reshape(block_len, seq_here, inner_here)
    gate_sig = jax.nn.sigmoid(gate_z)
    gated = y_flat * gate_z * gate_sig
    square_sum = head_total(jnp.sum(gated * gated, axis=-1, keepdims=True))
    scale_gated = lax.rsqrt(square_sum / INNER + EPS)
    mixed_out = (gated * scale_gated * gnorm_gain).astype(jnp.bfloat16)
    residual = x_float + head_total(flat_dot(mixed_out, full_out))
    scale_two = lax.rsqrt(jnp.mean(residual * residual, axis=-1, keepdims=True) + EPS)
    normed_two = (residual * scale_two * norm2_gain).astype(jnp.bfloat16)
    logits = flat_dot(normed_two, full_router)
    gate_probs = jax.nn.softmax(jnp.take_along_axis(logits, routes, axis=-1), axis=-1)
    share_gate = flat_dot(normed_two, full_sgate)
    share_up = flat_dot(normed_two, full_sup)
    share_sig = jax.nn.sigmoid(share_gate)
    share_act = (share_gate * share_sig * share_up).astype(jnp.bfloat16)
    share_part = flat_dot(share_act, full_sdown)
    slot_total = tok_here * top_count
    route_flat = routes.reshape(slot_total)
    expert_ids = jnp.arange(experts_all, dtype=jnp.int32)
    route_hits = (route_flat[:, None] == expert_ids[None, :]).astype(jnp.int32)
    slot_rank = jnp.sum(jnp.cumsum(route_hits, axis=0) * route_hits, axis=1) - 1
    target = route_flat * capacity + slot_rank
    entry_table = (
        jnp.zeros((experts_all * capacity,), jnp.int32)
        .at[target]
        .set(jnp.arange(slot_total, dtype=jnp.int32) + 1)
    )
    entry_live = entry_table > 0
    entry_slot = jnp.maximum(entry_table - 1, 0)
    entry_token = entry_slot // top_count
    tokens_flat = normed_two.reshape(tok_here, width)
    send_rows = jnp.where(
        entry_live[:, None], tokens_flat[entry_token], jnp.zeros((), jnp.bfloat16)
    ).reshape(experts_all, capacity, width)
    received = lax.all_to_all(send_rows, "seq", split_axis=0, concat_axis=0, tiled=True)
    input_row_block = received.reshape(seq_count, local_experts, received.shape[1], width)
    hid_gate = jnp.einsum(
        "jecd,edf->jecf", input_row_block, expert_gate, preferred_element_type=jnp.float32
    )
    hid_up = jnp.einsum(
        "jecd,edf->jecf", input_row_block, expert_up, preferred_element_type=jnp.float32
    )
    hid_act = (hid_gate * jax.nn.sigmoid(hid_gate) * hid_up).astype(jnp.bfloat16)
    half_out = jnp.einsum(
        "jecf,efd->jecd", hid_act, expert_down, preferred_element_type=jnp.float32
    ).astype(jnp.bfloat16)
    returned_rows = lax.all_to_all(
        half_out.reshape(received.shape), "seq", split_axis=0, concat_axis=0, tiled=True
    )
    kept_shape = (seq_count * local_experts, received.shape[1], hid_gate.shape[-1])
    returned_rows, rows_kept, gate_kept, up_kept = (
        returned_rows,
        received,
        hid_gate.reshape(kept_shape),
        hid_up.reshape(kept_shape),
    )
    slot_rows = returned_rows.reshape(-1, width)[target].reshape(tok_here, top_count, width)
    probs_flat = gate_probs.reshape(tok_here, top_count)
    routed_part = share_part.reshape(tok_here, width)
    for slot_index in range(top_count):
        routed_part = routed_part + probs_flat[:, slot_index, None] * slot_rows[
            :, slot_index
        ].astype(jnp.float32)
    moe_out = head_total(routed_part.reshape(block_len, seq_here, width))
    block_out = residual + moe_out
    gathered = (
        lax.all_gather(w_z, "seq", axis=0, tiled=True),
        lax.all_gather(w_x, "seq", axis=0, tiled=True),
        lax.all_gather(w_dt, "seq", axis=0, tiled=True),
        lax.all_gather(w_bc, "seq", axis=0, tiled=True),
        lax.all_gather(router, "seq", axis=0, tiled=True),
        lax.all_gather(shared_gate, "seq", axis=0, tiled=True),
        lax.all_gather(shared_up, "seq", axis=0, tiled=True),
        lax.all_gather(w_out, "seq", axis=1, tiled=True),
        lax.all_gather(shared_down, "seq", axis=1, tiled=True),
    )
    full_z, full_x, full_dt, full_bc, full_router, full_sgate, full_sup, full_out, full_sdown = (
        gathered
    )
    grad_out = cotangent.astype(jnp.float32)
    grad_flat = grad_out.reshape(tok_here, width)
    entry_prob = jnp.where(entry_live, gate_probs.reshape(-1)[entry_slot], 0.0)
    send_grads = (
        (entry_prob[:, None] * grad_flat[entry_token])
        .astype(jnp.bfloat16)
        .reshape(experts_all, capacity, width)
    )
    recv_grads = lax.all_to_all(send_grads, "seq", split_axis=0, concat_axis=0, tiled=True)
    grads_in = recv_grads.reshape(seq_count, local_experts, capacity, width)
    input_row_block = rows_kept.reshape(seq_count, local_experts, capacity, width)
    hid_gate = gate_kept.reshape(seq_count, local_experts, capacity, -1)
    hid_up = up_kept.reshape(seq_count, local_experts, capacity, -1)
    hid_sig = jax.nn.sigmoid(hid_gate)
    hid_act = (hid_gate * hid_sig * hid_up).astype(jnp.bfloat16)
    d_act = jnp.einsum("jecd,efd->jecf", grads_in, expert_down, preferred_element_type=jnp.float32)
    hidden_up_gradient = (d_act * hid_gate * hid_sig).astype(jnp.bfloat16)
    d_hid_gate = (d_act * hid_up * silu_slope(hid_gate, hid_sig)).astype(jnp.bfloat16)
    grad_edown = jnp.einsum("jecf,jecd->efd", hid_act, grads_in, preferred_element_type=jnp.float32)
    grad_egate = jnp.einsum(
        "uqpy,uqpn->qyn", input_row_block, d_hid_gate, preferred_element_type=jnp.float32
    )
    expert_up_gradient = jnp.einsum(
        "uqpy,uqpn->qyn", input_row_block, hidden_up_gradient, preferred_element_type=jnp.float32
    )
    d_rows = jnp.einsum(
        "jecf,edf->jecd", d_hid_gate, expert_gate, preferred_element_type=jnp.float32
    )
    d_rows = (
        d_rows
        + jnp.einsum(
            "jecf,edf->jecd", hidden_up_gradient, expert_up, preferred_element_type=jnp.float32
        )
    ).astype(jnp.bfloat16)
    back_rows = lax.all_to_all(
        d_rows.reshape(recv_grads.shape), "seq", split_axis=0, concat_axis=0, tiled=True
    )
    d_share_act = flat_dot_t(cotangent, full_sdown)
    d_share_up = (d_share_act * share_gate * share_sig).astype(jnp.bfloat16)
    d_share_gate = (d_share_act * share_up * silu_slope(share_gate, share_sig)).astype(jnp.bfloat16)
    grad_sdown = outer_sum(share_act, cotangent)
    grad_sgate = outer_sum(normed_two, d_share_gate)
    grad_sup = outer_sum(normed_two, d_share_up)
    d_normed_two = (
        flat_dot_t(d_share_gate, full_sgate) + flat_dot_t(d_share_up, full_sup)
    ).reshape(tok_here, width)
    prob_grad = jnp.stack(
        [
            jnp.sum(grad_flat * slot_rows[:, slot_index].astype(jnp.float32), axis=-1)
            for slot_index in range(top_count)
        ],
        axis=-1,
    )
    back_slots = back_rows.reshape(-1, width)[target].reshape(tok_here, top_count, width)
    for slot_index in range(top_count):
        d_normed_two = d_normed_two + back_slots[:, slot_index].astype(jnp.float32)
    d_normed_two, prob_grad = head_total(
        (
            d_normed_two.reshape(block_len, seq_here, width),
            prob_grad.reshape(block_len, seq_here, top_count),
        )
    )
    d_chosen = gate_probs * (prob_grad - jnp.sum(gate_probs * prob_grad, axis=-1, keepdims=True))
    d_logits = jnp.sum(
        d_chosen[..., None] * (routes[..., None] == expert_ids).astype(jnp.float32), axis=-2
    ).astype(jnp.bfloat16)
    grad_router = outer_sum(normed_two, d_logits)
    d_normed_two = d_normed_two + flat_dot_t(d_logits, full_router)
    d_resid_norm, grad_norm2 = norm_back(d_normed_two, residual, scale_two, norm2_gain)
    d_resid = grad_out + d_resid_norm
    d_resid_low = d_resid.astype(jnp.bfloat16)
    d_mixed = flat_dot_t(d_resid_low, full_out)
    grad_out_w = outer_sum(mixed_out, d_resid_low)
    gain_scaled = d_mixed * gnorm_gain
    grad_gnorm = jnp.sum((d_mixed * gated * scale_gated).reshape(-1, inner_here), axis=0)
    cross_sum = head_total(jnp.sum(gain_scaled * gated, axis=-1, keepdims=True))
    d_gated = (
        scale_gated * gain_scaled
        - gated * scale_gated * scale_gated * scale_gated * cross_sum / INNER
    )
    d_y = d_gated * gate_z * gate_sig
    d_gate_z = (d_gated * y_flat * silu_slope(gate_z, gate_sig)).astype(jnp.bfloat16)
    d_y_heads = d_y.reshape(x_heads.shape)
    grad_skip = jnp.sum(d_y_heads * x_heads, axis=(0, 1, 3))
    log_decay = jnp.cumsum(step_size * decay_rate, axis=0)
    enters = jnp.exp(log_decay) * (doc_ids == prev_doc[None, :]).astype(jnp.float32)[..., None]
    g_local = jnp.einsum("tsh,tshp,tsn->shpn", enters, d_y_heads, c_state, precision=HIGH)
    a_after, state_grad = entering(
        (a_total, g_local), "seq", carry_combine, (ones_start, zeros_start), True
    )

    def local_scan(x_part, step_part, b_part, c_part, rate_part, state_part):
        return ssm_local(
            x_part, step_part, b_part, c_part, rate_part, state_part, doc_ids, prev_doc
        )

    _, scan_back = jax.vjp(local_scan, x_heads, step_size, b_state, c_state, decay_rate, s_before)
    d_xh, d_step, d_bstate, d_cstate, d_rate, _ = scan_back((d_y_heads, state_grad))
    d_xh = d_xh + d_skip[:, None] * d_y_heads
    d_bc = head_total(jnp.concatenate([d_bstate, d_cstate], axis=-1))
    d_dt_pre = d_step * jax.nn.sigmoid(dt_pre)
    grad_dtb = jnp.sum(d_dt_pre, axis=(0, 1))
    grad_alog = d_rate * decay_rate
    d_conv_out = jnp.concatenate([d_xh.reshape(block_len, seq_here, inner_here), d_bc], axis=-1)

    def local_conv(ext_part, weight_part, shift_part):
        return conv_apply(ext_part, docs_ext, weight_part, shift_part)

    _, conv_back = jax.vjp(local_conv, conv_ext, conv_weight, conv_shift)
    d_ext, grad_cweight, grad_cshift = conv_back(d_conv_out)
    from_next = passed_along(shortened(d_ext[:edge_len]), "seq", -1)
    d_conv_in = d_ext[edge_len:] + jnp.concatenate(
        [jnp.zeros((block_len - edge_len,) + from_next.shape[1:], jnp.float32), from_next], 0
    )
    d_proj_x = d_conv_in[..., :inner_here].astype(jnp.bfloat16)
    d_proj_bc = d_conv_in[..., inner_here:].astype(jnp.bfloat16)
    d_dt_low = d_dt_pre.astype(jnp.bfloat16)
    grad_wz = outer_sum(normed_one, d_gate_z)
    grad_wx = outer_sum(normed_one, d_proj_x)
    grad_wbc = outer_sum(normed_one, d_proj_bc)
    grad_wdt = outer_sum(normed_one, d_dt_low)
    head_first = jnp.where(lax.axis_index("head") == 0, 1.0, 0.0)
    d_normed_one = (
        flat_dot_t(d_gate_z, full_z) + flat_dot_t(d_proj_x, full_x) + flat_dot_t(d_dt_low, full_dt)
    )
    d_normed_one = head_total(d_normed_one + head_first * flat_dot_t(d_proj_bc, full_bc))
    d_x_norm, grad_norm1 = norm_back(d_normed_one, x_float, scale_one, norm1_gain)
    input_grad = d_resid + d_x_norm
    reduced = (
        lax.psum_scatter(grad_wz, "seq", scatter_dimension=0, tiled=True),
        lax.psum_scatter(grad_wx, "seq", scatter_dimension=0, tiled=True),
        lax.psum_scatter(grad_wdt, "seq", scatter_dimension=0, tiled=True),
        lax.psum_scatter(grad_wbc, "seq", scatter_dimension=0, tiled=True),
        lax.psum_scatter(grad_router, "seq", scatter_dimension=0, tiled=True),
        lax.psum_scatter(grad_sgate, "seq", scatter_dimension=0, tiled=True),
        lax.psum_scatter(grad_sup, "seq", scatter_dimension=0, tiled=True),
        lax.psum_scatter(grad_out_w, "seq", scatter_dimension=1, tiled=True),
        lax.psum_scatter(grad_sdown, "seq", scatter_dimension=1, tiled=True),
    )
    red_z, red_x, red_dt, red_bc, red_router, red_sgate, red_sup, red_out, red_sdown = reduced
    small_sums = lax.psum(
        (
            grad_norm1,
            grad_norm2,
            grad_cweight,
            grad_cshift,
            grad_dtb,
            grad_alog,
            grad_skip,
            grad_gnorm,
        ),
        "seq",
    )
    sum_norm1, sum_norm2, sum_cweight, sum_cshift, sum_dtb, sum_alog, sum_skip, sum_gnorm = (
        small_sums
    )
    return (
        block_out,
        input_grad,
        sum_norm1,
        red_z,
        red_x,
        red_bc,
        red_dt,
        sum_cweight[:, :inner_here],
        sum_cweight[:, inner_here:],
        sum_cshift[:inner_here],
        sum_cshift[inner_here:],
        sum_dtb,
        sum_alog,
        sum_skip,
        sum_gnorm,
        red_out,
        sum_norm2,
        red_router,
        red_sgate,
        red_sup,
        red_sdown,
        grad_egate,
        expert_up_gradient,
        grad_edown,
    )


MESH = pl.DeviceIdType.MESH
VMEM = pltpu.VMEM


def peers():
    here, side = lax.axis_index("seq"), lax.axis_index("head")
    x, y, z = lax.rem(here, 2), lax.rem(here // 2, 2), here // 4
    col = x + 2 * y
    return here, side, z, col, (1 - x) + 2 * y, x + 2 * (1 - y), 3 - col


def layers(z):
    lo, hi = lax.rem(z, 2), z // 2
    return [2 * (1 - hi if k & 2 else hi) + (1 - lo if k & 1 else lo) for k in range(4)]


def greet(devices):
    barrier = pltpu.get_barrier_semaphore()
    for device in devices:
        pl.semaphore_signal(barrier, inc=1, device_id=device, device_id_type=MESH)
    pl.semaphore_wait(barrier, len(devices))


class Mail:
    def __init__(self, send, base=0):
        self.send, self.sent, self.base = send, [], base

    def put(self, src, dst, sem, to):
        copy = pltpu.make_async_remote_copy(
            src_ref=src,
            dst_ref=dst,
            send_sem=self.send.at[self.base + len(self.sent)],
            recv_sem=sem,
            device_id=to,
            device_id_type=MESH,
        )
        copy.start()
        self.sent.append(copy)

    def arrived(self, dst, sem):
        pltpu.make_async_remote_copy(
            src_ref=dst,
            dst_ref=dst,
            send_sem=self.send.at[0],
            recv_sem=sem,
            device_id=(0, 0),
            device_id_type=MESH,
        ).wait_recv()

    def finish(self):
        for copy in self.sent:
            copy.wait_send()


def rows_at(ref, start, size, step):
    return ref.at[pl.ds(pl.multiple_of(start, step), size)]


def gather_steps(mail, own_ref, out_ref, recv, recv_half, rows, half=None):
    here, side, z, col, cx, cy, cd = peers()
    zs = layers(z)
    base = 4 * z

    def block(place):
        return rows_at(out_ref, place * rows, rows, 16)

    def part(place, which):
        if half is None:
            width = out_ref.shape[1] // 2
            at = pl.ds(pl.multiple_of(place * rows, 16), rows)
            return out_ref.at[at, pl.ds(which * width, width)]
        size = rows - half if which else half
        return rows_at(out_ref, place * rows + which * half, size, 16)

    mail.put(own_ref, block(here), recv.at[3], (base + cx, side))
    mail.put(own_ref, block(here), recv.at[7], (base + cy, side))
    for k in (1, 2, 3):
        mail.put(own_ref, block(here), recv.at[k - 1], (4 * zs[k] + col, side))
    yield
    for k in range(4):
        if k:
            at = 4 * zs[k] + col
            mail.arrived(block(at), recv.at[k - 1])
            mail.put(block(at), block(at), recv.at[3 + k], (base + cx, side))
            mail.put(block(at), block(at), recv.at[7 + k], (base + cy, side))
            yield
        at = 4 * zs[k] + cx
        mail.arrived(block(at), recv.at[3 + k])
        mail.put(part(at, 0), part(at, 0), recv_half.at[k], (base + cy, side))
        at = 4 * zs[k] + cy
        mail.arrived(block(at), recv.at[7 + k])
        mail.put(part(at, 1), part(at, 1), recv_half.at[4 + k], (base + cx, side))
        yield
    for k in range(4):
        at = 4 * zs[k] + cd
        mail.arrived(part(at, 0), recv_half.at[k])
        mail.arrived(part(at, 1), recv_half.at[4 + k])
        yield


def near(side):
    here, side, z, col, cx, cy, cd = peers()
    zs = layers(z)
    return [(4 * z + cx, side), (4 * z + cy, side)] + [(4 * zs[k] + col, side) for k in (1, 2, 3)]


def note_puts(mail, src_of, notes_out, recv_n):
    here, side = peers()[:2]
    for k in range(1, 16):
        to = lax.rem(here + k, 16)
        mail.put(src_of(to), notes_out.at[here], recv_n.at[here], (to, side))


def note_waits(mail, notes_out, recv_n):
    here = peers()[0]
    for k in range(1, 16):
        place = lax.rem(here + k, 16)
        mail.arrived(notes_out.at[place], recv_n.at[place])


def gather_kernel(rows, own_ref, note_ref, out_ref, notes_out, send, recv, recv_half, recv_n, local):
    here, side = peers()[:2]
    greet(same_side(side, here))
    mine = pltpu.make_async_copy(own_ref, rows_at(out_ref, here * rows, rows, 16), local)
    mine.start()
    mail = Mail(send)
    steps = gather_steps(mail, own_ref, out_ref, recv, recv_half, rows, rows // 2)
    next(steps)
    notes_out[here] = note_ref[...]
    note_puts(mail, lambda to: note_ref, notes_out, recv_n)
    for _ in steps:
        pass
    note_waits(mail, notes_out, recv_n)
    mine.wait()
    mail.finish()


def gather_rows(block, note, number):
    rows, width = block.shape
    vmem = pl.BlockSpec(memory_space=VMEM)
    return pl.pallas_call(
        functools.partial(gather_kernel, rows),
        out_shape=(
            jax.ShapeDtypeStruct((16 * rows, width), block.dtype),
            jax.ShapeDtypeStruct((16,) + note.shape, note.dtype),
        ),
        in_specs=[vmem, vmem],
        out_specs=(vmem, vmem),
        scratch_shapes=[
            pltpu.SemaphoreType.DMA((34,)),
            pltpu.SemaphoreType.DMA((11,)),
            pltpu.SemaphoreType.DMA((8,)),
            pltpu.SemaphoreType.DMA((16,)),
            pltpu.SemaphoreType.DMA,
        ],
        compiler_params=pltpu.CompilerParams(
            collective_id=number, has_side_effects=True, vmem_limit_bytes=48 << 20
        ),
        name=f"gather_{number}",
    )(block, note)


def reduce_steps(mail, part_ref, out_ref, got, sums, recv, rows):
    here, side, z, col, cx, cy, cd = peers()
    zs = layers(z)
    base = 4 * z
    half = rows // 2
    got_a, got_b, got_x, got_y, got_z = got
    sum_x, sum_y, sum_z = sums
    to_x, to_y = (base + cx, side), (base + cy, side)
    f32 = jnp.float32

    def half_of(place, which):
        return rows_at(part_ref, place * rows + which * half, half, half)

    def far(k):
        at = 4 * zs[k] + cd
        mail.put(half_of(at, 0), got_a.at[k], recv.at[k], to_y)
        mail.put(half_of(at, 1), got_b.at[k], recv.at[4 + k], to_x)

    def plain(k):
        mail.put(half_of(4 * zs[k] + cx, 1), got_x.at[k, pl.ds(half, half)], recv.at[12 + k], to_x)
        mail.put(half_of(4 * zs[k] + cy, 0), got_y.at[k, pl.ds(0, half)], recv.at[16 + k], to_y)

    def joined(k):
        mail.arrived(got_a.at[k], recv.at[k])
        total = half_of(4 * zs[k] + cx, 0)[...].astype(f32) + got_a[k].astype(f32)
        sum_x[k] = total.astype(sum_x.dtype)
        mail.put(sum_x.at[k], got_x.at[k, pl.ds(0, half)], recv.at[8 + k], to_x)
        mail.arrived(got_b.at[k], recv.at[4 + k])
        total = half_of(4 * zs[k] + cy, 1)[...].astype(f32) + got_b[k].astype(f32)
        sum_y[k] = total.astype(sum_y.dtype)
        mail.put(sum_y.at[k], got_y.at[k, pl.ds(half, half)], recv.at[20 + k], to_y)

    def column(k):
        mail.arrived(got_x.at[k, pl.ds(half, half)], recv.at[12 + k])
        mail.arrived(got_y.at[k, pl.ds(0, half)], recv.at[16 + k])
        mail.arrived(got_x.at[k, pl.ds(0, half)], recv.at[8 + k])
        mail.arrived(got_y.at[k, pl.ds(half, half)], recv.at[20 + k])
        own = part_ref[pl.ds(pl.multiple_of((4 * zs[k] + col) * rows, rows), rows)].astype(f32)
        total = own + got_x[k].astype(f32) + got_y[k].astype(f32)
        if k:
            sum_z[k - 1] = total.astype(sum_z.dtype)
            mail.put(sum_z.at[k - 1], got_z.at[k - 1], recv.at[23 + k], (4 * zs[k] + col, side))
        else:
            out_ref[...] = total

    far(3)
    plain(3)
    yield
    far(2)
    plain(2)
    yield
    joined(3)
    yield
    far(1)
    plain(1)
    yield
    joined(2)
    yield
    column(3)
    yield
    far(0)
    plain(0)
    yield
    joined(1)
    yield
    column(2)
    yield
    joined(0)
    yield
    column(1)
    yield
    column(0)
    yield
    for k in (3, 2, 1):
        mail.arrived(got_z.at[k - 1], recv.at[23 + k])
        out_ref[...] += got_z[k - 1].astype(f32)


def reduce_scratch(rows, width, kind):
    half = rows // 2
    shapes = [(4, half), (4, half), (4, rows), (4, rows), (3, rows), (4, half), (4, half), (3, rows)]
    return [VMEM(shape + (width,), kind) for shape in shapes]


def same_side(side, here):
    return [(lax.rem(here + k, 16), side) for k in range(1, 16)]


def enter_kernel(
    own_ref,
    mine_ref,
    blocks_ref,
    small_ref,
    gate_ref,
    up_ref,
    down_ref,
    all_ref,
    extras_ref,
    extra_ref,
    cols_ref,
    small_other,
    gate_other,
    up_other,
    down_other,
    send,
    recv,
    recv_half,
    recv_m,
    recv_half_m,
    recv_w,
    recv_e,
    recv_s,
    local,
):
    here, side = peers()[:2]
    places = 16
    sibling = (here, 1 - side)
    greet(same_side(side, here) + [sibling])
    depth = blocks_ref.shape[1]
    rows, extra = own_ref.shape[0], mine_ref.shape[0]
    half_here = here // 8
    mail = Mail(send)
    mine = pltpu.make_async_copy(own_ref, rows_at(all_ref, here * rows, rows, 16), local.at[0])
    mine.start()
    mine_too = pltpu.make_async_copy(
        mine_ref, rows_at(extras_ref, here * extra, extra, 16), local.at[18]
    )
    mine_too.start()

    def strip(place):
        return rows_at(cols_ref, place * depth, depth, 16)

    steps = gather_steps(mail, own_ref, all_ref, recv, recv_half, rows, rows // 2)
    steps_too = gather_steps(mail, mine_ref, extras_ref, recv_m, recv_half_m, extra)
    next(steps_too)
    next(steps)
    mail.put(small_ref, small_other, recv_s.at[0], sibling)
    first = 8 * side + lax.rem(here, 8)
    is_mine = side == half_here
    for k in range(1, 8):
        to = 8 * side + lax.rem(here + k, 8)
        mail.put(blocks_ref.at[to - 8 * side], strip(here), recv_w.at[here], (to, side))

    @pl.when(is_mine)
    def _():
        pltpu.make_async_copy(blocks_ref.at[here - 8 * side], strip(here), local.at[1]).start()

    @pl.when(jnp.logical_not(is_mine))
    def _():
        pltpu.make_async_remote_copy(
            src_ref=blocks_ref.at[first - 8 * side],
            dst_ref=strip(here),
            send_sem=local.at[1],
            recv_sem=recv_w.at[here],
            device_id=(first, side),
            device_id_type=MESH,
        ).start()

    mail.put(gate_ref, gate_other, recv_s.at[1], sibling)
    mail.put(up_ref, up_other, recv_s.at[2], sibling)
    mail.put(down_ref, down_other, recv_s.at[3], sibling)
    for _ in steps_too:
        next(steps)
    for _ in steps:
        pass
    mine.wait()
    mine_too.wait()
    for place in range(places):
        at = pl.ds(place * extra, extra)
        mail.put(extras_ref.at[at], extra_ref.at[at], recv_e.at[place], sibling)

    def forward(place, sem):
        return pltpu.make_async_remote_copy(
            src_ref=strip(place),
            dst_ref=strip(place),
            send_sem=local.at[2 + sem],
            recv_sem=recv_w.at[place],
            device_id=sibling,
            device_id_type=MESH,
        )

    @pl.when(is_mine)
    def _():
        pltpu.make_async_copy(blocks_ref.at[here - 8 * side], strip(here), local.at[1]).wait()
        forward(here, 0).start()

    @pl.when(jnp.logical_not(is_mine))
    def _():
        forward(here, 0).wait_recv()
        pltpu.make_async_remote_copy(
            src_ref=blocks_ref.at[first - 8 * side],
            dst_ref=strip(here),
            send_sem=local.at[1],
            recv_sem=recv_w.at[here],
            device_id=(first, side),
            device_id_type=MESH,
        ).wait_send()

    for k in range(1, places):
        place = lax.rem(here + k, places)
        forward(place, k).wait_recv()

        @pl.when(is_mine)
        def _():
            forward(place, k).start()

    @pl.when(is_mine)
    def _():
        for k in range(places):
            forward(lax.rem(here + k, places), k).wait_send()

    mail.arrived(small_other, recv_s.at[0])
    mail.arrived(gate_other, recv_s.at[1])
    mail.arrived(up_other, recv_s.at[2])
    mail.arrived(down_other, recv_s.at[3])
    for place in range(places):
        mail.arrived(extra_ref.at[pl.ds(place * extra, extra)], recv_e.at[place])
    mail.finish()


def enter(own, mine, blocks, small, gate, up, down, number):
    rows, width = own.shape
    extra = mine.shape[0]
    depth, cols = blocks.shape[1:]
    shape = jax.ShapeDtypeStruct
    hbm = pl.BlockSpec(memory_space=pl.ANY)
    vmem = pl.BlockSpec(memory_space=VMEM)
    return pl.pallas_call(
        enter_kernel,
        out_shape=(
            shape((16 * rows, width), own.dtype),
            shape((16 * extra, width), own.dtype),
            shape((16 * extra, width), own.dtype),
            shape((16 * depth, cols), blocks.dtype),
            shape(small.shape, small.dtype),
            shape(gate.shape, gate.dtype),
            shape(up.shape, up.dtype),
            shape(down.shape, down.dtype),
        ),
        in_specs=[vmem, vmem, vmem, vmem, hbm, hbm, hbm],
        out_specs=(vmem, vmem, vmem, vmem, vmem, hbm, hbm, hbm),
        scratch_shapes=[
            pltpu.SemaphoreType.DMA((65,)),
            pltpu.SemaphoreType.DMA((11,)),
            pltpu.SemaphoreType.DMA((8,)),
            pltpu.SemaphoreType.DMA((11,)),
            pltpu.SemaphoreType.DMA((8,)),
            pltpu.SemaphoreType.DMA((16,)),
            pltpu.SemaphoreType.DMA((16,)),
            pltpu.SemaphoreType.DMA((4,)),
            pltpu.SemaphoreType.DMA((19,)),
        ],
        compiler_params=pltpu.CompilerParams(
            collective_id=number, has_side_effects=True, vmem_limit_bytes=48 << 20
        ),
        name="enter",
    )(own, mine, blocks, small, gate, up, down)


def leave_kernel(
    main_ref,
    bcr_ref,
    small_ref,
    main_out,
    bcr_out,
    small_out,
    got_main,
    got_bcr,
    send_main,
    send_bcr,
    bcr_parts,
    bcr_mine,
    bcr_sib,
    small_sum,
    small_got,
    send,
    recv_sib,
    recv_main,
    recv_bcr,
    recv_small,
    cond,
    local,
):
    here, side = peers()[:2]
    sibling = (here, 1 - side)
    half_here = here // 8
    is_main = side == half_here
    f32 = jnp.float32
    greet(same_side(side, here) + [sibling])
    mail = Mail(send)
    depth = main_ref.shape[1]
    mail.put(small_ref, small_got, recv_sib.at[1], sibling)

    def give_main():
        return pltpu.make_async_remote_copy(
            src_ref=main_ref,
            dst_ref=got_main,
            send_sem=cond.at[0],
            recv_sem=recv_sib.at[0],
            device_id=sibling,
            device_id_type=MESH,
        )

    def give_bcr():
        return pltpu.make_async_remote_copy(
            src_ref=bcr_ref,
            dst_ref=got_bcr,
            send_sem=cond.at[0],
            recv_sem=recv_sib.at[0],
            device_id=sibling,
            device_id_type=MESH,
        )

    def send_on(total, out, sem, slot, k):
        to = lax.rem(here + k, 16)
        return pltpu.make_async_remote_copy(
            src_ref=total.at[to],
            dst_ref=out.at[slot],
            send_sem=cond.at[k],
            recv_sem=sem.at[slot],
            device_id=(to, side),
            device_id_type=MESH,
        )

    slot = lax.rem(here, 8)

    @pl.when(is_main)
    def _():
        give_bcr().start()

    @pl.when(jnp.logical_not(is_main))
    def _():
        give_main().start()

    mail.arrived(small_got, recv_sib.at[1])
    small_sum[...] = small_ref[...] + small_got[...]
    small_out[here] = small_sum[...]
    for k in range(1, 16):
        to = lax.rem(here + k, 16)
        mail.put(small_sum, small_out.at[here], recv_small.at[here], (to, side))

    @pl.when(is_main)
    def _():
        give_main().wait_recv()
        for k in range(1, 16):
            to = lax.rem(here + k, 16)
            total = main_ref[to].astype(f32) + got_main[to].astype(f32)
            send_main[to] = total.astype(send_main.dtype)
            send_on(send_main, main_out, recv_main, slot, k).start()
        total = main_ref[here].astype(f32) + got_main[here].astype(f32)
        main_out[slot] = total.astype(main_out.dtype)

    @pl.when(jnp.logical_not(is_main))
    def _():
        give_bcr().wait_recv()
        for k in range(1, 16):
            to = lax.rem(here + k, 16)
            total = bcr_ref[to].astype(f32) + got_bcr[to].astype(f32)
            send_bcr[to] = total.astype(send_bcr.dtype)
            send_on(send_bcr, bcr_parts, recv_bcr, slot, k).start()
        total = bcr_ref[here].astype(f32) + got_bcr[here].astype(f32)
        bcr_parts[slot] = total.astype(bcr_parts.dtype)

    for j in range(8):
        from_main = 8 * side + j
        from_bcr = 8 * (1 - side) + j

        @pl.when(from_bcr != here)
        def _():
            mail.arrived(bcr_parts.at[j], recv_bcr.at[j])

    total = bcr_parts[0].astype(f32)
    for j in range(1, 8):
        total = total + bcr_parts[j].astype(f32)
    bcr_mine[...] = total
    mail.put(bcr_mine, bcr_sib, recv_sib.at[2], sibling)
    for j in range(8):
        from_main = 8 * side + j

        @pl.when(from_main != here)
        def _():
            mail.arrived(main_out.at[j], recv_main.at[j])

    for k in range(1, 16):
        place = lax.rem(here + k, 16)
        mail.arrived(small_out.at[place], recv_small.at[place])
    mail.arrived(bcr_sib, recv_sib.at[2])
    bcr_out[...] = bcr_mine[...] + bcr_sib[...]

    @pl.when(is_main)
    def _():
        give_bcr().wait_send()
        for k in range(1, 16):
            send_on(send_main, main_out, recv_main, slot, k).wait_send()

    @pl.when(jnp.logical_not(is_main))
    def _():
        give_main().wait_send()
        for k in range(1, 16):
            send_on(send_bcr, bcr_parts, recv_bcr, slot, k).wait_send()

    mail.finish()


def leave(main, bcr, small, number):
    shape = jax.ShapeDtypeStruct
    vmem = pl.BlockSpec(memory_space=VMEM)
    low = jnp.bfloat16
    return pl.pallas_call(
        leave_kernel,
        out_shape=(
            shape((8,) + main.shape[1:], low),
            shape(bcr.shape[1:], jnp.float32),
            shape((16,) + small.shape, jnp.float32),
        ),
        in_specs=[vmem] * 3,
        out_specs=(vmem, vmem, vmem),
        scratch_shapes=[
            VMEM(main.shape, low),
            VMEM(bcr.shape, low),
            VMEM(main.shape, low),
            VMEM(bcr.shape, low),
            VMEM((8,) + bcr.shape[1:], low),
            VMEM(bcr.shape[1:], jnp.float32),
            VMEM(bcr.shape[1:], jnp.float32),
            VMEM(small.shape, jnp.float32),
            VMEM(small.shape, jnp.float32),
            pltpu.SemaphoreType.DMA((17,)),
            pltpu.SemaphoreType.DMA((3,)),
            pltpu.SemaphoreType.DMA((8,)),
            pltpu.SemaphoreType.DMA((8,)),
            pltpu.SemaphoreType.DMA((16,)),
            pltpu.SemaphoreType.DMA((16,)),
            pltpu.SemaphoreType.DMA,
        ],
        compiler_params=pltpu.CompilerParams(
            collective_id=number, has_side_effects=True, vmem_limit_bytes=56 << 20
        ),
        name="leave",
    )(main, bcr, small)


def swap_kernel(count, *refs):
    own, other, (send, recv) = refs[:count], refs[count : 2 * count], refs[2 * count :]
    here, side = peers()[:2]
    greet([(here, 1 - side)])
    mail = Mail(send)
    for i in range(count):
        mail.put(own[i], other[i], recv.at[i], (here, 1 - side))
    for i in range(count):
        mail.arrived(other[i], recv.at[i])
    mail.finish()


def swap(arrays, number):
    count = len(arrays)
    hbm = pl.BlockSpec(memory_space=pl.ANY)
    return pl.pallas_call(
        functools.partial(swap_kernel, count),
        out_shape=tuple(jax.ShapeDtypeStruct(a.shape, a.dtype) for a in arrays),
        in_specs=[hbm] * count,
        out_specs=(hbm,) * count,
        scratch_shapes=[
            pltpu.SemaphoreType.DMA((count,)),
            pltpu.SemaphoreType.DMA((count,)),
        ],
        compiler_params=pltpu.CompilerParams(collective_id=number, has_side_effects=True),
        name=f"swap_{number}",
    )(*arrays)


CHUNK = 128
LAYER = 256
HEADW = 64


def mm(left, right, low=True, exact=False):
    return mm_of(left, right, ((1,), (0,)), low, exact)


def mm_nt(left, right, low=True, exact=False):
    return mm_of(left, right, ((1,), (1,)), low, exact)


def mm_tn(left, right, low=True, exact=False):
    return mm_of(left, right, ((0,), (0,)), low, exact)


def mm_of(left, right, dims, low, exact):
    if exact:
        return lax.dot_general(
            left, right, (dims, ((), ())), precision=HIGH, preferred_element_type=jnp.float32
        )
    if low:
        left, right = left.astype(jnp.bfloat16), right.astype(jnp.bfloat16)
    return lax.dot_general(left, right, (dims, ((), ())), preferred_element_type=jnp.float32)


def lanes(shape):
    return lax.broadcasted_iota(jnp.int32, shape, 1)


def by_head(parts, rows):
    lane = lanes((rows, 3 * HEADW))
    return jnp.where(lane < HEADW, parts[0], jnp.where(lane < 2 * HEADW, parts[1], parts[2]))


def spread_heads(array):
    return by_head([array[:, h : h + 1] for h in range(3)], array.shape[0])


def soft_plus(values):
    return jnp.maximum(values, 0.0) + jnp.log1p(jnp.exp(-jnp.abs(values)))


def chunk_tables(step, log_rate, doc_col, doc_row):
    row = lax.broadcasted_iota(jnp.int32, (CHUNK, CHUNK), 0)
    col = lax.broadcasted_iota(jnp.int32, (CHUNK, CHUNK), 1)
    below = (row >= col).astype(jnp.float32)
    logs = mm(below, step * log_rate, exact=True)
    logs_t, step_t = logs.T, step.T
    pair = (row >= col) & (doc_col == doc_row)
    tables = [
        jnp.exp(jnp.where(pair, logs[:, h : h + 1] - logs_t[h : h + 1], -1e9)) for h in range(3)
    ]
    return logs, tables, [step_t[h : h + 1] for h in range(3)]


def mix_forward_kernel(
    n1_ref,
    cols_ref,
    wbc_ref,
    wdt_ref,
    taps_ref,
    head_ref,
    gain_ref,
    info_ref,
    docrow_ref,
    g_ref,
    z_ref,
    ext_ref,
    pre_ref,
    dt_ref,
    y_ref,
    state_ref,
    out_ref,
    notes_out,
    g_all_ref,
    part_ref,
    gained_ref,
    notes_ref,
    *refs,
):
    got, sums, refs = refs[:5], refs[5:8], refs[8:]
    send, recv, recv_n, g_send, g_recv, g_recv_half, local = refs
    here, side, z_at = peers()[:3]
    greet(same_side(side, here))
    low, f32 = jnp.bfloat16, jnp.float32
    mine = pltpu.make_async_copy(g_ref, rows_at(g_all_ref, here * 64, 64, 16), local)
    mine.start()
    g_mail = Mail(g_send)
    g_steps = gather_steps(g_mail, g_ref, g_all_ref, g_recv, g_recv_half, 64, 32)
    next(g_steps)

    ext_ref[0:8] = jnp.zeros((8, ext_ref.shape[1]), f32)

    @pl.loop(0, 4)
    def _(i):
        at = pl.ds(pl.multiple_of(i * LAYER, LAYER), LAYER)
        shifted = pl.ds(pl.multiple_of(i * LAYER + 8, 8), LAYER)
        rows = n1_ref[at]
        z_ref[at] = mm(rows, cols_ref[:, 0:192])
        ext_ref[shifted, 0:256] = mm(rows, wbc_ref[...])
        ext_ref[shifted, 256:448] = mm(rows, cols_ref[:, 256:448])
        dt_ref[at] = mm(rows, wdt_ref[...]) + head_ref[0:1]

    next(g_steps)
    rate, skip = head_ref[1:2], spread_heads(head_ref[2:3])
    state = jnp.zeros((128, 192), f32)
    ones = jnp.ones((8, 192), f32)
    for c in range(8):
        r = c * CHUNK
        at = pl.ds(r, CHUNK)
        info = info_ref[at]
        pre = taps_ref[4:5] + taps_ref[3:4] * ext_ref[pl.ds(r + 8, CHUNK)]
        for k in (1, 2, 3):
            pre = pre + taps_ref[3 - k : 4 - k] * ext_ref[pl.ds(r + 8 - k, CHUNK)] * (
                info[:, k - 1 : k]
            )
        pre_ref[at] = pre
        act = pre * jax.nn.sigmoid(pre)
        b, cc, x = act[:, 0:128], act[:, 128:256], act[:, 256:448]
        step = soft_plus(dt_ref[at])
        logs, tables, step_t = chunk_tables(step, rate, info[:, 3:4], docrow_ref[0:1, at])
        cross = mm_nt(cc, b)
        stacked = jnp.concatenate([cross * tables[h] * step_t[h] for h in range(3)], 0)
        intra = mm(stacked, x)
        y = by_head([intra[h * CHUNK : (h + 1) * CHUNK] for h in range(3)], CHUNK)
        enters = jnp.exp(logs) * info[:, 4:5]
        state_ref[c] = state
        y = y + spread_heads(enters) * mm(cc, state) + skip * x
        y_ref[at] = y
        tail = jnp.exp(logs[CHUNK - 1 :] - logs) * info[:, 5:6] * step
        state = spread_heads(enters[CHUNK - 1 :]) * state + mm_tn(b, spread_heads(tail) * x)
        z = z_ref[at]
        gated = y * z * jax.nn.sigmoid(z)
        gained_ref[at] = (gated * gain_ref[0:1]).astype(low)
        squares = mm_nt(ones, gated * gated, exact=True)
        notes_ref[2 * c, :, 0:64] = squares[:, 0:64]
        notes_ref[2 * c + 1, :, 0:64] = squares[:, 64:128]
        next(g_steps, None)

    mail = Mail(send)
    zs = layers(z_at)
    steps = reduce_steps(mail, part_ref, out_ref, got, sums, recv, 64)
    left = [3, 2, 1, 0]
    for turn in range(13):
        if turn in (0, 1, 3, 6):
            at = pl.ds(pl.multiple_of(zs[left.pop(0)] * LAYER, LAYER), LAYER)
            part_ref[at] = mm_nt(gained_ref[at], cols_ref[:, 512:704]).astype(low)
        next(steps, None)
        if turn == 0:
            notes_out[here] = notes_ref[here]
            note_puts(mail, lambda to: notes_ref.at[to], notes_out, recv_n)
        if turn > 2:
            next(g_steps, None)
    for _ in g_steps:
        pass
    for _ in steps:
        pass
    note_waits(mail, notes_out, recv_n)
    mine.wait()
    g_mail.finish()
    mail.finish()


def mix_forward(n1, cols, wbc, wdt, taps, head, gain, info, docrow, g_own, number):
    shape, f32, low = jax.ShapeDtypeStruct, jnp.float32, jnp.bfloat16
    vmem = pl.BlockSpec(memory_space=VMEM)
    dma = pltpu.SemaphoreType.DMA
    outs = (
        shape((1024, 192), f32),
        shape((1032, 448), f32),
        shape((1024, 448), f32),
        shape((1024, 128), f32),
        shape((1024, 192), f32),
        shape((8, 128, 192), f32),
        shape((64, 1536), f32),
        shape((16, 8, 128), f32),
        shape((1024, 1536), low),
    )
    return pl.pallas_call(
        mix_forward_kernel,
        out_shape=outs,
        in_specs=[vmem] * 10,
        out_specs=(vmem,) * len(outs),
        scratch_shapes=[
            VMEM((1024, 1536), low),
            VMEM((1024, 192), low),
            VMEM((16, 8, 128), f32),
        ]
        + reduce_scratch(64, 1536, low)
        + [
            dma((42,)),
            dma((27,)),
            dma((16,)),
            dma((19,)),
            dma((11,)),
            dma((8,)),
            dma,
        ],
        compiler_params=pltpu.CompilerParams(
            collective_id=number, has_side_effects=True, vmem_limit_bytes=56 << 20
        ),
        name="mix_forward",
    )(n1, cols, wbc, wdt, taps, head, gain, info, docrow, g_own)


def moe_kernel(
    n2_ref,
    g_ref,
    cols_ref,
    eg_ref,
    ego_ref,
    eu_ref,
    euo_ref,
    ed_ref,
    edo_ref,
    router_ref,
    named_ref,
    out_ref,
    notes_out,
    probs_ref,
    moe_ref,
    gup_ref,
    gdown_ref,
    gsh_ref,
    part_ref,
    act_ref,
    hid_ref,
    notes_ref,
    *refs,
):
    got, sums, refs = refs[:5], refs[5:8], refs[8:]
    send, recv, recv_n = refs
    here, side, z_at = peers()[:3]
    greet(same_side(side, here))
    low, f32 = jnp.bfloat16, jnp.float32
    zs = layers(z_at)
    ones = jnp.ones((8, 256), f32)
    spare = lanes((LAYER, 128)) >= 64
    pieces = (
        (eg_ref, eu_ref, ed_ref, 0, 256),
        (ego_ref, euo_ref, edo_ref, 256, 256),
    )

    def layer(k):
        start = pl.multiple_of(zs[k] * LAYER, LAYER)
        at = pl.ds(start, LAYER)
        rows, grads = n2_ref[at], g_ref[at]
        logits = mm(rows, router_ref[...])
        named = named_ref[at]
        top = jnp.max(jnp.where(named > 0, logits, -1e30), axis=-1, keepdims=True)
        raised = jnp.exp(jnp.where(named > 0, logits - top, 0.0)) * named
        probs = raised / jnp.sum(raised, axis=-1, keepdims=True)
        probs_ref[at] = probs
        prob = jnp.sum(jnp.where(lanes((LAYER, 128)) == here, probs, 0.0), axis=-1, keepdims=True)
        dn2 = jnp.zeros((LAYER, 1536), f32)
        slopes = jnp.zeros((8, LAYER), f32)
        for gate_w, up_w, down_w, lane, size in pieces:
            gate = mm(rows, gate_w[...])
            up = mm(rows, up_w[...])
            d_act = mm_nt(grads, down_w[...])
            sig = jax.nn.sigmoid(gate)
            act = gate * sig * up
            act_ref[at, lane : lane + size] = (act * prob).astype(low)
            slopes = slopes + mm_nt(ones, act * d_act, exact=True)
            d_act = d_act * prob
            d_up = (d_act * gate * sig).astype(low)
            d_gate = (d_act * up * silu_slope(gate, sig)).astype(low)
            hid_ref[at, lane : lane + size] = d_gate
            hid_ref[at, 640 + lane : 640 + lane + size] = d_up
            dn2 = dn2 + mm_nt(d_gate, gate_w[...]) + mm_nt(d_up, up_w[...])
        gate = mm(rows, cols_ref[:, 128:256])
        up = mm(rows, cols_ref[:, 384:512])
        d_act = jnp.where(spare, mm(grads, cols_ref[:, 640:768]), 0.0)
        sig = jax.nn.sigmoid(gate)
        act_ref[at, 512:640] = jnp.where(spare, gate * sig * up, 0.0).astype(low)
        d_up = (d_act * gate * sig).astype(low)
        d_gate = (d_act * up * silu_slope(gate, sig)).astype(low)
        hid_ref[at, 512:640] = d_gate
        hid_ref[at, 1152:1280] = d_up
        dn2 = dn2 + mm_nt(d_gate, cols_ref[:, 128:256]) + mm_nt(d_up, cols_ref[:, 384:512])
        part_ref[at] = dn2.astype(low)
        for j in range(4):
            notes_ref[4 * zs[k] + j, :, 0:64] = slopes[:, 64 * j : 64 * (j + 1)]

    def later(task):
        if task < 5:
            cols = slice(256 * task, 256 * (task + 1))
            gup_ref[:, cols] = mm_tn(n2_ref[...], hid_ref[:, cols])
        elif task == 5:
            gdown_ref[...] = mm_tn(act_ref[:, 0:512], g_ref[...])
        elif task == 6:
            gsh_ref[...] = mm_tn(g_ref[...], act_ref[:, 512:640])
        else:
            at = pl.ds(256 * (task - 7), 256)
            total = mm(act_ref[at, 0:256], ed_ref[...]) + mm(act_ref[at, 256:512], edo_ref[...])
            total = total + mm_nt(act_ref[at, 512:640], cols_ref[:, 640:768])
            moe_ref[at] = total.astype(low)

    mail = Mail(send)
    steps = reduce_steps(mail, part_ref, out_ref, got, sums, recv, 64)
    left = [3, 2, 1, 0]
    tasks = list(range(11))
    for turn in range(13):
        if turn in (0, 1, 3, 6):
            layer(left.pop(0))
        next(steps, None)
        if turn == 6:
            notes_out[here] = notes_ref[here]
            note_puts(mail, lambda to: notes_ref.at[to], notes_out, recv_n)
        if turn >= 6 and tasks:
            later(tasks.pop(0))
            if tasks:
                later(tasks.pop(0))
    while tasks:
        later(tasks.pop(0))
    for _ in steps:
        pass
    note_waits(mail, notes_out, recv_n)
    mail.finish()


def moe(n2, g_all, cols, eg, ego, eu, euo, ed, edo, router, named, number):
    shape, f32, low = jax.ShapeDtypeStruct, jnp.float32, jnp.bfloat16
    vmem = pl.BlockSpec(memory_space=VMEM)
    dma = pltpu.SemaphoreType.DMA
    outs = (
        shape((64, 1536), f32),
        shape((16, 8, 128), f32),
        shape((1024, 128), f32),
        shape((1024, 1536), low),
        shape((1536, 1280), f32),
        shape((512, 1536), f32),
        shape((1536, 128), f32),
    )
    return pl.pallas_call(
        moe_kernel,
        out_shape=outs,
        in_specs=[vmem] * 11,
        out_specs=(vmem,) * len(outs),
        scratch_shapes=[
            VMEM((1024, 1536), low),
            VMEM((1024, 640), low),
            VMEM((1024, 1280), low),
            VMEM((16, 8, 128), f32),
        ]
        + reduce_scratch(64, 1536, low)
        + [dma((42,)), dma((27,)), dma((16,))],
        compiler_params=pltpu.CompilerParams(
            collective_id=number, has_side_effects=True, vmem_limit_bytes=58 << 20
        ),
        name="moe",
    )(n2, g_all, cols, eg, ego, eu, euo, ed, edo, router, named)


def mix_backward_kernel(
    dres_ref,
    n1_ref,
    cols_ref,
    wbc_ref,
    wdt_ref,
    taps_ref,
    head_ref,
    gain_ref,
    info_ref,
    docrow_ref,
    token_ref,
    z_ref,
    ext_ref,
    pre_ref,
    dt_ref,
    y_ref,
    state_ref,
    moe_ref,
    out_ref,
    block_ref,
    gmain_ref,
    gbc_ref,
    gdt_ref,
    gtaps_ref,
    gchan_ref,
    ghead_ref,
    part_ref,
    dm_ref,
    mixed_ref,
    din_ref,
    dpre_ref,
    *refs,
):
    got, sums, refs = refs[:5], refs[5:8], refs[8:]
    b_got, b_sums, refs = refs[:5], refs[5:8], refs[8:]
    send, recv, b_send, b_recv = refs
    here, side, z_at = peers()[:3]
    greet(near(side))
    low, f32 = jnp.bfloat16, jnp.float32
    zs = layers(z_at)
    b_mail = Mail(b_send)
    b_steps = reduce_steps(b_mail, moe_ref, block_ref, b_got, b_sums, b_recv, 64)
    next(b_steps)

    @pl.loop(0, 4)
    def _(i):
        at = pl.ds(pl.multiple_of(i * LAYER, LAYER), LAYER)
        dm_ref[at] = mm(dres_ref[at], cols_ref[:, 512:704])

    next(b_steps)
    rate, skip = head_ref[1:2], spread_heads(head_ref[2:3])
    onehot = (
        lax.broadcasted_iota(jnp.int32, (192, 128), 0) // HEADW
        == lax.broadcasted_iota(jnp.int32, (192, 128), 1)
    ).astype(f32)
    row = lax.broadcasted_iota(jnp.int32, (CHUNK, CHUNK), 0)
    lane = lanes((CHUNK, CHUNK))
    above = (row <= lane).astype(f32)
    lane192 = lanes((CHUNK, 192))
    masks = [((lane192 // HEADW) == h).astype(f32) for h in range(3)]
    d_state = jnp.zeros((128, 192), f32)
    g_gain = jnp.zeros((1, 192), f32)
    g_skip = jnp.zeros((1, 192), f32)
    g_rate = jnp.zeros((1, 128), f32)
    g_dt = jnp.zeros((1, 128), f32)
    g_taps = [jnp.zeros((1, 448), f32) for _ in range(5)]
    dpre_ref[1024:1032] = jnp.zeros((8, 448), f32)
    for c in range(7, -1, -1):
        r = c * CHUNK
        at = pl.ds(r, CHUNK)
        info, token = info_ref[at], token_ref[at]
        scale, pull = token[:, 0:1], token[:, 1:2]
        z, y, dm, gain = z_ref[at], y_ref[at], dm_ref[at], gain_ref[0:1]
        sig = jax.nn.sigmoid(z)
        gated = y * z * sig
        scaled = gated * scale
        mixed_ref[at] = (scaled * gain).astype(low)
        g_gain = g_gain + jnp.sum(dm * scaled, axis=0, keepdims=True)
        d_gated = scale * gain * dm - gated * pull
        d_y = d_gated * z * sig
        din_ref[at, 0:192] = (d_gated * y * silu_slope(z, sig)).astype(low)
        pre = pre_ref[at]
        pre_sig = jax.nn.sigmoid(pre)
        act = pre * pre_sig
        b, cc, x = act[:, 0:128], act[:, 128:256], act[:, 256:448]
        g_skip = g_skip + jnp.sum(d_y * x, axis=0, keepdims=True)
        dt = dt_ref[at]
        step = soft_plus(dt)
        logs, tables, step_t = chunk_tables(step, rate, info[:, 3:4], docrow_ref[0:1, at])
        cross = mm_nt(cc, b)
        decays = [tables[h] * step_t[h] for h in range(3)]
        stacked = jnp.concatenate([cross * decays[h] for h in range(3)], 0)
        d_ys = jnp.concatenate([d_y * masks[h] for h in range(3)], 0)
        d_stack = mm_nt(d_ys, x)
        d_x = skip * d_y + mm_tn(stacked, d_ys)
        state = state_ref[c]
        enters = jnp.exp(logs) * info[:, 4:5]
        enters_x = spread_heads(enters)
        d_in_y = enters_x * d_y
        from_state = mm(cc, state)
        tail_w = jnp.exp(logs[CHUNK - 1 :] - logs) * info[:, 5:6]
        tail = tail_w * step
        tail_x = spread_heads(tail)
        to_state = mm(b, d_state)
        d_x = d_x + tail_x * to_state
        both = mm(
            jnp.concatenate([d_y * from_state, x * to_state], 0), onehot, exact=True
        )
        d_enters, d_tail = both[:CHUNK], both[CHUNK:]
        d_cross = jnp.zeros((CHUNK, CHUNK), f32)
        row_sums = jnp.zeros((CHUNK, CHUNK), f32)
        col_sums = []
        for h in range(3):
            d_a = d_stack[h * CHUNK : (h + 1) * CHUNK]
            d_cross = d_cross + d_a * decays[h]
            plain = d_a * cross * tables[h]
            col_sums.append(jnp.sum(plain, axis=0, keepdims=True))
            total = jnp.sum(plain * step_t[h], axis=1, keepdims=True)
            row_sums = jnp.where(lane == h, total, row_sums)
        col_sums = jnp.concatenate(col_sums + [jnp.zeros((5, CHUNK), f32)], 0)
        col_sums = jnp.concatenate([col_sums, jnp.zeros((CHUNK - 8, CHUNK), f32)], 0).T
        d_c = mm(d_cross, b) + mm_nt(d_in_y, state)
        d_b = mm_tn(d_cross, cc) + mm_nt(tail_x * x, d_state)
        kept = enters[CHUNK - 1 :]
        d_kept = mm(
            jnp.broadcast_to(jnp.sum(d_state * state, axis=0, keepdims=True), (8, 192)),
            onehot,
            exact=True,
        )[0:1]
        pulled = d_tail * tail
        d_logs = row_sums - step * col_sums + d_enters * enters - pulled
        d_last = jnp.sum(pulled, axis=0, keepdims=True) + d_kept * kept
        d_logs = d_logs + jnp.where(row == CHUNK - 1, d_last, 0.0)
        d_l = mm(above, d_logs, exact=True)
        d_step = col_sums + d_tail * tail_w + d_l * rate
        g_rate = g_rate + jnp.sum(d_l * step, axis=0, keepdims=True)
        d_dt = jnp.where(lane < 3, d_step * jax.nn.sigmoid(dt), 0.0)
        g_dt = g_dt + jnp.sum(d_dt, axis=0, keepdims=True)
        din_ref[at, 768:896] = d_dt.astype(low)
        d_state = spread_heads(kept) * d_state + mm_tn(cc, d_in_y)
        d_pre = jnp.concatenate([d_b, d_c, d_x], 1) * silu_slope(pre, pre_sig)
        dpre_ref[at] = d_pre
        g_taps[4] = g_taps[4] + jnp.sum(d_pre, axis=0, keepdims=True)
        g_taps[3] = g_taps[3] + jnp.sum(d_pre * ext_ref[pl.ds(r + 8, CHUNK)], axis=0, keepdims=True)
        d_ext = taps_ref[3:4] * d_pre
        for k in (1, 2, 3):
            masked = d_pre * info[:, k - 1 : k]
            g_taps[3 - k] = g_taps[3 - k] + jnp.sum(
                masked * ext_ref[pl.ds(r + 8 - k, CHUNK)], axis=0, keepdims=True
            )
            after = pl.ds(r + k, CHUNK)
            d_ext = d_ext + taps_ref[3 - k : 4 - k] * (
                dpre_ref[after] * info_ref[after, k - 1 : k]
            )
        din_ref[at, 256:512] = d_ext[:, 0:256].astype(low)
        din_ref[at, 512:704] = d_ext[:, 256:448].astype(low)
        next(b_steps, None)
    for k in range(5):
        gtaps_ref[k : k + 1] = g_taps[k]
    gchan_ref[0:1] = g_gain
    gchan_ref[1:2] = g_skip
    ghead_ref[0:1] = g_dt
    ghead_ref[1:2] = g_rate * rate

    def layer(k):
        at = pl.ds(pl.multiple_of(zs[k] * LAYER, LAYER), LAYER)
        total = mm_nt(din_ref[at, 0:192], cols_ref[:, 0:192])
        total = total + mm_nt(din_ref[at, 256:512], wbc_ref[...])
        total = total + mm_nt(din_ref[at, 512:704], cols_ref[:, 256:448])
        total = total + mm_nt(din_ref[at, 768:896], wdt_ref[...])
        part_ref[at] = total.astype(low)

    def later(task):
        if task == 0:
            gmain_ref[:, 0:192] = mm_tn(n1_ref[...], din_ref[:, 0:192])
        elif task == 1:
            gmain_ref[:, 256:448] = mm_tn(n1_ref[...], din_ref[:, 512:704])
        elif task == 2:
            gmain_ref[:, 512:704] = mm_tn(dres_ref[...], mixed_ref[...])
        elif task == 3:
            gbc_ref[...] = mm_tn(n1_ref[...], din_ref[:, 256:512])
        else:
            gdt_ref[...] = mm_tn(n1_ref[...], din_ref[:, 768:896])

    mail = Mail(send)
    steps = reduce_steps(mail, part_ref, out_ref, got, sums, recv, 64)
    left, tasks = [3, 2, 1, 0], [0, 1, 2, 3, 4]
    for turn in range(13):
        if turn in (0, 1, 3, 6):
            layer(left.pop(0))
        next(steps, None)
        next(b_steps, None)
        if turn >= 6 and tasks:
            later(tasks.pop(0))
    while tasks:
        later(tasks.pop(0))
    for _ in b_steps:
        pass
    for _ in steps:
        pass
    b_mail.finish()
    mail.finish()


def mix_backward(*args, number):
    shape, f32, low = jax.ShapeDtypeStruct, jnp.float32, jnp.bfloat16
    vmem = pl.BlockSpec(memory_space=VMEM)
    dma = pltpu.SemaphoreType.DMA
    outs = (
        shape((64, 1536), f32),
        shape((64, 1536), f32),
        shape((1536, 768), f32),
        shape((1536, 256), f32),
        shape((1536, 128), f32),
        shape((8, 448), f32),
        shape((8, 192), f32),
        shape((8, 128), f32),
    )
    return pl.pallas_call(
        mix_backward_kernel,
        out_shape=outs,
        in_specs=[vmem] * len(args),
        out_specs=(vmem,) * len(outs),
        scratch_shapes=[
            VMEM((1024, 1536), low),
            VMEM((1024, 192), f32),
            VMEM((1024, 192), low),
            VMEM((1024, 896), low),
            VMEM((1032, 448), f32),
        ]
        + reduce_scratch(64, 1536, low)
        + reduce_scratch(64, 1536, low)
        + [dma((27,)), dma((27,)), dma((27,)), dma((27,))],
        compiler_params=pltpu.CompilerParams(
            collective_id=number, has_side_effects=True, vmem_limit_bytes=60 << 20
        ),
        name="mix_backward",
    )(*args)


def by_heads(
    hidden_in,
    doc_ids,
    routes,
    norm1_gain,
    w_z,
    w_x,
    w_bc,
    w_dt,
    conv_x,
    conv_bc,
    convb_x,
    convb_bc,
    dt_bias,
    a_log,
    d_skip,
    gnorm_gain,
    w_out,
    norm2_gain,
    router,
    shared_gate,
    shared_up,
    shared_down,
    expert_gate,
    expert_up,
    expert_down,
    cotangent,
):
    places = lax.axis_size("seq")
    here, side = lax.axis_index("seq"), lax.axis_index("head")
    block_len, _, width = hidden_in.shape
    length = block_len * places
    heads_all = 2 * dt_bias.shape[0]
    heads = heads_all // places
    inner = 2 * convb_x.shape[0]
    chans = inner // places
    head_size = chans // heads
    state = convb_bc.shape[0] // 2
    shared_all = 2 * shared_gate.shape[1]
    shared = shared_all // places
    experts = router.shape[1]
    top_count = routes.shape[-1]
    hidden = 2 * expert_gate.shape[2]

    half_here, slot = here // 8, lax.rem(here, 8)
    low, f32 = jnp.bfloat16, jnp.float32

    def mine_of(own, other):
        return jnp.where(side == half_here, own, other)

    def ordered(own, other, axis):
        pair = jnp.where(side == 0, jnp.stack([own, other], axis), jnp.stack([other, own], axis))
        return pair

    def padded(array, rows):
        flat = array.reshape(-1)
        return jnp.pad(flat, (0, rows * width - flat.shape[0])).reshape(rows, width)

    x_own = lax.dynamic_index_in_dim(hidden_in, side, 1, False).astype(f32)
    g_own = lax.dynamic_index_in_dim(cotangent, side, 1, False)
    scale_one = lax.rsqrt(jnp.mean(x_own * x_own, axis=-1, keepdims=True) + EPS)
    n1_own = (x_own * scale_one * norm1_gain).astype(low)
    ids = jnp.concatenate([doc_ids[:, :, None], routes], 2)
    ids = lax.dynamic_index_in_dim(ids, side, 1, False)
    bc_half = lax.dynamic_slice_in_dim(w_bc, side * state, state, 1)
    own_extra = jnp.concatenate(
        [
            bc_half.reshape(8, width),
            router.reshape(1, width),
            padded(w_dt, 2),
            padded(ids.astype(low), 1),
            jnp.zeros((4, width), low),
        ],
        0,
    )
    blocks = jnp.concatenate(
        [
            part.reshape(part.shape[0], 8, part.shape[1] // 8)
            for part in (w_z, shared_gate, w_x, shared_up, w_out.T, shared_down.T)
        ],
        2,
    ).transpose(1, 0, 2)
    small = jnp.concatenate(
        [
            conv_x,
            convb_x[None],
            gnorm_gain[None],
            jnp.pad(jnp.concatenate([dt_bias, a_log, d_skip]), (0, width - 72))[None],
            jnp.zeros((1, width), f32),
        ],
        0,
    )
    eg, eu, ed = expert_gate[0], expert_up[0], expert_down[0]
    n1, extra_own, extra_sib, cols, small_sib, eg_o, eu_o, ed_o = enter(
        n1_own, own_extra, blocks, small, eg, eu, ed, 1
    )
    extra_own = extra_own.reshape(places, 16, width)
    extra_sib = extra_sib.reshape(places, 16, width)
    wbc = ordered(
        extra_own[:, :8].reshape(width, state), extra_sib[:, :8].reshape(width, state), 1
    ).reshape(width, 2 * state)
    wrouter = extra_own[:, 8].reshape(width, experts)
    wdt = mine_of(extra_own[:, 9:11], extra_sib[:, 9:11]).reshape(places, 2 * width)
    wdt = wdt[:, : w_dt.shape[0] * w_dt.shape[1]].reshape(width, w_dt.shape[1])
    wdt = lax.dynamic_slice_in_dim(wdt, slot * heads, heads, 1)
    ids = extra_own[:, 11, : block_len * 7].reshape(length, 7).astype(jnp.int32)
    docs, picks = ids[:, 0], ids[:, 1:]
    small = mine_of(small, small_sib)
    wide_small = lax.dynamic_slice_in_dim(small, slot * chans, chans, 1)
    taps = jnp.concatenate(
        [
            jnp.concatenate([conv_bc, wide_small[:KER]], 1),
            jnp.concatenate([convb_bc, wide_small[KER]], 0)[None],
            jnp.zeros((3, 2 * state + chans), f32),
        ],
        0,
    )
    gn_gain = jnp.pad(wide_small[KER + 1][None], ((0, 7), (0, 0)))
    head_params = small[KER + 2, :72].reshape(3, 24)
    head_params = lax.dynamic_slice_in_dim(head_params, slot * heads, heads, 1)
    head_params = jnp.stack([head_params[0], -jnp.exp(head_params[1]), head_params[2]])
    head_params = jnp.pad(head_params, ((0, 5), (0, 128 - heads)))
    wdt = jnp.pad(wdt, ((0, 0), (0, 128 - heads)))
    wrouter = jnp.pad(wrouter, ((0, 0), (0, 128 - experts)))
    docs_f = docs.astype(f32)
    before = jnp.concatenate([jnp.full((KER - 1,), -1.0, f32), docs_f])
    groups = docs_f.reshape(length // CHUNK, CHUNK)
    ends = groups[:, -1]
    starts = jnp.concatenate([docs_f[:1], ends[:-1]])
    info = jnp.stack(
        [(before[KER - 1 - k : KER - 1 - k + length] == docs_f).astype(f32) for k in (1, 2, 3)]
        + [
            docs_f,
            (groups == starts[:, None]).astype(f32).reshape(-1),
            (groups == ends[:, None]).astype(f32).reshape(-1),
        ],
        1,
    )
    info = jnp.pad(info, ((0, 8), (0, 128 - info.shape[1])))
    docrow = jnp.broadcast_to(docs_f[None], (8, length))
    named = jnp.sum((picks[:, :, None] == jnp.arange(128)).astype(f32), axis=1)

    def note(values):
        return jnp.pad(values.reshape(1, block_len), ((0, 7), (0, 128 - block_len)))

    def noted(array):
        return array[:, 0, :block_len]

    weights = (cols, wbc, wdt, taps, head_params, gn_gain, info, docrow)
    z, ext, pre, dt, y, states, out_sum, squares, g_all = mix_forward(n1, *weights, g_own, 2)
    scale_own = lax.rsqrt(jnp.sum(noted(squares), axis=0) / inner + EPS)[:, None]
    out_own = scale_own * out_sum
    residual = x_own + out_own

    scale_two = lax.rsqrt(jnp.mean(residual * residual, axis=-1, keepdims=True) + EPS)
    n2_own = (residual * scale_two * norm2_gain).astype(low)
    n2, scale_gated = gather_rows(n2_own, note(scale_own), 3)
    scale_gated = noted(scale_gated).reshape(length)
    dn2, prob_grads, probs, moe_part, grad_up, grad_down, grad_sd = moe(
        n2, g_all, cols, eg, eg_o, eu, eu_o, ed, ed_o, wrouter, named, 4
    )
    prob_grads = noted(prob_grads).T
    probs_own = lax.dynamic_slice(probs, (here * block_len, 0), (block_len, experts))
    d_logits = (
        probs_own * (prob_grads - jnp.sum(probs_own * prob_grads, axis=-1, keepdims=True))
    ).astype(low)
    grad_router = outer_sum(n2_own, d_logits)
    dn2 = dn2 + flat_dot_t(d_logits, wrouter[:, :experts])
    d_norm, grad_norm2 = norm_back(dn2, residual, scale_two, norm2_gain)
    d_res = g_own.astype(f32) + d_norm
    d_res_low = d_res.astype(low)

    cross_own = jnp.sum(d_res_low.astype(f32) * out_own, axis=-1, keepdims=True) / scale_own
    d_res_all, cross = gather_rows(d_res_low, note(cross_own), 5)
    cross = noted(cross).reshape(length)
    pull = scale_gated * scale_gated * scale_gated * cross / inner
    token = jnp.pad(jnp.stack([scale_gated, pull], 1), ((0, 0), (0, 126)))
    dn1, block_sum, grad_main, grad_bc, grad_wdt, grad_taps, grad_chan, grad_head = mix_backward(
        d_res_all, n1, *weights, token, z, ext, pre, dt, y, states, moe_part, number=6
    )
    block_own = residual + block_sum
    d_x, grad_norm1 = norm_back(dn1, x_own, scale_one, norm1_gain)
    input_own = d_res + d_x

    grads = jnp.concatenate(
        [
            grad_main[:, :192],
            grad_up[:, 576:640],
            grad_main[:, 256:448],
            grad_up[:, 1216:1280],
            grad_main[:, 512:704],
            grad_sd[:, 64:],
        ],
        1,
    ).astype(low)
    main = grads.reshape(places, 96, 768)
    bcr = jnp.concatenate(
        [
            grad_bc.reshape(places, 96, 256),
            grad_router.reshape(places, 6, 256),
            jnp.zeros((places, 10, 256), f32),
        ],
        1,
    ).astype(low)
    grad_wdt = grad_wdt[:, :heads]
    grad_skip = jnp.sum(grad_chan[1].reshape(heads, head_size), axis=1)
    singles = jnp.concatenate(
        [
            grad_norm1,
            grad_norm2,
            grad_taps[:KER, : 2 * state].reshape(-1),
            grad_taps[KER, : 2 * state],
            grad_taps[:KER, 2 * state :].reshape(-1),
            grad_taps[KER, 2 * state :],
            grad_chan[0],
            grad_head[0, :heads],
            grad_head[1, :heads],
            grad_skip,
            grad_wdt.reshape(-1),
        ]
    )
    singles = jnp.pad(singles, (0, 88 * 128 - singles.shape[0])).reshape(88, 128)
    main, bcr, singles = leave(main, bcr, singles, 9)
    singles = singles.reshape(places, -1)
    sums = jnp.sum(singles[:, :4352], axis=0)
    sums = jnp.split(sums, [1536, 3072, 4096])
    lists = lax.dynamic_slice_in_dim(singles, 8 * side, 8, 0)[:, 4352:]
    lists = jnp.split(lists, [768, 960, 1152, 1155, 1158, 1161, 1161 + 4608], axis=1)

    def joined(part):
        return part.transpose(1, 0, 2).reshape(part.shape[1], -1)

    main = main.astype(f32)
    bc_sum = bcr[:96]
    router_sum = bcr[96:102].reshape(96, experts)
    wdt_sum = joined(lists[6].reshape(8, width, heads))
    wdt_sum = lax.dynamic_slice_in_dim(wdt_sum, here * 96, 96, 0)
    other = swap(
        (
            block_own,
            input_own,
            grad_up[:, 256:512].astype(low),
            grad_up[:, 896:1152].astype(low),
            grad_down[256:512].astype(low),
        ),
        10,
    )
    return (
        ordered(block_own, other[0], 1),
        ordered(input_own, other[1], 1),
        sums[0],
        joined(main[:, :, :192]),
        joined(main[:, :, 256:448]),
        bc_sum,
        wdt_sum,
        joined(lists[0].reshape(8, KER, chans)),
        sums[2].reshape(KER, 2 * state),
        lists[1].reshape(-1),
        sums[3],
        lists[3].reshape(-1),
        lists[4].reshape(-1),
        lists[5].reshape(-1),
        lists[2].reshape(-1),
        joined(main[:, :, 512:704]).T,
        sums[1],
        router_sum,
        joined(main[:, :, 192:256]),
        joined(main[:, :, 448:512]),
        joined(main[:, :, 704:768]).T,
        (grad_up[:, :256] + other[2].astype(f32))[None],
        (grad_up[:, 640:896] + other[3].astype(f32))[None],
        (grad_down[:256] + other[4].astype(f32))[None],
    )


def solution(mesh):
    places = mesh.shape["seq"]
    whole_heads = places == 16 and mesh.shape["head"] == 2
    placed = (
        P("seq", None, None),
        P("seq", None),
        P("seq", None, None),
        P(),
        P("seq", "head"),
        P("seq", "head"),
        P("seq", None),
        P("seq", "head"),
        P(None, "head"),
        P(),
        P("head"),
        P(),
        P("head"),
        P("head"),
        P("head"),
        P("head"),
        P("head", "seq"),
        P(),
        P("seq", None),
        P("seq", "head"),
        P("seq", "head"),
        P("head", "seq"),
        P("seq", None, "head"),
        P("seq", None, "head"),
        P("seq", "head", None),
        P("seq", None, None),
    )
    return jax.shard_map(
        by_heads if whole_heads else on_device,
        mesh=mesh,
        in_specs=placed,
        out_specs=(
            P("seq", None, None),
            P("seq", None, None),
            P(),
            P("seq", "head"),
            P("seq", "head"),
            P("seq", None),
            P("seq", "head"),
            P(None, "head"),
            P(),
            P("head"),
            P(),
            P("head"),
            P("head"),
            P("head"),
            P("head"),
            P("head", "seq"),
            P(),
            P("seq", None),
            P("seq", "head"),
            P("seq", "head"),
            P("head", "seq"),
            P("seq", None, "head"),
            P("seq", None, "head"),
            P("seq", "head", None),
        ),
        check_vma=False,
    )
```

```python
import jax
import jax.numpy as jnp
from jax import lax
from jax.experimental import pallas as pl
from jax.experimental.pallas import tpu as pltpu
from jax.sharding import PartitionSpec as P

KER = 4
INNER = 3072


EPS = 1e-05
HIGH = lax.Precision.HIGHEST


def passed_along(array, axis, by):
    length = lax.axis_size(axis)
    pairs = [(i, i + by) for i in range(length) if 0 <= i + by < length]
    return lax.ppermute(array, axis, pairs)


def entering(array, axis, combine, identity, reverse):
    length, here = (lax.axis_size(axis), lax.axis_index(axis))
    everything = jax.tree.map(
        lambda part, kind: lax.all_gather(part.astype(kind), axis),
        array,
        jax.tree.map(lambda a: jnp.bfloat16 if a.dtype == jnp.float32 else a.dtype, array),
    )
    start = jax.tree.map(
        lambda part, zero: jnp.broadcast_to(jnp.asarray(zero, part.dtype), part.shape),
        array,
        identity,
    )

    def hop(k, before):
        at = length - 1 - k if reverse else k
        reached = at > here if reverse else at < here
        new = combine(
            before, jax.tree.map(lambda part, own: part[at].astype(own.dtype), everything, array)
        )
        return jax.tree.map(lambda a, b: jnp.where(reached, a, b), new, before)

    return lax.fori_loop(0, length, hop, start)


def shortened(array):

    def short(part):
        return part.astype(jnp.bfloat16) if part.dtype == jnp.float32 else part

    return jax.tree.map(short, array)


def conv_apply(conv_ext, docs_ext, weight, conv_bias):
    length_here = conv_ext.shape[0] - (KER - 1)
    running = conv_bias
    for offset in range(KER):
        same_doc = (docs_ext[offset : offset + length_here] == docs_ext[KER - 1 :]).astype(
            jnp.float32
        )
        running = (
            running + weight[offset] * conv_ext[offset : offset + length_here] * same_doc[..., None]
        )
    return jax.nn.silu(running)


def group_parts(x_heads, step_size, b_state, decay_rate, doc_ids, prev_doc):
    log_decay = jnp.cumsum(step_size * decay_rate, axis=0)
    end_keep = (doc_ids == doc_ids[-1:]).astype(jnp.float32)
    weight = jnp.exp(log_decay[-1:] - log_decay) * end_keep[..., None] * step_size
    s_local = jnp.einsum("tsh,tshp,tsn->shpn", weight, x_heads, b_state, precision=HIGH)
    a_total = jnp.exp(log_decay[-1]) * (doc_ids[-1] == prev_doc).astype(jnp.float32)[:, None]
    return (s_local, a_total)


def group_output(x_heads, step_size, b_state, c_state, decay_rate, doc_ids, prev_doc, s_in):
    length_here = x_heads.shape[0]
    log_decay = jnp.cumsum(step_size * decay_rate, axis=0)
    causal = jnp.arange(length_here)[:, None] >= jnp.arange(length_here)[None, :]
    pair_mask = (causal[:, :, None] & (doc_ids[:, None, :] == doc_ids[None, :, :])).astype(
        jnp.float32
    )
    gap_decay = log_decay[:, None] - log_decay[None, :]
    decay_table = (
        jnp.exp(jnp.where(pair_mask[..., None] > 0, gap_decay, 0.0)) * pair_mask[..., None]
    )
    cross_dot = jnp.einsum("tsn,usn->tus", c_state, b_state, precision=HIGH)
    y_intra = jnp.einsum(
        "tush,ush,ushp->tshp",
        decay_table * cross_dot[..., None],
        step_size,
        x_heads,
        precision=HIGH,
    )
    enters = jnp.exp(log_decay) * (doc_ids == prev_doc[None, :]).astype(jnp.float32)[..., None]
    y_inter = jnp.einsum("tsn,shpn->tshp", c_state, s_in, precision=HIGH) * enters[..., None]
    return y_intra + y_inter


def ssm_local(x_heads, step_size, b_state, c_state, decay_rate, s_in, doc_ids, prev_doc):
    y_core = group_output(x_heads, step_size, b_state, c_state, decay_rate, doc_ids, prev_doc, s_in)
    s_local, a_total = group_parts(x_heads, step_size, b_state, decay_rate, doc_ids, prev_doc)
    return (y_core, a_total[..., None, None] * s_in + s_local)


def carry_combine(earlier, later_part):
    return (earlier[0] * later_part[0], later_part[0][..., None, None] * earlier[1] + later_part[1])


def head_total(partial_sum):
    return lax.psum(partial_sum, "head")


def flat_dot(left_side, right_side):
    lead_dims = left_side.shape[:-1]
    product = jnp.dot(
        left_side.reshape(-1, left_side.shape[-1]), right_side, preferred_element_type=jnp.float32
    )
    return product.reshape(lead_dims + (right_side.shape[-1],))


def flat_dot_t(left_side, right_side):
    lead_dims = left_side.shape[:-1]
    product = lax.dot_general(
        left_side.reshape(-1, left_side.shape[-1]),
        right_side,
        (((1,), (1,)), ((), ())),
        preferred_element_type=jnp.float32,
    )
    return product.reshape(lead_dims + (right_side.shape[0],))


def outer_sum(left_side, right_side):
    return lax.dot_general(
        left_side.reshape(-1, left_side.shape[-1]),
        right_side.reshape(-1, right_side.shape[-1]),
        (((0,), (0,)), ((), ())),
        preferred_element_type=jnp.float32,
    )


def silu_slope(values, sigmoid_of):
    return sigmoid_of * (1.0 + values * (1.0 - sigmoid_of))


def norm_back(grad_normed, values, scale_of, gain):
    scaled_grad = grad_normed * gain
    gain_grad = jnp.sum((grad_normed * values * scale_of).reshape(-1, values.shape[-1]), axis=0)
    cube = scale_of * scale_of * scale_of
    value_grad = scale_of * scaled_grad - values * cube * jnp.mean(
        scaled_grad * values, axis=-1, keepdims=True
    )
    return (value_grad, gain_grad)


def on_device(
    hidden_in,
    doc_ids,
    routes,
    norm1_gain,
    w_z,
    w_x,
    w_bc,
    w_dt,
    conv_x,
    conv_bc,
    convb_x,
    convb_bc,
    dt_bias,
    a_log,
    d_skip,
    gnorm_gain,
    w_out,
    norm2_gain,
    router,
    shared_gate,
    shared_up,
    shared_down,
    expert_gate,
    expert_up,
    expert_down,
    cotangent,
):
    block_len, seq_here, width = hidden_in.shape
    top_count = routes.shape[-1]
    heads_here = dt_bias.shape[0]
    inner_here = convb_x.shape[0]
    head_size = inner_here // heads_here
    state_size = convb_bc.shape[0] // 2
    seq_count = lax.axis_size("seq")
    local_experts = expert_gate.shape[0]
    experts_all = local_experts * seq_count
    tok_here = block_len * seq_here
    capacity = 2 * tok_here * top_count // experts_all
    edge_len = KER - 1
    x_float = hidden_in.astype(jnp.float32)
    scale_one = lax.rsqrt(jnp.mean(x_float * x_float, axis=-1, keepdims=True) + EPS)
    normed_one = (x_float * scale_one * norm1_gain).astype(jnp.bfloat16)
    gathered = (
        lax.all_gather(w_z, "seq", axis=0, tiled=True),
        lax.all_gather(w_x, "seq", axis=0, tiled=True),
        lax.all_gather(w_dt, "seq", axis=0, tiled=True),
        lax.all_gather(w_bc, "seq", axis=0, tiled=True),
        lax.all_gather(router, "seq", axis=0, tiled=True),
        lax.all_gather(shared_gate, "seq", axis=0, tiled=True),
        lax.all_gather(shared_up, "seq", axis=0, tiled=True),
        lax.all_gather(w_out, "seq", axis=1, tiled=True),
        lax.all_gather(shared_down, "seq", axis=1, tiled=True),
    )
    full_z, full_x, full_dt, full_bc, full_router, full_sgate, full_sup, full_out, full_sdown = (
        gathered
    )
    gate_z = flat_dot(normed_one, full_z)
    proj_x = flat_dot(normed_one, full_x)
    proj_bc = flat_dot(normed_one, full_bc)
    dt_pre = flat_dot(normed_one, full_dt) + dt_bias
    conv_in = jnp.concatenate([proj_x, proj_bc], axis=-1)
    tail_in, tail_doc = (
        passed_along(conv_in[block_len - edge_len :].astype(jnp.bfloat16), "seq", 1).astype(
            jnp.float32
        ),
        passed_along(
            doc_ids[block_len - edge_len :].astype(jnp.float32).astype(jnp.bfloat16), "seq", 1
        ).astype(jnp.float32),
    )
    conv_ext = jnp.concatenate([tail_in, conv_in], 0)
    docs_ext = jnp.concatenate([tail_doc.astype(jnp.int32), doc_ids], 0)
    conv_weight = jnp.concatenate([conv_x, conv_bc], -1)
    conv_shift = jnp.concatenate([convb_x, convb_bc], -1)
    conv_out = conv_apply(conv_ext, docs_ext, conv_weight, conv_shift)
    x_heads = conv_out[..., :inner_here].reshape(block_len, seq_here, heads_here, head_size)
    b_state = conv_out[..., inner_here : inner_here + state_size]
    c_state = conv_out[..., inner_here + state_size :]
    step_size = jax.nn.softplus(dt_pre)
    decay_rate = -jnp.exp(a_log)
    prev_doc = docs_ext[edge_len - 1]
    s_local, a_total = group_parts(x_heads, step_size, b_state, decay_rate, doc_ids, prev_doc)
    ones_start = jnp.ones_like(a_total)
    zeros_start = jnp.zeros_like(s_local)
    a_before, s_before = entering(
        (a_total, s_local), "seq", carry_combine, (ones_start, zeros_start), False
    )
    y_core = group_output(
        x_heads, step_size, b_state, c_state, decay_rate, doc_ids, prev_doc, s_before
    )
    y_heads = y_core + d_skip[:, None] * x_heads
    y_flat = y_heads.reshape(block_len, seq_here, inner_here)
    gate_sig = jax.nn.sigmoid(gate_z)
    gated = y_flat * gate_z * gate_sig
    square_sum = head_total(jnp.sum(gated * gated, axis=-1, keepdims=True))
    scale_gated = lax.rsqrt(square_sum / INNER + EPS)
    mixed_out = (gated * scale_gated * gnorm_gain).astype(jnp.bfloat16)
    residual = x_float + head_total(flat_dot(mixed_out, full_out))
    scale_two = lax.rsqrt(jnp.mean(residual * residual, axis=-1, keepdims=True) + EPS)
    normed_two = (residual * scale_two * norm2_gain).astype(jnp.bfloat16)
    logits = flat_dot(normed_two, full_router)
    gate_probs = jax.nn.softmax(jnp.take_along_axis(logits, routes, axis=-1), axis=-1)
    share_gate = flat_dot(normed_two, full_sgate)
    share_up = flat_dot(normed_two, full_sup)
    share_sig = jax.nn.sigmoid(share_gate)
    share_act = (share_gate * share_sig * share_up).astype(jnp.bfloat16)
    share_part = flat_dot(share_act, full_sdown)
    slot_total = tok_here * top_count
    route_flat = routes.reshape(slot_total)
    expert_ids = jnp.arange(experts_all, dtype=jnp.int32)
    route_hits = (route_flat[:, None] == expert_ids[None, :]).astype(jnp.int32)
    slot_rank = jnp.sum(jnp.cumsum(route_hits, axis=0) * route_hits, axis=1) - 1
    target = route_flat * capacity + slot_rank
    entry_table = (
        jnp.zeros((experts_all * capacity,), jnp.int32)
        .at[target]
        .set(jnp.arange(slot_total, dtype=jnp.int32) + 1)
    )
    entry_live = entry_table > 0
    entry_slot = jnp.maximum(entry_table - 1, 0)
    entry_token = entry_slot // top_count
    tokens_flat = normed_two.reshape(tok_here, width)
    send_rows = jnp.where(
        entry_live[:, None], tokens_flat[entry_token], jnp.zeros((), jnp.bfloat16)
    ).reshape(experts_all, capacity, width)
    received = lax.all_to_all(send_rows, "seq", split_axis=0, concat_axis=0, tiled=True)
    input_row_block = received.reshape(seq_count, local_experts, received.shape[1], width)
    hid_gate = jnp.einsum(
        "jecd,edf->jecf", input_row_block, expert_gate, preferred_element_type=jnp.float32
    )
    hid_up = jnp.einsum(
        "jecd,edf->jecf", input_row_block, expert_up, preferred_element_type=jnp.float32
    )
    hid_act = (hid_gate * jax.nn.sigmoid(hid_gate) * hid_up).astype(jnp.bfloat16)
    half_out = jnp.einsum(
        "jecf,efd->jecd", hid_act, expert_down, preferred_element_type=jnp.float32
    ).astype(jnp.bfloat16)
    returned_rows = lax.all_to_all(
        half_out.reshape(received.shape), "seq", split_axis=0, concat_axis=0, tiled=True
    )
    kept_shape = (seq_count * local_experts, received.shape[1], hid_gate.shape[-1])
    returned_rows, rows_kept, gate_kept, up_kept = (
        returned_rows,
        received,
        hid_gate.reshape(kept_shape),
        hid_up.reshape(kept_shape),
    )
    slot_rows = returned_rows.reshape(-1, width)[target].reshape(tok_here, top_count, width)
    probs_flat = gate_probs.reshape(tok_here, top_count)
    routed_part = share_part.reshape(tok_here, width)
    for slot_index in range(top_count):
        routed_part = routed_part + probs_flat[:, slot_index, None] * slot_rows[
            :, slot_index
        ].astype(jnp.float32)
    moe_out = head_total(routed_part.reshape(block_len, seq_here, width))
    block_out = residual + moe_out
    gathered = (
        lax.all_gather(w_z, "seq", axis=0, tiled=True),
        lax.all_gather(w_x, "seq", axis=0, tiled=True),
        lax.all_gather(w_dt, "seq", axis=0, tiled=True),
        lax.all_gather(w_bc, "seq", axis=0, tiled=True),
        lax.all_gather(router, "seq", axis=0, tiled=True),
        lax.all_gather(shared_gate, "seq", axis=0, tiled=True),
        lax.all_gather(shared_up, "seq", axis=0, tiled=True),
        lax.all_gather(w_out, "seq", axis=1, tiled=True),
        lax.all_gather(shared_down, "seq", axis=1, tiled=True),
    )
    full_z, full_x, full_dt, full_bc, full_router, full_sgate, full_sup, full_out, full_sdown = (
        gathered
    )
    grad_out = cotangent.astype(jnp.float32)
    grad_flat = grad_out.reshape(tok_here, width)
    entry_prob = jnp.where(entry_live, gate_probs.reshape(-1)[entry_slot], 0.0)
    send_grads = (
        (entry_prob[:, None] * grad_flat[entry_token])
        .astype(jnp.bfloat16)
        .reshape(experts_all, capacity, width)
    )
    recv_grads = lax.all_to_all(send_grads, "seq", split_axis=0, concat_axis=0, tiled=True)
    grads_in = recv_grads.reshape(seq_count, local_experts, capacity, width)
    input_row_block = rows_kept.reshape(seq_count, local_experts, capacity, width)
    hid_gate = gate_kept.reshape(seq_count, local_experts, capacity, -1)
    hid_up = up_kept.reshape(seq_count, local_experts, capacity, -1)
    hid_sig = jax.nn.sigmoid(hid_gate)
    hid_act = (hid_gate * hid_sig * hid_up).astype(jnp.bfloat16)
    d_act = jnp.einsum("jecd,efd->jecf", grads_in, expert_down, preferred_element_type=jnp.float32)
    hidden_up_gradient = (d_act * hid_gate * hid_sig).astype(jnp.bfloat16)
    d_hid_gate = (d_act * hid_up * silu_slope(hid_gate, hid_sig)).astype(jnp.bfloat16)
    grad_edown = jnp.einsum("jecf,jecd->efd", hid_act, grads_in, preferred_element_type=jnp.float32)
    grad_egate = jnp.einsum(
        "uqpy,uqpn->qyn", input_row_block, d_hid_gate, preferred_element_type=jnp.float32
    )
    expert_up_gradient = jnp.einsum(
        "uqpy,uqpn->qyn", input_row_block, hidden_up_gradient, preferred_element_type=jnp.float32
    )
    d_rows = jnp.einsum(
        "jecf,edf->jecd", d_hid_gate, expert_gate, preferred_element_type=jnp.float32
    )
    d_rows = (
        d_rows
        + jnp.einsum(
            "jecf,edf->jecd", hidden_up_gradient, expert_up, preferred_element_type=jnp.float32
        )
    ).astype(jnp.bfloat16)
    back_rows = lax.all_to_all(
        d_rows.reshape(recv_grads.shape), "seq", split_axis=0, concat_axis=0, tiled=True
    )
    d_share_act = flat_dot_t(cotangent, full_sdown)
    d_share_up = (d_share_act * share_gate * share_sig).astype(jnp.bfloat16)
    d_share_gate = (d_share_act * share_up * silu_slope(share_gate, share_sig)).astype(jnp.bfloat16)
    grad_sdown = outer_sum(share_act, cotangent)
    grad_sgate = outer_sum(normed_two, d_share_gate)
    grad_sup = outer_sum(normed_two, d_share_up)
    d_normed_two = (
        flat_dot_t(d_share_gate, full_sgate) + flat_dot_t(d_share_up, full_sup)
    ).reshape(tok_here, width)
    prob_grad = jnp.stack(
        [
            jnp.sum(grad_flat * slot_rows[:, slot_index].astype(jnp.float32), axis=-1)
            for slot_index in range(top_count)
        ],
        axis=-1,
    )
    back_slots = back_rows.reshape(-1, width)[target].reshape(tok_here, top_count, width)
    for slot_index in range(top_count):
        d_normed_two = d_normed_two + back_slots[:, slot_index].astype(jnp.float32)
    d_normed_two, prob_grad = head_total(
        (
            d_normed_two.reshape(block_len, seq_here, width),
            prob_grad.reshape(block_len, seq_here, top_count),
        )
    )
    d_chosen = gate_probs * (prob_grad - jnp.sum(gate_probs * prob_grad, axis=-1, keepdims=True))
    d_logits = jnp.sum(
        d_chosen[..., None] * (routes[..., None] == expert_ids).astype(jnp.float32), axis=-2
    ).astype(jnp.bfloat16)
    grad_router = outer_sum(normed_two, d_logits)
    d_normed_two = d_normed_two + flat_dot_t(d_logits, full_router)
    d_resid_norm, grad_norm2 = norm_back(d_normed_two, residual, scale_two, norm2_gain)
    d_resid = grad_out + d_resid_norm
    d_resid_low = d_resid.astype(jnp.bfloat16)
    d_mixed = flat_dot_t(d_resid_low, full_out)
    grad_out_w = outer_sum(mixed_out, d_resid_low)
    gain_scaled = d_mixed * gnorm_gain
    grad_gnorm = jnp.sum((d_mixed * gated * scale_gated).reshape(-1, inner_here), axis=0)
    cross_sum = head_total(jnp.sum(gain_scaled * gated, axis=-1, keepdims=True))
    d_gated = (
        scale_gated * gain_scaled
        - gated * scale_gated * scale_gated * scale_gated * cross_sum / INNER
    )
    d_y = d_gated * gate_z * gate_sig
    d_gate_z = (d_gated * y_flat * silu_slope(gate_z, gate_sig)).astype(jnp.bfloat16)
    d_y_heads = d_y.reshape(x_heads.shape)
    grad_skip = jnp.sum(d_y_heads * x_heads, axis=(0, 1, 3))
    log_decay = jnp.cumsum(step_size * decay_rate, axis=0)
    enters = jnp.exp(log_decay) * (doc_ids == prev_doc[None, :]).astype(jnp.float32)[..., None]
    g_local = jnp.einsum("tsh,tshp,tsn->shpn", enters, d_y_heads, c_state, precision=HIGH)
    a_after, state_grad = entering(
        (a_total, g_local), "seq", carry_combine, (ones_start, zeros_start), True
    )

    def local_scan(x_part, step_part, b_part, c_part, rate_part, state_part):
        return ssm_local(
            x_part, step_part, b_part, c_part, rate_part, state_part, doc_ids, prev_doc
        )

    _, scan_back = jax.vjp(local_scan, x_heads, step_size, b_state, c_state, decay_rate, s_before)
    d_xh, d_step, d_bstate, d_cstate, d_rate, _ = scan_back((d_y_heads, state_grad))
    d_xh = d_xh + d_skip[:, None] * d_y_heads
    d_bc = head_total(jnp.concatenate([d_bstate, d_cstate], axis=-1))
    d_dt_pre = d_step * jax.nn.sigmoid(dt_pre)
    grad_dtb = jnp.sum(d_dt_pre, axis=(0, 1))
    grad_alog = d_rate * decay_rate
    d_conv_out = jnp.concatenate([d_xh.reshape(block_len, seq_here, inner_here), d_bc], axis=-1)

    def local_conv(ext_part, weight_part, shift_part):
        return conv_apply(ext_part, docs_ext, weight_part, shift_part)

    _, conv_back = jax.vjp(local_conv, conv_ext, conv_weight, conv_shift)
    d_ext, grad_cweight, grad_cshift = conv_back(d_conv_out)
    from_next = passed_along(shortened(d_ext[:edge_len]), "seq", -1)
    d_conv_in = d_ext[edge_len:] + jnp.concatenate(
        [jnp.zeros((block_len - edge_len,) + from_next.shape[1:], jnp.float32), from_next], 0
    )
    d_proj_x = d_conv_in[..., :inner_here].astype(jnp.bfloat16)
    d_proj_bc = d_conv_in[..., inner_here:].astype(jnp.bfloat16)
    d_dt_low = d_dt_pre.astype(jnp.bfloat16)
    grad_wz = outer_sum(normed_one, d_gate_z)
    grad_wx = outer_sum(normed_one, d_proj_x)
    grad_wbc = outer_sum(normed_one, d_proj_bc)
    grad_wdt = outer_sum(normed_one, d_dt_low)
    head_first = jnp.where(lax.axis_index("head") == 0, 1.0, 0.0)
    d_normed_one = (
        flat_dot_t(d_gate_z, full_z) + flat_dot_t(d_proj_x, full_x) + flat_dot_t(d_dt_low, full_dt)
    )
    d_normed_one = head_total(d_normed_one + head_first * flat_dot_t(d_proj_bc, full_bc))
    d_x_norm, grad_norm1 = norm_back(d_normed_one, x_float, scale_one, norm1_gain)
    input_grad = d_resid + d_x_norm
    reduced = (
        lax.psum_scatter(grad_wz, "seq", scatter_dimension=0, tiled=True),
        lax.psum_scatter(grad_wx, "seq", scatter_dimension=0, tiled=True),
        lax.psum_scatter(grad_wdt, "seq", scatter_dimension=0, tiled=True),
        lax.psum_scatter(grad_wbc, "seq", scatter_dimension=0, tiled=True),
        lax.psum_scatter(grad_router, "seq", scatter_dimension=0, tiled=True),
        lax.psum_scatter(grad_sgate, "seq", scatter_dimension=0, tiled=True),
        lax.psum_scatter(grad_sup, "seq", scatter_dimension=0, tiled=True),
        lax.psum_scatter(grad_out_w, "seq", scatter_dimension=1, tiled=True),
        lax.psum_scatter(grad_sdown, "seq", scatter_dimension=1, tiled=True),
    )
    red_z, red_x, red_dt, red_bc, red_router, red_sgate, red_sup, red_out, red_sdown = reduced
    small_sums = lax.psum(
        (
            grad_norm1,
            grad_norm2,
            grad_cweight,
            grad_cshift,
            grad_dtb,
            grad_alog,
            grad_skip,
            grad_gnorm,
        ),
        "seq",
    )
    sum_norm1, sum_norm2, sum_cweight, sum_cshift, sum_dtb, sum_alog, sum_skip, sum_gnorm = (
        small_sums
    )
    return (
        block_out,
        input_grad,
        sum_norm1,
        red_z,
        red_x,
        red_bc,
        red_dt,
        sum_cweight[:, :inner_here],
        sum_cweight[:, inner_here:],
        sum_cshift[:inner_here],
        sum_cshift[inner_here:],
        sum_dtb,
        sum_alog,
        sum_skip,
        sum_gnorm,
        red_out,
        sum_norm2,
        red_router,
        red_sgate,
        red_sup,
        red_sdown,
        grad_egate,
        expert_up_gradient,
        grad_edown,
    )


MESH = pl.DeviceIdType.MESH
VMEM = pltpu.VMEM


def peers():
    here, side = lax.axis_index("seq"), lax.axis_index("head")
    x, y, z = lax.rem(here, 2), lax.rem(here // 2, 2), here // 4
    col = x + 2 * y
    return here, side, z, col, (1 - x) + 2 * y, x + 2 * (1 - y), 3 - col


def layers(z):
    lo, hi = lax.rem(z, 2), z // 2
    return [2 * (1 - hi if k & 2 else hi) + (1 - lo if k & 1 else lo) for k in range(4)]


def greet(devices):
    barrier = pltpu.get_barrier_semaphore()
    for device in devices:
        pl.semaphore_signal(barrier, inc=1, device_id=device, device_id_type=MESH)
    pl.semaphore_wait(barrier, len(devices))


class Mail:
    def __init__(self, send, base=0):
        self.send, self.sent, self.base = send, [], base

    def put(self, src, dst, sem, to):
        copy = pltpu.make_async_remote_copy(
            src_ref=src,
            dst_ref=dst,
            send_sem=self.send.at[self.base + len(self.sent)],
            recv_sem=sem,
            device_id=to,
            device_id_type=MESH,
        )
        copy.start()
        self.sent.append(copy)

    def arrived(self, dst, sem):
        pltpu.make_async_remote_copy(
            src_ref=dst,
            dst_ref=dst,
            send_sem=self.send.at[0],
            recv_sem=sem,
            device_id=(0, 0),
            device_id_type=MESH,
        ).wait_recv()

    def finish(self):
        for copy in self.sent:
            copy.wait_send()


def rows_at(ref, start, size, step):
    return ref.at[pl.ds(pl.multiple_of(start, step), size)]


def gather_steps(mail, own_ref, out_ref, recv, recv_half, rows, half=None):
    here, side, z, col, cx, cy, cd = peers()
    zs = layers(z)
    base = 4 * z

    def block(place):
        return rows_at(out_ref, place * rows, rows, 16)

    def part(place, which):
        if half is None:
            width = out_ref.shape[1] // 2
            at = pl.ds(pl.multiple_of(place * rows, 16), rows)
            return out_ref.at[at, pl.ds(which * width, width)]
        size = rows - half if which else half
        return rows_at(out_ref, place * rows + which * half, size, 16)

    mail.put(own_ref, block(here), recv.at[3], (base + cx, side))
    mail.put(own_ref, block(here), recv.at[7], (base + cy, side))
    for k in (1, 2, 3):
        mail.put(own_ref, block(here), recv.at[k - 1], (4 * zs[k] + col, side))
    yield
    for k in range(4):
        if k:
            at = 4 * zs[k] + col
            mail.arrived(block(at), recv.at[k - 1])
            mail.put(block(at), block(at), recv.at[3 + k], (base + cx, side))
            mail.put(block(at), block(at), recv.at[7 + k], (base + cy, side))
            yield
        at = 4 * zs[k] + cx
        mail.arrived(block(at), recv.at[3 + k])
        mail.put(part(at, 0), part(at, 0), recv_half.at[k], (base + cy, side))
        at = 4 * zs[k] + cy
        mail.arrived(block(at), recv.at[7 + k])
        mail.put(part(at, 1), part(at, 1), recv_half.at[4 + k], (base + cx, side))
        yield
    for k in range(4):
        at = 4 * zs[k] + cd
        mail.arrived(part(at, 0), recv_half.at[k])
        mail.arrived(part(at, 1), recv_half.at[4 + k])
        yield


def near(side):
    here, side, z, col, cx, cy, cd = peers()
    zs = layers(z)
    return [(4 * z + cx, side), (4 * z + cy, side)] + [(4 * zs[k] + col, side) for k in (1, 2, 3)]


def note_puts(mail, src_of, notes_out, recv_n):
    here, side = peers()[:2]
    for k in range(1, 16):
        to = lax.rem(here + k, 16)
        mail.put(src_of(to), notes_out.at[here], recv_n.at[here], (to, side))


def note_waits(mail, notes_out, recv_n):
    here = peers()[0]
    for k in range(1, 16):
        place = lax.rem(here + k, 16)
        mail.arrived(notes_out.at[place], recv_n.at[place])


def reduce_steps(mail, part_ref, out_ref, got, sums, recv, rows):
    here, side, z, col, cx, cy, cd = peers()
    zs = layers(z)
    base = 4 * z
    half = rows // 2
    got_a, got_b, got_x, got_y, got_z = got
    sum_x, sum_y, sum_z = sums
    to_x, to_y = (base + cx, side), (base + cy, side)
    f32 = jnp.float32

    def half_of(place, which):
        return rows_at(part_ref, place * rows + which * half, half, half)

    def far(k):
        at = 4 * zs[k] + cd
        mail.put(half_of(at, 0), got_a.at[k], recv.at[k], to_y)
        mail.put(half_of(at, 1), got_b.at[k], recv.at[4 + k], to_x)

    def plain(k):
        mail.put(half_of(4 * zs[k] + cx, 1), got_x.at[k, pl.ds(half, half)], recv.at[12 + k], to_x)
        mail.put(half_of(4 * zs[k] + cy, 0), got_y.at[k, pl.ds(0, half)], recv.at[16 + k], to_y)

    def joined(k):
        mail.arrived(got_a.at[k], recv.at[k])
        total = half_of(4 * zs[k] + cx, 0)[...].astype(f32) + got_a[k].astype(f32)
        sum_x[k] = total.astype(sum_x.dtype)
        mail.put(sum_x.at[k], got_x.at[k, pl.ds(0, half)], recv.at[8 + k], to_x)
        mail.arrived(got_b.at[k], recv.at[4 + k])
        total = half_of(4 * zs[k] + cy, 1)[...].astype(f32) + got_b[k].astype(f32)
        sum_y[k] = total.astype(sum_y.dtype)
        mail.put(sum_y.at[k], got_y.at[k, pl.ds(half, half)], recv.at[20 + k], to_y)

    def column(k):
        mail.arrived(got_x.at[k, pl.ds(half, half)], recv.at[12 + k])
        mail.arrived(got_y.at[k, pl.ds(0, half)], recv.at[16 + k])
        mail.arrived(got_x.at[k, pl.ds(0, half)], recv.at[8 + k])
        mail.arrived(got_y.at[k, pl.ds(half, half)], recv.at[20 + k])
        own = part_ref[pl.ds(pl.multiple_of((4 * zs[k] + col) * rows, rows), rows)].astype(f32)
        total = own + got_x[k].astype(f32) + got_y[k].astype(f32)
        if k:
            sum_z[k - 1] = total.astype(sum_z.dtype)
            mail.put(sum_z.at[k - 1], got_z.at[k - 1], recv.at[23 + k], (4 * zs[k] + col, side))
        else:
            out_ref[...] = total

    far(3)
    plain(3)
    yield
    far(2)
    plain(2)
    yield
    joined(3)
    yield
    far(1)
    plain(1)
    yield
    joined(2)
    yield
    column(3)
    yield
    far(0)
    plain(0)
    yield
    joined(1)
    yield
    column(2)
    yield
    joined(0)
    yield
    column(1)
    yield
    column(0)
    yield
    for k in (3, 2, 1):
        mail.arrived(got_z.at[k - 1], recv.at[23 + k])
        out_ref[...] += got_z[k - 1].astype(f32)


def reduce_scratch(rows, width, kind):
    half = rows // 2
    shapes = [(4, half), (4, half), (4, rows), (4, rows), (3, rows), (4, half), (4, half), (3, rows)]
    return [VMEM(shape + (width,), kind) for shape in shapes]


def same_side(side, here):
    return [(lax.rem(here + k, 16), side) for k in range(1, 16)]


DMA = pltpu.SemaphoreType.DMA


def remote(src, dst, send, recv, to):
    return pltpu.make_async_remote_copy(
        src_ref=src,
        dst_ref=dst,
        send_sem=send,
        recv_sem=recv,
        device_id=to,
        device_id_type=MESH,
    )


def call(kernel, name, number, outs, scratch, args, spaces=None, limit=60):
    vmem = pl.BlockSpec(memory_space=VMEM)
    hbm = pl.BlockSpec(memory_space=pl.ANY)
    ins_far, outs_far = spaces or ((), ())
    return pl.pallas_call(
        kernel,
        out_shape=tuple(jax.ShapeDtypeStruct(shape, kind) for shape, kind in outs),
        in_specs=[hbm if i in ins_far else vmem for i in range(len(args))],
        out_specs=tuple(hbm if i in outs_far else vmem for i in range(len(outs))),
        scratch_shapes=scratch,
        compiler_params=pltpu.CompilerParams(
            collective_id=number, has_side_effects=True, vmem_limit_bytes=limit << 20
        ),
        name=name,
    )(*args)


def enter_kernel(
    x_ref,
    norm_ref,
    mine_ref,
    wz_ref,
    sg_ref,
    wx_ref,
    su_ref,
    wo_ref,
    sd_ref,
    small_ref,
    gate_ref,
    up_ref,
    down_ref,
    all_ref,
    extras_ref,
    extra_ref,
    cols_ref,
    small_other,
    gate_other,
    up_other,
    down_other,
    own_ref,
    blocks_ref,
    send,
    recv,
    recv_half,
    recv_m,
    recv_half_m,
    recv_w,
    recv_e,
    recv_s,
    local,
):
    here, side = peers()[:2]
    places = 16
    sibling = (here, 1 - side)
    x = x_ref[...].astype(jnp.float32)
    scale = lax.rsqrt(jnp.mean(x * x, axis=-1, keepdims=True) + EPS)
    own_ref[...] = (x * scale * norm_ref[...]).astype(jnp.bfloat16)
    greet(same_side(side, here) + [sibling])
    depth = blocks_ref.shape[1]
    rows, extra = own_ref.shape[0], mine_ref.shape[0]
    half_here = here // 8
    mail = Mail(send)
    mine = pltpu.make_async_copy(own_ref, rows_at(all_ref, here * rows, rows, 16), local.at[0])
    mine.start()
    mine_too = pltpu.make_async_copy(
        mine_ref, rows_at(extras_ref, here * extra, extra, 16), local.at[18]
    )
    mine_too.start()

    def strip(place):
        return rows_at(cols_ref, place * depth, depth, 16)

    steps = gather_steps(mail, own_ref, all_ref, recv, recv_half, rows, rows // 2)
    steps_too = gather_steps(mail, mine_ref, extras_ref, recv_m, recv_half_m, extra)
    next(steps_too)
    next(steps)
    mail.put(small_ref, small_other, recv_s.at[0], sibling)
    for j in range(8):
        wide, narrow = slice(192 * j, 192 * (j + 1)), slice(64 * j, 64 * (j + 1))
        blocks_ref[j, :, 0:192] = wz_ref[:, wide]
        blocks_ref[j, :, 192:256] = sg_ref[:, narrow]
        blocks_ref[j, :, 256:448] = wx_ref[:, wide]
        blocks_ref[j, :, 448:512] = su_ref[:, narrow]
        blocks_ref[j, :, 512:704] = wo_ref[:, wide]
        blocks_ref[j, :, 704:768] = sd_ref[:, narrow]
    first = 8 * side + lax.rem(here, 8)
    is_mine = side == half_here
    for k in range(1, 8):
        to = 8 * side + lax.rem(here + k, 8)
        mail.put(blocks_ref.at[to - 8 * side], strip(here), recv_w.at[here], (to, side))

    def keep():
        return pltpu.make_async_copy(blocks_ref.at[here - 8 * side], strip(here), local.at[1])

    def give():
        block = blocks_ref.at[first - 8 * side]
        return remote(block, strip(here), local.at[1], recv_w.at[here], (first, side))

    @pl.when(is_mine)
    def _():
        keep().start()

    @pl.when(jnp.logical_not(is_mine))
    def _():
        give().start()

    mail.put(gate_ref, gate_other, recv_s.at[1], sibling)
    mail.put(up_ref, up_other, recv_s.at[2], sibling)
    mail.put(down_ref, down_other, recv_s.at[3], sibling)
    for _ in steps_too:
        next(steps)
    for _ in steps:
        pass
    mine.wait()
    mine_too.wait()
    for place in range(places):
        at = pl.ds(place * extra, extra)
        mail.put(extras_ref.at[at], extra_ref.at[at], recv_e.at[place], sibling)

    def forward(place, k):
        return remote(strip(place), strip(place), local.at[2 + k], recv_w.at[place], sibling)

    @pl.when(is_mine)
    def _():
        keep().wait()
        forward(here, 0).start()

    @pl.when(jnp.logical_not(is_mine))
    def _():
        forward(here, 0).wait_recv()
        give().wait_send()

    for k in range(1, places):
        place = lax.rem(here + k, places)
        forward(place, k).wait_recv()

        @pl.when(is_mine)
        def _():
            forward(place, k).start()

    @pl.when(is_mine)
    def _():
        for k in range(places):
            forward(lax.rem(here + k, places), k).wait_send()

    mail.arrived(small_other, recv_s.at[0])
    mail.arrived(gate_other, recv_s.at[1])
    mail.arrived(up_other, recv_s.at[2])
    mail.arrived(down_other, recv_s.at[3])
    for place in range(places):
        mail.arrived(extra_ref.at[pl.ds(place * extra, extra)], recv_e.at[place])
    mail.finish()


def enter(*args):
    low, f32 = jnp.bfloat16, jnp.float32
    return call(
        enter_kernel,
        "enter",
        1,
        (
            ((1024, 1536), low),
            ((1536, 256), low),
            ((1536, 256), low),
            ((1536, 768), low),
            ((8, 1536), f32),
            ((1536, 256), low),
            ((1536, 256), low),
            ((256, 1536), low),
        ),
        [
            VMEM((64, 1536), low),
            VMEM((8, 96, 768), low),
            DMA((65,)),
            DMA((11,)),
            DMA((8,)),
            DMA((11,)),
            DMA((8,)),
            DMA((16,)),
            DMA((16,)),
            DMA((4,)),
            DMA((19,)),
        ],
        args,
        ((10, 11, 12), (5, 6, 7)),
    )


def leave_kernel(
    main_ref,
    bcr_ref,
    small_ref,
    block_ref,
    input_ref,
    gz_ref,
    gx_ref,
    gsg_ref,
    gsu_ref,
    gout_ref,
    gsd_ref,
    bcr_out,
    norms_ref,
    tapbc_ref,
    tapx_ref,
    chan_ref,
    headg_ref,
    block_other,
    input_other,
    got_main,
    got_bcr,
    send_main,
    send_bcr,
    main_parts,
    bcr_parts,
    bcr_mine,
    bcr_sib,
    small_got,
    small_sum,
    small_all,
    send,
    recv_sib,
    recv_main,
    recv_bcr,
    recv_small,
    recv_pair,
    cond,
):
    here, side = peers()[:2]
    sibling = (here, 1 - side)
    is_main = side == here // 8
    f32 = jnp.float32
    greet(same_side(side, here) + [sibling])
    mail = Mail(send)
    mail.put(small_ref, small_got, recv_sib.at[1], sibling)

    def give_main():
        return remote(main_ref, got_main, cond.at[0], recv_sib.at[0], sibling)

    def give_bcr():
        return remote(bcr_ref, got_bcr, cond.at[0], recv_sib.at[0], sibling)

    def send_on(total, out, sem, slot, k):
        to = lax.rem(here + k, 16)
        return remote(total.at[to], out.at[slot], cond.at[k], sem.at[slot], (to, side))

    slot = lax.rem(here, 8)

    @pl.when(is_main)
    def _():
        give_bcr().start()

    @pl.when(jnp.logical_not(is_main))
    def _():
        give_main().start()

    mail.put(block_ref, block_other, recv_sib.at[3], sibling)
    mail.put(input_ref, input_other, recv_sib.at[4], sibling)
    mail.arrived(small_got, recv_sib.at[1])
    small_sum[...] = small_ref[...] + small_got[...]
    small_all[side, here] = small_sum[side]
    for k in range(1, 16):
        to = lax.rem(here + k, 16)
        mail.put(small_sum.at[side], small_all.at[side, here], recv_small.at[here], (to, side))

    @pl.when(is_main)
    def _():
        give_main().wait_recv()
        for k in range(1, 16):
            to = lax.rem(here + k, 16)
            total = main_ref[to].astype(f32) + got_main[to].astype(f32)
            send_main[to] = total.astype(send_main.dtype)
            send_on(send_main, main_parts, recv_main, slot, k).start()
        total = main_ref[here].astype(f32) + got_main[here].astype(f32)
        main_parts[slot] = total.astype(main_parts.dtype)

    @pl.when(jnp.logical_not(is_main))
    def _():
        give_bcr().wait_recv()
        for k in range(1, 16):
            to = lax.rem(here + k, 16)
            total = bcr_ref[to].astype(f32) + got_bcr[to].astype(f32)
            send_bcr[to] = total.astype(send_bcr.dtype)
            send_on(send_bcr, bcr_parts, recv_bcr, slot, k).start()
        total = bcr_ref[here].astype(f32) + got_bcr[here].astype(f32)
        bcr_parts[slot] = total.astype(bcr_parts.dtype)

    for k in range(1, 16):
        place = lax.rem(here + k, 16)
        mail.arrived(small_all.at[side, place], recv_small.at[place])
    mail.put(small_all.at[side], small_all.at[side], recv_pair, sibling)
    for j in range(8):

        @pl.when(8 * (1 - side) + j != here)
        def _():
            mail.arrived(bcr_parts.at[j], recv_bcr.at[j])

    total = bcr_parts[0].astype(f32)
    for j in range(1, 8):
        total = total + bcr_parts[j].astype(f32)
    bcr_mine[...] = total
    mail.put(bcr_mine, bcr_sib, recv_sib.at[2], sibling)
    mail.arrived(small_all.at[1 - side], recv_pair)
    norms = small_all[0, 0]
    for j in range(1, 16):
        norms = norms + small_all[0, j]
    norms_ref[...] = norms
    taps = small_all[1, 0, :, 0:256]
    for j in range(1, 16):
        taps = taps + small_all[1, j, :, 0:256]
    tapbc_ref[...] = taps
    for j in range(8):
        place = 8 * side + j
        wide = slice(192 * j, 192 * (j + 1))
        tapx_ref[:, wide] = small_all[1, place, :, 256:448]
        chan_ref[j] = small_all[1, place, 5:8, 0:256]
        headg_ref[j] = small_all[1, place, 5:8, 256:512]
    for j in range(8):

        @pl.when(8 * side + j != here)
        def _():
            mail.arrived(main_parts.at[j], recv_main.at[j])

        wide, narrow = slice(192 * j, 192 * (j + 1)), slice(64 * j, 64 * (j + 1))
        part = main_parts[j].astype(f32)
        gz_ref[:, wide] = part[:, 0:192]
        gsg_ref[:, narrow] = part[:, 192:256]
        gx_ref[:, wide] = part[:, 256:448]
        gsu_ref[:, narrow] = part[:, 448:512]
        gout_ref[:, wide] = part[:, 512:704]
        gsd_ref[:, narrow] = part[:, 704:768]
    mail.arrived(bcr_sib, recv_sib.at[2])
    bcr_out[...] = bcr_mine[...] + bcr_sib[...]
    mail.arrived(block_other, recv_sib.at[3])
    mail.arrived(input_other, recv_sib.at[4])

    @pl.when(is_main)
    def _():
        give_bcr().wait_send()
        for k in range(1, 16):
            send_on(send_main, main_parts, recv_main, slot, k).wait_send()

    @pl.when(jnp.logical_not(is_main))
    def _():
        give_main().wait_send()
        for k in range(1, 16):
            send_on(send_bcr, bcr_parts, recv_bcr, slot, k).wait_send()

    mail.finish()


def leave(*args):
    low, f32 = jnp.bfloat16, jnp.float32
    return call(
        leave_kernel,
        "leave",
        6,
        (
            ((96, 1536), f32),
            ((96, 1536), f32),
            ((96, 512), f32),
            ((96, 512), f32),
            ((96, 1536), f32),
            ((96, 512), f32),
            ((96, 384), f32),
            ((8, 512), f32),
            ((8, 256), f32),
            ((8, 1536), f32),
            ((8, 3, 256), f32),
            ((8, 3, 256), f32),
            ((64, 1536), f32),
            ((64, 1536), f32),
        ),
        [
            VMEM((16, 96, 768), low),
            VMEM((16, 96, 384), low),
            VMEM((16, 96, 768), low),
            VMEM((16, 96, 384), low),
            VMEM((8, 96, 768), low),
            VMEM((8, 96, 384), low),
            VMEM((96, 384), f32),
            VMEM((96, 384), f32),
            VMEM((2, 8, 512), f32),
            VMEM((2, 8, 512), f32),
            VMEM((2, 16, 8, 512), f32),
            DMA((20,)),
            DMA((5,)),
            DMA((8,)),
            DMA((8,)),
            DMA((16,)),
            DMA,
            DMA((16,)),
        ],
        args,
    )


CHUNK = 128
LAYER = 256
HEADW = 64


def mm(left, right, low=True, exact=False):
    return mm_of(left, right, ((1,), (0,)), low, exact)


def mm_nt(left, right, low=True, exact=False):
    return mm_of(left, right, ((1,), (1,)), low, exact)


def mm_tn(left, right, low=True, exact=False):
    return mm_of(left, right, ((0,), (0,)), low, exact)


def mm_of(left, right, dims, low, exact):
    if exact:
        return lax.dot_general(
            left, right, (dims, ((), ())), precision=HIGH, preferred_element_type=jnp.float32
        )
    if low:
        left, right = left.astype(jnp.bfloat16), right.astype(jnp.bfloat16)
    return lax.dot_general(left, right, (dims, ((), ())), preferred_element_type=jnp.float32)


def lanes(shape):
    return lax.broadcasted_iota(jnp.int32, shape, 1)


def by_head(parts, rows):
    lane = lanes((rows, 3 * HEADW))
    return jnp.where(lane < HEADW, parts[0], jnp.where(lane < 2 * HEADW, parts[1], parts[2]))


def spread_heads(array):
    return by_head([array[:, h : h + 1] for h in range(3)], array.shape[0])


def soft_plus(values):
    return jnp.maximum(values, 0.0) + jnp.log1p(jnp.exp(-jnp.abs(values)))


def chunk_tables(step, log_rate, doc_col, doc_row):
    row = lax.broadcasted_iota(jnp.int32, (CHUNK, CHUNK), 0)
    col = lax.broadcasted_iota(jnp.int32, (CHUNK, CHUNK), 1)
    below = (row >= col).astype(jnp.float32)
    logs = mm(below, step * log_rate, exact=True)
    logs_t, step_t = logs.T, step.T
    pair = (row >= col) & (doc_col == doc_row)
    tables = [
        jnp.exp(jnp.where(pair, logs[:, h : h + 1] - logs_t[h : h + 1], -1e9)) for h in range(3)
    ]
    return logs, tables, [step_t[h : h + 1] for h in range(3)]


def as_column(row):
    return jnp.concatenate([row, jnp.zeros((CHUNK - 8, CHUNK), jnp.float32)], 0).T


def as_row(column):
    wide = jnp.broadcast_to(column, (64, CHUNK))
    return jnp.concatenate([wide, jnp.zeros((64, CHUNK), jnp.float32)], 0).T[0:8]


def mix_forward_kernel(
    n1_ref,
    extras_ref,
    extra_ref,
    cols_ref,
    small_ref,
    small_other,
    tapbc_ref,
    biasbc_ref,
    g_ref,
    x_ref,
    norm_ref,
    z_ref,
    ext_ref,
    dt_ref,
    y_ref,
    state_ref,
    g_all_ref,
    n2_all_ref,
    scales_ref,
    res_ref,
    proj_ref,
    scale_ref,
    ids_ref,
    wbc_ref,
    wdt_ref,
    taps_ref,
    head_ref,
    gain_ref,
    part_ref,
    gained_ref,
    notes_ref,
    sum_ref,
    n2_ref,
    note_ref,
    notes_out,
    *refs,
):
    got, sums, refs = refs[:5], refs[5:8], refs[8:]
    send, recv, recv_n, g_send, g_recv, g_recv_half = refs[:6]
    n_send, n_recv, n_recv_half, n_recv_n, local = refs[6:]
    here, side, z_at = peers()[:3]
    half_here, slot = here // 8, lax.rem(here, 8)
    greet(same_side(side, here))
    low, f32 = jnp.bfloat16, jnp.float32
    mine = pltpu.make_async_copy(g_ref, rows_at(g_all_ref, here * 64, 64, 16), local.at[0])
    mine.start()
    g_mail = Mail(g_send)
    g_steps = gather_steps(g_mail, g_ref, g_all_ref, g_recv, g_recv_half, 64, 32)
    next(g_steps)

    small = jnp.where(side == half_here, small_ref[...], small_other[...])
    turned = pltpu.roll(small, lax.rem(1536 - 192 * slot, 1536), 1)
    taps_ref[0:4, 0:256] = tapbc_ref[...]
    taps_ref[4:5, 0:256] = biasbc_ref[...]
    taps_ref[5:8] = jnp.zeros((3, 448), f32)
    taps_ref[0:5, 256:448] = turned[0:5, 0:192]
    gain_ref[...] = jnp.broadcast_to(turned[5:6, 0:192], (8, 192))
    numbers = pltpu.roll(small[:, 0:128], lax.rem(128 - 3 * slot, 128), 1)[6:7]
    used = lanes((1, 128)) < 3
    head_ref[0:1] = jnp.where(used, numbers, 0.0)
    head_ref[1:2] = jnp.where(used, -jnp.exp(pltpu.roll(numbers, 104, 1)), 0.0)
    head_ref[2:3] = jnp.where(used, pltpu.roll(numbers, 80, 1), 0.0)
    wbc_ref[:, pl.ds(pl.multiple_of(side * 128, 128), 128)] = extras_ref[:, 0:128]
    wbc_ref[:, pl.ds(pl.multiple_of((1 - side) * 128, 128), 128)] = extra_ref[:, 0:128]
    wdt_ref[...] = jnp.where(side == half_here, extras_ref[:, 128:256], extra_ref[:, 128:256])
    ids_ref[0:8] = jnp.full((8, 128), -1.0, f32)
    ids_ref[1032:1040] = jnp.full((8, 128), -2.0, f32)
    for p in range(16):
        ids_ref[8 + 64 * p : 72 + 64 * p] = extras_ref[96 * p : 96 * p + 64, 128:256].astype(f32)
    notes_ref[...] = jnp.zeros(notes_ref.shape, f32)
    ext_ref[0:8] = jnp.zeros((8, 448), f32)

    @pl.loop(0, 4)
    def _(i):
        at = pl.ds(pl.multiple_of(i * LAYER, LAYER), LAYER)
        shifted = pl.ds(pl.multiple_of(i * LAYER + 8, 8), LAYER)
        rows = n1_ref[at]
        z_ref[at] = mm(rows, cols_ref[:, 0:192])
        ext_ref[shifted, 0:256] = mm(rows, wbc_ref[...])
        ext_ref[shifted, 256:448] = mm(rows, cols_ref[:, 256:448])
        dt_ref[at] = pltpu.roll(mm(rows, wdt_ref[...]), 112 - 3 * slot, 1) + head_ref[0:1]

    next(g_steps)
    rate, skip = head_ref[1:2], spread_heads(head_ref[2:3])
    state = jnp.zeros((128, 192), f32)
    ones = jnp.ones((8, 192), f32)
    for c in range(8):
        r = c * CHUNK
        at = pl.ds(r, CHUNK)
        ids = ids_ref[pl.ds(r + 8, CHUNK)]
        doc = ids[:, 40:41]
        pre = conv_pre(taps_ref, ext_ref, ids_ref, r, doc)
        act = pre * jax.nn.sigmoid(pre)
        b, cc, x = act[:, 0:128], act[:, 128:256], act[:, 256:448]
        step = soft_plus(dt_ref[at])
        logs, tables, step_t = chunk_tables(step, rate, doc, ids.T[40:41])
        cross = mm_nt(cc, b)
        stacked = jnp.concatenate([cross * tables[h] * step_t[h] for h in range(3)], 0)
        intra = mm(stacked, x)
        y = by_head([intra[h * CHUNK : (h + 1) * CHUNK] for h in range(3)], CHUNK)
        first, last = chunk_masks(ids_ref, r, doc)
        enters = jnp.exp(logs) * first
        state_ref[c] = state
        y = y + spread_heads(enters) * mm(cc, state) + skip * x
        y_ref[at] = y
        tail = jnp.exp(logs[CHUNK - 1 :] - logs) * last * step
        state = spread_heads(enters[CHUNK - 1 :]) * state + mm_tn(b, spread_heads(tail) * x)
        z = z_ref[at]
        gated = y * z * jax.nn.sigmoid(z)
        gained_ref[at] = (gated * gain_ref[0:1]).astype(low)
        squares = mm_nt(ones, gated * gated, exact=True)
        notes_ref[2 * c, :, 0:64] = squares[:, 0:64]
        notes_ref[2 * c + 1, :, 0:64] = squares[:, 64:128]
        next(g_steps, None)

    mail = Mail(send)
    zs = layers(z_at)

    def layer(k):
        at = pl.ds(pl.multiple_of(zs[k] * LAYER, LAYER), LAYER)

        @pl.loop(0, 6)
        def _(i):
            n = pl.ds(pl.multiple_of(i * 256, 256), 256)
            part_ref[at, n] = mm_nt(gained_ref[at], cols_ref[n, 512:704]).astype(low)

    steps = reduce_steps(mail, part_ref, sum_ref, got, sums, recv, 64)
    left = [3, 2, 1, 0]
    for turn in range(13):
        if turn in (0, 1, 3, 6):
            layer(left.pop(0))
        next(steps, None)
        if turn == 0:
            notes_out[here] = notes_ref[here]
            note_puts(mail, lambda to: notes_ref.at[to], notes_out, recv_n)
        if turn > 2:
            next(g_steps, None)
    for _ in g_steps:
        pass
    for _ in steps:
        pass
    note_waits(mail, notes_out, recv_n)
    squares = notes_out[0]
    for j in range(1, 16):
        squares = squares + notes_out[j]
    scale_row = lax.rsqrt(squares / INNER + EPS)
    note_ref[...] = scale_row
    scale = as_column(scale_row)[0:64, 0:1]
    scale_ref[...] = jnp.broadcast_to(scale, (64, 128))
    projected = scale * sum_ref[...]
    proj_ref[...] = projected
    residual = x_ref[...].astype(f32) + projected
    res_ref[...] = residual
    scale_two = lax.rsqrt(jnp.mean(residual * residual, axis=-1, keepdims=True) + EPS)
    n2_ref[...] = (residual * scale_two * norm_ref[...]).astype(low)
    mine_too = pltpu.make_async_copy(n2_ref, rows_at(n2_all_ref, here * 64, 64, 16), local.at[1])
    mine_too.start()
    n_mail = Mail(n_send)
    n_steps = gather_steps(n_mail, n2_ref, n2_all_ref, n_recv, n_recv_half, 64, 32)
    next(n_steps)
    scales_ref[here] = note_ref[...]
    note_puts(n_mail, lambda to: note_ref, scales_ref, n_recv_n)
    for _ in n_steps:
        pass
    note_waits(n_mail, scales_ref, n_recv_n)
    mine.wait()
    mine_too.wait()
    g_mail.finish()
    mail.finish()
    n_mail.finish()


def conv_pre(taps_ref, ext_ref, ids_ref, r, doc):
    pre = taps_ref[4:5] + taps_ref[3:4] * ext_ref[pl.ds(r + 8, CHUNK)]
    for k in (1, 2, 3):
        same = (ids_ref[pl.ds(r + 8 - k, CHUNK), 40:41] == doc).astype(jnp.float32)
        pre = pre + taps_ref[3 - k : 4 - k] * ext_ref[pl.ds(r + 8 - k, CHUNK)] * same
    return pre


def chunk_masks(ids_ref, r, doc):
    first = (ids_ref[r + 7 : r + 8, 40:41] == doc).astype(jnp.float32)
    last = (ids_ref[r + 7 + CHUNK : r + 8 + CHUNK, 40:41] == doc).astype(jnp.float32)
    return first, last


def mix_forward(*args):
    low, f32 = jnp.bfloat16, jnp.float32
    return call(
        mix_forward_kernel,
        "mix_forward",
        2,
        (
            ((1024, 192), f32),
            ((1032, 448), f32),
            ((1024, 128), f32),
            ((1024, 192), f32),
            ((8, 128, 192), f32),
            ((1024, 1536), low),
            ((1024, 1536), low),
            ((16, 8, 128), f32),
            ((64, 1536), f32),
            ((64, 1536), f32),
            ((64, 128), f32),
            ((1040, 128), f32),
            ((1536, 256), low),
            ((1536, 128), low),
            ((8, 448), f32),
            ((8, 128), f32),
            ((8, 192), f32),
        ),
        [
            VMEM((1024, 1536), low),
            VMEM((1024, 192), low),
            VMEM((16, 8, 128), f32),
            VMEM((64, 1536), f32),
            VMEM((64, 1536), low),
            VMEM((8, 128), f32),
            VMEM((16, 8, 128), f32),
        ]
        + reduce_scratch(64, 1536, low)
        + [
            DMA((42,)),
            DMA((27,)),
            DMA((16,)),
            DMA((19,)),
            DMA((11,)),
            DMA((8,)),
            DMA((34,)),
            DMA((11,)),
            DMA((8,)),
            DMA((16,)),
            DMA((2,)),
        ],
        args,
    )


def moe_kernel(
    n2_ref,
    g_ref,
    cols_ref,
    eg_ref,
    ego_ref,
    eu_ref,
    euo_ref,
    ed_ref,
    edo_ref,
    extras_ref,
    ids_ref,
    res_ref,
    proj_ref,
    scale_ref,
    norm_ref,
    g_own_ref,
    dres_ref,
    cross_ref,
    moe_ref,
    geg_ref,
    geu_ref,
    ged_ref,
    shared_ref,
    grouter_ref,
    gnorm_ref,
    dres_own_ref,
    part_ref,
    act_ref,
    hid_ref,
    probs_ref,
    notes_ref,
    notes_out,
    sum_ref,
    low_ref,
    note_ref,
    og_ref,
    ou_ref,
    od_ref,
    sg_ref,
    su_ref,
    sd_ref,
    *refs,
):
    got, sums, refs = refs[:5], refs[5:8], refs[8:]
    send, recv, recv_n, d_send, d_recv, d_recv_half, d_recv_n, e_send, e_recv, local = refs
    here, side, z_at = peers()[:3]
    sibling = (here, 1 - side)
    greet(same_side(side, here) + [sibling])
    low, f32 = jnp.bfloat16, jnp.float32
    zs = layers(z_at)
    ones = jnp.ones((8, 256), f32)
    spare = lanes((LAYER, 128)) >= 64
    lane = lanes((LAYER, 128))
    notes_ref[...] = jnp.zeros(notes_ref.shape, f32)
    pieces = (
        (eg_ref, eu_ref, ed_ref, 0, 256),
        (ego_ref, euo_ref, edo_ref, 256, 256),
    )

    def layer(k):
        start = pl.multiple_of(zs[k] * LAYER, LAYER)
        at = pl.ds(start, LAYER)
        rows, grads = n2_ref[at], g_ref[at]
        logits = mm(rows, extras_ref[:, 128:256])
        ids = ids_ref[pl.ds(pl.multiple_of(start + 8, 8), LAYER)]
        named = jnp.zeros((LAYER, 128), f32)
        for j in range(6):
            named = jnp.where(lane.astype(f32) == ids[:, 41 + j : 42 + j], 1.0, named)
        top = jnp.max(jnp.where(named > 0, logits, -1e30), axis=-1, keepdims=True)
        raised = jnp.exp(jnp.where(named > 0, logits - top, 0.0)) * named
        probs = raised / jnp.sum(raised, axis=-1, keepdims=True)
        probs_ref[at] = probs
        prob = jnp.sum(jnp.where(lane == here, probs, 0.0), axis=-1, keepdims=True)
        slopes = jnp.zeros((8, LAYER), f32)
        for gate_w, up_w, down_w, first, size in pieces:
            gate = mm(rows, gate_w[...])
            up = mm(rows, up_w[...])
            d_act = mm_nt(grads, down_w[...])
            sig = jax.nn.sigmoid(gate)
            act = gate * sig * up
            act_ref[at, first : first + size] = (act * prob).astype(low)
            slopes = slopes + mm_nt(ones, act * d_act, exact=True)
            d_act = d_act * prob
            hid_ref[at, first : first + size] = (d_act * up * silu_slope(gate, sig)).astype(low)
            hid_ref[at, 640 + first : 640 + first + size] = (d_act * gate * sig).astype(low)
        gate = mm(rows, cols_ref[:, 128:256])
        up = mm(rows, cols_ref[:, 384:512])
        d_act = jnp.where(spare, mm(grads, cols_ref[:, 640:768]), 0.0)
        sig = jax.nn.sigmoid(gate)
        act_ref[at, 512:640] = jnp.where(spare, gate * sig * up, 0.0).astype(low)
        hid_ref[at, 512:640] = (d_act * up * silu_slope(gate, sig)).astype(low)
        hid_ref[at, 1152:1280] = (d_act * gate * sig).astype(low)
        for j in range(4):
            notes_ref[4 * zs[k] + j, :, 0:64] = slopes[:, 64 * j : 64 * (j + 1)]

        @pl.loop(0, 6)
        def _(i):
            n = pl.ds(pl.multiple_of(i * 256, 256), 256)
            total = mm_nt(hid_ref[at, 0:256], eg_ref[n])
            total = total + mm_nt(hid_ref[at, 256:512], ego_ref[n])
            total = total + mm_nt(hid_ref[at, 512:640], cols_ref[n, 128:256])
            total = total + mm_nt(hid_ref[at, 640:896], eu_ref[n])
            total = total + mm_nt(hid_ref[at, 896:1152], euo_ref[n])
            total = total + mm_nt(hid_ref[at, 1152:1280], cols_ref[n, 384:512])
            part_ref[at, n] = total.astype(low)

    e_mail = Mail(e_send)

    def up_grads(first, last):
        @pl.loop(first, last)
        def _(i):
            n = pl.ds(pl.multiple_of(i * 256, 256), 256)
            total = mm_tn(n2_ref[:, n], hid_ref[...])
            geg_ref[n] = total[:, 0:256]
            og_ref[n] = total[:, 256:512].astype(low)
            shared_ref[n, 0:128] = total[:, 512:640].astype(low)
            geu_ref[n] = total[:, 640:896]
            ou_ref[n] = total[:, 896:1152].astype(low)
            shared_ref[n, 128:256] = total[:, 1152:1280].astype(low)

    def give_up():
        e_mail.put(og_ref, sg_ref, e_recv.at[0], sibling)
        e_mail.put(ou_ref, su_ref, e_recv.at[1], sibling)

    def down_grads():
        od_ref[...] = mm_tn(act_ref[:, 256:512], g_ref[...]).astype(low)
        e_mail.put(od_ref, sd_ref, e_recv.at[2], sibling)
        ged_ref[...] = mm_tn(act_ref[:, 0:256], g_ref[...])

    def shared_down():
        @pl.loop(0, 6)
        def _(i):
            n = pl.ds(pl.multiple_of(i * 256, 256), 256)
            shared_ref[n, 256:384] = mm_tn(g_ref[:, n], act_ref[:, 512:640]).astype(low)

    def moe_part(first, last):
        @pl.loop(first, last)
        def _(i):
            at = pl.ds(pl.multiple_of(i * LAYER, LAYER), LAYER)
            total = mm(act_ref[at, 0:256], ed_ref[...]) + mm(act_ref[at, 256:512], edo_ref[...])
            total = total + mm_nt(act_ref[at, 512:640], cols_ref[:, 640:768])
            moe_ref[at] = total.astype(low)

    mail = Mail(send)
    steps = reduce_steps(mail, part_ref, sum_ref, got, sums, recv, 64)
    left = [3, 2, 1, 0]
    tasks = {
        6: lambda: up_grads(0, 2),
        7: lambda: up_grads(2, 4),
        8: lambda: up_grads(4, 6),
        9: give_up,
        10: down_grads,
    }
    for turn in range(13):
        if turn in (0, 1, 3, 6):
            layer(left.pop(0))
        next(steps, None)
        if turn == 6:
            notes_out[here] = notes_ref[here]
            note_puts(mail, lambda to: notes_ref.at[to], notes_out, recv_n)
        if turn in tasks:
            tasks[turn]()
    for _ in steps:
        pass
    note_waits(mail, notes_out, recv_n)

    slopes = jnp.concatenate([notes_out[j, 0:1] for j in range(16)], 0)
    slopes = jnp.concatenate([slopes, jnp.zeros((112, 128), f32)], 0).T[0:64]
    own = pl.ds(pl.multiple_of(here * 64, 64), 64)
    probs = probs_ref[own]
    d_logits = probs * (slopes - jnp.sum(probs * slopes, axis=-1, keepdims=True))
    d_logits = d_logits.astype(low)
    grouter_ref[...] = mm_tn(n2_ref[own], d_logits).astype(low)
    dn2 = sum_ref[...] + mm_nt(d_logits, extras_ref[:, 128:256])
    residual = res_ref[...]
    value, gain = norm_step(dn2, residual, norm_ref[...])
    gnorm_ref[...] = gain
    d_res = g_own_ref[...].astype(f32) + value
    dres_own_ref[...] = d_res
    low_ref[...] = d_res.astype(low)
    cross = jnp.sum(low_ref[...].astype(f32) * proj_ref[...], axis=-1, keepdims=True)
    note_ref[...] = as_row(cross / scale_ref[:, 0:1])
    mine = pltpu.make_async_copy(low_ref, rows_at(dres_ref, here * 64, 64, 16), local)
    mine.start()
    d_mail = Mail(d_send)
    d_steps = gather_steps(d_mail, low_ref, dres_ref, d_recv, d_recv_half, 64, 32)
    next(d_steps)
    cross_ref[here] = note_ref[...]
    note_puts(d_mail, lambda to: note_ref, cross_ref, d_recv_n)
    next(d_steps)
    shared_down()
    for i in range(4):
        next(d_steps)
        moe_part(i, i + 1)
    e_mail.arrived(sg_ref, e_recv.at[0])
    geg_ref[...] += sg_ref[...].astype(f32)
    next(d_steps)
    e_mail.arrived(su_ref, e_recv.at[1])
    geu_ref[...] += su_ref[...].astype(f32)
    next(d_steps)
    e_mail.arrived(sd_ref, e_recv.at[2])
    ged_ref[...] += sd_ref[...].astype(f32)
    for _ in d_steps:
        pass
    note_waits(d_mail, cross_ref, d_recv_n)
    mine.wait()
    mail.finish()
    e_mail.finish()
    d_mail.finish()


def norm_step(grad, values, gain):
    scale = lax.rsqrt(jnp.mean(values * values, axis=-1, keepdims=True) + EPS)
    gain_grad = jnp.sum(grad * values * scale, axis=0, keepdims=True)
    scaled = grad * gain
    pull = scale * scale * scale * jnp.mean(scaled * values, axis=-1, keepdims=True)
    return scale * scaled - values * pull, gain_grad


def moe(*args):
    low, f32 = jnp.bfloat16, jnp.float32
    return call(
        moe_kernel,
        "moe",
        3,
        (
            ((1024, 1536), low),
            ((16, 8, 128), f32),
            ((1024, 1536), low),
            ((1536, 256), f32),
            ((1536, 256), f32),
            ((256, 1536), f32),
            ((1536, 384), low),
            ((1536, 128), low),
            ((1, 1536), f32),
            ((64, 1536), f32),
        ),
        [
            VMEM((1024, 1536), low),
            VMEM((1024, 640), low),
            VMEM((1024, 1280), low),
            VMEM((1024, 128), f32),
            VMEM((16, 8, 128), f32),
            VMEM((16, 8, 128), f32),
            VMEM((64, 1536), f32),
            VMEM((64, 1536), low),
            VMEM((8, 128), f32),
            VMEM((1536, 256), low),
            VMEM((1536, 256), low),
            VMEM((256, 1536), low),
            VMEM((1536, 256), low),
            VMEM((1536, 256), low),
            VMEM((256, 1536), low),
        ]
        + reduce_scratch(64, 1536, low)
        + [
            DMA((42,)),
            DMA((27,)),
            DMA((16,)),
            DMA((34,)),
            DMA((11,)),
            DMA((8,)),
            DMA((16,)),
            DMA((3,)),
            DMA((3,)),
            DMA,
        ],
        args,
    )


def mix_backward_kernel(
    dres_ref,
    cross_ref,
    scales_ref,
    n1_ref,
    cols_ref,
    wbc_ref,
    wdt_ref,
    taps_ref,
    head_ref,
    gain_ref,
    ids_ref,
    z_ref,
    ext_ref,
    dt_ref,
    y_ref,
    state_ref,
    moe_ref,
    shared_ref,
    grouter_ref,
    gnorm_ref,
    res_ref,
    dres_own_ref,
    x_ref,
    norm_ref,
    main_ref,
    bcr_ref,
    small_ref,
    block_ref,
    input_ref,
    part_ref,
    dm_ref,
    mixed_ref,
    din_ref,
    dpre_ref,
    sum_ref,
    *refs,
):
    got, sums, refs = refs[:5], refs[5:8], refs[8:]
    b_got, b_sums, refs = refs[:5], refs[5:8], refs[8:]
    send, recv, b_send, b_recv = refs
    here, side, z_at = peers()[:3]
    half_here, slot = here // 8, lax.rem(here, 8)
    greet(near(side))
    low, f32 = jnp.bfloat16, jnp.float32
    zs = layers(z_at)
    b_mail = Mail(b_send)
    b_steps = reduce_steps(b_mail, moe_ref, block_ref, b_got, b_sums, b_recv, 64)
    next(b_steps)

    @pl.loop(0, 4)
    def _(i):
        at = pl.ds(pl.multiple_of(i * LAYER, LAYER), LAYER)
        dm_ref[at] = mm(dres_ref[at], cols_ref[:, 512:704])

    next(b_steps)
    rate, skip = head_ref[1:2], spread_heads(head_ref[2:3])
    onehot = (
        lax.broadcasted_iota(jnp.int32, (192, 128), 0) // HEADW
        == lax.broadcasted_iota(jnp.int32, (192, 128), 1)
    ).astype(f32)
    row = lax.broadcasted_iota(jnp.int32, (CHUNK, CHUNK), 0)
    lane = lanes((CHUNK, CHUNK))
    above = (row <= lane).astype(f32)
    lane192 = lanes((CHUNK, 192))
    masks = [((lane192 // HEADW) == h).astype(f32) for h in range(3)]
    d_state = jnp.zeros((128, 192), f32)
    g_gain = jnp.zeros((1, 192), f32)
    g_skip = jnp.zeros((1, 192), f32)
    g_rate = jnp.zeros((1, 128), f32)
    g_dt = jnp.zeros((1, 128), f32)
    g_taps = [jnp.zeros((1, 448), f32) for _ in range(5)]
    dpre_ref[1024:1032] = jnp.zeros((8, 448), f32)
    din_ref[:, 128:256] = jnp.zeros((1024, 128), low)
    din_ref[:, 384:512] = jnp.zeros((1024, 128), low)
    mixed_ref[:, 128:256] = jnp.zeros((1024, 128), low)
    for c in range(7, -1, -1):
        r = c * CHUNK
        at = pl.ds(r, CHUNK)
        ids = ids_ref[pl.ds(r + 8, CHUNK)]
        doc = ids[:, 40:41]
        scale_row = jnp.concatenate(
            [scales_ref[2 * c, :, 0:64], scales_ref[2 * c + 1, :, 0:64]], 1
        )
        cross_row = jnp.concatenate([cross_ref[2 * c, :, 0:64], cross_ref[2 * c + 1, :, 0:64]], 1)
        scale = as_column(scale_row)[:, 0:1]
        pull = scale * scale * scale * as_column(cross_row)[:, 0:1] / INNER
        z, y, dm, gain = z_ref[at], y_ref[at], dm_ref[at], gain_ref[0:1]
        sig = jax.nn.sigmoid(z)
        gated = y * z * sig
        scaled = gated * scale
        mixed_ref[at, 0:192] = (scaled * gain).astype(low)
        g_gain = g_gain + jnp.sum(dm * scaled, axis=0, keepdims=True)
        d_gated = scale * gain * dm - gated * pull
        d_y = d_gated * z * sig
        din_ref[at, 0:192] = (d_gated * y * silu_slope(z, sig)).astype(low)
        pre = conv_pre(taps_ref, ext_ref, ids_ref, r, doc)
        pre_sig = jax.nn.sigmoid(pre)
        act = pre * pre_sig
        b, cc, x = act[:, 0:128], act[:, 128:256], act[:, 256:448]
        g_skip = g_skip + jnp.sum(d_y * x, axis=0, keepdims=True)
        dt = dt_ref[at]
        step = soft_plus(dt)
        logs, tables, step_t = chunk_tables(step, rate, doc, ids.T[40:41])
        cross = mm_nt(cc, b)
        decays = [tables[h] * step_t[h] for h in range(3)]
        stacked = jnp.concatenate([cross * decays[h] for h in range(3)], 0)
        d_ys = jnp.concatenate([d_y * masks[h] for h in range(3)], 0)
        d_stack = mm_nt(d_ys, x)
        d_x = skip * d_y + mm_tn(stacked, d_ys)
        state = state_ref[c]
        first, last = chunk_masks(ids_ref, r, doc)
        enters = jnp.exp(logs) * first
        d_in_y = spread_heads(enters) * d_y
        from_state = mm(cc, state)
        tail_w = jnp.exp(logs[CHUNK - 1 :] - logs) * last
        tail = tail_w * step
        tail_x = spread_heads(tail)
        to_state = mm(b, d_state)
        d_x = d_x + tail_x * to_state
        kept = enters[CHUNK - 1 :]
        d_kept = jnp.sum(d_state * state, axis=0, keepdims=True)
        folded = mm(
            jnp.concatenate(
                [d_y * from_state, x * to_state, jnp.broadcast_to(d_kept, (8, 192))], 0
            ),
            onehot,
            exact=True,
        )
        d_enters, d_tail = folded[:CHUNK], folded[CHUNK : 2 * CHUNK]
        d_kept = folded[2 * CHUNK : 2 * CHUNK + 1]
        d_cross = jnp.zeros((CHUNK, CHUNK), f32)
        row_sums = jnp.zeros((CHUNK, CHUNK), f32)
        col_sums = []
        for h in range(3):
            d_a = d_stack[h * CHUNK : (h + 1) * CHUNK]
            d_cross = d_cross + d_a * decays[h]
            plain = d_a * cross * tables[h]
            col_sums.append(jnp.sum(plain, axis=0, keepdims=True))
            total = jnp.sum(plain * step_t[h], axis=1, keepdims=True)
            row_sums = jnp.where(lane == h, total, row_sums)
        col_sums = as_column(jnp.concatenate(col_sums + [jnp.zeros((5, CHUNK), f32)], 0))
        d_c = mm(d_cross, b) + mm_nt(d_in_y, state)
        d_b = mm_tn(d_cross, cc) + mm_nt(tail_x * x, d_state)
        pulled = d_tail * tail
        d_logs = row_sums - step * col_sums + d_enters * enters - pulled
        d_last = jnp.sum(pulled, axis=0, keepdims=True) + d_kept * kept
        d_logs = d_logs + jnp.where(row == CHUNK - 1, d_last, 0.0)
        d_l = mm(above, d_logs, exact=True)
        d_step = col_sums + d_tail * tail_w + d_l * rate
        g_rate = g_rate + jnp.sum(d_l * step, axis=0, keepdims=True)
        d_dt = jnp.where(lane < 3, d_step * jax.nn.sigmoid(dt), 0.0)
        g_dt = g_dt + jnp.sum(d_dt, axis=0, keepdims=True)
        din_ref[at, 768:896] = pltpu.roll(d_dt, 16 + 3 * slot, 1).astype(low)
        d_state = spread_heads(kept) * d_state + mm_tn(cc, d_in_y)
        d_pre = jnp.concatenate([d_b, d_c, d_x], 1) * silu_slope(pre, pre_sig)
        dpre_ref[at] = d_pre
        g_taps[4] = g_taps[4] + jnp.sum(d_pre, axis=0, keepdims=True)
        g_taps[3] = g_taps[3] + jnp.sum(d_pre * ext_ref[pl.ds(r + 8, CHUNK)], axis=0, keepdims=True)
        d_ext = taps_ref[3:4] * d_pre
        for k in (1, 2, 3):
            same = (ids_ref[pl.ds(r + 8 - k, CHUNK), 40:41] == doc).astype(f32)
            g_taps[3 - k] = g_taps[3 - k] + jnp.sum(
                d_pre * same * ext_ref[pl.ds(r + 8 - k, CHUNK)], axis=0, keepdims=True
            )
            same = (ids_ref[pl.ds(r + 8 + k, CHUNK), 40:41] == doc).astype(f32)
            d_ext = d_ext + taps_ref[3 - k : 4 - k] * (dpre_ref[pl.ds(r + k, CHUNK)] * same)
        din_ref[at, 512:768] = d_ext[:, 0:256].astype(low)
        din_ref[at, 256:448] = d_ext[:, 256:448].astype(low)
        next(b_steps, None)
    small_ref[...] = jnp.zeros((2, 8, 512), f32)
    for k in range(5):
        small_ref[1, k : k + 1, 0:448] = g_taps[k]
    small_ref[1, 5:6, 0:192] = g_gain
    small_ref[1, 5:6, 256:448] = g_skip
    small_ref[1, 6:7, 0:128] = g_dt
    small_ref[1, 6:7, 256:384] = g_rate * rate

    def layer(k):
        at = pl.ds(pl.multiple_of(zs[k] * LAYER, LAYER), LAYER)

        @pl.loop(0, 6)
        def _(i):
            n = pl.ds(pl.multiple_of(i * 256, 256), 256)
            total = mm_nt(din_ref[at, 0:256], cols_ref[n, 0:256])
            total = total + mm_nt(din_ref[at, 256:512], cols_ref[n, 256:512])
            total = total + mm_nt(din_ref[at, 512:768], wbc_ref[n])
            total = total + mm_nt(din_ref[at, 768:896], wdt_ref[n])
            part_ref[at, n] = total.astype(low)

    moved = 24 * half_here

    def grads(first, last):
        @pl.loop(first, last)
        def _(i):
            n = pl.ds(pl.multiple_of(i * 256, 256), 256)
            total = mm_tn(n1_ref[:, n], din_ref[...])
            out = mm_tn(dres_ref[:, n], mixed_ref[...])
            main_ref[n, 0:128] = total[:, 0:128].astype(low)
            main_ref[n, 128:256] = total[:, 128:256].astype(low) + shared_ref[n, 0:128]
            main_ref[n, 256:384] = total[:, 256:384].astype(low)
            main_ref[n, 384:512] = total[:, 384:512].astype(low) + shared_ref[n, 128:256]
            main_ref[n, 512:640] = out[:, 0:128].astype(low)
            main_ref[n, 640:768] = out[:, 128:256].astype(low) + shared_ref[n, 256:384]
            bcr_ref[n, 0:256] = total[:, 512:768].astype(low)
            steps_part = pltpu.roll(total[:, 768:896], moved, 1)
            bcr_ref[n, 256:384] = (steps_part + grouter_ref[n].astype(f32)).astype(low)

    mail = Mail(send)
    steps = reduce_steps(mail, part_ref, sum_ref, got, sums, recv, 64)
    left = [3, 2, 1, 0]
    for turn in range(13):
        if turn in (0, 1, 3, 6):
            layer(left.pop(0))
        next(steps, None)
        next(b_steps, None)
        if turn in (7, 8, 9):
            grads(2 * (turn - 7), 2 * (turn - 6))
    for _ in b_steps:
        pass
    block_ref[...] += res_ref[...]
    for _ in steps:
        pass
    value, gain = norm_step(sum_ref[...], x_ref[...].astype(f32), norm_ref[...])
    input_ref[...] = dres_own_ref[...] + value
    for i in range(4):
        small_ref[0, i : i + 1, 0:384] = gain[:, 384 * i : 384 * (i + 1)]
        small_ref[0, 4 + i : 5 + i, 0:384] = gnorm_ref[:, 384 * i : 384 * (i + 1)]
    b_mail.finish()
    mail.finish()


def mix_backward(*args):
    low, f32 = jnp.bfloat16, jnp.float32
    return call(
        mix_backward_kernel,
        "mix_backward",
        4,
        (
            ((1536, 768), low),
            ((1536, 384), low),
            ((2, 8, 512), f32),
            ((64, 1536), f32),
            ((64, 1536), f32),
        ),
        [
            VMEM((1024, 1536), low),
            VMEM((1024, 192), f32),
            VMEM((1024, 256), low),
            VMEM((1024, 896), low),
            VMEM((1032, 448), f32),
            VMEM((64, 1536), f32),
        ]
        + reduce_scratch(64, 1536, low)
        + reduce_scratch(64, 1536, low)
        + [DMA((27,)), DMA((27,)), DMA((27,)), DMA((27,))],
        args,
        limit=62,
    )


def by_heads(
    hidden_in,
    doc_ids,
    routes,
    norm1_gain,
    w_z,
    w_x,
    w_bc,
    w_dt,
    conv_x,
    conv_bc,
    convb_x,
    convb_bc,
    dt_bias,
    a_log,
    d_skip,
    gnorm_gain,
    w_out,
    norm2_gain,
    router,
    shared_gate,
    shared_up,
    shared_down,
    expert_gate,
    expert_up,
    expert_down,
    cotangent,
):
    side = lax.axis_index("head")
    width = hidden_in.shape[-1]
    low, f32 = jnp.bfloat16, jnp.float32
    x_own = lax.dynamic_index_in_dim(hidden_in, side, 1, False)
    g_own = lax.dynamic_index_in_dim(cotangent, side, 1, False)
    ids = jnp.concatenate(
        [
            lax.dynamic_index_in_dim(doc_ids, side, 1, True),
            lax.dynamic_index_in_dim(routes, side, 1, False),
        ],
        1,
    )
    extra = jnp.concatenate(
        [
            lax.dynamic_slice_in_dim(w_bc, side * 128, 128, 1),
            router,
            w_dt,
            jnp.pad(ids.astype(low), ((0, 32), (0, 81))),
        ],
        1,
    )
    numbers = jnp.concatenate([dt_bias, a_log, d_skip])
    small = jnp.concatenate(
        [
            conv_x,
            convb_x[None],
            gnorm_gain[None],
            jnp.pad(numbers, (0, width - numbers.shape[0]))[None],
            jnp.zeros((1, width), f32),
        ],
        0,
    )
    eg, eu, ed = expert_gate[0], expert_up[0], expert_down[0]
    norm1, norm2 = norm1_gain[None], norm2_gain[None]
    n1, extras, extras_sib, cols, small_sib, eg_o, eu_o, ed_o = enter(
        x_own,
        norm1,
        extra,
        w_z,
        shared_gate,
        w_x,
        shared_up,
        w_out.T,
        shared_down.T,
        small,
        eg,
        eu,
        ed,
    )
    (
        z,
        ext,
        dt,
        y,
        states,
        g_all,
        n2,
        scales,
        residual,
        projected,
        scale_own,
        ids,
        wbc,
        wdt,
        taps,
        head,
        gain,
    ) = mix_forward(
        n1,
        extras,
        extras_sib,
        cols,
        small,
        small_sib,
        conv_bc,
        convb_bc[None],
        g_own,
        x_own,
        norm2,
    )
    (
        d_res_all,
        cross,
        moe_part,
        grad_eg,
        grad_eu,
        grad_ed,
        shared,
        grad_router,
        grad_norm2,
        d_res,
    ) = moe(
        n2,
        g_all,
        cols,
        eg,
        eg_o,
        eu,
        eu_o,
        ed,
        ed_o,
        extras,
        ids,
        residual,
        projected,
        scale_own,
        norm2,
        g_own,
    )
    main, bcr, small, block_own, input_own = mix_backward(
        d_res_all,
        cross,
        scales,
        n1,
        cols,
        wbc,
        wdt,
        taps,
        head,
        gain,
        ids,
        z,
        ext,
        dt,
        y,
        states,
        moe_part,
        shared,
        grad_router,
        grad_norm2,
        residual,
        d_res,
        x_own,
        norm1,
    )
    (
        grad_z,
        grad_x,
        grad_sg,
        grad_su,
        grad_out,
        grad_sd,
        bcr,
        norms,
        taps_bc,
        taps_x,
        chans,
        heads,
        block_sib,
        input_sib,
    ) = leave(main.reshape(16, 96, 768), bcr.reshape(16, 96, 384), small, block_own, input_own)

    def ordered(own, other):
        first = jnp.where(side == 0, own, other)
        second = jnp.where(side == 0, other, own)
        return jnp.stack([first, second], 1)

    grad_wdt = lax.dynamic_slice_in_dim(bcr, 272 + 24 * side, 24, 1)
    return (
        ordered(block_own, block_sib),
        ordered(input_own, input_sib),
        norms[0:4, 0:384].reshape(width),
        grad_z,
        grad_x,
        bcr[:, 0:256],
        grad_wdt,
        taps_x[0:4],
        taps_bc[0:4],
        taps_x[4],
        taps_bc[4],
        chans[:, 1, 0:3].reshape(24),
        heads[:, 1, 0:3].reshape(24),
        heads[:, 0, 0:192].reshape(24, 64).sum(1),
        chans[:, 0, 0:192].reshape(width),
        grad_out.T,
        norms[4:8, 0:384].reshape(width),
        bcr[:, 256:272],
        grad_sg,
        grad_su,
        grad_sd.T,
        grad_eg[None],
        grad_eu[None],
        grad_ed[None],
    )


def solution(mesh):
    places = mesh.shape["seq"]
    whole_heads = places == 16 and mesh.shape["head"] == 2
    placed = (
        P("seq", None, None),
        P("seq", None),
        P("seq", None, None),
        P(),
        P("seq", "head"),
        P("seq", "head"),
        P("seq", None),
        P("seq", "head"),
        P(None, "head"),
        P(),
        P("head"),
        P(),
        P("head"),
        P("head"),
        P("head"),
        P("head"),
        P("head", "seq"),
        P(),
        P("seq", None),
        P("seq", "head"),
        P("seq", "head"),
        P("head", "seq"),
        P("seq", None, "head"),
        P("seq", None, "head"),
        P("seq", "head", None),
        P("seq", None, None),
    )
    return jax.shard_map(
        by_heads if whole_heads else on_device,
        mesh=mesh,
        in_specs=placed,
        out_specs=(
            P("seq", None, None),
            P("seq", None, None),
            P(),
            P("seq", "head"),
            P("seq", "head"),
            P("seq", None),
            P("seq", "head"),
            P(None, "head"),
            P(),
            P("head"),
            P(),
            P("head"),
            P("head"),
            P("head"),
            P("head"),
            P("head", "seq"),
            P(),
            P("seq", None),
            P("seq", "head"),
            P("seq", "head"),
            P("head", "seq"),
            P("seq", None, "head"),
            P("seq", None, "head"),
            P("seq", "head", None),
        ),
        check_vma=False,
    )
```

```python
import jax
import jax.numpy as jnp
from jax import lax
from jax.experimental import pallas as pl
from jax.experimental.pallas import tpu as pltpu
from jax.sharding import PartitionSpec as P

KER = 4
INNER = 3072


EPS = 1e-05
HIGH = lax.Precision.HIGHEST


def passed_along(array, axis, by):
    length = lax.axis_size(axis)
    pairs = [(i, i + by) for i in range(length) if 0 <= i + by < length]
    return lax.ppermute(array, axis, pairs)


def entering(array, axis, combine, identity, reverse):
    length, here = (lax.axis_size(axis), lax.axis_index(axis))
    everything = jax.tree.map(
        lambda part, kind: lax.all_gather(part.astype(kind), axis),
        array,
        jax.tree.map(lambda a: jnp.bfloat16 if a.dtype == jnp.float32 else a.dtype, array),
    )
    start = jax.tree.map(
        lambda part, zero: jnp.broadcast_to(jnp.asarray(zero, part.dtype), part.shape),
        array,
        identity,
    )

    def hop(k, before):
        at = length - 1 - k if reverse else k
        reached = at > here if reverse else at < here
        new = combine(
            before, jax.tree.map(lambda part, own: part[at].astype(own.dtype), everything, array)
        )
        return jax.tree.map(lambda a, b: jnp.where(reached, a, b), new, before)

    return lax.fori_loop(0, length, hop, start)


def shortened(array):

    def short(part):
        return part.astype(jnp.bfloat16) if part.dtype == jnp.float32 else part

    return jax.tree.map(short, array)


def conv_apply(conv_ext, docs_ext, weight, conv_bias):
    length_here = conv_ext.shape[0] - (KER - 1)
    running = conv_bias
    for offset in range(KER):
        same_doc = (docs_ext[offset : offset + length_here] == docs_ext[KER - 1 :]).astype(
            jnp.float32
        )
        running = (
            running + weight[offset] * conv_ext[offset : offset + length_here] * same_doc[..., None]
        )
    return jax.nn.silu(running)


def group_parts(x_heads, step_size, b_state, decay_rate, doc_ids, prev_doc):
    log_decay = jnp.cumsum(step_size * decay_rate, axis=0)
    end_keep = (doc_ids == doc_ids[-1:]).astype(jnp.float32)
    weight = jnp.exp(log_decay[-1:] - log_decay) * end_keep[..., None] * step_size
    s_local = jnp.einsum("tsh,tshp,tsn->shpn", weight, x_heads, b_state, precision=HIGH)
    a_total = jnp.exp(log_decay[-1]) * (doc_ids[-1] == prev_doc).astype(jnp.float32)[:, None]
    return (s_local, a_total)


def group_output(x_heads, step_size, b_state, c_state, decay_rate, doc_ids, prev_doc, s_in):
    length_here = x_heads.shape[0]
    log_decay = jnp.cumsum(step_size * decay_rate, axis=0)
    causal = jnp.arange(length_here)[:, None] >= jnp.arange(length_here)[None, :]
    pair_mask = (causal[:, :, None] & (doc_ids[:, None, :] == doc_ids[None, :, :])).astype(
        jnp.float32
    )
    gap_decay = log_decay[:, None] - log_decay[None, :]
    decay_table = (
        jnp.exp(jnp.where(pair_mask[..., None] > 0, gap_decay, 0.0)) * pair_mask[..., None]
    )
    cross_dot = jnp.einsum("tsn,usn->tus", c_state, b_state, precision=HIGH)
    y_intra = jnp.einsum(
        "tush,ush,ushp->tshp",
        decay_table * cross_dot[..., None],
        step_size,
        x_heads,
        precision=HIGH,
    )
    enters = jnp.exp(log_decay) * (doc_ids == prev_doc[None, :]).astype(jnp.float32)[..., None]
    y_inter = jnp.einsum("tsn,shpn->tshp", c_state, s_in, precision=HIGH) * enters[..., None]
    return y_intra + y_inter


def ssm_local(x_heads, step_size, b_state, c_state, decay_rate, s_in, doc_ids, prev_doc):
    y_core = group_output(x_heads, step_size, b_state, c_state, decay_rate, doc_ids, prev_doc, s_in)
    s_local, a_total = group_parts(x_heads, step_size, b_state, decay_rate, doc_ids, prev_doc)
    return (y_core, a_total[..., None, None] * s_in + s_local)


def carry_combine(earlier, later_part):
    return (earlier[0] * later_part[0], later_part[0][..., None, None] * earlier[1] + later_part[1])


def head_total(partial_sum):
    return lax.psum(partial_sum, "head")


def flat_dot(left_side, right_side):
    lead_dims = left_side.shape[:-1]
    product = jnp.dot(
        left_side.reshape(-1, left_side.shape[-1]), right_side, preferred_element_type=jnp.float32
    )
    return product.reshape(lead_dims + (right_side.shape[-1],))


def flat_dot_t(left_side, right_side):
    lead_dims = left_side.shape[:-1]
    product = lax.dot_general(
        left_side.reshape(-1, left_side.shape[-1]),
        right_side,
        (((1,), (1,)), ((), ())),
        preferred_element_type=jnp.float32,
    )
    return product.reshape(lead_dims + (right_side.shape[0],))


def outer_sum(left_side, right_side):
    return lax.dot_general(
        left_side.reshape(-1, left_side.shape[-1]),
        right_side.reshape(-1, right_side.shape[-1]),
        (((0,), (0,)), ((), ())),
        preferred_element_type=jnp.float32,
    )


def silu_slope(values, sigmoid_of):
    return sigmoid_of * (1.0 + values * (1.0 - sigmoid_of))


def norm_back(grad_normed, values, scale_of, gain):
    scaled_grad = grad_normed * gain
    gain_grad = jnp.sum((grad_normed * values * scale_of).reshape(-1, values.shape[-1]), axis=0)
    cube = scale_of * scale_of * scale_of
    value_grad = scale_of * scaled_grad - values * cube * jnp.mean(
        scaled_grad * values, axis=-1, keepdims=True
    )
    return (value_grad, gain_grad)


def on_device(
    hidden_in,
    doc_ids,
    routes,
    norm1_gain,
    w_z,
    w_x,
    w_bc,
    w_dt,
    conv_x,
    conv_bc,
    convb_x,
    convb_bc,
    dt_bias,
    a_log,
    d_skip,
    gnorm_gain,
    w_out,
    norm2_gain,
    router,
    shared_gate,
    shared_up,
    shared_down,
    expert_gate,
    expert_up,
    expert_down,
    cotangent,
):
    block_len, seq_here, width = hidden_in.shape
    top_count = routes.shape[-1]
    heads_here = dt_bias.shape[0]
    inner_here = convb_x.shape[0]
    head_size = inner_here // heads_here
    state_size = convb_bc.shape[0] // 2
    seq_count = lax.axis_size("seq")
    local_experts = expert_gate.shape[0]
    experts_all = local_experts * seq_count
    tok_here = block_len * seq_here
    capacity = 2 * tok_here * top_count // experts_all
    edge_len = KER - 1
    x_float = hidden_in.astype(jnp.float32)
    scale_one = lax.rsqrt(jnp.mean(x_float * x_float, axis=-1, keepdims=True) + EPS)
    normed_one = (x_float * scale_one * norm1_gain).astype(jnp.bfloat16)
    gathered = (
        lax.all_gather(w_z, "seq", axis=0, tiled=True),
        lax.all_gather(w_x, "seq", axis=0, tiled=True),
        lax.all_gather(w_dt, "seq", axis=0, tiled=True),
        lax.all_gather(w_bc, "seq", axis=0, tiled=True),
        lax.all_gather(router, "seq", axis=0, tiled=True),
        lax.all_gather(shared_gate, "seq", axis=0, tiled=True),
        lax.all_gather(shared_up, "seq", axis=0, tiled=True),
        lax.all_gather(w_out, "seq", axis=1, tiled=True),
        lax.all_gather(shared_down, "seq", axis=1, tiled=True),
    )
    full_z, full_x, full_dt, full_bc, full_router, full_sgate, full_sup, full_out, full_sdown = (
        gathered
    )
    gate_z = flat_dot(normed_one, full_z)
    proj_x = flat_dot(normed_one, full_x)
    proj_bc = flat_dot(normed_one, full_bc)
    dt_pre = flat_dot(normed_one, full_dt) + dt_bias
    conv_in = jnp.concatenate([proj_x, proj_bc], axis=-1)
    tail_in, tail_doc = (
        passed_along(conv_in[block_len - edge_len :].astype(jnp.bfloat16), "seq", 1).astype(
            jnp.float32
        ),
        passed_along(
            doc_ids[block_len - edge_len :].astype(jnp.float32).astype(jnp.bfloat16), "seq", 1
        ).astype(jnp.float32),
    )
    conv_ext = jnp.concatenate([tail_in, conv_in], 0)
    docs_ext = jnp.concatenate([tail_doc.astype(jnp.int32), doc_ids], 0)
    conv_weight = jnp.concatenate([conv_x, conv_bc], -1)
    conv_shift = jnp.concatenate([convb_x, convb_bc], -1)
    conv_out = conv_apply(conv_ext, docs_ext, conv_weight, conv_shift)
    x_heads = conv_out[..., :inner_here].reshape(block_len, seq_here, heads_here, head_size)
    b_state = conv_out[..., inner_here : inner_here + state_size]
    c_state = conv_out[..., inner_here + state_size :]
    step_size = jax.nn.softplus(dt_pre)
    decay_rate = -jnp.exp(a_log)
    prev_doc = docs_ext[edge_len - 1]
    s_local, a_total = group_parts(x_heads, step_size, b_state, decay_rate, doc_ids, prev_doc)
    ones_start = jnp.ones_like(a_total)
    zeros_start = jnp.zeros_like(s_local)
    a_before, s_before = entering(
        (a_total, s_local), "seq", carry_combine, (ones_start, zeros_start), False
    )
    y_core = group_output(
        x_heads, step_size, b_state, c_state, decay_rate, doc_ids, prev_doc, s_before
    )
    y_heads = y_core + d_skip[:, None] * x_heads
    y_flat = y_heads.reshape(block_len, seq_here, inner_here)
    gate_sig = jax.nn.sigmoid(gate_z)
    gated = y_flat * gate_z * gate_sig
    square_sum = head_total(jnp.sum(gated * gated, axis=-1, keepdims=True))
    scale_gated = lax.rsqrt(square_sum / INNER + EPS)
    mixed_out = (gated * scale_gated * gnorm_gain).astype(jnp.bfloat16)
    residual = x_float + head_total(flat_dot(mixed_out, full_out))
    scale_two = lax.rsqrt(jnp.mean(residual * residual, axis=-1, keepdims=True) + EPS)
    normed_two = (residual * scale_two * norm2_gain).astype(jnp.bfloat16)
    logits = flat_dot(normed_two, full_router)
    gate_probs = jax.nn.softmax(jnp.take_along_axis(logits, routes, axis=-1), axis=-1)
    share_gate = flat_dot(normed_two, full_sgate)
    share_up = flat_dot(normed_two, full_sup)
    share_sig = jax.nn.sigmoid(share_gate)
    share_act = (share_gate * share_sig * share_up).astype(jnp.bfloat16)
    share_part = flat_dot(share_act, full_sdown)
    slot_total = tok_here * top_count
    route_flat = routes.reshape(slot_total)
    expert_ids = jnp.arange(experts_all, dtype=jnp.int32)
    route_hits = (route_flat[:, None] == expert_ids[None, :]).astype(jnp.int32)
    slot_rank = jnp.sum(jnp.cumsum(route_hits, axis=0) * route_hits, axis=1) - 1
    target = route_flat * capacity + slot_rank
    entry_table = (
        jnp.zeros((experts_all * capacity,), jnp.int32)
        .at[target]
        .set(jnp.arange(slot_total, dtype=jnp.int32) + 1)
    )
    entry_live = entry_table > 0
    entry_slot = jnp.maximum(entry_table - 1, 0)
    entry_token = entry_slot // top_count
    tokens_flat = normed_two.reshape(tok_here, width)
    send_rows = jnp.where(
        entry_live[:, None], tokens_flat[entry_token], jnp.zeros((), jnp.bfloat16)
    ).reshape(experts_all, capacity, width)
    received = lax.all_to_all(send_rows, "seq", split_axis=0, concat_axis=0, tiled=True)
    input_row_block = received.reshape(seq_count, local_experts, received.shape[1], width)
    hid_gate = jnp.einsum(
        "jecd,edf->jecf", input_row_block, expert_gate, preferred_element_type=jnp.float32
    )
    hid_up = jnp.einsum(
        "jecd,edf->jecf", input_row_block, expert_up, preferred_element_type=jnp.float32
    )
    hid_act = (hid_gate * jax.nn.sigmoid(hid_gate) * hid_up).astype(jnp.bfloat16)
    half_out = jnp.einsum(
        "jecf,efd->jecd", hid_act, expert_down, preferred_element_type=jnp.float32
    ).astype(jnp.bfloat16)
    returned_rows = lax.all_to_all(
        half_out.reshape(received.shape), "seq", split_axis=0, concat_axis=0, tiled=True
    )
    kept_shape = (seq_count * local_experts, received.shape[1], hid_gate.shape[-1])
    returned_rows, rows_kept, gate_kept, up_kept = (
        returned_rows,
        received,
        hid_gate.reshape(kept_shape),
        hid_up.reshape(kept_shape),
    )
    slot_rows = returned_rows.reshape(-1, width)[target].reshape(tok_here, top_count, width)
    probs_flat = gate_probs.reshape(tok_here, top_count)
    routed_part = share_part.reshape(tok_here, width)
    for slot_index in range(top_count):
        routed_part = routed_part + probs_flat[:, slot_index, None] * slot_rows[
            :, slot_index
        ].astype(jnp.float32)
    moe_out = head_total(routed_part.reshape(block_len, seq_here, width))
    block_out = residual + moe_out
    gathered = (
        lax.all_gather(w_z, "seq", axis=0, tiled=True),
        lax.all_gather(w_x, "seq", axis=0, tiled=True),
        lax.all_gather(w_dt, "seq", axis=0, tiled=True),
        lax.all_gather(w_bc, "seq", axis=0, tiled=True),
        lax.all_gather(router, "seq", axis=0, tiled=True),
        lax.all_gather(shared_gate, "seq", axis=0, tiled=True),
        lax.all_gather(shared_up, "seq", axis=0, tiled=True),
        lax.all_gather(w_out, "seq", axis=1, tiled=True),
        lax.all_gather(shared_down, "seq", axis=1, tiled=True),
    )
    full_z, full_x, full_dt, full_bc, full_router, full_sgate, full_sup, full_out, full_sdown = (
        gathered
    )
    grad_out = cotangent.astype(jnp.float32)
    grad_flat = grad_out.reshape(tok_here, width)
    entry_prob = jnp.where(entry_live, gate_probs.reshape(-1)[entry_slot], 0.0)
    send_grads = (
        (entry_prob[:, None] * grad_flat[entry_token])
        .astype(jnp.bfloat16)
        .reshape(experts_all, capacity, width)
    )
    recv_grads = lax.all_to_all(send_grads, "seq", split_axis=0, concat_axis=0, tiled=True)
    grads_in = recv_grads.reshape(seq_count, local_experts, capacity, width)
    input_row_block = rows_kept.reshape(seq_count, local_experts, capacity, width)
    hid_gate = gate_kept.reshape(seq_count, local_experts, capacity, -1)
    hid_up = up_kept.reshape(seq_count, local_experts, capacity, -1)
    hid_sig = jax.nn.sigmoid(hid_gate)
    hid_act = (hid_gate * hid_sig * hid_up).astype(jnp.bfloat16)
    d_act = jnp.einsum("jecd,efd->jecf", grads_in, expert_down, preferred_element_type=jnp.float32)
    hidden_up_gradient = (d_act * hid_gate * hid_sig).astype(jnp.bfloat16)
    d_hid_gate = (d_act * hid_up * silu_slope(hid_gate, hid_sig)).astype(jnp.bfloat16)
    grad_edown = jnp.einsum("jecf,jecd->efd", hid_act, grads_in, preferred_element_type=jnp.float32)
    grad_egate = jnp.einsum(
        "uqpy,uqpn->qyn", input_row_block, d_hid_gate, preferred_element_type=jnp.float32
    )
    expert_up_gradient = jnp.einsum(
        "uqpy,uqpn->qyn", input_row_block, hidden_up_gradient, preferred_element_type=jnp.float32
    )
    d_rows = jnp.einsum(
        "jecf,edf->jecd", d_hid_gate, expert_gate, preferred_element_type=jnp.float32
    )
    d_rows = (
        d_rows
        + jnp.einsum(
            "jecf,edf->jecd", hidden_up_gradient, expert_up, preferred_element_type=jnp.float32
        )
    ).astype(jnp.bfloat16)
    back_rows = lax.all_to_all(
        d_rows.reshape(recv_grads.shape), "seq", split_axis=0, concat_axis=0, tiled=True
    )
    d_share_act = flat_dot_t(cotangent, full_sdown)
    d_share_up = (d_share_act * share_gate * share_sig).astype(jnp.bfloat16)
    d_share_gate = (d_share_act * share_up * silu_slope(share_gate, share_sig)).astype(jnp.bfloat16)
    grad_sdown = outer_sum(share_act, cotangent)
    grad_sgate = outer_sum(normed_two, d_share_gate)
    grad_sup = outer_sum(normed_two, d_share_up)
    d_normed_two = (
        flat_dot_t(d_share_gate, full_sgate) + flat_dot_t(d_share_up, full_sup)
    ).reshape(tok_here, width)
    prob_grad = jnp.stack(
        [
            jnp.sum(grad_flat * slot_rows[:, slot_index].astype(jnp.float32), axis=-1)
            for slot_index in range(top_count)
        ],
        axis=-1,
    )
    back_slots = back_rows.reshape(-1, width)[target].reshape(tok_here, top_count, width)
    for slot_index in range(top_count):
        d_normed_two = d_normed_two + back_slots[:, slot_index].astype(jnp.float32)
    d_normed_two, prob_grad = head_total(
        (
            d_normed_two.reshape(block_len, seq_here, width),
            prob_grad.reshape(block_len, seq_here, top_count),
        )
    )
    d_chosen = gate_probs * (prob_grad - jnp.sum(gate_probs * prob_grad, axis=-1, keepdims=True))
    d_logits = jnp.sum(
        d_chosen[..., None] * (routes[..., None] == expert_ids).astype(jnp.float32), axis=-2
    ).astype(jnp.bfloat16)
    grad_router = outer_sum(normed_two, d_logits)
    d_normed_two = d_normed_two + flat_dot_t(d_logits, full_router)
    d_resid_norm, grad_norm2 = norm_back(d_normed_two, residual, scale_two, norm2_gain)
    d_resid = grad_out + d_resid_norm
    d_resid_low = d_resid.astype(jnp.bfloat16)
    d_mixed = flat_dot_t(d_resid_low, full_out)
    grad_out_w = outer_sum(mixed_out, d_resid_low)
    gain_scaled = d_mixed * gnorm_gain
    grad_gnorm = jnp.sum((d_mixed * gated * scale_gated).reshape(-1, inner_here), axis=0)
    cross_sum = head_total(jnp.sum(gain_scaled * gated, axis=-1, keepdims=True))
    d_gated = (
        scale_gated * gain_scaled
        - gated * scale_gated * scale_gated * scale_gated * cross_sum / INNER
    )
    d_y = d_gated * gate_z * gate_sig
    d_gate_z = (d_gated * y_flat * silu_slope(gate_z, gate_sig)).astype(jnp.bfloat16)
    d_y_heads = d_y.reshape(x_heads.shape)
    grad_skip = jnp.sum(d_y_heads * x_heads, axis=(0, 1, 3))
    log_decay = jnp.cumsum(step_size * decay_rate, axis=0)
    enters = jnp.exp(log_decay) * (doc_ids == prev_doc[None, :]).astype(jnp.float32)[..., None]
    g_local = jnp.einsum("tsh,tshp,tsn->shpn", enters, d_y_heads, c_state, precision=HIGH)
    a_after, state_grad = entering(
        (a_total, g_local), "seq", carry_combine, (ones_start, zeros_start), True
    )

    def local_scan(x_part, step_part, b_part, c_part, rate_part, state_part):
        return ssm_local(
            x_part, step_part, b_part, c_part, rate_part, state_part, doc_ids, prev_doc
        )

    _, scan_back = jax.vjp(local_scan, x_heads, step_size, b_state, c_state, decay_rate, s_before)
    d_xh, d_step, d_bstate, d_cstate, d_rate, _ = scan_back((d_y_heads, state_grad))
    d_xh = d_xh + d_skip[:, None] * d_y_heads
    d_bc = head_total(jnp.concatenate([d_bstate, d_cstate], axis=-1))
    d_dt_pre = d_step * jax.nn.sigmoid(dt_pre)
    grad_dtb = jnp.sum(d_dt_pre, axis=(0, 1))
    grad_alog = d_rate * decay_rate
    d_conv_out = jnp.concatenate([d_xh.reshape(block_len, seq_here, inner_here), d_bc], axis=-1)

    def local_conv(ext_part, weight_part, shift_part):
        return conv_apply(ext_part, docs_ext, weight_part, shift_part)

    _, conv_back = jax.vjp(local_conv, conv_ext, conv_weight, conv_shift)
    d_ext, grad_cweight, grad_cshift = conv_back(d_conv_out)
    from_next = passed_along(shortened(d_ext[:edge_len]), "seq", -1)
    d_conv_in = d_ext[edge_len:] + jnp.concatenate(
        [jnp.zeros((block_len - edge_len,) + from_next.shape[1:], jnp.float32), from_next], 0
    )
    d_proj_x = d_conv_in[..., :inner_here].astype(jnp.bfloat16)
    d_proj_bc = d_conv_in[..., inner_here:].astype(jnp.bfloat16)
    d_dt_low = d_dt_pre.astype(jnp.bfloat16)
    grad_wz = outer_sum(normed_one, d_gate_z)
    grad_wx = outer_sum(normed_one, d_proj_x)
    grad_wbc = outer_sum(normed_one, d_proj_bc)
    grad_wdt = outer_sum(normed_one, d_dt_low)
    head_first = jnp.where(lax.axis_index("head") == 0, 1.0, 0.0)
    d_normed_one = (
        flat_dot_t(d_gate_z, full_z) + flat_dot_t(d_proj_x, full_x) + flat_dot_t(d_dt_low, full_dt)
    )
    d_normed_one = head_total(d_normed_one + head_first * flat_dot_t(d_proj_bc, full_bc))
    d_x_norm, grad_norm1 = norm_back(d_normed_one, x_float, scale_one, norm1_gain)
    input_grad = d_resid + d_x_norm
    reduced = (
        lax.psum_scatter(grad_wz, "seq", scatter_dimension=0, tiled=True),
        lax.psum_scatter(grad_wx, "seq", scatter_dimension=0, tiled=True),
        lax.psum_scatter(grad_wdt, "seq", scatter_dimension=0, tiled=True),
        lax.psum_scatter(grad_wbc, "seq", scatter_dimension=0, tiled=True),
        lax.psum_scatter(grad_router, "seq", scatter_dimension=0, tiled=True),
        lax.psum_scatter(grad_sgate, "seq", scatter_dimension=0, tiled=True),
        lax.psum_scatter(grad_sup, "seq", scatter_dimension=0, tiled=True),
        lax.psum_scatter(grad_out_w, "seq", scatter_dimension=1, tiled=True),
        lax.psum_scatter(grad_sdown, "seq", scatter_dimension=1, tiled=True),
    )
    red_z, red_x, red_dt, red_bc, red_router, red_sgate, red_sup, red_out, red_sdown = reduced
    small_sums = lax.psum(
        (
            grad_norm1,
            grad_norm2,
            grad_cweight,
            grad_cshift,
            grad_dtb,
            grad_alog,
            grad_skip,
            grad_gnorm,
        ),
        "seq",
    )
    sum_norm1, sum_norm2, sum_cweight, sum_cshift, sum_dtb, sum_alog, sum_skip, sum_gnorm = (
        small_sums
    )
    return (
        block_out,
        input_grad,
        sum_norm1,
        red_z,
        red_x,
        red_bc,
        red_dt,
        sum_cweight[:, :inner_here],
        sum_cweight[:, inner_here:],
        sum_cshift[:inner_here],
        sum_cshift[inner_here:],
        sum_dtb,
        sum_alog,
        sum_skip,
        sum_gnorm,
        red_out,
        sum_norm2,
        red_router,
        red_sgate,
        red_sup,
        red_sdown,
        grad_egate,
        expert_up_gradient,
        grad_edown,
    )


MESH = pl.DeviceIdType.MESH
VMEM = pltpu.VMEM


def peers():
    here, side = lax.axis_index("seq"), lax.axis_index("head")
    x, y, z = lax.rem(here, 2), lax.rem(here // 2, 2), here // 4
    col = x + 2 * y
    return here, side, z, col, (1 - x) + 2 * y, x + 2 * (1 - y), 3 - col


def layers(z):
    lo, hi = lax.rem(z, 2), z // 2
    return [2 * (1 - hi if k & 2 else hi) + (1 - lo if k & 1 else lo) for k in range(4)]


def greet(devices):
    barrier = pltpu.get_barrier_semaphore()
    for device in devices:
        pl.semaphore_signal(barrier, inc=1, device_id=device, device_id_type=MESH)
    pl.semaphore_wait(barrier, len(devices))


class Mail:
    def __init__(self, send, base=0):
        self.send, self.sent, self.base = send, [], base

    def put(self, src, dst, sem, to):
        copy = pltpu.make_async_remote_copy(
            src_ref=src,
            dst_ref=dst,
            send_sem=self.send.at[self.base + len(self.sent)],
            recv_sem=sem,
            device_id=to,
            device_id_type=MESH,
        )
        copy.start()
        self.sent.append(copy)

    def arrived(self, dst, sem):
        pltpu.make_async_remote_copy(
            src_ref=dst,
            dst_ref=dst,
            send_sem=self.send.at[0],
            recv_sem=sem,
            device_id=(0, 0),
            device_id_type=MESH,
        ).wait_recv()

    def finish(self):
        for copy in self.sent:
            copy.wait_send()


def rows_at(ref, start, size, step):
    return ref.at[pl.ds(pl.multiple_of(start, step), size)]


def gather_steps(mail, own_ref, out_ref, recv, recv_half, rows, half=None):
    here, side, z, col, cx, cy, cd = peers()
    zs = layers(z)
    base = 4 * z
    to_x, to_y = (base + cx, side), (base + cy, side)

    def part(place, which, ref=None):
        if half is None:
            width = out_ref.shape[1] // 2
            lane = pl.ds(which * width, width)
            if ref is not None:
                return ref.at[:, lane]
            return out_ref.at[pl.ds(pl.multiple_of(place * rows, 16), rows), lane]
        size = rows - half if which else half
        if ref is not None:
            return ref.at[pl.ds(which * half, size)]
        return rows_at(out_ref, place * rows + which * half, size, 16)

    def onward(place, k, ref=None):
        for which in (0, 1):
            src = part(place, which, ref)
            mail.put(src, part(place, which), recv.at[6 + 4 * k + which], to_x)
            src = part(place, 1 - which, ref)
            mail.put(src, part(place, 1 - which), recv.at[8 + 4 * k + which], to_y)

    def across(k):
        at = 4 * zs[k] + cd
        mail.arrived(part(at, 0), recv_half.at[k])
        mail.arrived(part(at, 1), recv_half.at[4 + k])
        mail.arrived(part(4 * zs[k] + cx, 1), recv.at[7 + 4 * k])
        mail.arrived(part(4 * zs[k] + cy, 0), recv.at[9 + 4 * k])

    onward(here, 0, own_ref)
    for k in (1, 2, 3):
        for which in (0, 1):
            src = part(here, which, own_ref)
            sem = recv.at[2 * (k - 1) + which]
            mail.put(src, part(here, which), sem, (4 * zs[k] + col, side))
    yield
    for k in range(4):
        if k:
            at = 4 * zs[k] + col
            mail.arrived(part(at, 0), recv.at[2 * (k - 1)])
            mail.arrived(part(at, 1), recv.at[2 * (k - 1) + 1])
            onward(at, k)
            yield
        at = 4 * zs[k] + cx
        mail.arrived(part(at, 0), recv.at[6 + 4 * k])
        mail.put(part(at, 0), part(at, 0), recv_half.at[k], to_y)
        at = 4 * zs[k] + cy
        mail.arrived(part(at, 1), recv.at[8 + 4 * k])
        mail.put(part(at, 1), part(at, 1), recv_half.at[4 + k], to_x)
        yield
        if k:
            across(k - 1)
            yield
    across(3)
    yield


def near(side):
    here, side, z, col, cx, cy, cd = peers()
    zs = layers(z)
    return [(4 * z + cx, side), (4 * z + cy, side)] + [(4 * zs[k] + col, side) for k in (1, 2, 3)]


def note_puts(mail, src_of, notes_out, recv_n):
    here, side = peers()[:2]
    for k in range(1, 16):
        to = lax.rem(here + k, 16)
        mail.put(src_of(to), notes_out.at[here], recv_n.at[here], (to, side))


def note_waits(mail, notes_out, recv_n):
    here = peers()[0]
    for k in range(1, 16):
        place = lax.rem(here + k, 16)
        mail.arrived(notes_out.at[place], recv_n.at[place])


SUM_ORDER = (
    ("far", 3),
    ("far", 2),
    ("joined", 3),
    ("far", 1),
    ("joined", 2),
    ("column", 3),
    ("far", 0),
    ("joined", 1),
    ("column", 2),
    ("joined", 0),
    ("column", 1),
    ("column", 0),
)


def reduce_steps(mail, part_ref, out_ref, got, sums, recv, rows, order=SUM_ORDER):
    here, side, z, col, cx, cy, cd = peers()
    zs = layers(z)
    base = 4 * z
    half = rows // 2
    got_a, got_b, got_x, got_y, got_z = got
    sum_x, sum_y, sum_z = sums
    to_x, to_y = (base + cx, side), (base + cy, side)
    f32 = jnp.float32

    def half_of(place, which):
        return rows_at(part_ref, place * rows + which * half, half, half)

    def far(k):
        at = 4 * zs[k] + cd
        mail.put(half_of(at, 0), got_a.at[k], recv.at[k], to_y)
        mail.put(half_of(at, 1), got_b.at[k], recv.at[4 + k], to_x)

    def plain(k):
        mail.put(half_of(4 * zs[k] + cx, 1), got_x.at[k, pl.ds(half, half)], recv.at[12 + k], to_x)
        mail.put(half_of(4 * zs[k] + cy, 0), got_y.at[k, pl.ds(0, half)], recv.at[16 + k], to_y)

    def joined(k):
        mail.arrived(got_a.at[k], recv.at[k])
        total = half_of(4 * zs[k] + cx, 0)[...].astype(f32) + got_a[k].astype(f32)
        sum_x[k] = total.astype(sum_x.dtype)
        mail.put(sum_x.at[k], got_x.at[k, pl.ds(0, half)], recv.at[8 + k], to_x)
        mail.arrived(got_b.at[k], recv.at[4 + k])
        total = half_of(4 * zs[k] + cy, 1)[...].astype(f32) + got_b[k].astype(f32)
        sum_y[k] = total.astype(sum_y.dtype)
        mail.put(sum_y.at[k], got_y.at[k, pl.ds(half, half)], recv.at[20 + k], to_y)

    def column(k):
        mail.arrived(got_x.at[k, pl.ds(half, half)], recv.at[12 + k])
        mail.arrived(got_y.at[k, pl.ds(0, half)], recv.at[16 + k])
        mail.arrived(got_x.at[k, pl.ds(0, half)], recv.at[8 + k])
        mail.arrived(got_y.at[k, pl.ds(half, half)], recv.at[20 + k])
        own = part_ref[pl.ds(pl.multiple_of((4 * zs[k] + col) * rows, rows), rows)].astype(f32)
        total = own + got_x[k].astype(f32) + got_y[k].astype(f32)
        if k:
            sum_z[k - 1] = total.astype(sum_z.dtype)
            mail.put(sum_z.at[k - 1], got_z.at[k - 1], recv.at[23 + k], (4 * zs[k] + col, side))
        else:
            out_ref[...] = total

    for turn, k in order:
        if turn == "far":
            far(k)
            plain(k)
        elif turn == "joined":
            joined(k)
        else:
            column(k)
        yield
    for turn, k in order:
        if turn == "column" and k:
            mail.arrived(got_z.at[k - 1], recv.at[23 + k])
            out_ref[...] += got_z[k - 1].astype(f32)


def reduce_scratch(rows, width, kind):
    half = rows // 2
    shapes = [(4, half), (4, half), (4, rows), (4, rows), (3, rows), (4, half), (4, half), (3, rows)]
    return [VMEM(shape + (width,), kind) for shape in shapes]


def same_side(side, here):
    return [(lax.rem(here + k, 16), side) for k in range(1, 16)]


DMA = pltpu.SemaphoreType.DMA


def remote(src, dst, send, recv, to):
    return pltpu.make_async_remote_copy(
        src_ref=src,
        dst_ref=dst,
        send_sem=send,
        recv_sem=recv,
        device_id=to,
        device_id_type=MESH,
    )


def call(kernel, name, number, outs, scratch, args, spaces=None, limit=60):
    vmem = pl.BlockSpec(memory_space=VMEM)
    hbm = pl.BlockSpec(memory_space=pl.ANY)
    ins_far, outs_far = spaces or ((), ())
    return pl.pallas_call(
        kernel,
        out_shape=tuple(jax.ShapeDtypeStruct(shape, kind) for shape, kind in outs),
        in_specs=[hbm if i in ins_far else vmem for i in range(len(args))],
        out_specs=tuple(hbm if i in outs_far else vmem for i in range(len(outs))),
        scratch_shapes=scratch,
        compiler_params=pltpu.CompilerParams(
            collective_id=number, has_side_effects=True, vmem_limit_bytes=limit << 20
        ),
        name=name,
    )(*args)


def enter_kernel(
    x_ref,
    norm_ref,
    mine_ref,
    wz_ref,
    sg_ref,
    wx_ref,
    su_ref,
    wo_ref,
    sd_ref,
    small_ref,
    gate_ref,
    up_ref,
    down_ref,
    all_ref,
    extras_ref,
    extra_ref,
    cols_ref,
    small_other,
    gate_other,
    up_other,
    down_other,
    own_ref,
    blocks_ref,
    send,
    recv,
    recv_half,
    recv_m,
    recv_half_m,
    recv_w,
    recv_e,
    recv_s,
    local,
):
    here, side = peers()[:2]
    places = 16
    sibling = (here, 1 - side)
    x = x_ref[...].astype(jnp.float32)
    scale = lax.rsqrt(jnp.mean(x * x, axis=-1, keepdims=True) + EPS)
    own_ref[...] = (x * scale * norm_ref[...]).astype(jnp.bfloat16)
    greet(same_side(side, here) + [sibling])
    depth = blocks_ref.shape[1]
    rows, extra = own_ref.shape[0], mine_ref.shape[0]
    half_here = here // 8
    mail = Mail(send)
    mine = pltpu.make_async_copy(own_ref, rows_at(all_ref, here * rows, rows, 16), local.at[0])
    mine.start()
    mine_too = pltpu.make_async_copy(
        mine_ref, rows_at(extras_ref, here * extra, extra, 16), local.at[18]
    )
    mine_too.start()

    def strip(place):
        return rows_at(cols_ref, place * depth, depth, 16)

    steps = gather_steps(mail, own_ref, all_ref, recv, recv_half, rows, rows // 2)
    steps_too = gather_steps(mail, mine_ref, extras_ref, recv_m, recv_half_m, extra)
    next(steps_too)
    next(steps)
    mail.put(small_ref, small_other, recv_s.at[0], sibling)
    for j in range(8):
        wide, narrow = slice(192 * j, 192 * (j + 1)), slice(64 * j, 64 * (j + 1))
        blocks_ref[j, :, 0:192] = wz_ref[:, wide]
        blocks_ref[j, :, 192:256] = sg_ref[:, narrow]
        blocks_ref[j, :, 256:448] = wx_ref[:, wide]
        blocks_ref[j, :, 448:512] = su_ref[:, narrow]
        blocks_ref[j, :, 512:704] = wo_ref[:, wide]
        blocks_ref[j, :, 704:768] = sd_ref[:, narrow]
    first = 8 * side + lax.rem(here, 8)
    is_mine = side == half_here
    for k in range(1, 8):
        to = 8 * side + lax.rem(here + k, 8)
        mail.put(blocks_ref.at[to - 8 * side], strip(here), recv_w.at[here], (to, side))

    def keep():
        return pltpu.make_async_copy(blocks_ref.at[here - 8 * side], strip(here), local.at[1])

    def give():
        block = blocks_ref.at[first - 8 * side]
        return remote(block, strip(here), local.at[1], recv_w.at[here], (first, side))

    @pl.when(is_mine)
    def _():
        keep().start()

    @pl.when(jnp.logical_not(is_mine))
    def _():
        give().start()

    mail.put(gate_ref, gate_other, recv_s.at[1], sibling)
    mail.put(up_ref, up_other, recv_s.at[2], sibling)
    mail.put(down_ref, down_other, recv_s.at[3], sibling)
    for _ in steps_too:
        next(steps)
    for _ in steps:
        pass
    mine.wait()
    mine_too.wait()
    for place in range(places):
        at = pl.ds(place * extra, extra)
        mail.put(extras_ref.at[at], extra_ref.at[at], recv_e.at[place], sibling)

    def forward(place, k):
        return remote(strip(place), strip(place), local.at[2 + k], recv_w.at[place], sibling)

    @pl.when(is_mine)
    def _():
        keep().wait()
        forward(here, 0).start()

    @pl.when(jnp.logical_not(is_mine))
    def _():
        forward(here, 0).wait_recv()
        give().wait_send()

    for k in range(1, places):
        place = lax.rem(here + k, places)
        forward(place, k).wait_recv()

        @pl.when(is_mine)
        def _():
            forward(place, k).start()

    @pl.when(is_mine)
    def _():
        for k in range(places):
            forward(lax.rem(here + k, places), k).wait_send()

    mail.arrived(small_other, recv_s.at[0])
    mail.arrived(gate_other, recv_s.at[1])
    mail.arrived(up_other, recv_s.at[2])
    mail.arrived(down_other, recv_s.at[3])
    for place in range(places):
        mail.arrived(extra_ref.at[pl.ds(place * extra, extra)], recv_e.at[place])
    mail.finish()


def enter(*args):
    low, f32 = jnp.bfloat16, jnp.float32
    return call(
        enter_kernel,
        "enter",
        1,
        (
            ((1024, 1536), low),
            ((1536, 256), low),
            ((1536, 256), low),
            ((1536, 768), low),
            ((8, 1536), f32),
            ((1536, 256), low),
            ((1536, 256), low),
            ((256, 1536), low),
        ),
        [
            VMEM((64, 1536), low),
            VMEM((8, 96, 768), low),
            DMA((87,)),
            DMA((22,)),
            DMA((8,)),
            DMA((22,)),
            DMA((8,)),
            DMA((16,)),
            DMA((16,)),
            DMA((4,)),
            DMA((19,)),
        ],
        args,
        ((10, 11, 12), (5, 6, 7)),
        limit=8,
    )


def leave_kernel(
    main_ref,
    bcr_ref,
    small_ref,
    block_ref,
    input_ref,
    main_parts,
    bcr_out,
    small_all,
    block_other,
    input_other,
    got_main,
    got_bcr,
    bcr_parts,
    bcr_mine,
    bcr_sib,
    small_got,
    small_sum,
    send,
    recv_sib,
    recv_main,
    recv_bcr,
    recv_small,
    recv_pair,
    cond,
):
    here, side = peers()[:2]
    sibling = (here, 1 - side)
    is_main = side == here // 8
    f32 = jnp.float32
    greet(same_side(side, here) + [sibling])
    mail = Mail(send)
    mail.put(small_ref, small_got, recv_sib.at[1], sibling)

    def give_main():
        return remote(main_ref, got_main, cond.at[0], recv_sib.at[0], sibling)

    def give_bcr():
        return remote(bcr_ref, got_bcr, cond.at[0], recv_sib.at[0], sibling)

    def send_on(total, out, sem, slot, k):
        to = lax.rem(here + k, 16)
        return remote(total.at[to], out.at[slot], cond.at[k], sem.at[slot], (to, side))

    slot = lax.rem(here, 8)

    @pl.when(is_main)
    def _():
        give_bcr().start()

    @pl.when(jnp.logical_not(is_main))
    def _():
        give_main().start()

    mail.put(block_ref, block_other, recv_sib.at[3], sibling)
    mail.put(input_ref, input_other, recv_sib.at[4], sibling)
    mail.arrived(small_got, recv_sib.at[1])
    small_sum[...] = small_ref[...] + small_got[...]
    small_all[side, here] = small_sum[side]
    for k in range(1, 16):
        to = lax.rem(here + k, 16)
        mail.put(small_sum.at[side], small_all.at[side, here], recv_small.at[here], (to, side))

    @pl.when(is_main)
    def _():
        give_main().wait_recv()
        for k in range(1, 16):
            to = lax.rem(here + k, 16)
            total = main_ref[to].astype(f32) + got_main[to].astype(f32)
            got_main[to] = total.astype(got_main.dtype)
            send_on(got_main, main_parts, recv_main, slot, k).start()
        total = main_ref[here].astype(f32) + got_main[here].astype(f32)
        main_parts[slot] = total.astype(main_parts.dtype)

    @pl.when(jnp.logical_not(is_main))
    def _():
        give_bcr().wait_recv()
        for k in range(1, 16):
            to = lax.rem(here + k, 16)
            total = bcr_ref[to].astype(f32) + got_bcr[to].astype(f32)
            got_bcr[to] = total.astype(got_bcr.dtype)
            send_on(got_bcr, bcr_parts, recv_bcr, slot, k).start()
        total = bcr_ref[here].astype(f32) + got_bcr[here].astype(f32)
        bcr_parts[slot] = total.astype(bcr_parts.dtype)

    for k in range(1, 16):
        place = lax.rem(here + k, 16)
        mail.arrived(small_all.at[side, place], recv_small.at[place])
    mail.put(small_all.at[side], small_all.at[side], recv_pair, sibling)
    for j in range(8):

        @pl.when(8 * (1 - side) + j != here)
        def _():
            mail.arrived(bcr_parts.at[j], recv_bcr.at[j])

    total = bcr_parts[0].astype(f32)
    for j in range(1, 8):
        total = total + bcr_parts[j].astype(f32)
    bcr_mine[...] = total
    mail.put(bcr_mine, bcr_sib, recv_sib.at[2], sibling)
    mail.arrived(small_all.at[1 - side], recv_pair)
    for j in range(8):

        @pl.when(8 * side + j != here)
        def _():
            mail.arrived(main_parts.at[j], recv_main.at[j])

    mail.arrived(bcr_sib, recv_sib.at[2])
    bcr_out[...] = bcr_mine[...] + bcr_sib[...]
    mail.arrived(block_other, recv_sib.at[3])
    mail.arrived(input_other, recv_sib.at[4])

    @pl.when(is_main)
    def _():
        give_bcr().wait_send()
        for k in range(1, 16):
            send_on(got_main, main_parts, recv_main, slot, k).wait_send()

    @pl.when(jnp.logical_not(is_main))
    def _():
        give_main().wait_send()
        for k in range(1, 16):
            send_on(got_bcr, bcr_parts, recv_bcr, slot, k).wait_send()

    mail.finish()


def leave(*args):
    low, f32 = jnp.bfloat16, jnp.float32
    return call(
        leave_kernel,
        "leave",
        5,
        (
            ((8, 96, 768), low),
            ((96, 384), f32),
            ((2, 16, 8, 512), f32),
            ((64, 1536), f32),
            ((64, 1536), f32),
        ),
        [
            VMEM((16, 96, 768), low),
            VMEM((16, 96, 384), low),
            VMEM((8, 96, 384), low),
            VMEM((96, 384), f32),
            VMEM((96, 384), f32),
            VMEM((2, 8, 512), f32),
            VMEM((2, 8, 512), f32),
            DMA((20,)),
            DMA((5,)),
            DMA((8,)),
            DMA((8,)),
            DMA((16,)),
            DMA,
            DMA((16,)),
        ],
        args,
        limit=10,
    )


CHUNK = 128
LAYER = 256
HEADW = 64


def mm(left, right, low=True, exact=False):
    return mm_of(left, right, ((1,), (0,)), low, exact)


def mm_nt(left, right, low=True, exact=False):
    return mm_of(left, right, ((1,), (1,)), low, exact)


def mm_tn(left, right, low=True, exact=False):
    return mm_of(left, right, ((0,), (0,)), low, exact)


def mm_of(left, right, dims, low, exact):
    if exact:
        return lax.dot_general(
            left, right, (dims, ((), ())), precision=HIGH, preferred_element_type=jnp.float32
        )
    if low:
        left, right = left.astype(jnp.bfloat16), right.astype(jnp.bfloat16)
    return lax.dot_general(left, right, (dims, ((), ())), preferred_element_type=jnp.float32)


def lanes(shape):
    return lax.broadcasted_iota(jnp.int32, shape, 1)


def by_head(parts, rows):
    lane = lanes((rows, 3 * HEADW))
    return jnp.where(lane < HEADW, parts[0], jnp.where(lane < 2 * HEADW, parts[1], parts[2]))


def spread_heads(array):
    return by_head([array[:, h : h + 1] for h in range(3)], array.shape[0])


def soft_plus(values):
    return jnp.maximum(values, 0.0) + jnp.log1p(jnp.exp(-jnp.abs(values)))


def chunk_tables(step, log_rate, doc_col, doc_row):
    row = lax.broadcasted_iota(jnp.int32, (CHUNK, CHUNK), 0)
    col = lax.broadcasted_iota(jnp.int32, (CHUNK, CHUNK), 1)
    below = (row >= col).astype(jnp.float32)
    logs = mm(below, step * log_rate, exact=True)
    logs_t, step_t = logs.T, step.T
    pair = (row >= col) & (doc_col == doc_row)
    tables = [
        jnp.exp(jnp.where(pair, logs[:, h : h + 1] - logs_t[h : h + 1], -1e9)) for h in range(3)
    ]
    return logs, tables, [step_t[h : h + 1] for h in range(3)]


def as_column(row):
    return jnp.concatenate([row, jnp.zeros((CHUNK - 8, CHUNK), jnp.float32)], 0).T


def as_row(column):
    wide = jnp.broadcast_to(column, (64, CHUNK))
    return jnp.concatenate([wide, jnp.zeros((64, CHUNK), jnp.float32)], 0).T[0:8]


def mix_forward_kernel(
    n1_ref,
    extras_ref,
    extra_ref,
    cols_ref,
    small_ref,
    small_other,
    tapbc_ref,
    biasbc_ref,
    g_ref,
    x_ref,
    norm_ref,
    z_ref,
    ext_ref,
    dt_ref,
    y_ref,
    state_ref,
    g_all_ref,
    n2_ref,
    note_ref,
    res_ref,
    proj_ref,
    scale_ref,
    ids_ref,
    wbc_ref,
    wdt_ref,
    taps_ref,
    head_ref,
    gain_ref,
    part_ref,
    gained_ref,
    notes_ref,
    sum_ref,
    notes_out,
    *refs,
):
    got, sums, refs = refs[:5], refs[5:8], refs[8:]
    send, recv, recv_n, g_send, g_recv, g_recv_half, local = refs
    here, side, z_at = peers()[:3]
    half_here, slot = here // 8, lax.rem(here, 8)
    greet(same_side(side, here))
    low, f32 = jnp.bfloat16, jnp.float32
    mine = pltpu.make_async_copy(g_ref, rows_at(g_all_ref, here * 64, 64, 16), local)
    mine.start()
    g_mail = Mail(g_send)
    g_steps = gather_steps(g_mail, g_ref, g_all_ref, g_recv, g_recv_half, 64, 32)
    next(g_steps)

    small = jnp.where(side == half_here, small_ref[...], small_other[...])
    turned = pltpu.roll(small, lax.rem(1536 - 192 * slot, 1536), 1)
    taps_ref[0:4, 0:256] = tapbc_ref[...]
    taps_ref[4:5, 0:256] = biasbc_ref[...]
    taps_ref[5:8] = jnp.zeros((3, 448), f32)
    taps_ref[0:5, 256:448] = turned[0:5, 0:192]
    gain_ref[...] = jnp.broadcast_to(turned[5:6, 0:192], (8, 192))
    numbers = pltpu.roll(small[:, 0:128], lax.rem(128 - 3 * slot, 128), 1)[6:7]
    used = lanes((1, 128)) < 3
    head_ref[0:1] = jnp.where(used, numbers, 0.0)
    head_ref[1:2] = jnp.where(used, -jnp.exp(pltpu.roll(numbers, 104, 1)), 0.0)
    head_ref[2:3] = jnp.where(used, pltpu.roll(numbers, 80, 1), 0.0)
    wbc_ref[:, pl.ds(pl.multiple_of(side * 128, 128), 128)] = extras_ref[:, 0:128]
    wbc_ref[:, pl.ds(pl.multiple_of((1 - side) * 128, 128), 128)] = extra_ref[:, 0:128]
    wdt_ref[...] = jnp.where(side == half_here, extras_ref[:, 128:256], extra_ref[:, 128:256])
    ids_ref[0:8] = jnp.full((8, 128), -1.0, f32)
    ids_ref[1032:1040] = jnp.full((8, 128), -2.0, f32)
    for p in range(16):
        ids_ref[8 + 64 * p : 72 + 64 * p] = extras_ref[96 * p : 96 * p + 64, 128:256].astype(f32)
    notes_ref[...] = jnp.zeros(notes_ref.shape, f32)
    ext_ref[0:8] = jnp.zeros((8, 448), f32)

    @pl.loop(0, 4)
    def _(i):
        at = pl.ds(pl.multiple_of(i * LAYER, LAYER), LAYER)
        shifted = pl.ds(pl.multiple_of(i * LAYER + 8, 8), LAYER)
        rows = n1_ref[at]
        z_ref[at] = mm(rows, cols_ref[:, 0:192])
        ext_ref[shifted, 0:256] = mm(rows, wbc_ref[...])
        ext_ref[shifted, 256:448] = mm(rows, cols_ref[:, 256:448])
        dt_ref[at] = pltpu.roll(mm(rows, wdt_ref[...]), 112 - 3 * slot, 1) + head_ref[0:1]

    next(g_steps)
    rate, skip = head_ref[1:2], spread_heads(head_ref[2:3])
    state = jnp.zeros((128, 192), f32)
    ones = jnp.ones((8, 192), f32)
    for c in range(8):
        r = c * CHUNK
        at = pl.ds(r, CHUNK)
        ids = ids_ref[pl.ds(r + 8, CHUNK)]
        doc = ids[:, 40:41]
        pre = conv_pre(taps_ref, ext_ref, ids_ref, r, doc)
        act = pre * jax.nn.sigmoid(pre)
        b, cc, x = act[:, 0:128], act[:, 128:256], act[:, 256:448]
        step = soft_plus(dt_ref[at])
        logs, tables, step_t = chunk_tables(step, rate, doc, ids.T[40:41])
        cross = mm_nt(cc, b)
        stacked = jnp.concatenate([cross * tables[h] * step_t[h] for h in range(3)], 0)
        intra = mm(stacked, x)
        y = by_head([intra[h * CHUNK : (h + 1) * CHUNK] for h in range(3)], CHUNK)
        first, last = chunk_masks(ids_ref, r, doc)
        enters = jnp.exp(logs) * first
        state_ref[c] = state
        y = y + spread_heads(enters) * mm(cc, state) + skip * x
        y_ref[at] = y
        tail = jnp.exp(logs[CHUNK - 1 :] - logs) * last * step
        state = spread_heads(enters[CHUNK - 1 :]) * state + mm_tn(b, spread_heads(tail) * x)
        z = z_ref[at]
        gated = y * z * jax.nn.sigmoid(z)
        gained_ref[at] = (gated * gain_ref[0:1]).astype(low)
        squares = mm_nt(ones, gated * gated, exact=True)
        notes_ref[2 * c, :, 0:64] = squares[:, 0:64]
        notes_ref[2 * c + 1, :, 0:64] = squares[:, 64:128]
        next(g_steps, None)

    mail = Mail(send)
    zs = layers(z_at)

    def layer(k):
        at = pl.ds(pl.multiple_of(zs[k] * LAYER, LAYER), LAYER)

        @pl.loop(0, 6)
        def _(i):
            n = pl.ds(pl.multiple_of(i * 256, 256), 256)
            part_ref[at, n] = mm_nt(gained_ref[at], cols_ref[n, 512:704]).astype(low)

    steps = reduce_steps(mail, part_ref, sum_ref, got, sums, recv, 64)
    left = [3, 2, 1, 0]
    for turn in range(13):
        if turn in (0, 1, 3, 6):
            layer(left.pop(0))
        next(steps, None)
        if turn == 0:
            notes_out[here] = notes_ref[here]
            note_puts(mail, lambda to: notes_ref.at[to], notes_out, recv_n)
        if turn > 2:
            next(g_steps, None)
    for _ in g_steps:
        pass
    for _ in steps:
        pass
    note_waits(mail, notes_out, recv_n)
    squares = notes_out[0]
    for j in range(1, 16):
        squares = squares + notes_out[j]
    scale_row = lax.rsqrt(squares / INNER + EPS)
    note_ref[...] = scale_row
    scale = as_column(scale_row)[0:64, 0:1]
    scale_ref[...] = jnp.broadcast_to(scale, (64, 128))
    projected = scale * sum_ref[...]
    proj_ref[...] = projected
    residual = x_ref[...].astype(f32) + projected
    res_ref[...] = residual
    scale_two = lax.rsqrt(jnp.mean(residual * residual, axis=-1, keepdims=True) + EPS)
    n2_ref[...] = (residual * scale_two * norm_ref[...]).astype(low)
    mine.wait()
    g_mail.finish()
    mail.finish()


def conv_pre(taps_ref, ext_ref, ids_ref, r, doc):
    pre = taps_ref[4:5] + taps_ref[3:4] * ext_ref[pl.ds(r + 8, CHUNK)]
    for k in (1, 2, 3):
        same = (ids_ref[pl.ds(r + 8 - k, CHUNK), 40:41] == doc).astype(jnp.float32)
        pre = pre + taps_ref[3 - k : 4 - k] * ext_ref[pl.ds(r + 8 - k, CHUNK)] * same
    return pre


def chunk_masks(ids_ref, r, doc):
    first = (ids_ref[r + 7 : r + 8, 40:41] == doc).astype(jnp.float32)
    last = (ids_ref[r + 7 + CHUNK : r + 8 + CHUNK, 40:41] == doc).astype(jnp.float32)
    return first, last


def mix_forward(*args):
    low, f32 = jnp.bfloat16, jnp.float32
    return call(
        mix_forward_kernel,
        "mix_forward",
        2,
        (
            ((1024, 192), f32),
            ((1032, 448), f32),
            ((1024, 128), f32),
            ((1024, 192), f32),
            ((8, 128, 192), f32),
            ((1024, 1536), low),
            ((64, 1536), low),
            ((8, 128), f32),
            ((64, 1536), f32),
            ((64, 1536), f32),
            ((64, 128), f32),
            ((1040, 128), f32),
            ((1536, 256), low),
            ((1536, 128), low),
            ((8, 448), f32),
            ((8, 128), f32),
            ((8, 192), f32),
        ),
        [
            VMEM((1024, 1536), low),
            VMEM((1024, 192), low),
            VMEM((16, 8, 128), f32),
            VMEM((64, 1536), f32),
            VMEM((16, 8, 128), f32),
        ]
        + reduce_scratch(64, 1536, low)
        + [
            DMA((42,)),
            DMA((27,)),
            DMA((16,)),
            DMA((30,)),
            DMA((22,)),
            DMA((8,)),
            DMA,
        ],
        args,
        limit=16,
    )


def moe_kernel(
    own_ref,
    scale_note_ref,
    g_ref,
    cols_ref,
    eg_ref,
    ego_ref,
    eu_ref,
    euo_ref,
    ed_ref,
    edo_ref,
    extras_ref,
    ids_ref,
    res_ref,
    proj_ref,
    scale_ref,
    norm_ref,
    g_own_ref,
    dres_ref,
    cross_ref,
    scales_ref,
    moe_ref,
    geg_ref,
    geu_ref,
    ged_ref,
    sg_ref,
    su_ref,
    sd_ref,
    shared_ref,
    grouter_ref,
    gnorm_ref,
    dres_own_ref,
    n2_ref,
    act_ref,
    hid_ref,
    probs_ref,
    notes_ref,
    notes_out,
    sum_ref,
    low_ref,
    note_ref,
    og_ref,
    ou_ref,
    od_ref,
    *refs,
):
    got, sums, refs = refs[:5], refs[5:8], refs[8:]
    send, recv, recv_n, d_send, d_recv, d_recv_half, d_recv_n = refs[:7]
    n_send, n_recv, n_recv_half, n_recv_n, e_send, e_recv, local = refs[7:]
    here, side, z_at = peers()[:3]
    sibling = (here, 1 - side)
    greet(same_side(side, here) + [sibling])
    low, f32 = jnp.bfloat16, jnp.float32
    zs = layers(z_at)
    ones = jnp.ones((8, 256), f32)
    spare = lanes((LAYER, 128)) >= 64
    lane = lanes((LAYER, 128))
    keep = pltpu.make_async_copy(own_ref, rows_at(n2_ref, here * 64, 64, 16), local.at[1])
    keep.start()
    n_mail = Mail(n_send)
    n_steps = gather_steps(n_mail, own_ref, n2_ref, n_recv, n_recv_half, 64, 32)
    next(n_steps)
    scales_ref[here] = scale_note_ref[...]
    note_puts(n_mail, lambda to: scale_note_ref, scales_ref, n_recv_n)
    notes_ref[...] = jnp.zeros(notes_ref.shape, f32)
    pieces = (
        (eg_ref, eu_ref, ed_ref, 0, 256),
        (ego_ref, euo_ref, edo_ref, 256, 256),
    )

    def layer(k, piece):
        start = pl.multiple_of(zs[k] * LAYER, LAYER)
        at = pl.ds(start, LAYER)
        rows, grads = n2_ref[at], g_ref[at]
        if piece == 0:
            logits = mm(rows, extras_ref[:, 128:256])
            ids = ids_ref[pl.ds(pl.multiple_of(start + 8, 8), LAYER)]
            named = jnp.zeros((LAYER, 128), f32)
            for j in range(6):
                named = jnp.where(lane.astype(f32) == ids[:, 41 + j : 42 + j], 1.0, named)
            top = jnp.max(jnp.where(named > 0, logits, -1e30), axis=-1, keepdims=True)
            raised = jnp.exp(jnp.where(named > 0, logits - top, 0.0)) * named
            probs_ref[at] = raised / jnp.sum(raised, axis=-1, keepdims=True)
        if piece < 2:
            chosen = jnp.where(lane == here, probs_ref[at], 0.0)
            prob = jnp.sum(chosen, axis=-1, keepdims=True)
            gate_w, up_w, down_w, first, size = pieces[piece]
            gate = mm(rows, gate_w[...])
            up = mm(rows, up_w[...])
            d_act = mm_nt(grads, down_w[...])
            sig = jax.nn.sigmoid(gate)
            act = gate * sig * up
            act_ref[at, first : first + size] = (act * prob).astype(low)
            slopes = mm_nt(ones, act * d_act, exact=True)
            d_act = d_act * prob
            hid_ref[at, first : first + size] = (d_act * up * silu_slope(gate, sig)).astype(low)
            hid_ref[at, 640 + first : 640 + first + size] = (d_act * gate * sig).astype(low)
            for j in range(4):
                part = slopes[:, 64 * j : 64 * (j + 1)]
                if piece:
                    part = part + notes_ref[4 * zs[k] + j, :, 0:64]
                notes_ref[4 * zs[k] + j, :, 0:64] = part
            return
        gate = mm(rows, cols_ref[:, 128:256])
        up = mm(rows, cols_ref[:, 384:512])
        d_act = jnp.where(spare, mm(grads, cols_ref[:, 640:768]), 0.0)
        sig = jax.nn.sigmoid(gate)
        act_ref[at, 512:640] = jnp.where(spare, gate * sig * up, 0.0).astype(low)
        hid_ref[at, 512:640] = (d_act * up * silu_slope(gate, sig)).astype(low)
        hid_ref[at, 1152:1280] = (d_act * gate * sig).astype(low)

    def layer_back(k):
        at = pl.ds(pl.multiple_of(zs[k] * LAYER, LAYER), LAYER)

        @pl.loop(0, 6)
        def _(i):
            n = pl.ds(pl.multiple_of(i * 256, 256), 256)
            total = mm_nt(hid_ref[at, 0:256], eg_ref[n])
            total = total + mm_nt(hid_ref[at, 256:512], ego_ref[n])
            total = total + mm_nt(hid_ref[at, 512:640], cols_ref[n, 128:256])
            total = total + mm_nt(hid_ref[at, 640:896], eu_ref[n])
            total = total + mm_nt(hid_ref[at, 896:1152], euo_ref[n])
            total = total + mm_nt(hid_ref[at, 1152:1280], cols_ref[n, 384:512])
            moe_ref[at, n] = total.astype(low)

    e_mail = Mail(e_send)

    def up_grads(first, last):
        @pl.loop(first, last)
        def _(i):
            n = pl.ds(pl.multiple_of(i * 256, 256), 256)
            total = mm_tn(n2_ref[:, n], hid_ref[...])
            geg_ref[n] = total[:, 0:256]
            og_ref[n] = total[:, 256:512].astype(low)
            shared_ref[n, 0:128] = total[:, 512:640].astype(low)
            geu_ref[n] = total[:, 640:896]
            ou_ref[n] = total[:, 896:1152].astype(low)
            shared_ref[n, 128:256] = total[:, 1152:1280].astype(low)

    def give_up():
        e_mail.put(og_ref, sg_ref, e_recv.at[0], sibling)
        e_mail.put(ou_ref, su_ref, e_recv.at[1], sibling)

    def down_grads():
        od_ref[...] = mm_tn(act_ref[:, 256:512], g_ref[...]).astype(low)
        e_mail.put(od_ref, sd_ref, e_recv.at[2], sibling)
        ged_ref[...] = mm_tn(act_ref[:, 0:256], g_ref[...])

    def shared_down():
        @pl.loop(0, 6)
        def _(i):
            n = pl.ds(pl.multiple_of(i * 256, 256), 256)
            shared_ref[n, 256:384] = mm_tn(g_ref[:, n], act_ref[:, 512:640]).astype(low)

    def moe_part(first, last):
        @pl.loop(first, last)
        def _(i):
            at = pl.ds(pl.multiple_of(i * LAYER, LAYER), LAYER)
            total = mm(act_ref[at, 0:256], ed_ref[...]) + mm(act_ref[at, 256:512], edo_ref[...])
            total = total + mm_nt(act_ref[at, 512:640], cols_ref[:, 640:768])
            moe_ref[at] = total.astype(low)

    mail = Mail(send)
    order = [("far", 0), ("far", 1), ("joined", 0), ("far", 2), ("joined", 1), ("column", 0)]
    order += [("far", 3), ("joined", 2), ("column", 1), ("joined", 3), ("column", 2), ("column", 3)]
    steps = reduce_steps(mail, moe_ref, sum_ref, got, sums, recv, 64, order)

    for _ in range(4):
        next(n_steps)
    keep.wait()
    for j in range(4):
        layer(j, 0)
        next(n_steps, None)
        layer(j, 1)
        next(n_steps, None)
        layer(j, 2)
        layer_back(j)
        next(n_steps, None)
        for _ in range((1, 2, 3, 1)[j]):
            next(steps)
    notes_out[here] = notes_ref[here]
    note_puts(mail, lambda to: notes_ref.at[to], notes_out, recv_n)
    for j in range(3):
        next(steps)
        up_grads(2 * j, 2 * j + 2)
    give_up()
    next(steps)
    down_grads()
    for _ in steps:
        pass
    note_waits(mail, notes_out, recv_n)

    slopes = jnp.concatenate([notes_out[j, 0:1] for j in range(16)], 0)
    slopes = jnp.concatenate([slopes, jnp.zeros((112, 128), f32)], 0).T[0:64]
    own = pl.ds(pl.multiple_of(here * 64, 64), 64)
    probs = probs_ref[own]
    d_logits = probs * (slopes - jnp.sum(probs * slopes, axis=-1, keepdims=True))
    d_logits = d_logits.astype(low)
    grouter_ref[...] = mm_tn(n2_ref[own], d_logits).astype(low)
    dn2 = sum_ref[...] + mm_nt(d_logits, extras_ref[:, 128:256])
    residual = res_ref[...]
    value, gain = norm_step(dn2, residual, norm_ref[...])
    gnorm_ref[...] = gain
    d_res = g_own_ref[...].astype(f32) + value
    dres_own_ref[...] = d_res
    low_ref[...] = d_res.astype(low)
    cross = jnp.sum(low_ref[...].astype(f32) * proj_ref[...], axis=-1, keepdims=True)
    note_ref[...] = as_row(cross / scale_ref[:, 0:1])
    mine = pltpu.make_async_copy(low_ref, rows_at(dres_ref, here * 64, 64, 16), local.at[0])
    mine.start()
    d_mail = Mail(d_send)
    d_steps = gather_steps(d_mail, low_ref, dres_ref, d_recv, d_recv_half, 64, 32)
    next(d_steps)
    cross_ref[here] = note_ref[...]
    note_puts(d_mail, lambda to: note_ref, cross_ref, d_recv_n)
    next(d_steps)
    shared_down()
    mail.finish()
    for i in range(4):
        next(d_steps)
        moe_part(i, i + 1)
    for _ in d_steps:
        pass
    e_mail.arrived(sg_ref, e_recv.at[0])
    e_mail.arrived(su_ref, e_recv.at[1])
    e_mail.arrived(sd_ref, e_recv.at[2])
    note_waits(n_mail, scales_ref, n_recv_n)
    note_waits(d_mail, cross_ref, d_recv_n)
    mine.wait()
    n_mail.finish()
    e_mail.finish()
    d_mail.finish()


def norm_step(grad, values, gain):
    scale = lax.rsqrt(jnp.mean(values * values, axis=-1, keepdims=True) + EPS)
    gain_grad = jnp.sum(grad * values * scale, axis=0, keepdims=True)
    scaled = grad * gain
    pull = scale * scale * scale * jnp.mean(scaled * values, axis=-1, keepdims=True)
    return scale * scaled - values * pull, gain_grad


def moe(*args):
    low, f32 = jnp.bfloat16, jnp.float32
    return call(
        moe_kernel,
        "moe",
        3,
        (
            ((1024, 1536), low),
            ((16, 8, 128), f32),
            ((16, 8, 128), f32),
            ((1024, 1536), low),
            ((1536, 256), f32),
            ((1536, 256), f32),
            ((256, 1536), f32),
            ((1536, 256), low),
            ((1536, 256), low),
            ((256, 1536), low),
            ((1536, 384), low),
            ((1536, 128), low),
            ((1, 1536), f32),
            ((64, 1536), f32),
        ),
        [
            VMEM((1024, 1536), low),
            VMEM((1024, 640), low),
            VMEM((1024, 1280), low),
            VMEM((1024, 128), f32),
            VMEM((16, 8, 128), f32),
            VMEM((16, 8, 128), f32),
            VMEM((64, 1536), f32),
            VMEM((64, 1536), low),
            VMEM((8, 128), f32),
            VMEM((1536, 256), low),
            VMEM((1536, 256), low),
            VMEM((256, 1536), low),
        ]
        + reduce_scratch(64, 1536, low)
        + [
            DMA((42,)),
            DMA((27,)),
            DMA((16,)),
            DMA((45,)),
            DMA((22,)),
            DMA((8,)),
            DMA((16,)),
            DMA((45,)),
            DMA((22,)),
            DMA((8,)),
            DMA((16,)),
            DMA((3,)),
            DMA((3,)),
            DMA((2,)),
        ],
        args,
        limit=20,
    )


def mix_backward_kernel(
    dres_ref,
    cross_ref,
    scales_ref,
    n1_ref,
    cols_ref,
    wbc_ref,
    wdt_ref,
    taps_ref,
    head_ref,
    gain_ref,
    ids_ref,
    z_ref,
    ext_ref,
    dt_ref,
    y_ref,
    state_ref,
    moe_ref,
    shared_ref,
    grouter_ref,
    gnorm_ref,
    res_ref,
    dres_own_ref,
    x_ref,
    norm_ref,
    main_ref,
    bcr_ref,
    small_ref,
    block_ref,
    input_ref,
    part_ref,
    dm_ref,
    mixed_ref,
    din_ref,
    dpre_ref,
    sum_ref,
    *refs,
):
    got, sums, refs = refs[:5], refs[5:8], refs[8:]
    b_got, b_sums, refs = refs[:5], refs[5:8], refs[8:]
    send, recv, b_send, b_recv = refs
    here, side, z_at = peers()[:3]
    half_here, slot = here // 8, lax.rem(here, 8)
    greet(near(side))
    low, f32 = jnp.bfloat16, jnp.float32
    zs = layers(z_at)
    b_mail = Mail(b_send)
    b_steps = reduce_steps(b_mail, moe_ref, block_ref, b_got, b_sums, b_recv, 64)
    next(b_steps)

    @pl.loop(0, 4)
    def _(i):
        at = pl.ds(pl.multiple_of(i * LAYER, LAYER), LAYER)
        dm_ref[at] = mm(dres_ref[at], cols_ref[:, 512:704])

    next(b_steps)
    rate, skip = head_ref[1:2], spread_heads(head_ref[2:3])
    onehot = (
        lax.broadcasted_iota(jnp.int32, (192, 128), 0) // HEADW
        == lax.broadcasted_iota(jnp.int32, (192, 128), 1)
    ).astype(f32)
    row = lax.broadcasted_iota(jnp.int32, (CHUNK, CHUNK), 0)
    lane = lanes((CHUNK, CHUNK))
    above = (row <= lane).astype(f32)
    lane192 = lanes((CHUNK, 192))
    masks = [((lane192 // HEADW) == h).astype(f32) for h in range(3)]
    d_state = jnp.zeros((128, 192), f32)
    g_gain = jnp.zeros((1, 192), f32)
    g_skip = jnp.zeros((1, 192), f32)
    g_rate = jnp.zeros((1, 128), f32)
    g_dt = jnp.zeros((1, 128), f32)
    g_taps = [jnp.zeros((1, 448), f32) for _ in range(5)]
    dpre_ref[1024:1032] = jnp.zeros((8, 448), f32)
    din_ref[:, 128:256] = jnp.zeros((1024, 128), low)
    din_ref[:, 384:512] = jnp.zeros((1024, 128), low)
    mixed_ref[:, 128:256] = jnp.zeros((1024, 128), low)
    for c in range(7, -1, -1):
        r = c * CHUNK
        at = pl.ds(r, CHUNK)
        ids = ids_ref[pl.ds(r + 8, CHUNK)]
        doc = ids[:, 40:41]
        scale_row = jnp.concatenate(
            [scales_ref[2 * c, :, 0:64], scales_ref[2 * c + 1, :, 0:64]], 1
        )
        cross_row = jnp.concatenate([cross_ref[2 * c, :, 0:64], cross_ref[2 * c + 1, :, 0:64]], 1)
        scale = as_column(scale_row)[:, 0:1]
        pull = scale * scale * scale * as_column(cross_row)[:, 0:1] / INNER
        z, y, dm, gain = z_ref[at], y_ref[at], dm_ref[at], gain_ref[0:1]
        sig = jax.nn.sigmoid(z)
        gated = y * z * sig
        scaled = gated * scale
        mixed_ref[at, 0:192] = (scaled * gain).astype(low)
        g_gain = g_gain + jnp.sum(dm * scaled, axis=0, keepdims=True)
        d_gated = scale * gain * dm - gated * pull
        d_y = d_gated * z * sig
        din_ref[at, 0:192] = (d_gated * y * silu_slope(z, sig)).astype(low)
        pre = conv_pre(taps_ref, ext_ref, ids_ref, r, doc)
        pre_sig = jax.nn.sigmoid(pre)
        act = pre * pre_sig
        b, cc, x = act[:, 0:128], act[:, 128:256], act[:, 256:448]
        g_skip = g_skip + jnp.sum(d_y * x, axis=0, keepdims=True)
        dt = dt_ref[at]
        step = soft_plus(dt)
        logs, tables, step_t = chunk_tables(step, rate, doc, ids.T[40:41])
        cross = mm_nt(cc, b)
        decays = [tables[h] * step_t[h] for h in range(3)]
        stacked = jnp.concatenate([cross * decays[h] for h in range(3)], 0)
        d_ys = jnp.concatenate([d_y * masks[h] for h in range(3)], 0)
        d_stack = mm_nt(d_ys, x)
        d_x = skip * d_y + mm_tn(stacked, d_ys)
        state = state_ref[c]
        first, last = chunk_masks(ids_ref, r, doc)
        enters = jnp.exp(logs) * first
        d_in_y = spread_heads(enters) * d_y
        from_state = mm(cc, state)
        tail_w = jnp.exp(logs[CHUNK - 1 :] - logs) * last
        tail = tail_w * step
        tail_x = spread_heads(tail)
        to_state = mm(b, d_state)
        d_x = d_x + tail_x * to_state
        kept = enters[CHUNK - 1 :]
        d_kept = jnp.sum(d_state * state, axis=0, keepdims=True)
        folded = mm(
            jnp.concatenate(
                [d_y * from_state, x * to_state, jnp.broadcast_to(d_kept, (8, 192))], 0
            ),
            onehot,
            exact=True,
        )
        d_enters, d_tail = folded[:CHUNK], folded[CHUNK : 2 * CHUNK]
        d_kept = folded[2 * CHUNK : 2 * CHUNK + 1]
        d_cross = jnp.zeros((CHUNK, CHUNK), f32)
        row_sums = jnp.zeros((CHUNK, CHUNK), f32)
        col_sums = []
        for h in range(3):
            d_a = d_stack[h * CHUNK : (h + 1) * CHUNK]
            d_cross = d_cross + d_a * decays[h]
            plain = d_a * cross * tables[h]
            col_sums.append(jnp.sum(plain, axis=0, keepdims=True))
            total = jnp.sum(plain * step_t[h], axis=1, keepdims=True)
            row_sums = jnp.where(lane == h, total, row_sums)
        col_sums = as_column(jnp.concatenate(col_sums + [jnp.zeros((5, CHUNK), f32)], 0))
        d_c = mm(d_cross, b) + mm_nt(d_in_y, state)
        d_b = mm_tn(d_cross, cc) + mm_nt(tail_x * x, d_state)
        pulled = d_tail * tail
        d_logs = row_sums - step * col_sums + d_enters * enters - pulled
        d_last = jnp.sum(pulled, axis=0, keepdims=True) + d_kept * kept
        d_logs = d_logs + jnp.where(row == CHUNK - 1, d_last, 0.0)
        d_l = mm(above, d_logs, exact=True)
        d_step = col_sums + d_tail * tail_w + d_l * rate
        g_rate = g_rate + jnp.sum(d_l * step, axis=0, keepdims=True)
        d_dt = jnp.where(lane < 3, d_step * jax.nn.sigmoid(dt), 0.0)
        g_dt = g_dt + jnp.sum(d_dt, axis=0, keepdims=True)
        din_ref[at, 768:896] = pltpu.roll(d_dt, 16 + 3 * slot, 1).astype(low)
        d_state = spread_heads(kept) * d_state + mm_tn(cc, d_in_y)
        d_pre = jnp.concatenate([d_b, d_c, d_x], 1) * silu_slope(pre, pre_sig)
        dpre_ref[at] = d_pre
        g_taps[4] = g_taps[4] + jnp.sum(d_pre, axis=0, keepdims=True)
        g_taps[3] = g_taps[3] + jnp.sum(d_pre * ext_ref[pl.ds(r + 8, CHUNK)], axis=0, keepdims=True)
        d_ext = taps_ref[3:4] * d_pre
        for k in (1, 2, 3):
            same = (ids_ref[pl.ds(r + 8 - k, CHUNK), 40:41] == doc).astype(f32)
            g_taps[3 - k] = g_taps[3 - k] + jnp.sum(
                d_pre * same * ext_ref[pl.ds(r + 8 - k, CHUNK)], axis=0, keepdims=True
            )
            same = (ids_ref[pl.ds(r + 8 + k, CHUNK), 40:41] == doc).astype(f32)
            d_ext = d_ext + taps_ref[3 - k : 4 - k] * (dpre_ref[pl.ds(r + k, CHUNK)] * same)
        din_ref[at, 512:768] = d_ext[:, 0:256].astype(low)
        din_ref[at, 256:448] = d_ext[:, 256:448].astype(low)
        next(b_steps, None)
    small_ref[...] = jnp.zeros((2, 8, 512), f32)
    for k in range(5):
        small_ref[1, k : k + 1, 0:448] = g_taps[k]
    small_ref[1, 5:6, 0:192] = g_gain
    small_ref[1, 5:6, 256:448] = g_skip
    small_ref[1, 6:7, 0:128] = g_dt
    small_ref[1, 6:7, 256:384] = g_rate * rate

    def layer(k):
        at = pl.ds(pl.multiple_of(zs[k] * LAYER, LAYER), LAYER)

        @pl.loop(0, 6)
        def _(i):
            n = pl.ds(pl.multiple_of(i * 256, 256), 256)
            total = mm_nt(din_ref[at, 0:256], cols_ref[n, 0:256])
            total = total + mm_nt(din_ref[at, 256:512], cols_ref[n, 256:512])
            total = total + mm_nt(din_ref[at, 512:768], wbc_ref[n])
            total = total + mm_nt(din_ref[at, 768:896], wdt_ref[n])
            part_ref[at, n] = total.astype(low)

    moved = 24 * half_here

    def grads(first, last):
        @pl.loop(first, last)
        def _(i):
            n = pl.ds(pl.multiple_of(i * 256, 256), 256)
            total = mm_tn(n1_ref[:, n], din_ref[...])
            out = mm_tn(dres_ref[:, n], mixed_ref[...])
            main_ref[n, 0:128] = total[:, 0:128].astype(low)
            main_ref[n, 128:256] = total[:, 128:256].astype(low) + shared_ref[n, 0:128]
            main_ref[n, 256:384] = total[:, 256:384].astype(low)
            main_ref[n, 384:512] = total[:, 384:512].astype(low) + shared_ref[n, 128:256]
            main_ref[n, 512:640] = out[:, 0:128].astype(low)
            main_ref[n, 640:768] = out[:, 128:256].astype(low) + shared_ref[n, 256:384]
            bcr_ref[n, 0:256] = total[:, 512:768].astype(low)
            steps_part = pltpu.roll(total[:, 768:896], moved, 1)
            bcr_ref[n, 256:384] = (steps_part + grouter_ref[n].astype(f32)).astype(low)

    mail = Mail(send)
    steps = reduce_steps(mail, part_ref, sum_ref, got, sums, recv, 64)
    left = [3, 2, 1, 0]
    for turn in range(13):
        if turn in (0, 1, 3, 6):
            layer(left.pop(0))
        next(steps, None)
        next(b_steps, None)
        if turn in (7, 8, 9):
            grads(2 * (turn - 7), 2 * (turn - 6))
    for _ in b_steps:
        pass
    block_ref[...] += res_ref[...]
    for _ in steps:
        pass
    value, gain = norm_step(sum_ref[...], x_ref[...].astype(f32), norm_ref[...])
    input_ref[...] = dres_own_ref[...] + value
    for i in range(4):
        small_ref[0, i : i + 1, 0:384] = gain[:, 384 * i : 384 * (i + 1)]
        small_ref[0, 4 + i : 5 + i, 0:384] = gnorm_ref[:, 384 * i : 384 * (i + 1)]
    b_mail.finish()
    mail.finish()


def mix_backward(*args):
    low, f32 = jnp.bfloat16, jnp.float32
    return call(
        mix_backward_kernel,
        "mix_backward",
        4,
        (
            ((1536, 768), low),
            ((1536, 384), low),
            ((2, 8, 512), f32),
            ((64, 1536), f32),
            ((64, 1536), f32),
        ),
        [
            VMEM((1024, 1536), low),
            VMEM((1024, 192), f32),
            VMEM((1024, 256), low),
            VMEM((1024, 896), low),
            VMEM((1032, 448), f32),
            VMEM((64, 1536), f32),
        ]
        + reduce_scratch(64, 1536, low)
        + reduce_scratch(64, 1536, low)
        + [DMA((27,)), DMA((27,)), DMA((27,)), DMA((27,))],
        args,
        limit=24,
    )


def place_kernel(
    main_ref,
    bcr_ref,
    small_ref,
    block_own,
    block_other,
    input_own,
    input_other,
    geg_ref,
    geu_ref,
    ged_ref,
    sg_ref,
    su_ref,
    sd_ref,
    block_out,
    input_out,
    norm1_out,
    wz_out,
    wx_out,
    wbc_out,
    wdt_out,
    convx_out,
    convbc_out,
    biasx_out,
    biasbc_out,
    dt_out,
    log_out,
    skip_out,
    gnorm_out,
    wout_out,
    norm2_out,
    router_out,
    sgate_out,
    sup_out,
    sdown_out,
    eg_out,
    eu_out,
    ed_out,
):
    side = lax.axis_index("head")
    f32 = jnp.float32
    for own, other, out in (
        (block_own, block_other, block_out),
        (input_own, input_other, input_out),
    ):
        out[:, 0] = jnp.where(side == 0, own[...], other[...])
        out[:, 1] = jnp.where(side == 0, other[...], own[...])
    norms = small_ref[0, 0]
    taps = small_ref[1, 0, :, 0:256]
    for j in range(1, 16):
        norms = norms + small_ref[0, j]
        taps = taps + small_ref[1, j, :, 0:256]
    for i in range(4):
        norm1_out[0:1, 384 * i : 384 * (i + 1)] = norms[i : i + 1, 0:384]
        norm2_out[0:1, 384 * i : 384 * (i + 1)] = norms[4 + i : 5 + i, 0:384]
    convbc_out[...] = taps[0:4]
    biasbc_out[...] = taps[4:5]
    wbc_out[...] = bcr_ref[:, 0:256]
    router_out[...] = bcr_ref[:, 256:272]
    wdt_out[...] = pltpu.roll(bcr_ref[:, 256:384], 112 - 24 * side, 1)[:, 0:24]
    onehot = (
        lax.broadcasted_iota(jnp.int32, (192, 128), 0) // HEADW
        == lax.broadcasted_iota(jnp.int32, (192, 128), 1)
    ).astype(f32)
    for j in range(8):
        place = 8 * side + j
        wide, narrow = slice(192 * j, 192 * (j + 1)), slice(64 * j, 64 * (j + 1))
        convx_out[:, wide] = small_ref[1, place, 0:4, 256:448]
        biasx_out[:, wide] = small_ref[1, place, 4:5, 256:448]
        gnorm_out[:, wide] = small_ref[1, place, 5:6, 0:192]
        skips = jnp.broadcast_to(small_ref[1, place, 5:6, 256:448], (8, 192))
        skip_out[:, 3 * j : 3 * j + 3] = mm(skips, onehot, exact=True)[0:1, 0:3]
        dt_out[:, 3 * j : 3 * j + 3] = small_ref[1, place, 6:7, 0:3]
        log_out[:, 3 * j : 3 * j + 3] = small_ref[1, place, 6:7, 256:259]
        part = main_ref[j].astype(f32)
        wz_out[:, wide] = part[:, 0:192]
        sgate_out[:, narrow] = part[:, 192:256]
        wx_out[:, wide] = part[:, 256:448]
        sup_out[:, narrow] = part[:, 448:512]
        turned = jnp.concatenate([part[:, 512:768], jnp.zeros((32, 256), f32)], 0)
        turned = jnp.concatenate([turned[:, 0:128].T, turned[:, 128:256].T], 0)
        wout_out[192 * j : 192 * (j + 1)] = turned[0:192, 0:96]
        sdown_out[64 * j : 64 * (j + 1)] = turned[192:256, 0:96]
    eg_out[0] = geg_ref[...] + sg_ref[...].astype(f32)
    eu_out[0] = geu_ref[...] + su_ref[...].astype(f32)
    ed_out[0] = ged_ref[...] + sd_ref[...].astype(f32)


def place(*args):
    shapes = (
        (64, 2, 1536),
        (64, 2, 1536),
        (1, 1536),
        (96, 1536),
        (96, 1536),
        (96, 256),
        (96, 24),
        (4, 1536),
        (4, 256),
        (1, 1536),
        (1, 256),
        (1, 24),
        (1, 24),
        (1, 24),
        (1, 1536),
        (1536, 96),
        (1, 1536),
        (96, 16),
        (96, 512),
        (96, 512),
        (512, 96),
        (1, 1536, 256),
        (1, 1536, 256),
        (1, 256, 1536),
    )
    vmem = pl.BlockSpec(memory_space=VMEM)
    return pl.pallas_call(
        place_kernel,
        out_shape=tuple(jax.ShapeDtypeStruct(shape, jnp.float32) for shape in shapes),
        in_specs=[vmem] * len(args),
        out_specs=(vmem,) * len(shapes),
        compiler_params=pltpu.CompilerParams(vmem_limit_bytes=48 << 20),
        name="place",
    )(*args)


def by_heads(
    hidden_in,
    doc_ids,
    routes,
    norm1_gain,
    w_z,
    w_x,
    w_bc,
    w_dt,
    conv_x,
    conv_bc,
    convb_x,
    convb_bc,
    dt_bias,
    a_log,
    d_skip,
    gnorm_gain,
    w_out,
    norm2_gain,
    router,
    shared_gate,
    shared_up,
    shared_down,
    expert_gate,
    expert_up,
    expert_down,
    cotangent,
):
    side = lax.axis_index("head")
    width = hidden_in.shape[-1]
    low, f32 = jnp.bfloat16, jnp.float32
    x_own = lax.dynamic_index_in_dim(hidden_in, side, 1, False)
    g_own = lax.dynamic_index_in_dim(cotangent, side, 1, False)
    ids = jnp.concatenate(
        [
            lax.dynamic_index_in_dim(doc_ids, side, 1, True),
            lax.dynamic_index_in_dim(routes, side, 1, False),
        ],
        1,
    )
    extra = jnp.concatenate(
        [
            lax.dynamic_slice_in_dim(w_bc, side * 128, 128, 1),
            router,
            w_dt,
            jnp.pad(ids.astype(low), ((0, 32), (0, 81))),
        ],
        1,
    )
    numbers = jnp.concatenate([dt_bias, a_log, d_skip])
    small = jnp.concatenate(
        [
            conv_x,
            convb_x[None],
            gnorm_gain[None],
            jnp.pad(numbers, (0, width - numbers.shape[0]))[None],
            jnp.zeros((1, width), f32),
        ],
        0,
    )
    eg, eu, ed = expert_gate[0], expert_up[0], expert_down[0]
    norm1, norm2 = norm1_gain[None], norm2_gain[None]
    n1, extras, extras_sib, cols, small_sib, eg_o, eu_o, ed_o = enter(
        x_own,
        norm1,
        extra,
        w_z,
        shared_gate,
        w_x,
        shared_up,
        w_out.T,
        shared_down.T,
        small,
        eg,
        eu,
        ed,
    )
    (
        z,
        ext,
        dt,
        y,
        states,
        g_all,
        n2,
        scale_note,
        residual,
        projected,
        scale_own,
        ids,
        wbc,
        wdt,
        taps,
        head,
        gain,
    ) = mix_forward(
        n1,
        extras,
        extras_sib,
        cols,
        small,
        small_sib,
        conv_bc,
        convb_bc[None],
        g_own,
        x_own,
        norm2,
    )
    (
        d_res_all,
        cross,
        scales,
        moe_part,
        *grad_experts,
        shared,
        grad_router,
        grad_norm2,
        d_res,
    ) = moe(
        n2,
        scale_note,
        g_all,
        cols,
        eg,
        eg_o,
        eu,
        eu_o,
        ed,
        ed_o,
        extras,
        ids,
        residual,
        projected,
        scale_own,
        norm2,
        g_own,
    )
    main, bcr, small, block_own, input_own = mix_backward(
        d_res_all,
        cross,
        scales,
        n1,
        cols,
        wbc,
        wdt,
        taps,
        head,
        gain,
        ids,
        z,
        ext,
        dt,
        y,
        states,
        moe_part,
        shared,
        grad_router,
        grad_norm2,
        residual,
        d_res,
        x_own,
        norm1,
    )
    main, bcr, small, block_sib, input_sib = leave(
        main.reshape(16, 96, 768), bcr.reshape(16, 96, 384), small, block_own, input_own
    )
    results = list(
        place(main, bcr, small, block_own, block_sib, input_own, input_sib, *grad_experts)
    )
    for i in (2, 9, 10, 11, 12, 13, 14, 16):
        results[i] = results[i].reshape(-1)
    return tuple(results)


def solution(mesh):
    places = mesh.shape["seq"]
    whole_heads = places == 16 and mesh.shape["head"] == 2
    placed = (
        P("seq", None, None),
        P("seq", None),
        P("seq", None, None),
        P(),
        P("seq", "head"),
        P("seq", "head"),
        P("seq", None),
        P("seq", "head"),
        P(None, "head"),
        P(),
        P("head"),
        P(),
        P("head"),
        P("head"),
        P("head"),
        P("head"),
        P("head", "seq"),
        P(),
        P("seq", None),
        P("seq", "head"),
        P("seq", "head"),
        P("head", "seq"),
        P("seq", None, "head"),
        P("seq", None, "head"),
        P("seq", "head", None),
        P("seq", None, None),
    )
    return jax.shard_map(
        by_heads if whole_heads else on_device,
        mesh=mesh,
        in_specs=placed,
        out_specs=(
            P("seq", None, None),
            P("seq", None, None),
            P(),
            P("seq", "head"),
            P("seq", "head"),
            P("seq", None),
            P("seq", "head"),
            P(None, "head"),
            P(),
            P("head"),
            P(),
            P("head"),
            P("head"),
            P("head"),
            P("head"),
            P("head", "seq"),
            P(),
            P("seq", None),
            P("seq", "head"),
            P("seq", "head"),
            P("head", "seq"),
            P("seq", None, "head"),
            P("seq", None, "head"),
            P("seq", "head", None),
        ),
        check_vma=False,
    )
```

```python
import jax
import jax.numpy as jnp
from jax import lax
from jax.experimental import pallas as pl
from jax.experimental.pallas import tpu as pltpu
from jax.sharding import PartitionSpec as P

KER = 4
INNER = 3072


EPS = 1e-05
HIGH = lax.Precision.HIGHEST


def passed_along(array, axis, by):
    length = lax.axis_size(axis)
    pairs = [(i, i + by) for i in range(length) if 0 <= i + by < length]
    return lax.ppermute(array, axis, pairs)


def entering(array, axis, combine, identity, reverse):
    length, here = (lax.axis_size(axis), lax.axis_index(axis))
    everything = jax.tree.map(
        lambda part, kind: lax.all_gather(part.astype(kind), axis),
        array,
        jax.tree.map(lambda a: jnp.bfloat16 if a.dtype == jnp.float32 else a.dtype, array),
    )
    start = jax.tree.map(
        lambda part, zero: jnp.broadcast_to(jnp.asarray(zero, part.dtype), part.shape),
        array,
        identity,
    )

    def hop(k, before):
        at = length - 1 - k if reverse else k
        reached = at > here if reverse else at < here
        new = combine(
            before, jax.tree.map(lambda part, own: part[at].astype(own.dtype), everything, array)
        )
        return jax.tree.map(lambda a, b: jnp.where(reached, a, b), new, before)

    return lax.fori_loop(0, length, hop, start)


def shortened(array):

    def short(part):
        return part.astype(jnp.bfloat16) if part.dtype == jnp.float32 else part

    return jax.tree.map(short, array)


def conv_apply(conv_ext, docs_ext, weight, conv_bias):
    length_here = conv_ext.shape[0] - (KER - 1)
    running = conv_bias
    for offset in range(KER):
        same_doc = (docs_ext[offset : offset + length_here] == docs_ext[KER - 1 :]).astype(
            jnp.float32
        )
        running = (
            running + weight[offset] * conv_ext[offset : offset + length_here] * same_doc[..., None]
        )
    return jax.nn.silu(running)


def group_parts(x_heads, step_size, b_state, decay_rate, doc_ids, prev_doc):
    log_decay = jnp.cumsum(step_size * decay_rate, axis=0)
    end_keep = (doc_ids == doc_ids[-1:]).astype(jnp.float32)
    weight = jnp.exp(log_decay[-1:] - log_decay) * end_keep[..., None] * step_size
    s_local = jnp.einsum("tsh,tshp,tsn->shpn", weight, x_heads, b_state, precision=HIGH)
    a_total = jnp.exp(log_decay[-1]) * (doc_ids[-1] == prev_doc).astype(jnp.float32)[:, None]
    return (s_local, a_total)


def group_output(x_heads, step_size, b_state, c_state, decay_rate, doc_ids, prev_doc, s_in):
    length_here = x_heads.shape[0]
    log_decay = jnp.cumsum(step_size * decay_rate, axis=0)
    causal = jnp.arange(length_here)[:, None] >= jnp.arange(length_here)[None, :]
    pair_mask = (causal[:, :, None] & (doc_ids[:, None, :] == doc_ids[None, :, :])).astype(
        jnp.float32
    )
    gap_decay = log_decay[:, None] - log_decay[None, :]
    decay_table = (
        jnp.exp(jnp.where(pair_mask[..., None] > 0, gap_decay, 0.0)) * pair_mask[..., None]
    )
    cross_dot = jnp.einsum("tsn,usn->tus", c_state, b_state, precision=HIGH)
    y_intra = jnp.einsum(
        "tush,ush,ushp->tshp",
        decay_table * cross_dot[..., None],
        step_size,
        x_heads,
        precision=HIGH,
    )
    enters = jnp.exp(log_decay) * (doc_ids == prev_doc[None, :]).astype(jnp.float32)[..., None]
    y_inter = jnp.einsum("tsn,shpn->tshp", c_state, s_in, precision=HIGH) * enters[..., None]
    return y_intra + y_inter


def ssm_local(x_heads, step_size, b_state, c_state, decay_rate, s_in, doc_ids, prev_doc):
    y_core = group_output(x_heads, step_size, b_state, c_state, decay_rate, doc_ids, prev_doc, s_in)
    s_local, a_total = group_parts(x_heads, step_size, b_state, decay_rate, doc_ids, prev_doc)
    return (y_core, a_total[..., None, None] * s_in + s_local)


def carry_combine(earlier, later_part):
    return (earlier[0] * later_part[0], later_part[0][..., None, None] * earlier[1] + later_part[1])


def head_total(partial_sum):
    return lax.psum(partial_sum, "head")


def flat_dot(left_side, right_side):
    lead_dims = left_side.shape[:-1]
    product = jnp.dot(
        left_side.reshape(-1, left_side.shape[-1]), right_side, preferred_element_type=jnp.float32
    )
    return product.reshape(lead_dims + (right_side.shape[-1],))


def flat_dot_t(left_side, right_side):
    lead_dims = left_side.shape[:-1]
    product = lax.dot_general(
        left_side.reshape(-1, left_side.shape[-1]),
        right_side,
        (((1,), (1,)), ((), ())),
        preferred_element_type=jnp.float32,
    )
    return product.reshape(lead_dims + (right_side.shape[0],))


def outer_sum(left_side, right_side):
    return lax.dot_general(
        left_side.reshape(-1, left_side.shape[-1]),
        right_side.reshape(-1, right_side.shape[-1]),
        (((0,), (0,)), ((), ())),
        preferred_element_type=jnp.float32,
    )


def silu_slope(values, sigmoid_of):
    return sigmoid_of * (1.0 + values * (1.0 - sigmoid_of))


def norm_back(grad_normed, values, scale_of, gain):
    scaled_grad = grad_normed * gain
    gain_grad = jnp.sum((grad_normed * values * scale_of).reshape(-1, values.shape[-1]), axis=0)
    cube = scale_of * scale_of * scale_of
    value_grad = scale_of * scaled_grad - values * cube * jnp.mean(
        scaled_grad * values, axis=-1, keepdims=True
    )
    return (value_grad, gain_grad)


def on_device(
    hidden_in,
    doc_ids,
    routes,
    norm1_gain,
    w_z,
    w_x,
    w_bc,
    w_dt,
    conv_x,
    conv_bc,
    convb_x,
    convb_bc,
    dt_bias,
    a_log,
    d_skip,
    gnorm_gain,
    w_out,
    norm2_gain,
    router,
    shared_gate,
    shared_up,
    shared_down,
    expert_gate,
    expert_up,
    expert_down,
    cotangent,
):
    block_len, seq_here, width = hidden_in.shape
    top_count = routes.shape[-1]
    heads_here = dt_bias.shape[0]
    inner_here = convb_x.shape[0]
    head_size = inner_here // heads_here
    state_size = convb_bc.shape[0] // 2
    seq_count = lax.axis_size("seq")
    local_experts = expert_gate.shape[0]
    experts_all = local_experts * seq_count
    tok_here = block_len * seq_here
    capacity = 2 * tok_here * top_count // experts_all
    edge_len = KER - 1
    x_float = hidden_in.astype(jnp.float32)
    scale_one = lax.rsqrt(jnp.mean(x_float * x_float, axis=-1, keepdims=True) + EPS)
    normed_one = (x_float * scale_one * norm1_gain).astype(jnp.bfloat16)
    gathered = (
        lax.all_gather(w_z, "seq", axis=0, tiled=True),
        lax.all_gather(w_x, "seq", axis=0, tiled=True),
        lax.all_gather(w_dt, "seq", axis=0, tiled=True),
        lax.all_gather(w_bc, "seq", axis=0, tiled=True),
        lax.all_gather(router, "seq", axis=0, tiled=True),
        lax.all_gather(shared_gate, "seq", axis=0, tiled=True),
        lax.all_gather(shared_up, "seq", axis=0, tiled=True),
        lax.all_gather(w_out, "seq", axis=1, tiled=True),
        lax.all_gather(shared_down, "seq", axis=1, tiled=True),
    )
    full_z, full_x, full_dt, full_bc, full_router, full_sgate, full_sup, full_out, full_sdown = (
        gathered
    )
    gate_z = flat_dot(normed_one, full_z)
    proj_x = flat_dot(normed_one, full_x)
    proj_bc = flat_dot(normed_one, full_bc)
    dt_pre = flat_dot(normed_one, full_dt) + dt_bias
    conv_in = jnp.concatenate([proj_x, proj_bc], axis=-1)
    tail_in, tail_doc = (
        passed_along(conv_in[block_len - edge_len :].astype(jnp.bfloat16), "seq", 1).astype(
            jnp.float32
        ),
        passed_along(
            doc_ids[block_len - edge_len :].astype(jnp.float32).astype(jnp.bfloat16), "seq", 1
        ).astype(jnp.float32),
    )
    conv_ext = jnp.concatenate([tail_in, conv_in], 0)
    docs_ext = jnp.concatenate([tail_doc.astype(jnp.int32), doc_ids], 0)
    conv_weight = jnp.concatenate([conv_x, conv_bc], -1)
    conv_shift = jnp.concatenate([convb_x, convb_bc], -1)
    conv_out = conv_apply(conv_ext, docs_ext, conv_weight, conv_shift)
    x_heads = conv_out[..., :inner_here].reshape(block_len, seq_here, heads_here, head_size)
    b_state = conv_out[..., inner_here : inner_here + state_size]
    c_state = conv_out[..., inner_here + state_size :]
    step_size = jax.nn.softplus(dt_pre)
    decay_rate = -jnp.exp(a_log)
    prev_doc = docs_ext[edge_len - 1]
    s_local, a_total = group_parts(x_heads, step_size, b_state, decay_rate, doc_ids, prev_doc)
    ones_start = jnp.ones_like(a_total)
    zeros_start = jnp.zeros_like(s_local)
    a_before, s_before = entering(
        (a_total, s_local), "seq", carry_combine, (ones_start, zeros_start), False
    )
    y_core = group_output(
        x_heads, step_size, b_state, c_state, decay_rate, doc_ids, prev_doc, s_before
    )
    y_heads = y_core + d_skip[:, None] * x_heads
    y_flat = y_heads.reshape(block_len, seq_here, inner_here)
    gate_sig = jax.nn.sigmoid(gate_z)
    gated = y_flat * gate_z * gate_sig
    square_sum = head_total(jnp.sum(gated * gated, axis=-1, keepdims=True))
    scale_gated = lax.rsqrt(square_sum / INNER + EPS)
    mixed_out = (gated * scale_gated * gnorm_gain).astype(jnp.bfloat16)
    residual = x_float + head_total(flat_dot(mixed_out, full_out))
    scale_two = lax.rsqrt(jnp.mean(residual * residual, axis=-1, keepdims=True) + EPS)
    normed_two = (residual * scale_two * norm2_gain).astype(jnp.bfloat16)
    logits = flat_dot(normed_two, full_router)
    gate_probs = jax.nn.softmax(jnp.take_along_axis(logits, routes, axis=-1), axis=-1)
    share_gate = flat_dot(normed_two, full_sgate)
    share_up = flat_dot(normed_two, full_sup)
    share_sig = jax.nn.sigmoid(share_gate)
    share_act = (share_gate * share_sig * share_up).astype(jnp.bfloat16)
    share_part = flat_dot(share_act, full_sdown)
    slot_total = tok_here * top_count
    route_flat = routes.reshape(slot_total)
    expert_ids = jnp.arange(experts_all, dtype=jnp.int32)
    route_hits = (route_flat[:, None] == expert_ids[None, :]).astype(jnp.int32)
    slot_rank = jnp.sum(jnp.cumsum(route_hits, axis=0) * route_hits, axis=1) - 1
    target = route_flat * capacity + slot_rank
    entry_table = (
        jnp.zeros((experts_all * capacity,), jnp.int32)
        .at[target]
        .set(jnp.arange(slot_total, dtype=jnp.int32) + 1)
    )
    entry_live = entry_table > 0
    entry_slot = jnp.maximum(entry_table - 1, 0)
    entry_token = entry_slot // top_count
    tokens_flat = normed_two.reshape(tok_here, width)
    send_rows = jnp.where(
        entry_live[:, None], tokens_flat[entry_token], jnp.zeros((), jnp.bfloat16)
    ).reshape(experts_all, capacity, width)
    received = lax.all_to_all(send_rows, "seq", split_axis=0, concat_axis=0, tiled=True)
    input_row_block = received.reshape(seq_count, local_experts, received.shape[1], width)
    hid_gate = jnp.einsum(
        "jecd,edf->jecf", input_row_block, expert_gate, preferred_element_type=jnp.float32
    )
    hid_up = jnp.einsum(
        "jecd,edf->jecf", input_row_block, expert_up, preferred_element_type=jnp.float32
    )
    hid_act = (hid_gate * jax.nn.sigmoid(hid_gate) * hid_up).astype(jnp.bfloat16)
    half_out = jnp.einsum(
        "jecf,efd->jecd", hid_act, expert_down, preferred_element_type=jnp.float32
    ).astype(jnp.bfloat16)
    returned_rows = lax.all_to_all(
        half_out.reshape(received.shape), "seq", split_axis=0, concat_axis=0, tiled=True
    )
    kept_shape = (seq_count * local_experts, received.shape[1], hid_gate.shape[-1])
    returned_rows, rows_kept, gate_kept, up_kept = (
        returned_rows,
        received,
        hid_gate.reshape(kept_shape),
        hid_up.reshape(kept_shape),
    )
    slot_rows = returned_rows.reshape(-1, width)[target].reshape(tok_here, top_count, width)
    probs_flat = gate_probs.reshape(tok_here, top_count)
    routed_part = share_part.reshape(tok_here, width)
    for slot_index in range(top_count):
        routed_part = routed_part + probs_flat[:, slot_index, None] * slot_rows[
            :, slot_index
        ].astype(jnp.float32)
    moe_out = head_total(routed_part.reshape(block_len, seq_here, width))
    block_out = residual + moe_out
    gathered = (
        lax.all_gather(w_z, "seq", axis=0, tiled=True),
        lax.all_gather(w_x, "seq", axis=0, tiled=True),
        lax.all_gather(w_dt, "seq", axis=0, tiled=True),
        lax.all_gather(w_bc, "seq", axis=0, tiled=True),
        lax.all_gather(router, "seq", axis=0, tiled=True),
        lax.all_gather(shared_gate, "seq", axis=0, tiled=True),
        lax.all_gather(shared_up, "seq", axis=0, tiled=True),
        lax.all_gather(w_out, "seq", axis=1, tiled=True),
        lax.all_gather(shared_down, "seq", axis=1, tiled=True),
    )
    full_z, full_x, full_dt, full_bc, full_router, full_sgate, full_sup, full_out, full_sdown = (
        gathered
    )
    grad_out = cotangent.astype(jnp.float32)
    grad_flat = grad_out.reshape(tok_here, width)
    entry_prob = jnp.where(entry_live, gate_probs.reshape(-1)[entry_slot], 0.0)
    send_grads = (
        (entry_prob[:, None] * grad_flat[entry_token])
        .astype(jnp.bfloat16)
        .reshape(experts_all, capacity, width)
    )
    recv_grads = lax.all_to_all(send_grads, "seq", split_axis=0, concat_axis=0, tiled=True)
    grads_in = recv_grads.reshape(seq_count, local_experts, capacity, width)
    input_row_block = rows_kept.reshape(seq_count, local_experts, capacity, width)
    hid_gate = gate_kept.reshape(seq_count, local_experts, capacity, -1)
    hid_up = up_kept.reshape(seq_count, local_experts, capacity, -1)
    hid_sig = jax.nn.sigmoid(hid_gate)
    hid_act = (hid_gate * hid_sig * hid_up).astype(jnp.bfloat16)
    d_act = jnp.einsum("jecd,efd->jecf", grads_in, expert_down, preferred_element_type=jnp.float32)
    hidden_up_gradient = (d_act * hid_gate * hid_sig).astype(jnp.bfloat16)
    d_hid_gate = (d_act * hid_up * silu_slope(hid_gate, hid_sig)).astype(jnp.bfloat16)
    grad_edown = jnp.einsum("jecf,jecd->efd", hid_act, grads_in, preferred_element_type=jnp.float32)
    grad_egate = jnp.einsum(
        "uqpy,uqpn->qyn", input_row_block, d_hid_gate, preferred_element_type=jnp.float32
    )
    expert_up_gradient = jnp.einsum(
        "uqpy,uqpn->qyn", input_row_block, hidden_up_gradient, preferred_element_type=jnp.float32
    )
    d_rows = jnp.einsum(
        "jecf,edf->jecd", d_hid_gate, expert_gate, preferred_element_type=jnp.float32
    )
    d_rows = (
        d_rows
        + jnp.einsum(
            "jecf,edf->jecd", hidden_up_gradient, expert_up, preferred_element_type=jnp.float32
        )
    ).astype(jnp.bfloat16)
    back_rows = lax.all_to_all(
        d_rows.reshape(recv_grads.shape), "seq", split_axis=0, concat_axis=0, tiled=True
    )
    d_share_act = flat_dot_t(cotangent, full_sdown)
    d_share_up = (d_share_act * share_gate * share_sig).astype(jnp.bfloat16)
    d_share_gate = (d_share_act * share_up * silu_slope(share_gate, share_sig)).astype(jnp.bfloat16)
    grad_sdown = outer_sum(share_act, cotangent)
    grad_sgate = outer_sum(normed_two, d_share_gate)
    grad_sup = outer_sum(normed_two, d_share_up)
    d_normed_two = (
        flat_dot_t(d_share_gate, full_sgate) + flat_dot_t(d_share_up, full_sup)
    ).reshape(tok_here, width)
    prob_grad = jnp.stack(
        [
            jnp.sum(grad_flat * slot_rows[:, slot_index].astype(jnp.float32), axis=-1)
            for slot_index in range(top_count)
        ],
        axis=-1,
    )
    back_slots = back_rows.reshape(-1, width)[target].reshape(tok_here, top_count, width)
    for slot_index in range(top_count):
        d_normed_two = d_normed_two + back_slots[:, slot_index].astype(jnp.float32)
    d_normed_two, prob_grad = head_total(
        (
            d_normed_two.reshape(block_len, seq_here, width),
            prob_grad.reshape(block_len, seq_here, top_count),
        )
    )
    d_chosen = gate_probs * (prob_grad - jnp.sum(gate_probs * prob_grad, axis=-1, keepdims=True))
    d_logits = jnp.sum(
        d_chosen[..., None] * (routes[..., None] == expert_ids).astype(jnp.float32), axis=-2
    ).astype(jnp.bfloat16)
    grad_router = outer_sum(normed_two, d_logits)
    d_normed_two = d_normed_two + flat_dot_t(d_logits, full_router)
    d_resid_norm, grad_norm2 = norm_back(d_normed_two, residual, scale_two, norm2_gain)
    d_resid = grad_out + d_resid_norm
    d_resid_low = d_resid.astype(jnp.bfloat16)
    d_mixed = flat_dot_t(d_resid_low, full_out)
    grad_out_w = outer_sum(mixed_out, d_resid_low)
    gain_scaled = d_mixed * gnorm_gain
    grad_gnorm = jnp.sum((d_mixed * gated * scale_gated).reshape(-1, inner_here), axis=0)
    cross_sum = head_total(jnp.sum(gain_scaled * gated, axis=-1, keepdims=True))
    d_gated = (
        scale_gated * gain_scaled
        - gated * scale_gated * scale_gated * scale_gated * cross_sum / INNER
    )
    d_y = d_gated * gate_z * gate_sig
    d_gate_z = (d_gated * y_flat * silu_slope(gate_z, gate_sig)).astype(jnp.bfloat16)
    d_y_heads = d_y.reshape(x_heads.shape)
    grad_skip = jnp.sum(d_y_heads * x_heads, axis=(0, 1, 3))
    log_decay = jnp.cumsum(step_size * decay_rate, axis=0)
    enters = jnp.exp(log_decay) * (doc_ids == prev_doc[None, :]).astype(jnp.float32)[..., None]
    g_local = jnp.einsum("tsh,tshp,tsn->shpn", enters, d_y_heads, c_state, precision=HIGH)
    a_after, state_grad = entering(
        (a_total, g_local), "seq", carry_combine, (ones_start, zeros_start), True
    )

    def local_scan(x_part, step_part, b_part, c_part, rate_part, state_part):
        return ssm_local(
            x_part, step_part, b_part, c_part, rate_part, state_part, doc_ids, prev_doc
        )

    _, scan_back = jax.vjp(local_scan, x_heads, step_size, b_state, c_state, decay_rate, s_before)
    d_xh, d_step, d_bstate, d_cstate, d_rate, _ = scan_back((d_y_heads, state_grad))
    d_xh = d_xh + d_skip[:, None] * d_y_heads
    d_bc = head_total(jnp.concatenate([d_bstate, d_cstate], axis=-1))
    d_dt_pre = d_step * jax.nn.sigmoid(dt_pre)
    grad_dtb = jnp.sum(d_dt_pre, axis=(0, 1))
    grad_alog = d_rate * decay_rate
    d_conv_out = jnp.concatenate([d_xh.reshape(block_len, seq_here, inner_here), d_bc], axis=-1)

    def local_conv(ext_part, weight_part, shift_part):
        return conv_apply(ext_part, docs_ext, weight_part, shift_part)

    _, conv_back = jax.vjp(local_conv, conv_ext, conv_weight, conv_shift)
    d_ext, grad_cweight, grad_cshift = conv_back(d_conv_out)
    from_next = passed_along(shortened(d_ext[:edge_len]), "seq", -1)
    d_conv_in = d_ext[edge_len:] + jnp.concatenate(
        [jnp.zeros((block_len - edge_len,) + from_next.shape[1:], jnp.float32), from_next], 0
    )
    d_proj_x = d_conv_in[..., :inner_here].astype(jnp.bfloat16)
    d_proj_bc = d_conv_in[..., inner_here:].astype(jnp.bfloat16)
    d_dt_low = d_dt_pre.astype(jnp.bfloat16)
    grad_wz = outer_sum(normed_one, d_gate_z)
    grad_wx = outer_sum(normed_one, d_proj_x)
    grad_wbc = outer_sum(normed_one, d_proj_bc)
    grad_wdt = outer_sum(normed_one, d_dt_low)
    head_first = jnp.where(lax.axis_index("head") == 0, 1.0, 0.0)
    d_normed_one = (
        flat_dot_t(d_gate_z, full_z) + flat_dot_t(d_proj_x, full_x) + flat_dot_t(d_dt_low, full_dt)
    )
    d_normed_one = head_total(d_normed_one + head_first * flat_dot_t(d_proj_bc, full_bc))
    d_x_norm, grad_norm1 = norm_back(d_normed_one, x_float, scale_one, norm1_gain)
    input_grad = d_resid + d_x_norm
    reduced = (
        lax.psum_scatter(grad_wz, "seq", scatter_dimension=0, tiled=True),
        lax.psum_scatter(grad_wx, "seq", scatter_dimension=0, tiled=True),
        lax.psum_scatter(grad_wdt, "seq", scatter_dimension=0, tiled=True),
        lax.psum_scatter(grad_wbc, "seq", scatter_dimension=0, tiled=True),
        lax.psum_scatter(grad_router, "seq", scatter_dimension=0, tiled=True),
        lax.psum_scatter(grad_sgate, "seq", scatter_dimension=0, tiled=True),
        lax.psum_scatter(grad_sup, "seq", scatter_dimension=0, tiled=True),
        lax.psum_scatter(grad_out_w, "seq", scatter_dimension=1, tiled=True),
        lax.psum_scatter(grad_sdown, "seq", scatter_dimension=1, tiled=True),
    )
    red_z, red_x, red_dt, red_bc, red_router, red_sgate, red_sup, red_out, red_sdown = reduced
    small_sums = lax.psum(
        (
            grad_norm1,
            grad_norm2,
            grad_cweight,
            grad_cshift,
            grad_dtb,
            grad_alog,
            grad_skip,
            grad_gnorm,
        ),
        "seq",
    )
    sum_norm1, sum_norm2, sum_cweight, sum_cshift, sum_dtb, sum_alog, sum_skip, sum_gnorm = (
        small_sums
    )
    return (
        block_out,
        input_grad,
        sum_norm1,
        red_z,
        red_x,
        red_bc,
        red_dt,
        sum_cweight[:, :inner_here],
        sum_cweight[:, inner_here:],
        sum_cshift[:inner_here],
        sum_cshift[inner_here:],
        sum_dtb,
        sum_alog,
        sum_skip,
        sum_gnorm,
        red_out,
        sum_norm2,
        red_router,
        red_sgate,
        red_sup,
        red_sdown,
        grad_egate,
        expert_up_gradient,
        grad_edown,
    )


MESH = pl.DeviceIdType.MESH
VMEM = pltpu.VMEM


def peers():
    here, side = lax.axis_index("seq"), lax.axis_index("head")
    x, y, z = lax.rem(here, 2), lax.rem(here // 2, 2), here // 4
    col = x + 2 * y
    return here, side, z, col, (1 - x) + 2 * y, x + 2 * (1 - y), 3 - col


def layers(z):
    lo, hi = lax.rem(z, 2), z // 2
    return [2 * (1 - hi if k & 2 else hi) + (1 - lo if k & 1 else lo) for k in range(4)]


def greet(devices):
    barrier = pltpu.get_barrier_semaphore()
    for device in devices:
        pl.semaphore_signal(barrier, inc=1, device_id=device, device_id_type=MESH)
    pl.semaphore_wait(barrier, len(devices))


class Mail:
    def __init__(self, send, base=0):
        self.send, self.sent, self.base = send, [], base

    def put(self, src, dst, sem, to):
        copy = pltpu.make_async_remote_copy(
            src_ref=src,
            dst_ref=dst,
            send_sem=self.send.at[self.base + len(self.sent)],
            recv_sem=sem,
            device_id=to,
            device_id_type=MESH,
        )
        copy.start()
        self.sent.append(copy)

    def arrived(self, dst, sem):
        pltpu.make_async_remote_copy(
            src_ref=dst,
            dst_ref=dst,
            send_sem=self.send.at[0],
            recv_sem=sem,
            device_id=(0, 0),
            device_id_type=MESH,
        ).wait_recv()

    def finish(self):
        for copy in self.sent:
            copy.wait_send()


def rows_at(ref, start, size, step):
    return ref.at[pl.ds(pl.multiple_of(start, step), size)]


def gather_steps(mail, own_ref, out_ref, recv, recv_half, rows, half=None):
    here, side, z, col, cx, cy, cd = peers()
    zs = layers(z)
    base = 4 * z
    to_x, to_y = (base + cx, side), (base + cy, side)

    def part(place, which, ref=None):
        if half is None:
            width = out_ref.shape[1] // 2
            lane = pl.ds(which * width, width)
            if ref is not None:
                return ref.at[:, lane]
            return out_ref.at[pl.ds(pl.multiple_of(place * rows, 16), rows), lane]
        size = rows - half if which else half
        if ref is not None:
            return ref.at[pl.ds(which * half, size)]
        return rows_at(out_ref, place * rows + which * half, size, 16)

    def onward(place, k, ref=None):
        for which in (0, 1):
            src = part(place, which, ref)
            mail.put(src, part(place, which), recv.at[6 + 4 * k + which], to_x)
            src = part(place, 1 - which, ref)
            mail.put(src, part(place, 1 - which), recv.at[8 + 4 * k + which], to_y)

    def across(k):
        at = 4 * zs[k] + cd
        mail.arrived(part(at, 0), recv_half.at[k])
        mail.arrived(part(at, 1), recv_half.at[4 + k])
        mail.arrived(part(4 * zs[k] + cx, 1), recv.at[7 + 4 * k])
        mail.arrived(part(4 * zs[k] + cy, 0), recv.at[9 + 4 * k])

    onward(here, 0, own_ref)
    for k in (1, 2, 3):
        for which in (0, 1):
            src = part(here, which, own_ref)
            sem = recv.at[2 * (k - 1) + which]
            mail.put(src, part(here, which), sem, (4 * zs[k] + col, side))
    yield
    for k in range(4):
        if k:
            at = 4 * zs[k] + col
            mail.arrived(part(at, 0), recv.at[2 * (k - 1)])
            mail.arrived(part(at, 1), recv.at[2 * (k - 1) + 1])
            onward(at, k)
            yield
        at = 4 * zs[k] + cx
        mail.arrived(part(at, 0), recv.at[6 + 4 * k])
        mail.put(part(at, 0), part(at, 0), recv_half.at[k], to_y)
        at = 4 * zs[k] + cy
        mail.arrived(part(at, 1), recv.at[8 + 4 * k])
        mail.put(part(at, 1), part(at, 1), recv_half.at[4 + k], to_x)
        yield
        if k:
            across(k - 1)
            yield
    across(3)
    yield


def near(side):
    here, side, z, col, cx, cy, cd = peers()
    zs = layers(z)
    return [(4 * z + cx, side), (4 * z + cy, side)] + [(4 * zs[k] + col, side) for k in (1, 2, 3)]


def note_puts(mail, src_of, notes_out, recv_n):
    here, side = peers()[:2]
    for k in range(1, 16):
        to = lax.rem(here + k, 16)
        mail.put(src_of(to), notes_out.at[here], recv_n.at[here], (to, side))


def note_waits(mail, notes_out, recv_n):
    here = peers()[0]
    for k in range(1, 16):
        place = lax.rem(here + k, 16)
        mail.arrived(notes_out.at[place], recv_n.at[place])


SUM_ORDER = (
    ("far", 3),
    ("far", 2),
    ("joined", 3),
    ("far", 1),
    ("joined", 2),
    ("column", 3),
    ("far", 0),
    ("joined", 1),
    ("column", 2),
    ("joined", 0),
    ("column", 1),
    ("column", 0),
)


def reduce_steps(mail, part_ref, out_ref, got, sums, recv, rows, order=SUM_ORDER):
    here, side, z, col, cx, cy, cd = peers()
    zs = layers(z)
    base = 4 * z
    half = rows // 2
    got_a, got_b, got_x, got_y, got_z = got
    sum_x, sum_y, sum_z = sums
    to_x, to_y = (base + cx, side), (base + cy, side)
    f32 = jnp.float32

    def half_of(place, which):
        return rows_at(part_ref, place * rows + which * half, half, half)

    def far(k):
        at = 4 * zs[k] + cd
        mail.put(half_of(at, 0), got_a.at[k], recv.at[k], to_y)
        mail.put(half_of(at, 1), got_b.at[k], recv.at[4 + k], to_x)

    def plain(k):
        mail.put(half_of(4 * zs[k] + cx, 1), got_x.at[k, pl.ds(half, half)], recv.at[12 + k], to_x)
        mail.put(half_of(4 * zs[k] + cy, 0), got_y.at[k, pl.ds(0, half)], recv.at[16 + k], to_y)

    def joined(k):
        mail.arrived(got_a.at[k], recv.at[k])
        total = half_of(4 * zs[k] + cx, 0)[...].astype(f32) + got_a[k].astype(f32)
        sum_x[k] = total.astype(sum_x.dtype)
        mail.put(sum_x.at[k], got_x.at[k, pl.ds(0, half)], recv.at[8 + k], to_x)
        mail.arrived(got_b.at[k], recv.at[4 + k])
        total = half_of(4 * zs[k] + cy, 1)[...].astype(f32) + got_b[k].astype(f32)
        sum_y[k] = total.astype(sum_y.dtype)
        mail.put(sum_y.at[k], got_y.at[k, pl.ds(half, half)], recv.at[20 + k], to_y)

    def column(k):
        mail.arrived(got_x.at[k, pl.ds(half, half)], recv.at[12 + k])
        mail.arrived(got_y.at[k, pl.ds(0, half)], recv.at[16 + k])
        mail.arrived(got_x.at[k, pl.ds(0, half)], recv.at[8 + k])
        mail.arrived(got_y.at[k, pl.ds(half, half)], recv.at[20 + k])
        own = part_ref[pl.ds(pl.multiple_of((4 * zs[k] + col) * rows, rows), rows)].astype(f32)
        total = own + got_x[k].astype(f32) + got_y[k].astype(f32)
        if k:
            sum_z[k - 1] = total.astype(sum_z.dtype)
            mail.put(sum_z.at[k - 1], got_z.at[k - 1], recv.at[23 + k], (4 * zs[k] + col, side))
        else:
            out_ref[...] = total

    for turn, k in order:
        if turn == "far":
            far(k)
            plain(k)
        elif turn == "joined":
            joined(k)
        else:
            column(k)
        yield
    for turn, k in order:
        if turn == "column" and k:
            mail.arrived(got_z.at[k - 1], recv.at[23 + k])
            out_ref[...] += got_z[k - 1].astype(f32)


def reduce_scratch(rows, width, kind):
    half = rows // 2
    shapes = [(4, half), (4, half), (4, rows), (4, rows), (3, rows), (4, half), (4, half), (3, rows)]
    return [VMEM(shape + (width,), kind) for shape in shapes]


def same_side(side, here):
    return [(lax.rem(here + k, 16), side) for k in range(1, 16)]


DMA = pltpu.SemaphoreType.DMA


def remote(src, dst, send, recv, to):
    return pltpu.make_async_remote_copy(
        src_ref=src,
        dst_ref=dst,
        send_sem=send,
        recv_sem=recv,
        device_id=to,
        device_id_type=MESH,
    )


def call(kernel, name, number, outs, scratch, args, spaces=None, limit=60):
    vmem = pl.BlockSpec(memory_space=VMEM)
    hbm = pl.BlockSpec(memory_space=pltpu.HBM)
    ins_far, outs_far = spaces or ((), ())
    args = [
        pltpu.with_memory_space_constraint(array, pltpu.HBM) if i in ins_far else array
        for i, array in enumerate(args)
    ]
    return pl.pallas_call(
        kernel,
        out_shape=tuple(
            pltpu.HBM(*out) if i in outs_far else jax.ShapeDtypeStruct(*out)
            for i, out in enumerate(outs)
        ),
        in_specs=[hbm if i in ins_far else vmem for i in range(len(args))],
        out_specs=tuple(hbm if i in outs_far else vmem for i in range(len(outs))),
        scratch_shapes=scratch,
        compiler_params=pltpu.CompilerParams(
            collective_id=number, has_side_effects=True, vmem_limit_bytes=limit << 20
        ),
        name=name,
    )(*args)


def of_side(ref, side):
    return jnp.where(side == 0, ref[:, 0], ref[:, 1])


def enter_kernel(
    hidden_far,
    cot_far,
    wbc_far,
    router_far,
    wdt_far,
    docs_far,
    routes_far,
    wo_far,
    sd_far,
    wz_far,
    sg_far,
    wx_far,
    su_far,
    convx_far,
    biasx_far,
    gnorm_far,
    bias_far,
    log_far,
    skip_far,
    norm1_far,
    norm2_far,
    convbc_far,
    biasbc_far,
    gate_ref,
    up_ref,
    down_ref,
    all_ref,
    extras_ref,
    extra_ref,
    cols_ref,
    own_ref,
    floats_ref,
    small_other,
    gate_other,
    up_other,
    down_other,
    n1_ref,
    mine_ref,
    misc_ref,
    blocks_ref,
    hidden_ref,
    cot_ref,
    wbc_ref,
    router_ref,
    wdt_ref,
    docs_ref,
    routes_ref,
    wo_ref,
    sd_ref,
    wz_ref,
    sg_ref,
    wx_ref,
    su_ref,
    convx_ref,
    biasx_ref,
    gnorm_ref,
    bias_ref,
    log_ref,
    skip_ref,
    norm1_ref,
    norm2_ref,
    convbc_ref,
    biasbc_ref,
    loaded,
    send,
    recv,
    recv_half,
    recv_m,
    recv_half_m,
    recv_w,
    recv_e,
    recv_s,
    local,
):
    here, side = peers()[:2]
    places = 16
    sibling = (here, 1 - side)
    far = (wz_far, sg_far, wx_far, su_far, wo_far, sd_far, convx_far, biasx_far, gnorm_far)
    far += (bias_far, log_far, skip_far, norm1_far, norm2_far, convbc_far, biasbc_far)
    far += (hidden_far, cot_far, wbc_far, router_far, wdt_far, docs_far, routes_far)
    close = (wz_ref, sg_ref, wx_ref, su_ref, wo_ref, sd_ref, convx_ref, biasx_ref, gnorm_ref)
    close += (bias_ref, log_ref, skip_ref, norm1_ref, norm2_ref, convbc_ref, biasbc_ref)
    close += (hidden_ref, cot_ref, wbc_ref, router_ref, wdt_ref, docs_ref, routes_ref)
    loads = [pltpu.make_async_copy(*both, loaded.at[i]) for i, both in enumerate(zip(far, close))]
    for load in loads[6:] + loads[:6]:
        load.start()
    floats_ref[...] = jnp.zeros(floats_ref.shape, jnp.float32)
    misc_ref[...] = jnp.zeros(misc_ref.shape, jnp.float32)
    for load in loads[6:]:
        load.wait()
    f32, low = jnp.float32, jnp.bfloat16
    own_ref[0:64] = of_side(hidden_ref, side)
    own_ref[64:128] = of_side(cot_ref, side)
    mine_ref[:, 0:128] = jnp.where(side == 0, wbc_ref[:, 0:128], wbc_ref[:, 128:256])
    misc_ref[0:16, 0:96] = router_ref[...].astype(f32)
    misc_ref[16:40, 0:96] = wdt_ref[...].astype(f32)
    misc_ref[40:41, 0:64] = jnp.where(side == 0, docs_ref[0:1], docs_ref[1:2]).astype(f32)
    misc_ref[41:47, 0:64] = jnp.where(side == 0, routes_ref[0], routes_ref[1]).astype(f32)
    mine_ref[:, 128:256] = misc_ref[...].T[0:96].astype(low)
    floats_ref[0:4] = convx_ref[...]
    floats_ref[4:5] = biasx_ref[...][None, :]
    floats_ref[5:6] = gnorm_ref[...][None, :]
    floats_ref[6:7, 0:24] = bias_ref[...][None, :]
    floats_ref[6:7, 24:48] = log_ref[...][None, :]
    floats_ref[6:7, 48:72] = skip_ref[...][None, :]
    floats_ref[7:8] = norm1_ref[...][None, :]
    floats_ref[8:9] = norm2_ref[...][None, :]
    floats_ref[9:13, 0:256] = convbc_ref[...]
    floats_ref[13:14, 0:256] = biasbc_ref[...][None, :]
    x = own_ref[0:64].astype(jnp.float32)
    scale = lax.rsqrt(jnp.mean(x * x, axis=-1, keepdims=True) + EPS)
    n1_ref[...] = (x * scale * floats_ref[7:8]).astype(jnp.bfloat16)
    greet(same_side(side, here) + [sibling])
    depth = blocks_ref.shape[1]
    rows, extra = n1_ref.shape[0], mine_ref.shape[0]
    half_here = here // 8
    mail = Mail(send)
    mine = pltpu.make_async_copy(n1_ref, rows_at(all_ref, here * rows, rows, 16), local.at[0])
    mine.start()
    mine_too = pltpu.make_async_copy(
        mine_ref, rows_at(extras_ref, here * extra, extra, 16), local.at[18]
    )
    mine_too.start()

    def strip(place):
        return cols_ref.at[pl.ds(pl.multiple_of(place * depth, 16), depth), pl.ds(0, 768)]

    steps = gather_steps(mail, n1_ref, all_ref, recv, recv_half, rows, rows // 2)
    steps_too = gather_steps(mail, mine_ref, extras_ref, recv_m, recv_half_m, extra)
    next(steps_too)
    next(steps)
    mail.put(floats_ref.at[pl.ds(0, 8)], small_other, recv_s.at[0], sibling)
    for load in loads[:6]:
        load.wait()
    for j in range(8):
        at = 0
        for width, ref in (
            (192, wz_ref),
            (64, sg_ref),
            (192, wx_ref),
            (64, su_ref),
            (192, wo_ref),
            (64, sd_ref),
        ):
            blocks_ref[j, :, at : at + width] = ref[:, width * j : width * (j + 1)]
            at += width
    first = 8 * side + lax.rem(here, 8)
    is_mine = side == half_here
    for k in range(1, 8):
        to = 8 * side + lax.rem(here + k, 8)
        mail.put(blocks_ref.at[to - 8 * side], strip(here), recv_w.at[here], (to, side))

    def keep():
        return pltpu.make_async_copy(blocks_ref.at[here - 8 * side], strip(here), local.at[1])

    def give():
        block = blocks_ref.at[first - 8 * side]
        return remote(block, strip(here), local.at[1], recv_w.at[here], (first, side))

    @pl.when(is_mine)
    def _():
        keep().start()

    @pl.when(jnp.logical_not(is_mine))
    def _():
        give().start()

    mail.put(gate_ref, gate_other, recv_s.at[1], sibling)
    mail.put(up_ref, up_other, recv_s.at[2], sibling)
    mail.put(down_ref, down_other, recv_s.at[3], sibling)
    for _ in steps_too:
        next(steps)
    for _ in steps:
        pass
    mine.wait()
    mine_too.wait()
    for place in range(places):
        at = pl.ds(place * extra, extra)
        mail.put(extras_ref.at[at], extra_ref.at[at], recv_e.at[place], sibling)

    def forward(place, k):
        return remote(strip(place), strip(place), local.at[2 + k], recv_w.at[place], sibling)

    @pl.when(is_mine)
    def _():
        keep().wait()
        forward(here, 0).start()

    @pl.when(jnp.logical_not(is_mine))
    def _():
        forward(here, 0).wait_recv()
        give().wait_send()

    for k in range(1, places):
        place = lax.rem(here + k, places)
        forward(place, k).wait_recv()

        @pl.when(is_mine)
        def _():
            forward(place, k).start()

    @pl.when(is_mine)
    def _():
        for k in range(places):
            forward(lax.rem(here + k, places), k).wait_send()

    mail.arrived(small_other, recv_s.at[0])
    mail.arrived(gate_other, recv_s.at[1])
    mail.arrived(up_other, recv_s.at[2])
    mail.arrived(down_other, recv_s.at[3])
    for place in range(places):
        mail.arrived(extra_ref.at[pl.ds(place * extra, extra)], recv_e.at[place])
    cols_ref[:, pl.ds(pl.multiple_of(768 + side * 128, 128), 128)] = extras_ref[:, 0:128]
    cols_ref[:, pl.ds(pl.multiple_of(896 - side * 128, 128), 128)] = extra_ref[:, 0:128]
    is_own = side == half_here
    cols_ref[:, 1024:1152] = jnp.where(is_own, extras_ref[:, 128:256], extra_ref[:, 128:256])
    mail.finish()


def enter(*args):
    low, f32 = jnp.bfloat16, jnp.float32
    return call(
        enter_kernel,
        "enter",
        1,
        (
            ((1024, 1536), low),
            ((1536, 256), low),
            ((1536, 256), low),
            ((1536, 1152), low),
            ((128, 1536), low),
            ((16, 1536), f32),
            ((8, 1536), f32),
            ((1536, 256), low),
            ((1536, 256), low),
            ((256, 1536), low),
        ),
        [
            VMEM((64, 1536), low),
            VMEM((96, 256), low),
            VMEM((128, 128), f32),
            VMEM((8, 96, 768), low),
        ]
        + [VMEM(array.shape, array.dtype) for array in args[:23]]
        + [
            DMA((23,)),
            DMA((87,)),
            DMA((22,)),
            DMA((8,)),
            DMA((22,)),
            DMA((8,)),
            DMA((16,)),
            DMA((16,)),
            DMA((4,)),
            DMA((19,)),
        ],
        args,
        (range(26), (7, 8, 9)),
        limit=12,
    )


def leave_kernel(
    main_ref,
    bcr_ref,
    small_ref,
    block_ref,
    input_ref,
    main_parts,
    bcr_out,
    small_all,
    block_other,
    input_other,
    got_main,
    got_bcr,
    bcr_part,
    bcr_mine,
    bcr_sib,
    small_got,
    small_sum,
    *refs,
):
    got, sums, refs = refs[:5], refs[5:8], refs[8:]
    send, recv_sib, recv_main, recv_small, recv_pair, cond, r_send, r_recv = refs
    here, side = peers()[:2]
    sibling = (here, 1 - side)
    is_main = side == here // 8
    f32 = jnp.float32
    greet(same_side(side, here) + [sibling])
    mail = Mail(send)
    mail.put(small_ref, small_got, recv_sib.at[1], sibling)

    def give_main():
        return remote(main_ref, got_main, cond.at[0], recv_sib.at[0], sibling)

    def send_on(total, out, sem, slot, k):
        to = lax.rem(here + k, 16)
        return remote(total.at[to], out.at[slot], cond.at[k], sem.at[slot], (to, side))

    slot = lax.rem(here, 8)

    half = bcr_ref.at[:, pl.ds(pl.multiple_of((1 - side) * 128, 128), 128)]
    mail.put(half, got_bcr, recv_sib.at[5], sibling)

    @pl.when(jnp.logical_not(is_main))
    def _():
        give_main().start()

    mail.put(block_ref, block_other, recv_sib.at[3], sibling)
    mail.put(input_ref, input_other, recv_sib.at[4], sibling)
    mail.arrived(small_got, recv_sib.at[1])
    small_sum[...] = small_ref[...] + small_got[...]
    small_all[side, here] = small_sum[side]
    for k in range(1, 16):
        to = lax.rem(here + k, 16)
        mail.put(small_sum.at[side], small_all.at[side, here], recv_small.at[here], (to, side))

    mail.arrived(got_bcr, recv_sib.at[5])
    mine = bcr_ref[:, pl.ds(pl.multiple_of(side * 128, 128), 128)]
    bcr_part[:, 0:128] = (mine.astype(f32) + got_bcr[...].astype(f32)).astype(bcr_part.dtype)
    bcr_part[:, 128:256] = bcr_ref[:, 256:384]
    r_mail = Mail(r_send)
    steps = reduce_steps(r_mail, bcr_part, bcr_mine, got, sums, r_recv, 96)
    next(steps)
    next(steps)

    @pl.when(is_main)
    def _():
        give_main().wait_recv()
        for k in range(1, 16):
            to = lax.rem(here + k, 16)
            total = main_ref[to].astype(f32) + got_main[to].astype(f32)
            got_main[to] = total.astype(got_main.dtype)
            send_on(got_main, main_parts, recv_main, slot, k).start()
        total = main_ref[here].astype(f32) + got_main[here].astype(f32)
        main_parts[slot] = total.astype(main_parts.dtype)

    for _ in steps:
        pass
    mail.put(bcr_mine, bcr_sib, recv_sib.at[2], sibling)
    for k in range(1, 16):
        place = lax.rem(here + k, 16)
        mail.arrived(small_all.at[side, place], recv_small.at[place])
    mail.put(small_all.at[side], small_all.at[side], recv_pair, sibling)
    mail.arrived(small_all.at[1 - side], recv_pair)
    for j in range(8):

        @pl.when(8 * side + j != here)
        def _():
            mail.arrived(main_parts.at[j], recv_main.at[j])

    mail.arrived(bcr_sib, recv_sib.at[2])
    bcr_out[:, pl.ds(pl.multiple_of(side * 128, 128), 128)] = bcr_mine[:, 0:128]
    bcr_out[:, pl.ds(pl.multiple_of((1 - side) * 128, 128), 128)] = bcr_sib[:, 0:128]
    bcr_out[:, 256:384] = bcr_mine[:, 128:256] + bcr_sib[:, 128:256]
    mail.arrived(block_other, recv_sib.at[3])
    mail.arrived(input_other, recv_sib.at[4])

    @pl.when(is_main)
    def _():
        for k in range(1, 16):
            send_on(got_main, main_parts, recv_main, slot, k).wait_send()

    @pl.when(jnp.logical_not(is_main))
    def _():
        give_main().wait_send()

    r_mail.finish()
    mail.finish()


def leave(*args):
    low, f32 = jnp.bfloat16, jnp.float32
    return call(
        leave_kernel,
        "leave",
        5,
        (
            ((8, 96, 768), low),
            ((96, 384), f32),
            ((2, 16, 8, 512), f32),
            ((64, 1536), f32),
            ((64, 1536), f32),
        ),
        [
            VMEM((16, 96, 768), low),
            VMEM((1536, 128), low),
            VMEM((1536, 256), low),
            VMEM((96, 256), f32),
            VMEM((96, 256), f32),
            VMEM((2, 8, 512), f32),
            VMEM((2, 8, 512), f32),
        ]
        + reduce_scratch(96, 256, low)
        + [
            DMA((21,)),
            DMA((6,)),
            DMA((8,)),
            DMA((16,)),
            DMA,
            DMA((16,)),
            DMA((27,)),
            DMA((27,)),
        ],
        args,
        limit=10,
    )


CHUNK = 128
LAYER = 256
HEADW = 64


def mm(left, right, low=True, exact=False):
    return mm_of(left, right, ((1,), (0,)), low, exact)


def mm_nt(left, right, low=True, exact=False):
    return mm_of(left, right, ((1,), (1,)), low, exact)


def mm_tn(left, right, low=True, exact=False):
    return mm_of(left, right, ((0,), (0,)), low, exact)


def mm_of(left, right, dims, low, exact):
    if exact:
        return lax.dot_general(
            left, right, (dims, ((), ())), precision=HIGH, preferred_element_type=jnp.float32
        )
    if low:
        left, right = left.astype(jnp.bfloat16), right.astype(jnp.bfloat16)
    return lax.dot_general(left, right, (dims, ((), ())), preferred_element_type=jnp.float32)


def lanes(shape):
    return lax.broadcasted_iota(jnp.int32, shape, 1)


def by_head(parts, rows):
    lane = lanes((rows, 3 * HEADW))
    return jnp.where(lane < HEADW, parts[0], jnp.where(lane < 2 * HEADW, parts[1], parts[2]))


def spread_heads(array):
    return by_head([array[:, h : h + 1] for h in range(3)], array.shape[0])


def soft_plus(values):
    return jnp.maximum(values, 0.0) + jnp.log1p(jnp.exp(-jnp.abs(values)))


def chunk_tables(step, log_rate, doc_col, doc_row):
    row = lax.broadcasted_iota(jnp.int32, (CHUNK, CHUNK), 0)
    col = lax.broadcasted_iota(jnp.int32, (CHUNK, CHUNK), 1)
    below = (row >= col).astype(jnp.float32)
    logs = mm(below, step * log_rate, exact=True)
    logs_t, step_t = logs.T, step.T
    pair = (row >= col) & (doc_col == doc_row)
    tables = [
        jnp.exp(jnp.where(pair, logs[:, h : h + 1] - logs_t[h : h + 1], -1e9)) for h in range(3)
    ]
    return logs, tables, [step_t[h : h + 1] for h in range(3)]


def as_column(row):
    return jnp.concatenate([row, jnp.zeros((CHUNK - 8, CHUNK), jnp.float32)], 0).T


def as_row(column):
    wide = jnp.broadcast_to(column, (64, CHUNK))
    return jnp.concatenate([wide, jnp.zeros((64, CHUNK), jnp.float32)], 0).T[0:8]


KEPT = dict(z=(0, 192), y=(256, 192), dt=(512, 128), ids=(640, 128), ext=(768, 448), state=(1280, 192))


class Part:
    def __init__(self, ref, lane, width, row=0, height=None):
        self.ref, self.lane, self.width, self.row = ref, lane, width, row
        self.height = ref.shape[0] if height is None else height

    def at_of(self, index):
        rows, cols = index if isinstance(index, tuple) else (index, slice(None))
        if rows is Ellipsis:
            rows = slice(None)
        if isinstance(rows, slice):
            stop = self.height if rows.stop is None else rows.stop
            rows = slice(self.row + (rows.start or 0), self.row + stop)
        stop = self.width if cols.stop is None else cols.stop
        return rows, slice(self.lane + (cols.start or 0), self.lane + stop)

    def __getitem__(self, index):
        return self.ref[self.at_of(index)]

    def __setitem__(self, index, value):
        self.ref[self.at_of(index)] = value


def kept_views(kept_ref):
    return [Part(kept_ref, *KEPT[name]) for name in ("z", "y", "dt", "ids", "ext", "state")]


def const_views(consts_ref):
    return [
        Part(consts_ref, 0, 448, 0, 8),
        Part(consts_ref, 0, 128, 8, 8),
        Part(consts_ref, 128, 192, 8, 8),
    ]


def mix_forward_kernel(
    n1_ref,
    extras_ref,
    cols_ref,
    floats_ref,
    small_other,
    own_ref,
    kept_far,
    g_all_ref,
    n2_ref,
    note_ref,
    res_ref,
    scale_ref,
    ids_out,
    consts_ref,
    part_ref,
    gained_ref,
    notes_ref,
    sum_ref,
    notes_out,
    kept_ref,
    kept_sem,
    *refs,
):
    z_ref, y_ref, dt_ref, ids_ref, ext_ref, state_ref = kept_views(kept_ref)
    taps_ref, head_ref, gain_ref = const_views(consts_ref)
    g_ref = own_ref.at[pl.ds(64, 64)]
    got, sums, refs = refs[:5], refs[5:8], refs[8:]
    send, recv, recv_n, g_send, g_recv, g_recv_half, local = refs
    here, side, z_at = peers()[:3]
    half_here, slot = here // 8, lax.rem(here, 8)
    greet(same_side(side, here))
    low, f32 = jnp.bfloat16, jnp.float32
    mine = pltpu.make_async_copy(g_ref, rows_at(g_all_ref, here * 64, 64, 16), local)
    mine.start()
    g_mail = Mail(g_send)
    g_steps = gather_steps(g_mail, g_ref, g_all_ref, g_recv, g_recv_half, 64, 32)
    next(g_steps)

    small = jnp.where(side == half_here, floats_ref[0:8], small_other[...])
    turned = pltpu.roll(small, lax.rem(1536 - 192 * slot, 1536), 1)
    taps_ref[0:5, 0:256] = floats_ref[9:14, 0:256]
    taps_ref[5:8] = jnp.zeros((3, 448), f32)
    taps_ref[0:5, 256:448] = turned[0:5, 0:192]
    gain_ref[...] = jnp.broadcast_to(turned[5:6, 0:192], (8, 192))
    numbers = pltpu.roll(small[:, 0:128], lax.rem(128 - 3 * slot, 128), 1)[6:7]
    used = lanes((1, 128)) < 3
    head_ref[0:1] = jnp.where(used, numbers, 0.0)
    head_ref[1:2] = jnp.where(used, -jnp.exp(pltpu.roll(numbers, 104, 1)), 0.0)
    head_ref[2:3] = jnp.where(used, pltpu.roll(numbers, 80, 1), 0.0)
    ids_ref[0:8] = jnp.full((8, 128), -1.0, f32)
    ids_ref[1032:1040] = jnp.full((8, 128), -2.0, f32)
    for p in range(16):
        ids_ref[8 + 64 * p : 72 + 64 * p] = extras_ref[96 * p : 96 * p + 64, 128:256].astype(f32)
    ids_out[...] = ids_ref[...]
    notes_ref[...] = jnp.zeros(notes_ref.shape, f32)
    ext_ref[0:8] = jnp.zeros((8, 448), f32)

    @pl.loop(0, 4)
    def _(i):
        at = pl.ds(pl.multiple_of(i * LAYER, LAYER), LAYER)
        shifted = pl.ds(pl.multiple_of(i * LAYER + 8, 8), LAYER)
        rows = n1_ref[at]
        z_ref[at] = mm(rows, cols_ref[:, 0:192])
        ext_ref[shifted, 0:256] = mm(rows, cols_ref[:, 768:1024])
        ext_ref[shifted, 256:448] = mm(rows, cols_ref[:, 256:448])
        dt_ref[at] = pltpu.roll(mm(rows, cols_ref[:, 1024:1152]), 112 - 3 * slot, 1) + head_ref[0:1]

    next(g_steps)
    rate, skip = head_ref[1:2], spread_heads(head_ref[2:3])
    state = jnp.zeros((128, 192), f32)
    ones = jnp.ones((8, 192), f32)
    for c in range(8):
        r = c * CHUNK
        at = pl.ds(r, CHUNK)
        ids = ids_ref[pl.ds(r + 8, CHUNK)]
        doc = ids[:, 40:41]
        pre = conv_pre(taps_ref, ext_ref, ids_ref, r, doc)
        act = pre * jax.nn.sigmoid(pre)
        b, cc, x = act[:, 0:128], act[:, 128:256], act[:, 256:448]
        step = soft_plus(dt_ref[at])
        logs, tables, step_t = chunk_tables(step, rate, doc, ids.T[40:41])
        cross = mm_nt(cc, b)
        stacked = jnp.concatenate([cross * tables[h] * step_t[h] for h in range(3)], 0)
        intra = mm(stacked, x)
        y = by_head([intra[h * CHUNK : (h + 1) * CHUNK] for h in range(3)], CHUNK)
        first, last = chunk_masks(ids_ref, r, doc)
        enters = jnp.exp(logs) * first
        state_ref[at] = state
        y = y + spread_heads(enters) * mm(cc, state) + skip * x
        y_ref[at] = y
        tail = jnp.exp(logs[CHUNK - 1 :] - logs) * last * step
        state = spread_heads(enters[CHUNK - 1 :]) * state + mm_tn(b, spread_heads(tail) * x)
        z = z_ref[at]
        gated = y * z * jax.nn.sigmoid(z)
        gained_ref[at] = (gated * gain_ref[0:1]).astype(low)
        squares = mm_nt(ones, gated * gated, exact=True)
        notes_ref[2 * c, :, 0:64] = squares[:, 0:64]
        notes_ref[2 * c + 1, :, 0:64] = squares[:, 64:128]
        next(g_steps, None)

    keep = pltpu.make_async_copy(kept_ref, kept_far, kept_sem)
    keep.start()
    mail = Mail(send)
    zs = layers(z_at)

    def layer(k):
        at = pl.ds(pl.multiple_of(zs[k] * LAYER, LAYER), LAYER)

        @pl.loop(0, 6)
        def _(i):
            n = pl.ds(pl.multiple_of(i * 256, 256), 256)
            part_ref[at, n] = mm_nt(gained_ref[at], cols_ref[n, 512:704]).astype(low)

    steps = reduce_steps(mail, part_ref, sum_ref, got, sums, recv, 64)
    left = [3, 2, 1, 0]
    for turn in range(13):
        if turn in (0, 1, 3, 6):
            layer(left.pop(0))
        next(steps, None)
        if turn == 0:
            notes_out[here] = notes_ref[here]
            note_puts(mail, lambda to: notes_ref.at[to], notes_out, recv_n)
        if turn > 2:
            next(g_steps, None)
    for _ in g_steps:
        pass
    for _ in steps:
        pass
    note_waits(mail, notes_out, recv_n)
    squares = notes_out[0]
    for j in range(1, 16):
        squares = squares + notes_out[j]
    scale_row = lax.rsqrt(squares / INNER + EPS)
    note_ref[...] = scale_row
    scale = as_column(scale_row)[0:64, 0:1]
    scale_ref[...] = jnp.broadcast_to(scale, (64, 128))
    projected = scale * sum_ref[...]
    res_ref[64:128] = projected
    residual = own_ref[0:64].astype(f32) + projected
    res_ref[0:64] = residual
    scale_two = lax.rsqrt(jnp.mean(residual * residual, axis=-1, keepdims=True) + EPS)
    n2_ref[...] = (residual * scale_two * floats_ref[8:9]).astype(low)
    keep.wait()
    mine.wait()
    g_mail.finish()
    mail.finish()


def conv_pre(taps_ref, ext_ref, ids_ref, r, doc):
    pre = taps_ref[4:5] + taps_ref[3:4] * ext_ref[pl.ds(r + 8, CHUNK)]
    for k in (1, 2, 3):
        same = (ids_ref[pl.ds(r + 8 - k, CHUNK), 40:41] == doc).astype(jnp.float32)
        pre = pre + taps_ref[3 - k : 4 - k] * ext_ref[pl.ds(r + 8 - k, CHUNK)] * same
    return pre


def chunk_masks(ids_ref, r, doc):
    first = (ids_ref[r + 7 : r + 8, 40:41] == doc).astype(jnp.float32)
    last = (ids_ref[r + 7 + CHUNK : r + 8 + CHUNK, 40:41] == doc).astype(jnp.float32)
    return first, last


def mix_forward(*args):
    low, f32 = jnp.bfloat16, jnp.float32
    return call(
        mix_forward_kernel,
        "mix_forward",
        2,
        (
            ((1040, 1536), f32),
            ((1024, 1536), low),
            ((64, 1536), low),
            ((8, 128), f32),
            ((128, 1536), f32),
            ((64, 128), f32),
            ((1040, 128), f32),
            ((16, 512), f32),
        ),
        [
            VMEM((1024, 1536), low),
            VMEM((1024, 192), low),
            VMEM((16, 8, 128), f32),
            VMEM((64, 1536), f32),
            VMEM((16, 8, 128), f32),
            VMEM((1040, 1536), f32),
            DMA,
        ]
        + reduce_scratch(64, 1536, low)
        + [
            DMA((42,)),
            DMA((27,)),
            DMA((16,)),
            DMA((30,)),
            DMA((22,)),
            DMA((8,)),
            DMA,
        ],
        args,
        ((), (0,)),
        limit=24,
    )


def moe_kernel(
    own_ref,
    scale_note_ref,
    g_ref,
    cols_ref,
    eg_ref,
    ego_ref,
    eu_ref,
    euo_ref,
    ed_ref,
    edo_ref,
    extras_ref,
    ids_ref,
    res_ref,
    scale_ref,
    floats_ref,
    mine_ref,
    dres_ref,
    pair_ref,
    moe_ref,
    geg_far,
    geu_far,
    ged_far,
    sg_ref,
    su_ref,
    sd_ref,
    shared_ref,
    dres_own_ref,
    n2_ref,
    act_ref,
    hid_ref,
    probs_ref,
    notes_ref,
    notes_out,
    sum_ref,
    low_ref,
    note_ref,
    og_ref,
    ou_ref,
    od_ref,
    geg_ref,
    geu_ref,
    ged_ref,
    *refs,
):
    got, sums, refs = refs[:5], refs[5:8], refs[8:]
    send, recv, recv_n, d_send, d_recv, d_recv_half, d_recv_n = refs[:7]
    n_send, n_recv, n_recv_half, n_recv_n, e_send, e_recv, local = refs[7:]
    cross_ref, scales_ref = pair_ref.at[0], pair_ref.at[1]
    here, side, z_at = peers()[:3]
    sibling = (here, 1 - side)
    greet(same_side(side, here) + [sibling])
    low, f32 = jnp.bfloat16, jnp.float32
    zs = layers(z_at)
    ones = jnp.ones((8, 256), f32)
    spare = lanes((LAYER, 128)) >= 64
    lane = lanes((LAYER, 128))
    keep = pltpu.make_async_copy(own_ref, rows_at(n2_ref, here * 64, 64, 16), local.at[1])
    keep.start()
    n_mail = Mail(n_send)
    n_steps = gather_steps(n_mail, own_ref, n2_ref, n_recv, n_recv_half, 64, 32)
    next(n_steps)
    scales_ref[here] = scale_note_ref[...]
    note_puts(n_mail, lambda to: scale_note_ref, scales_ref, n_recv_n)
    notes_ref[...] = jnp.zeros(notes_ref.shape, f32)
    pieces = (
        (eg_ref, eu_ref, ed_ref, 0, 256),
        (ego_ref, euo_ref, edo_ref, 256, 256),
    )

    def layer(k, piece):
        start = pl.multiple_of(zs[k] * LAYER, LAYER)
        at = pl.ds(start, LAYER)
        rows, grads = n2_ref[at], g_ref[at]
        if piece == 0:
            logits = mm(rows, extras_ref[:, 128:256])
            ids = ids_ref[pl.ds(pl.multiple_of(start + 8, 8), LAYER)]
            named = jnp.zeros((LAYER, 128), f32)
            for j in range(6):
                named = jnp.where(lane.astype(f32) == ids[:, 41 + j : 42 + j], 1.0, named)
            top = jnp.max(jnp.where(named > 0, logits, -1e30), axis=-1, keepdims=True)
            raised = jnp.exp(jnp.where(named > 0, logits - top, 0.0)) * named
            probs_ref[at] = raised / jnp.sum(raised, axis=-1, keepdims=True)
        if piece < 2:
            chosen = jnp.where(lane == here, probs_ref[at], 0.0)
            prob = jnp.sum(chosen, axis=-1, keepdims=True)
            gate_w, up_w, down_w, first, size = pieces[piece]
            gate = mm(rows, gate_w[...])
            up = mm(rows, up_w[...])
            d_act = mm_nt(grads, down_w[...])
            sig = jax.nn.sigmoid(gate)
            act = gate * sig * up
            act_ref[at, first : first + size] = (act * prob).astype(low)
            slopes = mm_nt(ones, act * d_act, exact=True)
            d_act = d_act * prob
            hid_ref[at, first : first + size] = (d_act * up * silu_slope(gate, sig)).astype(low)
            hid_ref[at, 640 + first : 640 + first + size] = (d_act * gate * sig).astype(low)
            for j in range(4):
                part = slopes[:, 64 * j : 64 * (j + 1)]
                if piece:
                    part = part + notes_ref[4 * zs[k] + j, :, 0:64]
                notes_ref[4 * zs[k] + j, :, 0:64] = part
            return
        gate = mm(rows, cols_ref[:, 128:256])
        up = mm(rows, cols_ref[:, 384:512])
        d_act = jnp.where(spare, mm(grads, cols_ref[:, 640:768]), 0.0)
        sig = jax.nn.sigmoid(gate)
        act_ref[at, 512:640] = jnp.where(spare, gate * sig * up, 0.0).astype(low)
        hid_ref[at, 512:640] = (d_act * up * silu_slope(gate, sig)).astype(low)
        hid_ref[at, 1152:1280] = (d_act * gate * sig).astype(low)

    def layer_back(k):
        at = pl.ds(pl.multiple_of(zs[k] * LAYER, LAYER), LAYER)

        @pl.loop(0, 6)
        def _(i):
            n = pl.ds(pl.multiple_of(i * 256, 256), 256)
            total = mm_nt(hid_ref[at, 0:256], eg_ref[n])
            total = total + mm_nt(hid_ref[at, 256:512], ego_ref[n])
            total = total + mm_nt(hid_ref[at, 512:640], cols_ref[n, 128:256])
            total = total + mm_nt(hid_ref[at, 640:896], eu_ref[n])
            total = total + mm_nt(hid_ref[at, 896:1152], euo_ref[n])
            total = total + mm_nt(hid_ref[at, 1152:1280], cols_ref[n, 384:512])
            moe_ref[at, n] = total.astype(low)

    e_mail = Mail(e_send)

    def up_grads(first, last):
        @pl.loop(first, last)
        def _(i):
            n = pl.ds(pl.multiple_of(i * 256, 256), 256)
            total = mm_tn(n2_ref[:, n], hid_ref[...])
            geg_ref[n] = total[:, 0:256]
            og_ref[n] = total[:, 256:512].astype(low)
            shared_ref[n, 0:128] = total[:, 512:640].astype(low)
            geu_ref[n] = total[:, 640:896]
            ou_ref[n] = total[:, 896:1152].astype(low)
            shared_ref[n, 128:256] = total[:, 1152:1280].astype(low)

    def give_up():
        e_mail.put(og_ref, sg_ref, e_recv.at[0], sibling)
        e_mail.put(ou_ref, su_ref, e_recv.at[1], sibling)

    def down_grads():
        od_ref[...] = mm_tn(act_ref[:, 256:512], g_ref[...]).astype(low)
        e_mail.put(od_ref, sd_ref, e_recv.at[2], sibling)
        ged_ref[...] = mm_tn(act_ref[:, 0:256], g_ref[...])

    def shared_down():
        @pl.loop(0, 6)
        def _(i):
            n = pl.ds(pl.multiple_of(i * 256, 256), 256)
            shared_ref[n, 256:384] = mm_tn(g_ref[:, n], act_ref[:, 512:640]).astype(low)

    def moe_part(first, last):
        @pl.loop(first, last)
        def _(i):
            at = pl.ds(pl.multiple_of(i * LAYER, LAYER), LAYER)
            total = mm(act_ref[at, 0:256], ed_ref[...]) + mm(act_ref[at, 256:512], edo_ref[...])
            total = total + mm_nt(act_ref[at, 512:640], cols_ref[:, 640:768])
            moe_ref[at] = total.astype(low)

    mail = Mail(send)
    order = [("far", 0), ("far", 1), ("joined", 0), ("far", 2), ("joined", 1), ("column", 0)]
    order += [("far", 3), ("joined", 2), ("column", 1), ("joined", 3), ("column", 2), ("column", 3)]
    steps = reduce_steps(mail, moe_ref, sum_ref, got, sums, recv, 64, order)

    for _ in range(4):
        next(n_steps)
    keep.wait()
    for j in range(4):
        layer(j, 0)
        next(n_steps, None)
        layer(j, 1)
        next(n_steps, None)
        layer(j, 2)
        layer_back(j)
        next(n_steps, None)
        for _ in range((1, 2, 3, 1)[j]):
            next(steps)
    notes_out[here] = notes_ref[here]
    note_puts(mail, lambda to: notes_ref.at[to], notes_out, recv_n)
    for j in range(3):
        next(steps)
        up_grads(2 * j, 2 * j + 2)
    give_up()
    next(steps)
    down_grads()
    for _ in steps:
        pass
    note_waits(mail, notes_out, recv_n)

    slopes = jnp.concatenate([notes_out[j, 0:1] for j in range(16)], 0)
    slopes = jnp.concatenate([slopes, jnp.zeros((112, 128), f32)], 0).T[0:64]
    own = pl.ds(pl.multiple_of(here * 64, 64), 64)
    probs = probs_ref[own]
    d_logits = probs * (slopes - jnp.sum(probs * slopes, axis=-1, keepdims=True))
    d_logits = d_logits.astype(low)
    shared_ref[:, 384:512] = mm_tn(n2_ref[own], d_logits).astype(low)
    dn2 = sum_ref[...] + mm_nt(d_logits, extras_ref[:, 128:256])
    value, gain = norm_step(dn2, res_ref[0:64], floats_ref[8:9])
    dres_own_ref[64:72] = jnp.broadcast_to(gain, (8, 1536))
    d_res = mine_ref[64:128].astype(f32) + value
    dres_own_ref[0:64] = d_res
    low_ref[...] = d_res.astype(low)
    cross = jnp.sum(low_ref[...].astype(f32) * res_ref[64:128], axis=-1, keepdims=True)
    note_ref[...] = as_row(cross / scale_ref[:, 0:1])
    mine = pltpu.make_async_copy(low_ref, rows_at(dres_ref, here * 64, 64, 16), local.at[0])
    mine.start()
    d_mail = Mail(d_send)
    d_steps = gather_steps(d_mail, low_ref, dres_ref, d_recv, d_recv_half, 64, 32)
    next(d_steps)
    cross_ref[here] = note_ref[...]
    note_puts(d_mail, lambda to: note_ref, cross_ref, d_recv_n)
    next(d_steps)
    stores = [
        pltpu.make_async_copy(geg_ref, geg_far, local.at[2]),
        pltpu.make_async_copy(geu_ref, geu_far, local.at[3]),
        pltpu.make_async_copy(ged_ref, ged_far, local.at[4]),
    ]
    for store in stores:
        store.start()
    shared_down()
    mail.finish()
    for i in range(4):
        next(d_steps)
        moe_part(i, i + 1)
    for _ in d_steps:
        pass
    e_mail.arrived(sg_ref, e_recv.at[0])
    e_mail.arrived(su_ref, e_recv.at[1])
    e_mail.arrived(sd_ref, e_recv.at[2])
    note_waits(n_mail, scales_ref, n_recv_n)
    note_waits(d_mail, cross_ref, d_recv_n)
    mine.wait()
    for store in stores:
        store.wait()
    n_mail.finish()
    e_mail.finish()
    d_mail.finish()


def norm_step(grad, values, gain):
    scale = lax.rsqrt(jnp.mean(values * values, axis=-1, keepdims=True) + EPS)
    gain_grad = jnp.sum(grad * values * scale, axis=0, keepdims=True)
    scaled = grad * gain
    pull = scale * scale * scale * jnp.mean(scaled * values, axis=-1, keepdims=True)
    return scale * scaled - values * pull, gain_grad


def moe(*args):
    low, f32 = jnp.bfloat16, jnp.float32
    return call(
        moe_kernel,
        "moe",
        3,
        (
            ((1024, 1536), low),
            ((2, 16, 8, 128), f32),
            ((1024, 1536), low),
            ((1536, 256), f32),
            ((1536, 256), f32),
            ((256, 1536), f32),
            ((1536, 256), low),
            ((1536, 256), low),
            ((256, 1536), low),
            ((1536, 512), low),
            ((72, 1536), f32),
        ),
        [
            VMEM((1024, 1536), low),
            VMEM((1024, 640), low),
            VMEM((1024, 1280), low),
            VMEM((1024, 128), f32),
            VMEM((16, 8, 128), f32),
            VMEM((16, 8, 128), f32),
            VMEM((64, 1536), f32),
            VMEM((64, 1536), low),
            VMEM((8, 128), f32),
            VMEM((1536, 256), low),
            VMEM((1536, 256), low),
            VMEM((256, 1536), low),
            VMEM((1536, 256), f32),
            VMEM((1536, 256), f32),
            VMEM((256, 1536), f32),
        ]
        + reduce_scratch(64, 1536, low)
        + [
            DMA((42,)),
            DMA((27,)),
            DMA((16,)),
            DMA((45,)),
            DMA((22,)),
            DMA((8,)),
            DMA((16,)),
            DMA((45,)),
            DMA((22,)),
            DMA((8,)),
            DMA((16,)),
            DMA((3,)),
            DMA((3,)),
            DMA((5,)),
        ],
        args,
        ((), (3, 4, 5, 6, 7, 8)),
        limit=27,
    )


def mix_backward_kernel(
    dres_ref,
    pair_ref,
    n1_far,
    cols_ref,
    consts_ref,
    kept_far,
    moe_ref,
    shared_ref,
    res_ref,
    dres_own_ref,
    own_ref,
    floats_ref,
    main_ref,
    bcr_ref,
    small_ref,
    block_ref,
    input_ref,
    part_ref,
    dm_ref,
    mixed_ref,
    din_ref,
    dpre_ref,
    sum_ref,
    n1_ref,
    kept_ref,
    loaded,
    *refs,
):
    got, sums, refs = refs[:5], refs[5:8], refs[8:]
    b_got, b_sums, refs = refs[:5], refs[5:8], refs[8:]
    send, recv, b_send, b_recv = refs
    loads = (
        pltpu.make_async_copy(kept_far, kept_ref, loaded.at[0]),
        pltpu.make_async_copy(n1_far, n1_ref, loaded.at[1]),
    )
    for load in loads:
        load.start()
    z_ref, y_ref, dt_ref, ids_ref, ext_ref, state_ref = kept_views(kept_ref)
    taps_ref, head_ref, gain_ref = const_views(consts_ref)
    cross_ref, scales_ref = pair_ref.at[0], pair_ref.at[1]
    here, side, z_at = peers()[:3]
    half_here, slot = here // 8, lax.rem(here, 8)
    greet(near(side))
    low, f32 = jnp.bfloat16, jnp.float32
    zs = layers(z_at)
    b_mail = Mail(b_send)
    b_steps = reduce_steps(b_mail, moe_ref, block_ref, b_got, b_sums, b_recv, 64)
    next(b_steps)

    @pl.loop(0, 4)
    def _(i):
        at = pl.ds(pl.multiple_of(i * LAYER, LAYER), LAYER)
        dm_ref[at] = mm(dres_ref[at], cols_ref[:, 512:704])

    next(b_steps)
    loads[0].wait()
    rate, skip = head_ref[1:2], spread_heads(head_ref[2:3])
    onehot = (
        lax.broadcasted_iota(jnp.int32, (192, 128), 0) // HEADW
        == lax.broadcasted_iota(jnp.int32, (192, 128), 1)
    ).astype(f32)
    row = lax.broadcasted_iota(jnp.int32, (CHUNK, CHUNK), 0)
    lane = lanes((CHUNK, CHUNK))
    above = (row <= lane).astype(f32)
    lane192 = lanes((CHUNK, 192))
    masks = [((lane192 // HEADW) == h).astype(f32) for h in range(3)]
    d_state = jnp.zeros((128, 192), f32)
    g_gain = jnp.zeros((1, 192), f32)
    g_skip = jnp.zeros((1, 192), f32)
    g_rate = jnp.zeros((1, 128), f32)
    g_dt = jnp.zeros((1, 128), f32)
    g_taps = [jnp.zeros((1, 448), f32) for _ in range(5)]
    dpre_ref[0:8] = jnp.zeros((8, 448), f32)
    din_ref[:, 128:256] = jnp.zeros((1024, 128), low)
    din_ref[:, 384:512] = jnp.zeros((1024, 128), low)
    mixed_ref[:, 128:256] = jnp.zeros((1024, 128), low)
    for c in range(7, -1, -1):
        r = c * CHUNK
        at = pl.ds(r, CHUNK)
        ids = ids_ref[pl.ds(r + 8, CHUNK)]
        doc = ids[:, 40:41]
        scale_row = jnp.concatenate(
            [scales_ref[2 * c, :, 0:64], scales_ref[2 * c + 1, :, 0:64]], 1
        )
        cross_row = jnp.concatenate([cross_ref[2 * c, :, 0:64], cross_ref[2 * c + 1, :, 0:64]], 1)
        scale = as_column(scale_row)[:, 0:1]
        pull = scale * scale * scale * as_column(cross_row)[:, 0:1] / INNER
        z, y, dm, gain = z_ref[at], y_ref[at], dm_ref[at], gain_ref[0:1]
        sig = jax.nn.sigmoid(z)
        gated = y * z * sig
        scaled = gated * scale
        mixed_ref[at, 0:192] = (scaled * gain).astype(low)
        g_gain = g_gain + jnp.sum(dm * scaled, axis=0, keepdims=True)
        d_gated = scale * gain * dm - gated * pull
        d_y = d_gated * z * sig
        din_ref[at, 0:192] = (d_gated * y * silu_slope(z, sig)).astype(low)
        pre = conv_pre(taps_ref, ext_ref, ids_ref, r, doc)
        pre_sig = jax.nn.sigmoid(pre)
        act = pre * pre_sig
        b, cc, x = act[:, 0:128], act[:, 128:256], act[:, 256:448]
        g_skip = g_skip + jnp.sum(d_y * x, axis=0, keepdims=True)
        dt = dt_ref[at]
        step = soft_plus(dt)
        logs, tables, step_t = chunk_tables(step, rate, doc, ids.T[40:41])
        cross = mm_nt(cc, b)
        decays = [tables[h] * step_t[h] for h in range(3)]
        stacked = jnp.concatenate([cross * decays[h] for h in range(3)], 0)
        d_ys = jnp.concatenate([d_y * masks[h] for h in range(3)], 0)
        d_stack = mm_nt(d_ys, x)
        d_x = skip * d_y + mm_tn(stacked, d_ys)
        state = state_ref[at]
        first, last = chunk_masks(ids_ref, r, doc)
        enters = jnp.exp(logs) * first
        d_in_y = spread_heads(enters) * d_y
        from_state = mm(cc, state)
        tail_w = jnp.exp(logs[CHUNK - 1 :] - logs) * last
        tail = tail_w * step
        tail_x = spread_heads(tail)
        to_state = mm(b, d_state)
        d_x = d_x + tail_x * to_state
        kept = enters[CHUNK - 1 :]
        d_kept = jnp.sum(d_state * state, axis=0, keepdims=True)
        folded = mm(
            jnp.concatenate(
                [d_y * from_state, x * to_state, jnp.broadcast_to(d_kept, (8, 192))], 0
            ),
            onehot,
            exact=True,
        )
        d_enters, d_tail = folded[:CHUNK], folded[CHUNK : 2 * CHUNK]
        d_kept = folded[2 * CHUNK : 2 * CHUNK + 1]
        d_cross = jnp.zeros((CHUNK, CHUNK), f32)
        row_sums = jnp.zeros((CHUNK, CHUNK), f32)
        col_sums = []
        for h in range(3):
            d_a = d_stack[h * CHUNK : (h + 1) * CHUNK]
            d_cross = d_cross + d_a * decays[h]
            plain = d_a * cross * tables[h]
            col_sums.append(jnp.sum(plain, axis=0, keepdims=True))
            total = jnp.sum(plain * step_t[h], axis=1, keepdims=True)
            row_sums = jnp.where(lane == h, total, row_sums)
        col_sums = as_column(jnp.concatenate(col_sums + [jnp.zeros((5, CHUNK), f32)], 0))
        d_c = mm(d_cross, b) + mm_nt(d_in_y, state)
        d_b = mm_tn(d_cross, cc) + mm_nt(tail_x * x, d_state)
        pulled = d_tail * tail
        d_logs = row_sums - step * col_sums + d_enters * enters - pulled
        d_last = jnp.sum(pulled, axis=0, keepdims=True) + d_kept * kept
        d_logs = d_logs + jnp.where(row == CHUNK - 1, d_last, 0.0)
        d_l = mm(above, d_logs, exact=True)
        d_step = col_sums + d_tail * tail_w + d_l * rate
        g_rate = g_rate + jnp.sum(d_l * step, axis=0, keepdims=True)
        d_dt = jnp.where(lane < 3, d_step * jax.nn.sigmoid(dt), 0.0)
        g_dt = g_dt + jnp.sum(d_dt, axis=0, keepdims=True)
        din_ref[at, 768:896] = pltpu.roll(d_dt, 16 + 3 * slot, 1).astype(low)
        d_state = spread_heads(kept) * d_state + mm_tn(cc, d_in_y)
        d_pre = jnp.concatenate([d_b, d_c, d_x], 1) * silu_slope(pre, pre_sig)
        dpre_ref[CHUNK : CHUNK + 8] = dpre_ref[0:8]
        dpre_ref[0:CHUNK] = d_pre
        g_taps[4] = g_taps[4] + jnp.sum(d_pre, axis=0, keepdims=True)
        g_taps[3] = g_taps[3] + jnp.sum(d_pre * ext_ref[pl.ds(r + 8, CHUNK)], axis=0, keepdims=True)
        d_ext = taps_ref[3:4] * d_pre
        for k in (1, 2, 3):
            same = (ids_ref[pl.ds(r + 8 - k, CHUNK), 40:41] == doc).astype(f32)
            g_taps[3 - k] = g_taps[3 - k] + jnp.sum(
                d_pre * same * ext_ref[pl.ds(r + 8 - k, CHUNK)], axis=0, keepdims=True
            )
            same = (ids_ref[pl.ds(r + 8 + k, CHUNK), 40:41] == doc).astype(f32)
            d_ext = d_ext + taps_ref[3 - k : 4 - k] * (dpre_ref[k : k + CHUNK] * same)
        din_ref[at, 512:768] = d_ext[:, 0:256].astype(low)
        din_ref[at, 256:448] = d_ext[:, 256:448].astype(low)
        next(b_steps, None)
    loads[1].wait()
    small_ref[...] = jnp.zeros((2, 8, 512), f32)
    for k in range(5):
        small_ref[1, k : k + 1, 0:448] = g_taps[k]
    small_ref[1, 5:6, 0:192] = g_gain
    small_ref[1, 5:6, 256:448] = g_skip
    small_ref[1, 6:7, 0:128] = g_dt
    small_ref[1, 6:7, 256:384] = g_rate * rate

    def layer(k):
        at = pl.ds(pl.multiple_of(zs[k] * LAYER, LAYER), LAYER)

        @pl.loop(0, 6)
        def _(i):
            n = pl.ds(pl.multiple_of(i * 256, 256), 256)
            total = mm_nt(din_ref[at, 0:256], cols_ref[n, 0:256])
            total = total + mm_nt(din_ref[at, 256:512], cols_ref[n, 256:512])
            total = total + mm_nt(din_ref[at, 512:768], cols_ref[n, 768:1024])
            total = total + mm_nt(din_ref[at, 768:896], cols_ref[n, 1024:1152])
            part_ref[at, n] = total.astype(low)

    moved = 24 * half_here

    def grads(first, last):
        @pl.loop(first, last)
        def _(i):
            n = pl.ds(pl.multiple_of(i * 256, 256), 256)
            total = mm_tn(n1_ref[:, n], din_ref[...])
            out = mm_tn(dres_ref[:, n], mixed_ref[...])
            main_ref[n, 0:128] = total[:, 0:128].astype(low)
            main_ref[n, 128:256] = total[:, 128:256].astype(low) + shared_ref[n, 0:128]
            main_ref[n, 256:384] = total[:, 256:384].astype(low)
            main_ref[n, 384:512] = total[:, 384:512].astype(low) + shared_ref[n, 128:256]
            main_ref[n, 512:640] = out[:, 0:128].astype(low)
            main_ref[n, 640:768] = out[:, 128:256].astype(low) + shared_ref[n, 256:384]
            bcr_ref[n, 0:256] = total[:, 512:768].astype(low)
            steps_part = pltpu.roll(total[:, 768:896], moved, 1)
            bcr_ref[n, 256:384] = (steps_part + shared_ref[n, 384:512].astype(f32)).astype(low)

    mail = Mail(send)
    steps = reduce_steps(mail, part_ref, sum_ref, got, sums, recv, 64)
    left = [3, 2, 1, 0]
    for turn in range(13):
        if turn in (0, 1, 3, 6):
            layer(left.pop(0))
        next(steps, None)
        next(b_steps, None)
        if turn in (7, 8, 9):
            grads(2 * (turn - 7), 2 * (turn - 6))
    for _ in b_steps:
        pass
    block_ref[...] += res_ref[0:64]
    for _ in steps:
        pass
    value, gain = norm_step(sum_ref[...], own_ref[0:64].astype(f32), floats_ref[7:8])
    input_ref[...] = dres_own_ref[0:64] + value
    for i in range(4):
        small_ref[0, i : i + 1, 0:384] = gain[:, 384 * i : 384 * (i + 1)]
        small_ref[0, 4 + i : 5 + i, 0:384] = dres_own_ref[64:65, 384 * i : 384 * (i + 1)]
    b_mail.finish()
    mail.finish()


def mix_backward(*args):
    low, f32 = jnp.bfloat16, jnp.float32
    return call(
        mix_backward_kernel,
        "mix_backward",
        4,
        (
            ((1536, 768), low),
            ((1536, 384), low),
            ((2, 8, 512), f32),
            ((64, 1536), f32),
            ((64, 1536), f32),
        ),
        [
            VMEM((1024, 1536), low),
            VMEM((1024, 192), f32),
            VMEM((1024, 256), low),
            VMEM((1024, 896), low),
            VMEM((CHUNK + 8, 448), f32),
            VMEM((64, 1536), f32),
            VMEM((1024, 1536), low),
            VMEM((1040, 1536), f32),
            DMA((2,)),
        ]
        + reduce_scratch(64, 1536, low)
        + reduce_scratch(64, 1536, low)
        + [DMA((27,)), DMA((27,)), DMA((27,)), DMA((27,))],
        args,
        ((2, 5), ()),
        limit=34,
    )


def place_kernel(
    main_ref,
    bcr_ref,
    small_ref,
    block_own,
    block_other,
    input_own,
    input_other,
    geg_ref,
    geu_ref,
    ged_ref,
    sg_ref,
    su_ref,
    sd_ref,
    block_out,
    input_out,
    norm1_out,
    wz_out,
    wx_out,
    wbc_out,
    wdt_out,
    convx_out,
    convbc_out,
    biasx_out,
    biasbc_out,
    dt_out,
    log_out,
    skip_out,
    gnorm_out,
    wout_out,
    norm2_out,
    router_out,
    sgate_out,
    sup_out,
    sdown_out,
    eg_out,
    eu_out,
    ed_out,
    biasx_row,
    gnorm_row,
    heads_row,
):
    side = lax.axis_index("head")
    f32 = jnp.float32
    for own, other, out in (
        (block_own, block_other, block_out),
        (input_own, input_other, input_out),
    ):
        out[:, 0] = jnp.where(side == 0, own[...], other[...])
        out[:, 1] = jnp.where(side == 0, other[...], own[...])
    norms = small_ref[0, 0]
    taps = small_ref[1, 0, :, 0:256]
    for j in range(1, 16):
        norms = norms + small_ref[0, j]
        taps = taps + small_ref[1, j, :, 0:256]
    for i in range(4):
        norm1_out[384 * i : 384 * (i + 1)] = norms[i, 0:384]
        norm2_out[384 * i : 384 * (i + 1)] = norms[4 + i, 0:384]
    convbc_out[...] = taps[0:4]
    biasbc_out[...] = taps[4]
    wbc_out[...] = bcr_ref[:, 0:256]
    turned = jnp.concatenate([bcr_ref[:, 256:384], jnp.zeros((32, 128), f32)], 0).T
    router_out[...] = turned[0:16, 0:96]
    wdt_out[...] = jnp.where(side == 0, turned[16:40, 0:96], turned[40:64, 0:96])
    onehot = (
        lax.broadcasted_iota(jnp.int32, (192, 128), 0) // HEADW
        == lax.broadcasted_iota(jnp.int32, (192, 128), 1)
    ).astype(f32)
    for j in range(8):
        place = 8 * side + j
        wide, narrow = slice(192 * j, 192 * (j + 1)), slice(64 * j, 64 * (j + 1))
        convx_out[:, wide] = small_ref[1, place, 0:4, 256:448]
        biasx_row[:, wide] = small_ref[1, place, 4:5, 256:448]
        gnorm_row[:, wide] = small_ref[1, place, 5:6, 0:192]
        skips = jnp.broadcast_to(small_ref[1, place, 5:6, 256:448], (8, 192))
        heads_row[2:3, 3 * j : 3 * j + 3] = mm(skips, onehot, exact=True)[0:1, 0:3]
        heads_row[0:1, 3 * j : 3 * j + 3] = small_ref[1, place, 6:7, 0:3]
        heads_row[1:2, 3 * j : 3 * j + 3] = small_ref[1, place, 6:7, 256:259]
        part = main_ref[j].astype(f32)
        wz_out[:, wide] = part[:, 0:192]
        sgate_out[:, narrow] = part[:, 192:256]
        wx_out[:, wide] = part[:, 256:448]
        sup_out[:, narrow] = part[:, 448:512]
        wout_out[:, wide] = part[:, 512:704]
        sdown_out[:, narrow] = part[:, 704:768]
    biasx_out[...] = biasx_row[0]
    gnorm_out[...] = gnorm_row[0]
    dt_out[...] = heads_row[0, 0:24]
    log_out[...] = heads_row[1, 0:24]
    skip_out[...] = heads_row[2, 0:24]
    eg_out[0] = geg_ref[...] + sg_ref[...].astype(f32)
    eu_out[0] = geu_ref[...] + su_ref[...].astype(f32)
    ed_out[0] = ged_ref[...] + sd_ref[...].astype(f32)


def place(*args):
    shapes = (
        (64, 2, 1536),
        (64, 2, 1536),
        (1536,),
        (96, 1536),
        (96, 1536),
        (96, 256),
        (24, 96),
        (4, 1536),
        (4, 256),
        (1536,),
        (256,),
        (24,),
        (24,),
        (24,),
        (1536,),
        (96, 1536),
        (1536,),
        (16, 96),
        (96, 512),
        (96, 512),
        (96, 512),
        (1, 1536, 256),
        (1, 1536, 256),
        (1, 256, 1536),
    )
    vmem = pl.BlockSpec(memory_space=VMEM)
    return pl.pallas_call(
        place_kernel,
        out_shape=tuple(jax.ShapeDtypeStruct(shape, jnp.float32) for shape in shapes),
        in_specs=[vmem] * len(args),
        out_specs=(vmem,) * len(shapes),
        scratch_shapes=[
            VMEM((1, 1536), jnp.float32),
            VMEM((1, 1536), jnp.float32),
            VMEM((8, 128), jnp.float32),
        ],
        compiler_params=pltpu.CompilerParams(vmem_limit_bytes=48 << 20),
        name="place",
    )(*args)


def by_heads(
    hidden_in,
    doc_ids,
    routes,
    norm1_gain,
    w_z,
    w_x,
    w_bc,
    w_dt,
    conv_x,
    conv_bc,
    convb_x,
    convb_bc,
    dt_bias,
    a_log,
    d_skip,
    gnorm_gain,
    w_out,
    norm2_gain,
    router,
    shared_gate,
    shared_up,
    shared_down,
    expert_gate,
    expert_up,
    expert_down,
    cotangent,
):
    eg, eu, ed = expert_gate[0], expert_up[0], expert_down[0]
    n1, extras, _, cols, own, floats, small_sib, eg_o, eu_o, ed_o = enter(
        hidden_in,
        cotangent,
        w_bc,
        router.T,
        w_dt.T,
        doc_ids.T,
        routes.transpose(1, 2, 0),
        w_out.T,
        shared_down.T,
        w_z,
        shared_gate,
        w_x,
        shared_up,
        conv_x,
        convb_x,
        gnorm_gain,
        dt_bias,
        a_log,
        d_skip,
        norm1_gain,
        norm2_gain,
        conv_bc,
        convb_bc,
        eg,
        eu,
        ed,
    )
    kept, g_all, n2, scale_note, residual, scale_own, ids, consts = mix_forward(
        n1, extras, cols, floats, small_sib, own
    )
    d_res_all, pair, moe_part, *grad_experts, shared, d_res = moe(
        n2,
        scale_note,
        g_all,
        cols,
        eg,
        eg_o,
        eu,
        eu_o,
        ed,
        ed_o,
        extras,
        ids,
        residual,
        scale_own,
        floats,
        own,
    )
    main, bcr, small, block_own, input_own = mix_backward(
        d_res_all, pair, n1, cols, consts, kept, moe_part, shared, residual, d_res, own, floats
    )
    main, bcr, small, block_sib, input_sib = leave(
        main.reshape(16, 96, 768), bcr, small, block_own, input_own
    )
    results = list(
        place(main, bcr, small, block_own, block_sib, input_own, input_sib, *grad_experts)
    )
    for i in (6, 15, 17, 20):
        results[i] = results[i].T
    return tuple(results)


def solution(mesh):
    places = mesh.shape["seq"]
    whole_heads = places == 16 and mesh.shape["head"] == 2
    placed = (
        P("seq", None, None),
        P("seq", None),
        P("seq", None, None),
        P(),
        P("seq", "head"),
        P("seq", "head"),
        P("seq", None),
        P("seq", "head"),
        P(None, "head"),
        P(),
        P("head"),
        P(),
        P("head"),
        P("head"),
        P("head"),
        P("head"),
        P("head", "seq"),
        P(),
        P("seq", None),
        P("seq", "head"),
        P("seq", "head"),
        P("head", "seq"),
        P("seq", None, "head"),
        P("seq", None, "head"),
        P("seq", "head", None),
        P("seq", None, None),
    )
    return jax.shard_map(
        by_heads if whole_heads else on_device,
        mesh=mesh,
        in_specs=placed,
        out_specs=(
            P("seq", None, None),
            P("seq", None, None),
            P(),
            P("seq", "head"),
            P("seq", "head"),
            P("seq", None),
            P("seq", "head"),
            P(None, "head"),
            P(),
            P("head"),
            P(),
            P("head"),
            P("head"),
            P("head"),
            P("head"),
            P("head", "seq"),
            P(),
            P("seq", None),
            P("seq", "head"),
            P("seq", "head"),
            P("head", "seq"),
            P("seq", None, "head"),
            P("seq", None, "head"),
            P("seq", "head", None),
        ),
        check_vma=False,
    )
```

```python
import jax
import jax.numpy as jnp
from jax import lax
from jax.experimental import pallas as pl
from jax.experimental.pallas import tpu as pltpu
from jax.sharding import PartitionSpec as P

KER = 4
INNER = 3072


EPS = 1e-05
HIGH = lax.Precision.HIGHEST


def passed_along(array, axis, by):
    length = lax.axis_size(axis)
    pairs = [(i, i + by) for i in range(length) if 0 <= i + by < length]
    return lax.ppermute(array, axis, pairs)


def entering(array, axis, combine, identity, reverse):
    length, here = (lax.axis_size(axis), lax.axis_index(axis))
    everything = jax.tree.map(
        lambda part, kind: lax.all_gather(part.astype(kind), axis),
        array,
        jax.tree.map(lambda a: jnp.bfloat16 if a.dtype == jnp.float32 else a.dtype, array),
    )
    start = jax.tree.map(
        lambda part, zero: jnp.broadcast_to(jnp.asarray(zero, part.dtype), part.shape),
        array,
        identity,
    )

    def hop(k, before):
        at = length - 1 - k if reverse else k
        reached = at > here if reverse else at < here
        new = combine(
            before, jax.tree.map(lambda part, own: part[at].astype(own.dtype), everything, array)
        )
        return jax.tree.map(lambda a, b: jnp.where(reached, a, b), new, before)

    return lax.fori_loop(0, length, hop, start)


def shortened(array):

    def short(part):
        return part.astype(jnp.bfloat16) if part.dtype == jnp.float32 else part

    return jax.tree.map(short, array)


def conv_apply(conv_ext, docs_ext, weight, conv_bias):
    length_here = conv_ext.shape[0] - (KER - 1)
    running = conv_bias
    for offset in range(KER):
        same_doc = (docs_ext[offset : offset + length_here] == docs_ext[KER - 1 :]).astype(
            jnp.float32
        )
        running = (
            running + weight[offset] * conv_ext[offset : offset + length_here] * same_doc[..., None]
        )
    return jax.nn.silu(running)


def group_parts(x_heads, step_size, b_state, decay_rate, doc_ids, prev_doc):
    log_decay = jnp.cumsum(step_size * decay_rate, axis=0)
    end_keep = (doc_ids == doc_ids[-1:]).astype(jnp.float32)
    weight = jnp.exp(log_decay[-1:] - log_decay) * end_keep[..., None] * step_size
    s_local = jnp.einsum("tsh,tshp,tsn->shpn", weight, x_heads, b_state, precision=HIGH)
    a_total = jnp.exp(log_decay[-1]) * (doc_ids[-1] == prev_doc).astype(jnp.float32)[:, None]
    return (s_local, a_total)


def group_output(x_heads, step_size, b_state, c_state, decay_rate, doc_ids, prev_doc, s_in):
    length_here = x_heads.shape[0]
    log_decay = jnp.cumsum(step_size * decay_rate, axis=0)
    causal = jnp.arange(length_here)[:, None] >= jnp.arange(length_here)[None, :]
    pair_mask = (causal[:, :, None] & (doc_ids[:, None, :] == doc_ids[None, :, :])).astype(
        jnp.float32
    )
    gap_decay = log_decay[:, None] - log_decay[None, :]
    decay_table = (
        jnp.exp(jnp.where(pair_mask[..., None] > 0, gap_decay, 0.0)) * pair_mask[..., None]
    )
    cross_dot = jnp.einsum("tsn,usn->tus", c_state, b_state, precision=HIGH)
    y_intra = jnp.einsum(
        "tush,ush,ushp->tshp",
        decay_table * cross_dot[..., None],
        step_size,
        x_heads,
        precision=HIGH,
    )
    enters = jnp.exp(log_decay) * (doc_ids == prev_doc[None, :]).astype(jnp.float32)[..., None]
    y_inter = jnp.einsum("tsn,shpn->tshp", c_state, s_in, precision=HIGH) * enters[..., None]
    return y_intra + y_inter


def ssm_local(x_heads, step_size, b_state, c_state, decay_rate, s_in, doc_ids, prev_doc):
    y_core = group_output(x_heads, step_size, b_state, c_state, decay_rate, doc_ids, prev_doc, s_in)
    s_local, a_total = group_parts(x_heads, step_size, b_state, decay_rate, doc_ids, prev_doc)
    return (y_core, a_total[..., None, None] * s_in + s_local)


def carry_combine(earlier, later_part):
    return (earlier[0] * later_part[0], later_part[0][..., None, None] * earlier[1] + later_part[1])


def head_total(partial_sum):
    return lax.psum(partial_sum, "head")


def flat_dot(left_side, right_side):
    lead_dims = left_side.shape[:-1]
    product = jnp.dot(
        left_side.reshape(-1, left_side.shape[-1]), right_side, preferred_element_type=jnp.float32
    )
    return product.reshape(lead_dims + (right_side.shape[-1],))


def flat_dot_t(left_side, right_side):
    lead_dims = left_side.shape[:-1]
    product = lax.dot_general(
        left_side.reshape(-1, left_side.shape[-1]),
        right_side,
        (((1,), (1,)), ((), ())),
        preferred_element_type=jnp.float32,
    )
    return product.reshape(lead_dims + (right_side.shape[0],))


def outer_sum(left_side, right_side):
    return lax.dot_general(
        left_side.reshape(-1, left_side.shape[-1]),
        right_side.reshape(-1, right_side.shape[-1]),
        (((0,), (0,)), ((), ())),
        preferred_element_type=jnp.float32,
    )


def silu_slope(values, sigmoid_of):
    return sigmoid_of * (1.0 + values * (1.0 - sigmoid_of))


def norm_back(grad_normed, values, scale_of, gain):
    scaled_grad = grad_normed * gain
    gain_grad = jnp.sum((grad_normed * values * scale_of).reshape(-1, values.shape[-1]), axis=0)
    cube = scale_of * scale_of * scale_of
    value_grad = scale_of * scaled_grad - values * cube * jnp.mean(
        scaled_grad * values, axis=-1, keepdims=True
    )
    return (value_grad, gain_grad)


def on_device(
    hidden_in,
    doc_ids,
    routes,
    norm1_gain,
    w_z,
    w_x,
    w_bc,
    w_dt,
    conv_x,
    conv_bc,
    convb_x,
    convb_bc,
    dt_bias,
    a_log,
    d_skip,
    gnorm_gain,
    w_out,
    norm2_gain,
    router,
    shared_gate,
    shared_up,
    shared_down,
    expert_gate,
    expert_up,
    expert_down,
    cotangent,
):
    block_len, seq_here, width = hidden_in.shape
    top_count = routes.shape[-1]
    heads_here = dt_bias.shape[0]
    inner_here = convb_x.shape[0]
    head_size = inner_here // heads_here
    state_size = convb_bc.shape[0] // 2
    seq_count = lax.axis_size("seq")
    local_experts = expert_gate.shape[0]
    experts_all = local_experts * seq_count
    tok_here = block_len * seq_here
    capacity = 2 * tok_here * top_count // experts_all
    edge_len = KER - 1
    x_float = hidden_in.astype(jnp.float32)
    scale_one = lax.rsqrt(jnp.mean(x_float * x_float, axis=-1, keepdims=True) + EPS)
    normed_one = (x_float * scale_one * norm1_gain).astype(jnp.bfloat16)
    gathered = (
        lax.all_gather(w_z, "seq", axis=0, tiled=True),
        lax.all_gather(w_x, "seq", axis=0, tiled=True),
        lax.all_gather(w_dt, "seq", axis=0, tiled=True),
        lax.all_gather(w_bc, "seq", axis=0, tiled=True),
        lax.all_gather(router, "seq", axis=0, tiled=True),
        lax.all_gather(shared_gate, "seq", axis=0, tiled=True),
        lax.all_gather(shared_up, "seq", axis=0, tiled=True),
        lax.all_gather(w_out, "seq", axis=1, tiled=True),
        lax.all_gather(shared_down, "seq", axis=1, tiled=True),
    )
    full_z, full_x, full_dt, full_bc, full_router, full_sgate, full_sup, full_out, full_sdown = (
        gathered
    )
    gate_z = flat_dot(normed_one, full_z)
    proj_x = flat_dot(normed_one, full_x)
    proj_bc = flat_dot(normed_one, full_bc)
    dt_pre = flat_dot(normed_one, full_dt) + dt_bias
    conv_in = jnp.concatenate([proj_x, proj_bc], axis=-1)
    tail_in, tail_doc = (
        passed_along(conv_in[block_len - edge_len :].astype(jnp.bfloat16), "seq", 1).astype(
            jnp.float32
        ),
        passed_along(
            doc_ids[block_len - edge_len :].astype(jnp.float32).astype(jnp.bfloat16), "seq", 1
        ).astype(jnp.float32),
    )
    conv_ext = jnp.concatenate([tail_in, conv_in], 0)
    docs_ext = jnp.concatenate([tail_doc.astype(jnp.int32), doc_ids], 0)
    conv_weight = jnp.concatenate([conv_x, conv_bc], -1)
    conv_shift = jnp.concatenate([convb_x, convb_bc], -1)
    conv_out = conv_apply(conv_ext, docs_ext, conv_weight, conv_shift)
    x_heads = conv_out[..., :inner_here].reshape(block_len, seq_here, heads_here, head_size)
    b_state = conv_out[..., inner_here : inner_here + state_size]
    c_state = conv_out[..., inner_here + state_size :]
    step_size = jax.nn.softplus(dt_pre)
    decay_rate = -jnp.exp(a_log)
    prev_doc = docs_ext[edge_len - 1]
    s_local, a_total = group_parts(x_heads, step_size, b_state, decay_rate, doc_ids, prev_doc)
    ones_start = jnp.ones_like(a_total)
    zeros_start = jnp.zeros_like(s_local)
    a_before, s_before = entering(
        (a_total, s_local), "seq", carry_combine, (ones_start, zeros_start), False
    )
    y_core = group_output(
        x_heads, step_size, b_state, c_state, decay_rate, doc_ids, prev_doc, s_before
    )
    y_heads = y_core + d_skip[:, None] * x_heads
    y_flat = y_heads.reshape(block_len, seq_here, inner_here)
    gate_sig = jax.nn.sigmoid(gate_z)
    gated = y_flat * gate_z * gate_sig
    square_sum = head_total(jnp.sum(gated * gated, axis=-1, keepdims=True))
    scale_gated = lax.rsqrt(square_sum / INNER + EPS)
    mixed_out = (gated * scale_gated * gnorm_gain).astype(jnp.bfloat16)
    residual = x_float + head_total(flat_dot(mixed_out, full_out))
    scale_two = lax.rsqrt(jnp.mean(residual * residual, axis=-1, keepdims=True) + EPS)
    normed_two = (residual * scale_two * norm2_gain).astype(jnp.bfloat16)
    logits = flat_dot(normed_two, full_router)
    gate_probs = jax.nn.softmax(jnp.take_along_axis(logits, routes, axis=-1), axis=-1)
    share_gate = flat_dot(normed_two, full_sgate)
    share_up = flat_dot(normed_two, full_sup)
    share_sig = jax.nn.sigmoid(share_gate)
    share_act = (share_gate * share_sig * share_up).astype(jnp.bfloat16)
    share_part = flat_dot(share_act, full_sdown)
    slot_total = tok_here * top_count
    route_flat = routes.reshape(slot_total)
    expert_ids = jnp.arange(experts_all, dtype=jnp.int32)
    route_hits = (route_flat[:, None] == expert_ids[None, :]).astype(jnp.int32)
    slot_rank = jnp.sum(jnp.cumsum(route_hits, axis=0) * route_hits, axis=1) - 1
    target = route_flat * capacity + slot_rank
    entry_table = (
        jnp.zeros((experts_all * capacity,), jnp.int32)
        .at[target]
        .set(jnp.arange(slot_total, dtype=jnp.int32) + 1)
    )
    entry_live = entry_table > 0
    entry_slot = jnp.maximum(entry_table - 1, 0)
    entry_token = entry_slot // top_count
    tokens_flat = normed_two.reshape(tok_here, width)
    send_rows = jnp.where(
        entry_live[:, None], tokens_flat[entry_token], jnp.zeros((), jnp.bfloat16)
    ).reshape(experts_all, capacity, width)
    received = lax.all_to_all(send_rows, "seq", split_axis=0, concat_axis=0, tiled=True)
    input_row_block = received.reshape(seq_count, local_experts, received.shape[1], width)
    hid_gate = jnp.einsum(
        "jecd,edf->jecf", input_row_block, expert_gate, preferred_element_type=jnp.float32
    )
    hid_up = jnp.einsum(
        "jecd,edf->jecf", input_row_block, expert_up, preferred_element_type=jnp.float32
    )
    hid_act = (hid_gate * jax.nn.sigmoid(hid_gate) * hid_up).astype(jnp.bfloat16)
    half_out = jnp.einsum(
        "jecf,efd->jecd", hid_act, expert_down, preferred_element_type=jnp.float32
    ).astype(jnp.bfloat16)
    returned_rows = lax.all_to_all(
        half_out.reshape(received.shape), "seq", split_axis=0, concat_axis=0, tiled=True
    )
    kept_shape = (seq_count * local_experts, received.shape[1], hid_gate.shape[-1])
    returned_rows, rows_kept, gate_kept, up_kept = (
        returned_rows,
        received,
        hid_gate.reshape(kept_shape),
        hid_up.reshape(kept_shape),
    )
    slot_rows = returned_rows.reshape(-1, width)[target].reshape(tok_here, top_count, width)
    probs_flat = gate_probs.reshape(tok_here, top_count)
    routed_part = share_part.reshape(tok_here, width)
    for slot_index in range(top_count):
        routed_part = routed_part + probs_flat[:, slot_index, None] * slot_rows[
            :, slot_index
        ].astype(jnp.float32)
    moe_out = head_total(routed_part.reshape(block_len, seq_here, width))
    block_out = residual + moe_out
    gathered = (
        lax.all_gather(w_z, "seq", axis=0, tiled=True),
        lax.all_gather(w_x, "seq", axis=0, tiled=True),
        lax.all_gather(w_dt, "seq", axis=0, tiled=True),
        lax.all_gather(w_bc, "seq", axis=0, tiled=True),
        lax.all_gather(router, "seq", axis=0, tiled=True),
        lax.all_gather(shared_gate, "seq", axis=0, tiled=True),
        lax.all_gather(shared_up, "seq", axis=0, tiled=True),
        lax.all_gather(w_out, "seq", axis=1, tiled=True),
        lax.all_gather(shared_down, "seq", axis=1, tiled=True),
    )
    full_z, full_x, full_dt, full_bc, full_router, full_sgate, full_sup, full_out, full_sdown = (
        gathered
    )
    grad_out = cotangent.astype(jnp.float32)
    grad_flat = grad_out.reshape(tok_here, width)
    entry_prob = jnp.where(entry_live, gate_probs.reshape(-1)[entry_slot], 0.0)
    send_grads = (
        (entry_prob[:, None] * grad_flat[entry_token])
        .astype(jnp.bfloat16)
        .reshape(experts_all, capacity, width)
    )
    recv_grads = lax.all_to_all(send_grads, "seq", split_axis=0, concat_axis=0, tiled=True)
    grads_in = recv_grads.reshape(seq_count, local_experts, capacity, width)
    input_row_block = rows_kept.reshape(seq_count, local_experts, capacity, width)
    hid_gate = gate_kept.reshape(seq_count, local_experts, capacity, -1)
    hid_up = up_kept.reshape(seq_count, local_experts, capacity, -1)
    hid_sig = jax.nn.sigmoid(hid_gate)
    hid_act = (hid_gate * hid_sig * hid_up).astype(jnp.bfloat16)
    d_act = jnp.einsum("jecd,efd->jecf", grads_in, expert_down, preferred_element_type=jnp.float32)
    hidden_up_gradient = (d_act * hid_gate * hid_sig).astype(jnp.bfloat16)
    d_hid_gate = (d_act * hid_up * silu_slope(hid_gate, hid_sig)).astype(jnp.bfloat16)
    grad_edown = jnp.einsum("jecf,jecd->efd", hid_act, grads_in, preferred_element_type=jnp.float32)
    grad_egate = jnp.einsum(
        "uqpy,uqpn->qyn", input_row_block, d_hid_gate, preferred_element_type=jnp.float32
    )
    expert_up_gradient = jnp.einsum(
        "uqpy,uqpn->qyn", input_row_block, hidden_up_gradient, preferred_element_type=jnp.float32
    )
    d_rows = jnp.einsum(
        "jecf,edf->jecd", d_hid_gate, expert_gate, preferred_element_type=jnp.float32
    )
    d_rows = (
        d_rows
        + jnp.einsum(
            "jecf,edf->jecd", hidden_up_gradient, expert_up, preferred_element_type=jnp.float32
        )
    ).astype(jnp.bfloat16)
    back_rows = lax.all_to_all(
        d_rows.reshape(recv_grads.shape), "seq", split_axis=0, concat_axis=0, tiled=True
    )
    d_share_act = flat_dot_t(cotangent, full_sdown)
    d_share_up = (d_share_act * share_gate * share_sig).astype(jnp.bfloat16)
    d_share_gate = (d_share_act * share_up * silu_slope(share_gate, share_sig)).astype(jnp.bfloat16)
    grad_sdown = outer_sum(share_act, cotangent)
    grad_sgate = outer_sum(normed_two, d_share_gate)
    grad_sup = outer_sum(normed_two, d_share_up)
    d_normed_two = (
        flat_dot_t(d_share_gate, full_sgate) + flat_dot_t(d_share_up, full_sup)
    ).reshape(tok_here, width)
    prob_grad = jnp.stack(
        [
            jnp.sum(grad_flat * slot_rows[:, slot_index].astype(jnp.float32), axis=-1)
            for slot_index in range(top_count)
        ],
        axis=-1,
    )
    back_slots = back_rows.reshape(-1, width)[target].reshape(tok_here, top_count, width)
    for slot_index in range(top_count):
        d_normed_two = d_normed_two + back_slots[:, slot_index].astype(jnp.float32)
    d_normed_two, prob_grad = head_total(
        (
            d_normed_two.reshape(block_len, seq_here, width),
            prob_grad.reshape(block_len, seq_here, top_count),
        )
    )
    d_chosen = gate_probs * (prob_grad - jnp.sum(gate_probs * prob_grad, axis=-1, keepdims=True))
    d_logits = jnp.sum(
        d_chosen[..., None] * (routes[..., None] == expert_ids).astype(jnp.float32), axis=-2
    ).astype(jnp.bfloat16)
    grad_router = outer_sum(normed_two, d_logits)
    d_normed_two = d_normed_two + flat_dot_t(d_logits, full_router)
    d_resid_norm, grad_norm2 = norm_back(d_normed_two, residual, scale_two, norm2_gain)
    d_resid = grad_out + d_resid_norm
    d_resid_low = d_resid.astype(jnp.bfloat16)
    d_mixed = flat_dot_t(d_resid_low, full_out)
    grad_out_w = outer_sum(mixed_out, d_resid_low)
    gain_scaled = d_mixed * gnorm_gain
    grad_gnorm = jnp.sum((d_mixed * gated * scale_gated).reshape(-1, inner_here), axis=0)
    cross_sum = head_total(jnp.sum(gain_scaled * gated, axis=-1, keepdims=True))
    d_gated = (
        scale_gated * gain_scaled
        - gated * scale_gated * scale_gated * scale_gated * cross_sum / INNER
    )
    d_y = d_gated * gate_z * gate_sig
    d_gate_z = (d_gated * y_flat * silu_slope(gate_z, gate_sig)).astype(jnp.bfloat16)
    d_y_heads = d_y.reshape(x_heads.shape)
    grad_skip = jnp.sum(d_y_heads * x_heads, axis=(0, 1, 3))
    log_decay = jnp.cumsum(step_size * decay_rate, axis=0)
    enters = jnp.exp(log_decay) * (doc_ids == prev_doc[None, :]).astype(jnp.float32)[..., None]
    g_local = jnp.einsum("tsh,tshp,tsn->shpn", enters, d_y_heads, c_state, precision=HIGH)
    a_after, state_grad = entering(
        (a_total, g_local), "seq", carry_combine, (ones_start, zeros_start), True
    )

    def local_scan(x_part, step_part, b_part, c_part, rate_part, state_part):
        return ssm_local(
            x_part, step_part, b_part, c_part, rate_part, state_part, doc_ids, prev_doc
        )

    _, scan_back = jax.vjp(local_scan, x_heads, step_size, b_state, c_state, decay_rate, s_before)
    d_xh, d_step, d_bstate, d_cstate, d_rate, _ = scan_back((d_y_heads, state_grad))
    d_xh = d_xh + d_skip[:, None] * d_y_heads
    d_bc = head_total(jnp.concatenate([d_bstate, d_cstate], axis=-1))
    d_dt_pre = d_step * jax.nn.sigmoid(dt_pre)
    grad_dtb = jnp.sum(d_dt_pre, axis=(0, 1))
    grad_alog = d_rate * decay_rate
    d_conv_out = jnp.concatenate([d_xh.reshape(block_len, seq_here, inner_here), d_bc], axis=-1)

    def local_conv(ext_part, weight_part, shift_part):
        return conv_apply(ext_part, docs_ext, weight_part, shift_part)

    _, conv_back = jax.vjp(local_conv, conv_ext, conv_weight, conv_shift)
    d_ext, grad_cweight, grad_cshift = conv_back(d_conv_out)
    from_next = passed_along(shortened(d_ext[:edge_len]), "seq", -1)
    d_conv_in = d_ext[edge_len:] + jnp.concatenate(
        [jnp.zeros((block_len - edge_len,) + from_next.shape[1:], jnp.float32), from_next], 0
    )
    d_proj_x = d_conv_in[..., :inner_here].astype(jnp.bfloat16)
    d_proj_bc = d_conv_in[..., inner_here:].astype(jnp.bfloat16)
    d_dt_low = d_dt_pre.astype(jnp.bfloat16)
    grad_wz = outer_sum(normed_one, d_gate_z)
    grad_wx = outer_sum(normed_one, d_proj_x)
    grad_wbc = outer_sum(normed_one, d_proj_bc)
    grad_wdt = outer_sum(normed_one, d_dt_low)
    head_first = jnp.where(lax.axis_index("head") == 0, 1.0, 0.0)
    d_normed_one = (
        flat_dot_t(d_gate_z, full_z) + flat_dot_t(d_proj_x, full_x) + flat_dot_t(d_dt_low, full_dt)
    )
    d_normed_one = head_total(d_normed_one + head_first * flat_dot_t(d_proj_bc, full_bc))
    d_x_norm, grad_norm1 = norm_back(d_normed_one, x_float, scale_one, norm1_gain)
    input_grad = d_resid + d_x_norm
    reduced = (
        lax.psum_scatter(grad_wz, "seq", scatter_dimension=0, tiled=True),
        lax.psum_scatter(grad_wx, "seq", scatter_dimension=0, tiled=True),
        lax.psum_scatter(grad_wdt, "seq", scatter_dimension=0, tiled=True),
        lax.psum_scatter(grad_wbc, "seq", scatter_dimension=0, tiled=True),
        lax.psum_scatter(grad_router, "seq", scatter_dimension=0, tiled=True),
        lax.psum_scatter(grad_sgate, "seq", scatter_dimension=0, tiled=True),
        lax.psum_scatter(grad_sup, "seq", scatter_dimension=0, tiled=True),
        lax.psum_scatter(grad_out_w, "seq", scatter_dimension=1, tiled=True),
        lax.psum_scatter(grad_sdown, "seq", scatter_dimension=1, tiled=True),
    )
    red_z, red_x, red_dt, red_bc, red_router, red_sgate, red_sup, red_out, red_sdown = reduced
    small_sums = lax.psum(
        (
            grad_norm1,
            grad_norm2,
            grad_cweight,
            grad_cshift,
            grad_dtb,
            grad_alog,
            grad_skip,
            grad_gnorm,
        ),
        "seq",
    )
    sum_norm1, sum_norm2, sum_cweight, sum_cshift, sum_dtb, sum_alog, sum_skip, sum_gnorm = (
        small_sums
    )
    return (
        block_out,
        input_grad,
        sum_norm1,
        red_z,
        red_x,
        red_bc,
        red_dt,
        sum_cweight[:, :inner_here],
        sum_cweight[:, inner_here:],
        sum_cshift[:inner_here],
        sum_cshift[inner_here:],
        sum_dtb,
        sum_alog,
        sum_skip,
        sum_gnorm,
        red_out,
        sum_norm2,
        red_router,
        red_sgate,
        red_sup,
        red_sdown,
        grad_egate,
        expert_up_gradient,
        grad_edown,
    )


MESH = pl.DeviceIdType.MESH
VMEM = pltpu.VMEM


def peers():
    here, side = lax.axis_index("seq"), lax.axis_index("head")
    x, y, z = lax.rem(here, 2), lax.rem(here // 2, 2), here // 4
    col = x + 2 * y
    return here, side, z, col, (1 - x) + 2 * y, x + 2 * (1 - y), 3 - col


def layers(z):
    lo, hi = lax.rem(z, 2), z // 2
    return [2 * (1 - hi if k & 2 else hi) + (1 - lo if k & 1 else lo) for k in range(4)]


def call_out(devices):
    barrier = pltpu.get_barrier_semaphore()
    for device in devices:
        pl.semaphore_signal(barrier, inc=1, device_id=device, device_id_type=MESH)
    return len(devices)


def greet(devices):
    pl.semaphore_wait(pltpu.get_barrier_semaphore(), call_out(devices))


class Mail:
    def __init__(self, send, base=0):
        self.send, self.sent, self.base = send, [], base

    def put(self, src, dst, sem, to):
        copy = pltpu.make_async_remote_copy(
            src_ref=src,
            dst_ref=dst,
            send_sem=self.send.at[self.base + len(self.sent)],
            recv_sem=sem,
            device_id=to,
            device_id_type=MESH,
        )
        copy.start()
        self.sent.append(copy)

    def arrived(self, dst, sem):
        pltpu.make_async_remote_copy(
            src_ref=dst,
            dst_ref=dst,
            send_sem=self.send.at[0],
            recv_sem=sem,
            device_id=(0, 0),
            device_id_type=MESH,
        ).wait_recv()

    def finish(self):
        for copy in self.sent:
            copy.wait_send()


def rows_at(ref, start, size, step):
    return ref.at[pl.ds(pl.multiple_of(start, step), size)]


def gather_steps(mail, own_ref, out_ref, recv, recv_half, rows, half=None):
    here, side, z, col, cx, cy, cd = peers()
    zs = layers(z)
    base = 4 * z
    to_x, to_y = (base + cx, side), (base + cy, side)

    def part(place, which, ref=None):
        if half is None:
            width = out_ref.shape[1] // 2
            lane = pl.ds(which * width, width)
            if ref is not None:
                return ref.at[:, lane]
            return out_ref.at[pl.ds(pl.multiple_of(place * rows, 16), rows), lane]
        size = rows - half if which else half
        if ref is not None:
            return ref.at[pl.ds(which * half, size)]
        return rows_at(out_ref, place * rows + which * half, size, 16)

    def onward(place, k, ref=None):
        for which in (0, 1):
            src = part(place, which, ref)
            mail.put(src, part(place, which), recv.at[6 + 4 * k + which], to_x)
            src = part(place, 1 - which, ref)
            mail.put(src, part(place, 1 - which), recv.at[8 + 4 * k + which], to_y)

    def across(k):
        at = 4 * zs[k] + cd
        mail.arrived(part(at, 0), recv_half.at[k])
        mail.arrived(part(at, 1), recv_half.at[4 + k])
        mail.arrived(part(4 * zs[k] + cx, 1), recv.at[7 + 4 * k])
        mail.arrived(part(4 * zs[k] + cy, 0), recv.at[9 + 4 * k])

    onward(here, 0, own_ref)
    for k in (1, 2, 3):
        for which in (0, 1):
            src = part(here, which, own_ref)
            sem = recv.at[2 * (k - 1) + which]
            mail.put(src, part(here, which), sem, (4 * zs[k] + col, side))
    yield
    for k in range(4):
        if k:
            at = 4 * zs[k] + col
            mail.arrived(part(at, 0), recv.at[2 * (k - 1)])
            mail.arrived(part(at, 1), recv.at[2 * (k - 1) + 1])
            onward(at, k)
            yield
        at = 4 * zs[k] + cx
        mail.arrived(part(at, 0), recv.at[6 + 4 * k])
        mail.put(part(at, 0), part(at, 0), recv_half.at[k], to_y)
        at = 4 * zs[k] + cy
        mail.arrived(part(at, 1), recv.at[8 + 4 * k])
        mail.put(part(at, 1), part(at, 1), recv_half.at[4 + k], to_x)
        yield
        if k:
            across(k - 1)
            yield
    across(3)
    yield


def near(side):
    here, side, z, col, cx, cy, cd = peers()
    zs = layers(z)
    return [(4 * z + cx, side), (4 * z + cy, side)] + [(4 * zs[k] + col, side) for k in (1, 2, 3)]


def note_puts(mail, src_of, notes_out, recv_n):
    here, side = peers()[:2]
    for k in range(1, 16):
        to = lax.rem(here + k, 16)
        mail.put(src_of(to), notes_out.at[here], recv_n.at[here], (to, side))


def note_waits(mail, notes_out, recv_n):
    here = peers()[0]
    for k in range(1, 16):
        place = lax.rem(here + k, 16)
        mail.arrived(notes_out.at[place], recv_n.at[place])


SUM_ORDER = (
    ("far", 3),
    ("joined", 3),
    ("far", 2),
    ("joined", 2),
    ("column", 3),
    ("far", 1),
    ("joined", 1),
    ("column", 2),
    ("far", 0),
    ("column", 1),
    ("joined", 0),
    ("column", 0),
)


def reduce_steps(mail, part_ref, out_ref, got, sums, recv, rows, order=SUM_ORDER):
    here, side, z, col, cx, cy, cd = peers()
    zs = layers(z)
    base = 4 * z
    half = rows // 2
    got_a, got_b, got_x, got_y, got_z = got
    sum_x, sum_y, sum_z = sums
    to_x, to_y = (base + cx, side), (base + cy, side)
    f32 = jnp.float32

    def half_of(place, which):
        return rows_at(part_ref, place * rows + which * half, half, half)

    def far(k):
        at = 4 * zs[k] + cd
        mail.put(half_of(at, 0), got_a.at[k], recv.at[k], to_y)
        mail.put(half_of(at, 1), got_b.at[k], recv.at[4 + k], to_x)

    def plain(k):
        mail.put(half_of(4 * zs[k] + cx, 1), got_x.at[k, pl.ds(half, half)], recv.at[12 + k], to_x)
        mail.put(half_of(4 * zs[k] + cy, 0), got_y.at[k, pl.ds(0, half)], recv.at[16 + k], to_y)

    def joined(k):
        mail.arrived(got_a.at[k], recv.at[k])
        total = half_of(4 * zs[k] + cx, 0)[...].astype(f32) + got_a[k].astype(f32)
        sum_x[k] = total.astype(sum_x.dtype)
        mail.put(sum_x.at[k], got_x.at[k, pl.ds(0, half)], recv.at[8 + k], to_x)
        mail.arrived(got_b.at[k], recv.at[4 + k])
        total = half_of(4 * zs[k] + cy, 1)[...].astype(f32) + got_b[k].astype(f32)
        sum_y[k] = total.astype(sum_y.dtype)
        mail.put(sum_y.at[k], got_y.at[k, pl.ds(half, half)], recv.at[20 + k], to_y)

    def column(k):
        mail.arrived(got_x.at[k, pl.ds(half, half)], recv.at[12 + k])
        mail.arrived(got_y.at[k, pl.ds(0, half)], recv.at[16 + k])
        mail.arrived(got_x.at[k, pl.ds(0, half)], recv.at[8 + k])
        mail.arrived(got_y.at[k, pl.ds(half, half)], recv.at[20 + k])
        own = part_ref[pl.ds(pl.multiple_of((4 * zs[k] + col) * rows, rows), rows)].astype(f32)
        total = own + got_x[k].astype(f32) + got_y[k].astype(f32)
        if k:
            sum_z[k - 1] = total.astype(sum_z.dtype)
            mail.put(sum_z.at[k - 1], got_z.at[k - 1], recv.at[23 + k], (4 * zs[k] + col, side))
        else:
            out_ref[...] = total

    for turn, k in order:
        if turn == "far":
            far(k)
            plain(k)
        elif turn == "joined":
            joined(k)
        else:
            column(k)
        yield
    for turn, k in order:
        if turn == "column" and k:
            mail.arrived(got_z.at[k - 1], recv.at[23 + k])
            out_ref[...] += got_z[k - 1].astype(f32)


def reduce_scratch(rows, width, kind):
    half = rows // 2
    shapes = [(4, half), (4, half), (4, rows), (4, rows), (3, rows), (4, half), (4, half), (3, rows)]
    return [VMEM(shape + (width,), kind) for shape in shapes]


def same_side(side, here):
    return [(lax.rem(here + k, 16), side) for k in range(1, 16)]


DMA = pltpu.SemaphoreType.DMA


def remote(src, dst, send, recv, to):
    return pltpu.make_async_remote_copy(
        src_ref=src,
        dst_ref=dst,
        send_sem=send,
        recv_sem=recv,
        device_id=to,
        device_id_type=MESH,
    )


def call(kernel, name, number, outs, scratch, args, spaces=None, limit=60):
    vmem = pl.BlockSpec(memory_space=VMEM)
    hbm = pl.BlockSpec(memory_space=pltpu.HBM)
    ins_far, outs_far = spaces or ((), ())
    args = [
        pltpu.with_memory_space_constraint(array, pltpu.HBM) if i in ins_far else array
        for i, array in enumerate(args)
    ]
    return pl.pallas_call(
        kernel,
        out_shape=tuple(
            pltpu.HBM(*out) if i in outs_far else jax.ShapeDtypeStruct(*out)
            for i, out in enumerate(outs)
        ),
        in_specs=[hbm if i in ins_far else vmem for i in range(len(args))],
        out_specs=tuple(hbm if i in outs_far else vmem for i in range(len(outs))),
        scratch_shapes=scratch,
        compiler_params=pltpu.CompilerParams(
            collective_id=number, has_side_effects=True, vmem_limit_bytes=limit << 20
        ),
        name=name,
    )(*args)


def of_side(ref, side):
    return jnp.where(side == 0, ref[:, 0], ref[:, 1])


def enter_kernel(
    hidden_far,
    cot_far,
    wbc_far,
    router_far,
    wdt_far,
    docs_far,
    routes_far,
    wo_far,
    sd_far,
    wz_far,
    sg_far,
    wx_far,
    su_far,
    convx_far,
    biasx_far,
    gnorm_far,
    bias_far,
    log_far,
    skip_far,
    norm1_far,
    norm2_far,
    convbc_far,
    biasbc_far,
    gate_ref,
    up_ref,
    down_ref,
    all_ref,
    extras_ref,
    extra_ref,
    cols_ref,
    own_ref,
    floats_ref,
    small_other,
    gate_other,
    up_other,
    down_other,
    n1_ref,
    mine_ref,
    misc_ref,
    blocks_ref,
    hidden_ref,
    cot_ref,
    wbc_ref,
    router_ref,
    wdt_ref,
    docs_ref,
    routes_ref,
    wo_ref,
    sd_ref,
    wz_ref,
    sg_ref,
    wx_ref,
    su_ref,
    convx_ref,
    biasx_ref,
    gnorm_ref,
    bias_ref,
    log_ref,
    skip_ref,
    norm1_ref,
    norm2_ref,
    convbc_ref,
    biasbc_ref,
    loaded,
    send,
    recv,
    recv_half,
    recv_m,
    recv_half_m,
    recv_w,
    recv_e,
    recv_s,
    local,
):
    here, side = peers()[:2]
    places = 16
    sibling = (here, 1 - side)
    peer_count = call_out(same_side(side, here) + [sibling])
    far = (wz_far, sg_far, wx_far, su_far, wo_far, sd_far, convx_far, biasx_far, gnorm_far)
    far += (bias_far, log_far, skip_far, norm1_far, norm2_far, convbc_far, biasbc_far)
    far += (hidden_far, cot_far, wbc_far, router_far, wdt_far, docs_far, routes_far)
    close = (wz_ref, sg_ref, wx_ref, su_ref, wo_ref, sd_ref, convx_ref, biasx_ref, gnorm_ref)
    close += (bias_ref, log_ref, skip_ref, norm1_ref, norm2_ref, convbc_ref, biasbc_ref)
    close += (hidden_ref, cot_ref, wbc_ref, router_ref, wdt_ref, docs_ref, routes_ref)
    loads = [pltpu.make_async_copy(*both, loaded.at[i]) for i, both in enumerate(zip(far, close))]
    for load in loads[6:] + loads[:6]:
        load.start()
    floats_ref[...] = jnp.zeros(floats_ref.shape, jnp.float32)
    misc_ref[...] = jnp.zeros(misc_ref.shape, jnp.float32)
    for load in loads[6:]:
        load.wait()
    f32, low = jnp.float32, jnp.bfloat16
    own_ref[0:64] = of_side(hidden_ref, side)
    own_ref[64:128] = of_side(cot_ref, side)
    mine_ref[:, 0:128] = jnp.where(side == 0, wbc_ref[:, 0:128], wbc_ref[:, 128:256])
    misc_ref[0:16, 0:96] = router_ref[...].astype(f32)
    misc_ref[16:40, 0:96] = wdt_ref[...].astype(f32)
    misc_ref[40:41, 0:64] = jnp.where(side == 0, docs_ref[0:1], docs_ref[1:2]).astype(f32)
    misc_ref[41:47, 0:64] = jnp.where(side == 0, routes_ref[0], routes_ref[1]).astype(f32)
    mine_ref[:, 128:256] = misc_ref[...].T[0:96].astype(low)
    floats_ref[0:4] = convx_ref[...]
    floats_ref[4:5] = biasx_ref[...][None, :]
    floats_ref[5:6] = gnorm_ref[...][None, :]
    floats_ref[6:7, 0:24] = bias_ref[...][None, :]
    floats_ref[6:7, 24:48] = log_ref[...][None, :]
    floats_ref[6:7, 48:72] = skip_ref[...][None, :]
    floats_ref[7:8] = norm1_ref[...][None, :]
    floats_ref[8:9] = norm2_ref[...][None, :]
    floats_ref[9:13, 0:256] = convbc_ref[...]
    floats_ref[13:14, 0:256] = biasbc_ref[...][None, :]
    x = own_ref[0:64].astype(jnp.float32)
    scale = lax.rsqrt(jnp.mean(x * x, axis=-1, keepdims=True) + EPS)
    n1_ref[...] = (x * scale * floats_ref[7:8]).astype(jnp.bfloat16)
    pl.semaphore_wait(pltpu.get_barrier_semaphore(), peer_count)
    depth = blocks_ref.shape[1]
    rows, extra = n1_ref.shape[0], mine_ref.shape[0]
    half_here = here // 8
    mail = Mail(send)
    mine = pltpu.make_async_copy(n1_ref, rows_at(all_ref, here * rows, rows, 16), local.at[0])
    mine.start()
    mine_too = pltpu.make_async_copy(
        mine_ref, rows_at(extras_ref, here * extra, extra, 16), local.at[18]
    )
    mine_too.start()

    def strip(place):
        return cols_ref.at[pl.ds(pl.multiple_of(place * depth, 16), depth), pl.ds(0, 768)]

    steps = gather_steps(mail, n1_ref, all_ref, recv, recv_half, rows, rows // 2)
    steps_too = gather_steps(mail, mine_ref, extras_ref, recv_m, recv_half_m, extra)
    next(steps_too)
    next(steps)
    mail.put(floats_ref.at[pl.ds(0, 8)], small_other, recv_s.at[0], sibling)
    for load in loads[:6]:
        load.wait()
    for j in range(8):
        at = 0
        for width, ref in (
            (192, wo_ref),
            (64, sd_ref),
            (192, wz_ref),
            (64, sg_ref),
            (192, wx_ref),
            (64, su_ref),
        ):
            blocks_ref[j, :, at : at + width] = ref[:, width * j : width * (j + 1)]
            at += width
    first = 8 * side + lax.rem(here, 8)
    is_mine = side == half_here
    def send_strip(k):
        to = 8 * side + lax.rem(here + k, 8)
        mail.put(blocks_ref.at[to - 8 * side], strip(here), recv_w.at[here], (to, side))

    send_strip(1)

    def keep():
        return pltpu.make_async_copy(blocks_ref.at[here - 8 * side], strip(here), local.at[1])

    def give():
        block = blocks_ref.at[first - 8 * side]
        return remote(block, strip(here), local.at[1], recv_w.at[here], (first, side))

    @pl.when(is_mine)
    def _():
        keep().start()

    @pl.when(jnp.logical_not(is_mine))
    def _():
        give().start()

    mail.put(gate_ref, gate_other, recv_s.at[1], sibling)
    mail.put(up_ref, up_other, recv_s.at[2], sibling)
    mail.put(down_ref, down_other, recv_s.at[3], sibling)
    def forward(place, k):
        return remote(strip(place), strip(place), local.at[2 + k], recv_w.at[place], sibling)

    def pass_on(k):
        place = lax.rem(here + k, places)
        forward(place, k).wait_recv()

        @pl.when(is_mine)
        def _():
            forward(place, k).start()

    turn = 0
    for _ in steps_too:
        next(steps)
        turn += 1
        if turn < 7:
            send_strip(turn + 1)
        if turn == 6:

            @pl.when(is_mine)
            def _():
                keep().wait()
                forward(here, 0).start()

            @pl.when(jnp.logical_not(is_mine))
            def _():
                forward(here, 0).wait_recv()
                give().wait_send()

    for _ in steps:
        pass
    mine.wait()
    mine_too.wait()
    for place in range(places):
        at = pl.ds(place * extra, extra)
        mail.put(extras_ref.at[at], extra_ref.at[at], recv_e.at[place], sibling)
    for k in range(1, places):
        pass_on(k)

    @pl.when(is_mine)
    def _():
        for k in range(places):
            forward(lax.rem(here + k, places), k).wait_send()

    mail.arrived(small_other, recv_s.at[0])
    mail.arrived(gate_other, recv_s.at[1])
    mail.arrived(up_other, recv_s.at[2])
    mail.arrived(down_other, recv_s.at[3])
    for place in range(places):
        mail.arrived(extra_ref.at[pl.ds(place * extra, extra)], recv_e.at[place])
    cols_ref[:, pl.ds(pl.multiple_of(768 + side * 128, 128), 128)] = extras_ref[:, 0:128]
    cols_ref[:, pl.ds(pl.multiple_of(896 - side * 128, 128), 128)] = extra_ref[:, 0:128]
    is_own = side == half_here
    cols_ref[:, 1024:1152] = jnp.where(is_own, extras_ref[:, 128:256], extra_ref[:, 128:256])
    mail.finish()


def enter(*args):
    low, f32 = jnp.bfloat16, jnp.float32
    return call(
        enter_kernel,
        "enter",
        1,
        (
            ((1024, 1536), low),
            ((1536, 256), low),
            ((1536, 256), low),
            ((1536, 1152), low),
            ((128, 1536), low),
            ((16, 1536), f32),
            ((8, 1536), f32),
            ((1536, 256), low),
            ((1536, 256), low),
            ((256, 1536), low),
        ),
        [
            VMEM((64, 1536), low),
            VMEM((96, 256), low),
            VMEM((128, 128), f32),
            VMEM((8, 96, 768), low),
        ]
        + [VMEM(array.shape, array.dtype) for array in args[:23]]
        + [
            DMA((23,)),
            DMA((87,)),
            DMA((22,)),
            DMA((8,)),
            DMA((22,)),
            DMA((8,)),
            DMA((16,)),
            DMA((16,)),
            DMA((4,)),
            DMA((19,)),
        ],
        args,
        (range(26), (7, 8, 9)),
        limit=12,
    )


FAR_FIRST = (8, 7, 9, 6, 10, 5, 11, 4, 12, 3, 13, 2, 14, 1, 15)


def leave_kernel(
    main_ref,
    bcr_ref,
    small_ref,
    block_ref,
    input_ref,
    main_parts,
    bcr_out,
    small_all,
    block_other,
    input_other,
    got_main,
    got_bcr,
    bcr_part,
    bcr_mine,
    bcr_sib,
    small_got,
    small_sum,
    *refs,
):
    got, sums, refs = refs[:5], refs[5:8], refs[8:]
    send, recv_sib, recv_main, recv_small, recv_pair, cond, r_send, r_recv = refs
    here, side = peers()[:2]
    sibling = (here, 1 - side)
    is_main = side == here // 8
    f32 = jnp.float32
    greet(same_side(side, here) + [sibling])
    mail = Mail(send)
    mail.put(small_ref, small_got, recv_sib.at[1], sibling)

    def give_main():
        return remote(main_ref, got_main, cond.at[0], recv_sib.at[0], sibling)

    def send_on(total, out, sem, slot, k):
        to = lax.rem(here + k, 16)
        return remote(total.at[to], out.at[slot], cond.at[k], sem.at[slot], (to, side))

    slot = lax.rem(here, 8)

    half = bcr_ref.at[:, pl.ds(pl.multiple_of((1 - side) * 128, 128), 128)]
    mail.put(half, got_bcr, recv_sib.at[5], sibling)

    @pl.when(jnp.logical_not(is_main))
    def _():
        give_main().start()

    mail.put(block_ref, block_other, recv_sib.at[3], sibling)
    mail.put(input_ref, input_other, recv_sib.at[4], sibling)
    mail.arrived(small_got, recv_sib.at[1])
    small_sum[...] = small_ref[...] + small_got[...]
    small_all[side, here] = small_sum[side]
    for k in range(1, 16):
        to = lax.rem(here + k, 16)
        mail.put(small_sum.at[side], small_all.at[side, here], recv_small.at[here], (to, side))

    mail.arrived(got_bcr, recv_sib.at[5])
    mine = bcr_ref[:, pl.ds(pl.multiple_of(side * 128, 128), 128)]
    bcr_part[:, 0:128] = (mine.astype(f32) + got_bcr[...].astype(f32)).astype(bcr_part.dtype)
    bcr_part[:, 128:256] = bcr_ref[:, 256:384]
    r_mail = Mail(r_send)
    steps = reduce_steps(r_mail, bcr_part, bcr_mine, got, sums, r_recv, 96)
    next(steps)
    next(steps)

    def hand_back(first, last):
        @pl.when(is_main)
        def _():
            if first == 1:
                give_main().wait_recv()
            for k in FAR_FIRST[first - 1 : last - 1]:
                to = lax.rem(here + k, 16)
                total = main_ref[to].astype(f32) + got_main[to].astype(f32)
                got_main[to] = total.astype(got_main.dtype)
                send_on(got_main, main_parts, recv_main, slot, k).start()
            if last == 16:
                total = main_ref[here].astype(f32) + got_main[here].astype(f32)
                main_parts[slot] = total.astype(main_parts.dtype)

    hand_back(1, 3)
    for j in range(6):
        next(steps)
        hand_back(3 + 2 * j, 5 + 2 * j)
    hand_back(15, 16)
    for _ in steps:
        pass
    mail.put(bcr_mine, bcr_sib, recv_sib.at[2], sibling)
    for k in range(1, 16):
        place = lax.rem(here + k, 16)
        mail.arrived(small_all.at[side, place], recv_small.at[place])
    mail.put(small_all.at[side], small_all.at[side], recv_pair, sibling)
    mail.arrived(small_all.at[1 - side], recv_pair)
    for j in range(8):

        @pl.when(8 * side + j != here)
        def _():
            mail.arrived(main_parts.at[j], recv_main.at[j])

    mail.arrived(bcr_sib, recv_sib.at[2])
    bcr_out[:, pl.ds(pl.multiple_of(side * 128, 128), 128)] = bcr_mine[:, 0:128]
    bcr_out[:, pl.ds(pl.multiple_of((1 - side) * 128, 128), 128)] = bcr_sib[:, 0:128]
    bcr_out[:, 256:384] = bcr_mine[:, 128:256] + bcr_sib[:, 128:256]
    mail.arrived(block_other, recv_sib.at[3])
    mail.arrived(input_other, recv_sib.at[4])

    @pl.when(is_main)
    def _():
        for k in range(1, 16):
            send_on(got_main, main_parts, recv_main, slot, k).wait_send()

    @pl.when(jnp.logical_not(is_main))
    def _():
        give_main().wait_send()

    r_mail.finish()
    mail.finish()


def leave(*args):
    low, f32 = jnp.bfloat16, jnp.float32
    return call(
        leave_kernel,
        "leave",
        5,
        (
            ((8, 96, 768), low),
            ((96, 384), f32),
            ((2, 16, 8, 512), f32),
            ((64, 1536), f32),
            ((64, 1536), f32),
        ),
        [
            VMEM((16, 96, 768), low),
            VMEM((1536, 128), low),
            VMEM((1536, 256), low),
            VMEM((96, 256), f32),
            VMEM((96, 256), f32),
            VMEM((2, 8, 512), f32),
            VMEM((2, 8, 512), f32),
        ]
        + reduce_scratch(96, 256, low)
        + [
            DMA((21,)),
            DMA((6,)),
            DMA((8,)),
            DMA((16,)),
            DMA,
            DMA((16,)),
            DMA((27,)),
            DMA((27,)),
        ],
        args,
        limit=10,
    )


CHUNK = 128
LAYER = 256
HEADW = 64


def mm(left, right, low=True, exact=False):
    return mm_of(left, right, ((1,), (0,)), low, exact)


def mm_nt(left, right, low=True, exact=False):
    return mm_of(left, right, ((1,), (1,)), low, exact)


def mm_tn(left, right, low=True, exact=False):
    return mm_of(left, right, ((0,), (0,)), low, exact)


def mm_of(left, right, dims, low, exact):
    if exact:
        return lax.dot_general(
            left, right, (dims, ((), ())), precision=HIGH, preferred_element_type=jnp.float32
        )
    if low:
        left, right = left.astype(jnp.bfloat16), right.astype(jnp.bfloat16)
    return lax.dot_general(left, right, (dims, ((), ())), preferred_element_type=jnp.float32)


def lanes(shape):
    return lax.broadcasted_iota(jnp.int32, shape, 1)


def by_head(parts, rows):
    lane = lanes((rows, 3 * HEADW))
    return jnp.where(lane < HEADW, parts[0], jnp.where(lane < 2 * HEADW, parts[1], parts[2]))


def spread_heads(array):
    return by_head([array[:, h : h + 1] for h in range(3)], array.shape[0])


def soft_plus(values):
    return jnp.maximum(values, 0.0) + jnp.log1p(jnp.exp(-jnp.abs(values)))


def chunk_tables(step, log_rate, doc_col, doc_row):
    row = lax.broadcasted_iota(jnp.int32, (CHUNK, CHUNK), 0)
    col = lax.broadcasted_iota(jnp.int32, (CHUNK, CHUNK), 1)
    below = (row >= col).astype(jnp.float32)
    logs = mm(below, step * log_rate, exact=True)
    logs_t, step_t = logs.T, step.T
    pair = (row >= col) & (doc_col == doc_row)
    tables = [
        jnp.exp(jnp.where(pair, logs[:, h : h + 1] - logs_t[h : h + 1], -1e9)) for h in range(3)
    ]
    return logs, tables, [step_t[h : h + 1] for h in range(3)]


def as_column(row):
    return jnp.concatenate([row, jnp.zeros((CHUNK - 8, CHUNK), jnp.float32)], 0).T


def as_row(column):
    wide = jnp.broadcast_to(column, (64, CHUNK))
    return jnp.concatenate([wide, jnp.zeros((64, CHUNK), jnp.float32)], 0).T[0:8]


KEPT = dict(z=(0, 192), y=(256, 192), dt=(512, 128), ids=(640, 128), ext=(768, 448), state=(1280, 192))


class Part:
    def __init__(self, ref, lane, width, row=0, height=None):
        self.ref, self.lane, self.width, self.row = ref, lane, width, row
        self.height = ref.shape[0] if height is None else height

    def at_of(self, index):
        rows, cols = index if isinstance(index, tuple) else (index, slice(None))
        if rows is Ellipsis:
            rows = slice(None)
        if isinstance(rows, slice):
            stop = self.height if rows.stop is None else rows.stop
            rows = slice(self.row + (rows.start or 0), self.row + stop)
        stop = self.width if cols.stop is None else cols.stop
        return rows, slice(self.lane + (cols.start or 0), self.lane + stop)

    def __getitem__(self, index):
        return self.ref[self.at_of(index)]

    def __setitem__(self, index, value):
        self.ref[self.at_of(index)] = value


def kept_views(kept_ref):
    return [Part(kept_ref, *KEPT[name]) for name in ("z", "y", "dt", "ids", "ext", "state")]


def const_views(consts_ref):
    return [
        Part(consts_ref, 0, 448, 0, 8),
        Part(consts_ref, 0, 128, 8, 8),
        Part(consts_ref, 128, 192, 8, 8),
    ]


def mix_forward_kernel(
    n1_ref,
    extras_ref,
    cols_ref,
    floats_ref,
    small_other,
    own_ref,
    kept_far,
    g_all_ref,
    n2_ref,
    note_ref,
    res_ref,
    scale_ref,
    ids_out,
    consts_ref,
    part_ref,
    gained_ref,
    notes_ref,
    sum_ref,
    notes_out,
    kept_ref,
    kept_sem,
    *refs,
):
    z_ref, y_ref, dt_ref, ids_ref, ext_ref, state_ref = kept_views(kept_ref)
    taps_ref, head_ref, gain_ref = const_views(consts_ref)
    g_ref = own_ref.at[pl.ds(64, 64)]
    got, sums, refs = refs[:5], refs[5:8], refs[8:]
    send, recv, recv_n, g_send, g_recv, g_recv_half, local = refs
    here, side, z_at = peers()[:3]
    half_here, slot = here // 8, lax.rem(here, 8)
    greet(same_side(side, here))
    low, f32 = jnp.bfloat16, jnp.float32
    mine = pltpu.make_async_copy(g_ref, rows_at(g_all_ref, here * 64, 64, 16), local)
    mine.start()
    g_mail = Mail(g_send)
    g_steps = gather_steps(g_mail, g_ref, g_all_ref, g_recv, g_recv_half, 64, 32)
    next(g_steps)

    small = jnp.where(side == half_here, floats_ref[0:8], small_other[...])
    turned = pltpu.roll(small, lax.rem(1536 - 192 * slot, 1536), 1)
    taps_ref[0:5, 0:256] = floats_ref[9:14, 0:256]
    taps_ref[5:8] = jnp.zeros((3, 448), f32)
    taps_ref[0:5, 256:448] = turned[0:5, 0:192]
    gain_ref[...] = jnp.broadcast_to(turned[5:6, 0:192], (8, 192))
    numbers = pltpu.roll(small[:, 0:128], lax.rem(128 - 3 * slot, 128), 1)[6:7]
    used = lanes((1, 128)) < 3
    head_ref[0:1] = jnp.where(used, numbers, 0.0)
    head_ref[1:2] = jnp.where(used, -jnp.exp(pltpu.roll(numbers, 104, 1)), 0.0)
    head_ref[2:3] = jnp.where(used, pltpu.roll(numbers, 80, 1), 0.0)
    ids_ref[0:8] = jnp.full((8, 128), -1.0, f32)
    ids_ref[1032:1040] = jnp.full((8, 128), -2.0, f32)
    for p in range(16):
        ids_ref[8 + 64 * p : 72 + 64 * p] = extras_ref[96 * p : 96 * p + 64, 128:256].astype(f32)
    ids_out[...] = ids_ref[...]
    notes_ref[...] = jnp.zeros(notes_ref.shape, f32)
    ext_ref[0:8] = jnp.zeros((8, 448), f32)

    @pl.loop(0, 4)
    def _(i):
        at = pl.ds(pl.multiple_of(i * LAYER, LAYER), LAYER)
        shifted = pl.ds(pl.multiple_of(i * LAYER + 8, 8), LAYER)
        rows = n1_ref[at]
        proj = mm(rows, cols_ref[:, 256:1152])
        z_ref[at] = proj[:, 0:192]
        ext_ref[shifted, 0:256] = proj[:, 512:768]
        ext_ref[shifted, 256:448] = proj[:, 256:448]
        dt_ref[at] = pltpu.roll(proj[:, 768:896], 112 - 3 * slot, 1) + head_ref[0:1]

    next(g_steps)
    rate, skip = head_ref[1:2], spread_heads(head_ref[2:3])
    state = jnp.zeros((128, 192), f32)
    ones = jnp.ones((8, 192), f32)
    for c in range(8):
        r = c * CHUNK
        at = pl.ds(r, CHUNK)
        ids = ids_ref[pl.ds(r + 8, CHUNK)]
        doc = ids[:, 40:41]
        pre = conv_pre(taps_ref, ext_ref, ids_ref, r, doc)
        act = pre * jax.nn.sigmoid(pre)
        b, cc, x = act[:, 0:128], act[:, 128:256], act[:, 256:448]
        step = soft_plus(dt_ref[at])
        logs, tables, step_t = chunk_tables(step, rate, doc, ids.T[40:41])
        cross = mm_nt(cc, b)
        stacked = jnp.concatenate([cross * tables[h] * step_t[h] for h in range(3)], 0)
        intra = mm(stacked, x)
        y = by_head([intra[h * CHUNK : (h + 1) * CHUNK] for h in range(3)], CHUNK)
        first, last = chunk_masks(ids_ref, r, doc)
        enters = jnp.exp(logs) * first
        state_ref[at] = state
        y = y + spread_heads(enters) * mm(cc, state) + skip * x
        y_ref[at] = y
        tail = jnp.exp(logs[CHUNK - 1 :] - logs) * last * step
        state = spread_heads(enters[CHUNK - 1 :]) * state + mm_tn(b, spread_heads(tail) * x)
        z = z_ref[at]
        gated = y * z * jax.nn.sigmoid(z)
        gained_ref[at] = (gated * gain_ref[0:1]).astype(low)
        squares = mm_nt(ones, gated * gated, exact=True)
        notes_ref[2 * c, :, 0:64] = squares[:, 0:64]
        notes_ref[2 * c + 1, :, 0:64] = squares[:, 64:128]
        next(g_steps, None)

    keep = pltpu.make_async_copy(kept_ref, kept_far, kept_sem)
    keep.start()
    mail = Mail(send)
    zs = layers(z_at)

    def layer(k):
        at = pl.ds(pl.multiple_of(zs[k] * LAYER, LAYER), LAYER)

        @pl.loop(0, 3)
        def _(i):
            n = pl.ds(pl.multiple_of(i * 512, 512), 512)
            part_ref[at, n] = mm_nt(gained_ref[at], cols_ref[n, 0:192]).astype(low)

    steps = reduce_steps(mail, part_ref, sum_ref, got, sums, recv, 64)
    left = [3, 2, 1, 0]
    for turn in range(13):
        if turn in (0, 2, 5, 8):
            layer(left.pop(0))
        next(steps, None)
        if turn == 0:
            notes_out[here] = notes_ref[here]
            note_puts(mail, lambda to: notes_ref.at[to], notes_out, recv_n)
        if turn > 2:
            next(g_steps, None)
    for _ in g_steps:
        pass
    for _ in steps:
        pass
    note_waits(mail, notes_out, recv_n)
    squares = notes_out[0]
    for j in range(1, 16):
        squares = squares + notes_out[j]
    scale_row = lax.rsqrt(squares / INNER + EPS)
    note_ref[...] = scale_row
    scale = as_column(scale_row)[0:64, 0:1]
    scale_ref[...] = jnp.broadcast_to(scale, (64, 128))
    projected = scale * sum_ref[...]
    res_ref[64:128] = projected
    residual = own_ref[0:64].astype(f32) + projected
    res_ref[0:64] = residual
    scale_two = lax.rsqrt(jnp.mean(residual * residual, axis=-1, keepdims=True) + EPS)
    n2_ref[...] = (residual * scale_two * floats_ref[8:9]).astype(low)
    keep.wait()
    mine.wait()
    g_mail.finish()
    mail.finish()


def conv_pre(taps_ref, ext_ref, ids_ref, r, doc):
    pre = taps_ref[4:5] + taps_ref[3:4] * ext_ref[pl.ds(r + 8, CHUNK)]
    for k in (1, 2, 3):
        same = (ids_ref[pl.ds(r + 8 - k, CHUNK), 40:41] == doc).astype(jnp.float32)
        pre = pre + taps_ref[3 - k : 4 - k] * ext_ref[pl.ds(r + 8 - k, CHUNK)] * same
    return pre


def chunk_masks(ids_ref, r, doc):
    first = (ids_ref[r + 7 : r + 8, 40:41] == doc).astype(jnp.float32)
    last = (ids_ref[r + 7 + CHUNK : r + 8 + CHUNK, 40:41] == doc).astype(jnp.float32)
    return first, last


def mix_forward(*args):
    low, f32 = jnp.bfloat16, jnp.float32
    return call(
        mix_forward_kernel,
        "mix_forward",
        2,
        (
            ((1040, 1536), f32),
            ((1024, 1536), low),
            ((64, 1536), low),
            ((8, 128), f32),
            ((128, 1536), f32),
            ((64, 128), f32),
            ((1040, 128), f32),
            ((16, 512), f32),
        ),
        [
            VMEM((1024, 1536), low),
            VMEM((1024, 192), low),
            VMEM((16, 8, 128), f32),
            VMEM((64, 1536), f32),
            VMEM((16, 8, 128), f32),
            VMEM((1040, 1536), f32),
            DMA,
        ]
        + reduce_scratch(64, 1536, low)
        + [
            DMA((42,)),
            DMA((27,)),
            DMA((16,)),
            DMA((30,)),
            DMA((22,)),
            DMA((8,)),
            DMA,
        ],
        args,
        ((), (0,)),
        limit=24,
    )


def moe_kernel(
    own_ref,
    scale_note_ref,
    g_ref,
    cols_ref,
    eg_far,
    ego_far,
    eu_far,
    euo_far,
    ed_far,
    edo_far,
    extras_ref,
    ids_ref,
    res_ref,
    scale_ref,
    floats_ref,
    mine_ref,
    dres_ref,
    pair_ref,
    moe_ref,
    geg_far,
    geu_far,
    ged_far,
    sg_ref,
    su_ref,
    sd_ref,
    shared_ref,
    dres_own_ref,
    n2_ref,
    act_ref,
    hid_ref,
    probs_ref,
    notes_ref,
    notes_out,
    sum_ref,
    low_ref,
    note_ref,
    og_ref,
    ou_ref,
    od_ref,
    geg_ref,
    geu_ref,
    ged_ref,
    up_ref,
    down_ref,
    both_ref,
    loaded,
    *refs,
):
    got, sums, refs = refs[:5], refs[5:8], refs[8:]
    send, recv, recv_n, d_send, d_recv, d_recv_half, d_recv_n = refs[:7]
    n_send, n_recv, n_recv_half, n_recv_n, e_send, e_recv, local = refs[7:]
    cross_ref, scales_ref = pair_ref.at[0], pair_ref.at[1]
    loads = [
        pltpu.make_async_copy(far, close, loaded.at[i])
        for i, (far, close) in enumerate(
            (
                (eg_far, up_ref.at[:, pl.ds(0, 256)]),
                (ego_far, up_ref.at[:, pl.ds(256, 256)]),
                (eu_far, up_ref.at[:, pl.ds(640, 256)]),
                (euo_far, up_ref.at[:, pl.ds(896, 256)]),
                (ed_far, down_ref.at[pl.ds(0, 256)]),
                (edo_far, down_ref.at[pl.ds(256, 256)]),
            )
        )
    ]
    for load in loads:
        load.start()
    here, side, z_at = peers()[:3]
    sibling = (here, 1 - side)
    greet(same_side(side, here) + [sibling])
    low, f32 = jnp.bfloat16, jnp.float32
    zs = layers(z_at)
    keep = pltpu.make_async_copy(own_ref, rows_at(n2_ref, here * 64, 64, 16), local.at[1])
    keep.start()
    n_mail = Mail(n_send)
    n_steps = gather_steps(n_mail, own_ref, n2_ref, n_recv, n_recv_half, 64, 32)
    next(n_steps)
    scales_ref[here] = scale_note_ref[...]
    note_puts(n_mail, lambda to: scale_note_ref, scales_ref, n_recv_n)
    notes_ref[...] = jnp.zeros(notes_ref.shape, f32)
    lane = lanes((LAYER, 128))
    lane640 = lanes((LAYER, 640))
    up_ref[:, 512:640] = cols_ref[:, 384:512]
    up_ref[:, 1152:1280] = cols_ref[:, 640:768]
    for i in range(12):
        n = slice(128 * i, 128 * (i + 1))
        down_ref[512:640, n] = cols_ref[n, 128:256].astype(f32).T.astype(low)
    for load in loads:
        load.wait()

    def layer(k, piece):
        start = pl.multiple_of(zs[k] * LAYER, LAYER)
        at = pl.ds(start, LAYER)
        if piece == 0:
            rows = n2_ref[at]
            logits = mm(rows, extras_ref[:, 128:256])
            ids = ids_ref[pl.ds(pl.multiple_of(start + 8, 8), LAYER)]
            named = jnp.zeros((LAYER, 128), f32)
            for j in range(6):
                named = jnp.where(lane.astype(f32) == ids[:, 41 + j : 42 + j], 1.0, named)
            top = jnp.max(jnp.where(named > 0, logits, -1e30), axis=-1, keepdims=True)
            raised = jnp.exp(jnp.where(named > 0, logits - top, 0.0)) * named
            probs_ref[at] = raised / jnp.sum(raised, axis=-1, keepdims=True)
            both_ref[...] = mm(rows, up_ref[...])
            return
        if piece == 1:
            chosen = jnp.where(lane == here, probs_ref[at], 0.0)
            prob = jnp.sum(chosen, axis=-1, keepdims=True)
            weight = jnp.where(lane640 < 512, prob, jnp.where(lane640 < 576, 0.0, 1.0))
            gate, up = both_ref[:, 0:640], both_ref[:, 640:1280]
            d_act = mm_nt(g_ref[at], down_ref[...])
            sig = jax.nn.sigmoid(gate)
            act = gate * sig * up
            act_ref[at] = (act * weight).astype(low)
            slopes = jnp.sum((act * d_act)[:, 0:512], axis=-1, keepdims=True)
            d_act = d_act * weight
            hid_ref[at, 0:640] = (d_act * up * silu_slope(gate, sig)).astype(low)
            hid_ref[at, 640:1280] = (d_act * gate * sig).astype(low)
            for j in range(4):
                notes_ref[4 * zs[k] + j] = as_row(slopes[64 * j : 64 * (j + 1)])
            return

        @pl.loop(0, 3)
        def _(i):
            n = pl.ds(pl.multiple_of(i * 512, 512), 512)
            moe_ref[at, n] = mm_nt(hid_ref[at], up_ref[n]).astype(low)

    e_mail = Mail(e_send)

    def up_grads(first, last):
        @pl.loop(first, last)
        def _(i):
            n = pl.ds(pl.multiple_of(i * 256, 256), 256)
            total = mm_tn(n2_ref[:, n], hid_ref[...])
            geg_ref[n] = total[:, 0:256]
            og_ref[n] = total[:, 256:512].astype(low)
            shared_ref[n, 0:128] = total[:, 512:640].astype(low)
            geu_ref[n] = total[:, 640:896]
            ou_ref[n] = total[:, 896:1152].astype(low)
            shared_ref[n, 128:256] = total[:, 1152:1280].astype(low)

    def give_up():
        e_mail.put(og_ref, sg_ref, e_recv.at[0], sibling)
        e_mail.put(ou_ref, su_ref, e_recv.at[1], sibling)

    def down_grads():
        od_ref[...] = mm_tn(act_ref[:, 256:512], g_ref[...]).astype(low)
        e_mail.put(od_ref, sd_ref, e_recv.at[2], sibling)
        ged_ref[...] = mm_tn(act_ref[:, 0:256], g_ref[...])

    def shared_down():
        @pl.loop(0, 6)
        def _(i):
            n = pl.ds(pl.multiple_of(i * 256, 256), 256)
            shared_ref[n, 256:384] = mm_tn(g_ref[:, n], act_ref[:, 512:640]).astype(low)

    def moe_part(first, last):
        @pl.loop(first, last)
        def _(i):
            at = pl.ds(pl.multiple_of(i * LAYER, LAYER), LAYER)
            total = mm(act_ref[at], down_ref[...])
            moe_ref[at] = total.astype(low)

    mail = Mail(send)
    steps = reduce_steps(mail, moe_ref, sum_ref, got, sums, recv, 64)

    for _ in range(4):
        next(n_steps)
    keep.wait()
    for j in range(4):
        layer(j, 0)
        next(n_steps, None)
        layer(j, 1)
        next(n_steps, None)
        layer(j, 2)
        next(n_steps, None)
    for turn in range(10):
        next(steps)
        if turn == 1:
            notes_out[here] = notes_ref[here]
            note_puts(mail, lambda to: notes_ref.at[to], notes_out, recv_n)
    up_grads(0, 3)
    next(steps)
    for _ in steps:
        pass
    note_waits(mail, notes_out, recv_n)

    slopes = jnp.concatenate([notes_out[j, 0:1] for j in range(16)], 0)
    slopes = jnp.concatenate([slopes, jnp.zeros((112, 128), f32)], 0).T[0:64]
    own = pl.ds(pl.multiple_of(here * 64, 64), 64)
    probs = probs_ref[own]
    d_logits = probs * (slopes - jnp.sum(probs * slopes, axis=-1, keepdims=True))
    d_logits = d_logits.astype(low)
    shared_ref[:, 384:512] = mm_tn(n2_ref[own], d_logits).astype(low)
    dn2 = sum_ref[...] + mm_nt(d_logits, extras_ref[:, 128:256])
    value, gain = norm_step(dn2, res_ref[0:64], floats_ref[8:9])
    dres_own_ref[64:72] = jnp.broadcast_to(gain, (8, 1536))
    d_res = mine_ref[64:128].astype(f32) + value
    dres_own_ref[0:64] = d_res
    low_ref[...] = d_res.astype(low)
    cross = jnp.sum(low_ref[...].astype(f32) * res_ref[64:128], axis=-1, keepdims=True)
    note_ref[...] = as_row(cross / scale_ref[:, 0:1])
    mine = pltpu.make_async_copy(low_ref, rows_at(dres_ref, here * 64, 64, 16), local.at[0])
    mine.start()
    d_mail = Mail(d_send)
    d_steps = gather_steps(d_mail, low_ref, dres_ref, d_recv, d_recv_half, 64, 32)
    next(d_steps)
    cross_ref[here] = note_ref[...]
    note_puts(d_mail, lambda to: note_ref, cross_ref, d_recv_n)
    next(d_steps)
    mail.finish()
    for i in range(3):
        up_grads(3 + i, 4 + i)
        next(d_steps)
    give_up()
    down_grads()
    next(d_steps)
    stores = [
        pltpu.make_async_copy(geg_ref, geg_far, local.at[2]),
        pltpu.make_async_copy(geu_ref, geu_far, local.at[3]),
        pltpu.make_async_copy(ged_ref, ged_far, local.at[4]),
    ]
    for store in stores:
        store.start()
    for i in range(4):
        moe_part(i, i + 1)
        next(d_steps)
    shared_down()
    for _ in d_steps:
        pass
    e_mail.arrived(sg_ref, e_recv.at[0])
    e_mail.arrived(su_ref, e_recv.at[1])
    e_mail.arrived(sd_ref, e_recv.at[2])
    note_waits(n_mail, scales_ref, n_recv_n)
    note_waits(d_mail, cross_ref, d_recv_n)
    mine.wait()
    for store in stores:
        store.wait()
    n_mail.finish()
    e_mail.finish()
    d_mail.finish()


def norm_step(grad, values, gain):
    scale = lax.rsqrt(jnp.mean(values * values, axis=-1, keepdims=True) + EPS)
    gain_grad = jnp.sum(grad * values * scale, axis=0, keepdims=True)
    scaled = grad * gain
    pull = scale * scale * scale * jnp.mean(scaled * values, axis=-1, keepdims=True)
    return scale * scaled - values * pull, gain_grad


def moe(*args):
    low, f32 = jnp.bfloat16, jnp.float32
    return call(
        moe_kernel,
        "moe",
        3,
        (
            ((1024, 1536), low),
            ((2, 16, 8, 128), f32),
            ((1024, 1536), low),
            ((1536, 256), f32),
            ((1536, 256), f32),
            ((256, 1536), f32),
            ((1536, 256), low),
            ((1536, 256), low),
            ((256, 1536), low),
            ((1536, 512), low),
            ((72, 1536), f32),
        ),
        [
            VMEM((1024, 1536), low),
            VMEM((1024, 640), low),
            VMEM((1024, 1280), low),
            VMEM((1024, 128), f32),
            VMEM((16, 8, 128), f32),
            VMEM((16, 8, 128), f32),
            VMEM((64, 1536), f32),
            VMEM((64, 1536), low),
            VMEM((8, 128), f32),
            VMEM((1536, 256), low),
            VMEM((1536, 256), low),
            VMEM((256, 1536), low),
            VMEM((1536, 256), f32),
            VMEM((1536, 256), f32),
            VMEM((256, 1536), f32),
            VMEM((1536, 1280), low),
            VMEM((640, 1536), low),
            VMEM((LAYER, 1280), f32),
            DMA((6,)),
        ]
        + reduce_scratch(64, 1536, low)
        + [
            DMA((42,)),
            DMA((27,)),
            DMA((16,)),
            DMA((45,)),
            DMA((22,)),
            DMA((8,)),
            DMA((16,)),
            DMA((45,)),
            DMA((22,)),
            DMA((8,)),
            DMA((16,)),
            DMA((3,)),
            DMA((3,)),
            DMA((5,)),
        ],
        args,
        (range(4, 10), (3, 4, 5, 6, 7, 8)),
        limit=36,
    )


def mix_backward_kernel(
    dres_ref,
    pair_ref,
    n1_far,
    cols_ref,
    consts_ref,
    kept_far,
    moe_ref,
    shared_ref,
    res_ref,
    dres_own_ref,
    own_ref,
    floats_ref,
    main_ref,
    bcr_ref,
    small_ref,
    block_ref,
    input_ref,
    part_ref,
    dm_ref,
    mixed_ref,
    din_ref,
    dpre_ref,
    sum_ref,
    n1_ref,
    kept_ref,
    loaded,
    *refs,
):
    got, sums, refs = refs[:5], refs[5:8], refs[8:]
    b_got, b_sums, refs = refs[:5], refs[5:8], refs[8:]
    send, recv, b_send, b_recv = refs
    loads = (
        pltpu.make_async_copy(kept_far, kept_ref, loaded.at[0]),
        pltpu.make_async_copy(n1_far, n1_ref, loaded.at[1]),
    )
    for load in loads:
        load.start()
    z_ref, y_ref, dt_ref, ids_ref, ext_ref, state_ref = kept_views(kept_ref)
    taps_ref, head_ref, gain_ref = const_views(consts_ref)
    cross_ref, scales_ref = pair_ref.at[0], pair_ref.at[1]
    here, side, z_at = peers()[:3]
    half_here, slot = here // 8, lax.rem(here, 8)
    greet(near(side))
    low, f32 = jnp.bfloat16, jnp.float32
    zs = layers(z_at)
    b_mail = Mail(b_send)
    order = [("far", 3), ("far", 2), ("joined", 3), ("far", 1), ("joined", 2), ("column", 3)]
    order += [("far", 0), ("joined", 1), ("column", 2), ("joined", 0), ("column", 1), ("column", 0)]
    b_steps = reduce_steps(b_mail, moe_ref, block_ref, b_got, b_sums, b_recv, 64, order)
    next(b_steps)

    @pl.loop(0, 4)
    def _(i):
        at = pl.ds(pl.multiple_of(i * LAYER, LAYER), LAYER)
        dm_ref[at] = mm(dres_ref[at], cols_ref[:, 0:192])

    next(b_steps)
    loads[0].wait()
    rate, skip = head_ref[1:2], spread_heads(head_ref[2:3])
    onehot = (
        lax.broadcasted_iota(jnp.int32, (192, 128), 0) // HEADW
        == lax.broadcasted_iota(jnp.int32, (192, 128), 1)
    ).astype(f32)
    row = lax.broadcasted_iota(jnp.int32, (CHUNK, CHUNK), 0)
    lane = lanes((CHUNK, CHUNK))
    above = (row <= lane).astype(f32)
    lane192 = lanes((CHUNK, 192))
    masks = [((lane192 // HEADW) == h).astype(f32) for h in range(3)]
    d_state = jnp.zeros((128, 192), f32)
    g_gain = jnp.zeros((1, 192), f32)
    g_skip = jnp.zeros((1, 192), f32)
    g_rate = jnp.zeros((1, 128), f32)
    g_dt = jnp.zeros((1, 128), f32)
    g_taps = [jnp.zeros((1, 448), f32) for _ in range(5)]
    dpre_ref[0:8] = jnp.zeros((8, 448), f32)
    din_ref[:, 128:256] = jnp.zeros((1024, 128), low)
    din_ref[:, 384:512] = jnp.zeros((1024, 128), low)
    mixed_ref[:, 128:256] = jnp.zeros((1024, 128), low)
    for c in range(7, -1, -1):
        r = c * CHUNK
        at = pl.ds(r, CHUNK)
        ids = ids_ref[pl.ds(r + 8, CHUNK)]
        doc = ids[:, 40:41]
        scale_row = jnp.concatenate(
            [scales_ref[2 * c, :, 0:64], scales_ref[2 * c + 1, :, 0:64]], 1
        )
        cross_row = jnp.concatenate([cross_ref[2 * c, :, 0:64], cross_ref[2 * c + 1, :, 0:64]], 1)
        scale = as_column(scale_row)[:, 0:1]
        pull = scale * scale * scale * as_column(cross_row)[:, 0:1] / INNER
        z, y, dm, gain = z_ref[at], y_ref[at], dm_ref[at], gain_ref[0:1]
        sig = jax.nn.sigmoid(z)
        gated = y * z * sig
        scaled = gated * scale
        mixed_ref[at, 0:192] = (scaled * gain).astype(low)
        g_gain = g_gain + jnp.sum(dm * scaled, axis=0, keepdims=True)
        d_gated = scale * gain * dm - gated * pull
        d_y = d_gated * z * sig
        din_ref[at, 0:192] = (d_gated * y * silu_slope(z, sig)).astype(low)
        pre = conv_pre(taps_ref, ext_ref, ids_ref, r, doc)
        pre_sig = jax.nn.sigmoid(pre)
        act = pre * pre_sig
        b, cc, x = act[:, 0:128], act[:, 128:256], act[:, 256:448]
        g_skip = g_skip + jnp.sum(d_y * x, axis=0, keepdims=True)
        dt = dt_ref[at]
        step = soft_plus(dt)
        logs, tables, step_t = chunk_tables(step, rate, doc, ids.T[40:41])
        cross = mm_nt(cc, b)
        decays = [tables[h] * step_t[h] for h in range(3)]
        stacked = jnp.concatenate([cross * decays[h] for h in range(3)], 0)
        d_ys = jnp.concatenate([d_y * masks[h] for h in range(3)], 0)
        d_stack = mm_nt(d_ys, x)
        d_x = skip * d_y + mm_tn(stacked, d_ys)
        state = state_ref[at]
        first, last = chunk_masks(ids_ref, r, doc)
        enters = jnp.exp(logs) * first
        d_in_y = spread_heads(enters) * d_y
        from_state = mm(cc, state)
        tail_w = jnp.exp(logs[CHUNK - 1 :] - logs) * last
        tail = tail_w * step
        tail_x = spread_heads(tail)
        to_state = mm(b, d_state)
        d_x = d_x + tail_x * to_state
        kept = enters[CHUNK - 1 :]
        d_kept = jnp.sum(d_state * state, axis=0, keepdims=True)
        folded = mm(
            jnp.concatenate(
                [d_y * from_state, x * to_state, jnp.broadcast_to(d_kept, (8, 192))], 0
            ),
            onehot,
            exact=True,
        )
        d_enters, d_tail = folded[:CHUNK], folded[CHUNK : 2 * CHUNK]
        d_kept = folded[2 * CHUNK : 2 * CHUNK + 1]
        d_cross = jnp.zeros((CHUNK, CHUNK), f32)
        row_sums = jnp.zeros((CHUNK, CHUNK), f32)
        col_sums = []
        for h in range(3):
            d_a = d_stack[h * CHUNK : (h + 1) * CHUNK]
            d_cross = d_cross + d_a * decays[h]
            plain = d_a * cross * tables[h]
            col_sums.append(jnp.sum(plain, axis=0, keepdims=True))
            total = jnp.sum(plain * step_t[h], axis=1, keepdims=True)
            row_sums = jnp.where(lane == h, total, row_sums)
        col_sums = as_column(jnp.concatenate(col_sums + [jnp.zeros((5, CHUNK), f32)], 0))
        d_c = mm(d_cross, b) + mm_nt(d_in_y, state)
        d_b = mm_tn(d_cross, cc) + mm_nt(tail_x * x, d_state)
        pulled = d_tail * tail
        d_logs = row_sums - step * col_sums + d_enters * enters - pulled
        d_last = jnp.sum(pulled, axis=0, keepdims=True) + d_kept * kept
        d_logs = d_logs + jnp.where(row == CHUNK - 1, d_last, 0.0)
        d_l = mm(above, d_logs, exact=True)
        d_step = col_sums + d_tail * tail_w + d_l * rate
        g_rate = g_rate + jnp.sum(d_l * step, axis=0, keepdims=True)
        d_dt = jnp.where(lane < 3, d_step * jax.nn.sigmoid(dt), 0.0)
        g_dt = g_dt + jnp.sum(d_dt, axis=0, keepdims=True)
        din_ref[at, 768:896] = pltpu.roll(d_dt, 16 + 3 * slot, 1).astype(low)
        d_state = spread_heads(kept) * d_state + mm_tn(cc, d_in_y)
        d_pre = jnp.concatenate([d_b, d_c, d_x], 1) * silu_slope(pre, pre_sig)
        dpre_ref[CHUNK : CHUNK + 8] = dpre_ref[0:8]
        dpre_ref[0:CHUNK] = d_pre
        g_taps[4] = g_taps[4] + jnp.sum(d_pre, axis=0, keepdims=True)
        g_taps[3] = g_taps[3] + jnp.sum(d_pre * ext_ref[pl.ds(r + 8, CHUNK)], axis=0, keepdims=True)
        d_ext = taps_ref[3:4] * d_pre
        for k in (1, 2, 3):
            same = (ids_ref[pl.ds(r + 8 - k, CHUNK), 40:41] == doc).astype(f32)
            g_taps[3 - k] = g_taps[3 - k] + jnp.sum(
                d_pre * same * ext_ref[pl.ds(r + 8 - k, CHUNK)], axis=0, keepdims=True
            )
            same = (ids_ref[pl.ds(r + 8 + k, CHUNK), 40:41] == doc).astype(f32)
            d_ext = d_ext + taps_ref[3 - k : 4 - k] * (dpre_ref[k : k + CHUNK] * same)
        din_ref[at, 512:768] = d_ext[:, 0:256].astype(low)
        din_ref[at, 256:448] = d_ext[:, 256:448].astype(low)
        next(b_steps, None)
    loads[1].wait()
    small_ref[...] = jnp.zeros((2, 8, 512), f32)
    for k in range(5):
        small_ref[1, k : k + 1, 0:448] = g_taps[k]
    small_ref[1, 5:6, 0:192] = g_gain
    small_ref[1, 5:6, 256:448] = g_skip
    small_ref[1, 6:7, 0:128] = g_dt
    small_ref[1, 6:7, 256:384] = g_rate * rate

    def layer(k):
        at = pl.ds(pl.multiple_of(zs[k] * LAYER, LAYER), LAYER)

        @pl.loop(0, 3)
        def _(i):
            n = pl.ds(pl.multiple_of(i * 512, 512), 512)
            part_ref[at, n] = mm_nt(din_ref[at], cols_ref[n, 256:1152]).astype(low)

    moved = 24 * half_here

    def grads(first, last):
        @pl.loop(first, last)
        def _(i):
            n = pl.ds(pl.multiple_of(i * 256, 256), 256)
            total = mm_tn(n1_ref[:, n], din_ref[...])
            out = mm_tn(dres_ref[:, n], mixed_ref[...])
            main_ref[n, 0:128] = out[:, 0:128].astype(low)
            main_ref[n, 128:256] = out[:, 128:256].astype(low) + shared_ref[n, 256:384]
            main_ref[n, 256:384] = total[:, 0:128].astype(low)
            main_ref[n, 384:512] = total[:, 128:256].astype(low) + shared_ref[n, 0:128]
            main_ref[n, 512:640] = total[:, 256:384].astype(low)
            main_ref[n, 640:768] = total[:, 384:512].astype(low) + shared_ref[n, 128:256]
            bcr_ref[n, 0:256] = total[:, 512:768].astype(low)
            steps_part = pltpu.roll(total[:, 768:896], moved, 1)
            bcr_ref[n, 256:384] = (steps_part + shared_ref[n, 384:512].astype(f32)).astype(low)

    mail = Mail(send)
    steps = reduce_steps(mail, part_ref, sum_ref, got, sums, recv, 64, order)
    left = [3, 2, 1, 0]
    for turn in range(13):
        if turn in (0, 1, 3, 6):
            layer(left.pop(0))
        next(steps, None)
        next(b_steps, None)
        if turn in (7, 8, 9):
            grads(2 * (turn - 7), 2 * (turn - 6))
    for _ in b_steps:
        pass
    block_ref[...] += res_ref[0:64]
    for _ in steps:
        pass
    value, gain = norm_step(sum_ref[...], own_ref[0:64].astype(f32), floats_ref[7:8])
    input_ref[...] = dres_own_ref[0:64] + value
    for i in range(4):
        small_ref[0, i : i + 1, 0:384] = gain[:, 384 * i : 384 * (i + 1)]
        small_ref[0, 4 + i : 5 + i, 0:384] = dres_own_ref[64:65, 384 * i : 384 * (i + 1)]
    b_mail.finish()
    mail.finish()


def mix_backward(*args):
    low, f32 = jnp.bfloat16, jnp.float32
    return call(
        mix_backward_kernel,
        "mix_backward",
        4,
        (
            ((1536, 768), low),
            ((1536, 384), low),
            ((2, 8, 512), f32),
            ((64, 1536), f32),
            ((64, 1536), f32),
        ),
        [
            VMEM((1024, 1536), low),
            VMEM((1024, 192), f32),
            VMEM((1024, 256), low),
            VMEM((1024, 896), low),
            VMEM((CHUNK + 8, 448), f32),
            VMEM((64, 1536), f32),
            VMEM((1024, 1536), low),
            VMEM((1040, 1536), f32),
            DMA((2,)),
        ]
        + reduce_scratch(64, 1536, low)
        + reduce_scratch(64, 1536, low)
        + [DMA((27,)), DMA((27,)), DMA((27,)), DMA((27,))],
        args,
        ((2, 5), ()),
        limit=34,
    )


def place_kernel(
    main_ref,
    bcr_ref,
    small_ref,
    block_own,
    block_other,
    input_own,
    input_other,
    geg_ref,
    geu_ref,
    ged_ref,
    sg_ref,
    su_ref,
    sd_ref,
    block_out,
    input_out,
    norm1_out,
    wz_out,
    wx_out,
    wbc_out,
    wdt_out,
    convx_out,
    convbc_out,
    biasx_out,
    biasbc_out,
    dt_out,
    log_out,
    skip_out,
    gnorm_out,
    wout_out,
    norm2_out,
    router_out,
    sgate_out,
    sup_out,
    sdown_out,
    eg_out,
    eu_out,
    ed_out,
    biasx_row,
    gnorm_row,
    heads_row,
):
    side = lax.axis_index("head")
    f32 = jnp.float32
    for own, other, out in (
        (block_own, block_other, block_out),
        (input_own, input_other, input_out),
    ):
        out[:, 0] = jnp.where(side == 0, own[...], other[...])
        out[:, 1] = jnp.where(side == 0, other[...], own[...])
    norms = small_ref[0, 0]
    taps = small_ref[1, 0, :, 0:256]
    for j in range(1, 16):
        norms = norms + small_ref[0, j]
        taps = taps + small_ref[1, j, :, 0:256]
    for i in range(4):
        norm1_out[384 * i : 384 * (i + 1)] = norms[i, 0:384]
        norm2_out[384 * i : 384 * (i + 1)] = norms[4 + i, 0:384]
    convbc_out[...] = taps[0:4]
    biasbc_out[...] = taps[4]
    wbc_out[...] = bcr_ref[:, 0:256]
    turned = jnp.concatenate([bcr_ref[:, 256:384], jnp.zeros((32, 128), f32)], 0).T
    router_out[...] = turned[0:16, 0:96]
    wdt_out[...] = jnp.where(side == 0, turned[16:40, 0:96], turned[40:64, 0:96])
    onehot = (
        lax.broadcasted_iota(jnp.int32, (192, 128), 0) // HEADW
        == lax.broadcasted_iota(jnp.int32, (192, 128), 1)
    ).astype(f32)
    for j in range(8):
        place = 8 * side + j
        wide, narrow = slice(192 * j, 192 * (j + 1)), slice(64 * j, 64 * (j + 1))
        convx_out[:, wide] = small_ref[1, place, 0:4, 256:448]
        biasx_row[:, wide] = small_ref[1, place, 4:5, 256:448]
        gnorm_row[:, wide] = small_ref[1, place, 5:6, 0:192]
        skips = jnp.broadcast_to(small_ref[1, place, 5:6, 256:448], (8, 192))
        heads_row[2:3, 3 * j : 3 * j + 3] = mm(skips, onehot, exact=True)[0:1, 0:3]
        heads_row[0:1, 3 * j : 3 * j + 3] = small_ref[1, place, 6:7, 0:3]
        heads_row[1:2, 3 * j : 3 * j + 3] = small_ref[1, place, 6:7, 256:259]
        part = main_ref[j].astype(f32)
        wz_out[:, wide] = part[:, 256:448]
        sgate_out[:, narrow] = part[:, 448:512]
        wx_out[:, wide] = part[:, 512:704]
        sup_out[:, narrow] = part[:, 704:768]
        wout_out[:, wide] = part[:, 0:192]
        sdown_out[:, narrow] = part[:, 192:256]
    biasx_out[...] = biasx_row[0]
    gnorm_out[...] = gnorm_row[0]
    dt_out[...] = heads_row[0, 0:24]
    log_out[...] = heads_row[1, 0:24]
    skip_out[...] = heads_row[2, 0:24]
    eg_out[0] = geg_ref[...] + sg_ref[...].astype(f32)
    eu_out[0] = geu_ref[...] + su_ref[...].astype(f32)
    ed_out[0] = ged_ref[...] + sd_ref[...].astype(f32)


def place(*args):
    shapes = (
        (64, 2, 1536),
        (64, 2, 1536),
        (1536,),
        (96, 1536),
        (96, 1536),
        (96, 256),
        (24, 96),
        (4, 1536),
        (4, 256),
        (1536,),
        (256,),
        (24,),
        (24,),
        (24,),
        (1536,),
        (96, 1536),
        (1536,),
        (16, 96),
        (96, 512),
        (96, 512),
        (96, 512),
        (1, 1536, 256),
        (1, 1536, 256),
        (1, 256, 1536),
    )
    vmem = pl.BlockSpec(memory_space=VMEM)
    return pl.pallas_call(
        place_kernel,
        out_shape=tuple(jax.ShapeDtypeStruct(shape, jnp.float32) for shape in shapes),
        in_specs=[vmem] * len(args),
        out_specs=(vmem,) * len(shapes),
        scratch_shapes=[
            VMEM((1, 1536), jnp.float32),
            VMEM((1, 1536), jnp.float32),
            VMEM((8, 128), jnp.float32),
        ],
        compiler_params=pltpu.CompilerParams(vmem_limit_bytes=48 << 20),
        name="place",
    )(*args)


def by_heads(
    hidden_in,
    doc_ids,
    routes,
    norm1_gain,
    w_z,
    w_x,
    w_bc,
    w_dt,
    conv_x,
    conv_bc,
    convb_x,
    convb_bc,
    dt_bias,
    a_log,
    d_skip,
    gnorm_gain,
    w_out,
    norm2_gain,
    router,
    shared_gate,
    shared_up,
    shared_down,
    expert_gate,
    expert_up,
    expert_down,
    cotangent,
):
    eg, eu, ed = expert_gate[0], expert_up[0], expert_down[0]
    n1, extras, _, cols, own, floats, small_sib, eg_o, eu_o, ed_o = enter(
        hidden_in,
        cotangent,
        w_bc,
        router.T,
        w_dt.T,
        doc_ids.T,
        routes.transpose(1, 2, 0),
        w_out.T,
        shared_down.T,
        w_z,
        shared_gate,
        w_x,
        shared_up,
        conv_x,
        convb_x,
        gnorm_gain,
        dt_bias,
        a_log,
        d_skip,
        norm1_gain,
        norm2_gain,
        conv_bc,
        convb_bc,
        eg,
        eu,
        ed,
    )
    kept, g_all, n2, scale_note, residual, scale_own, ids, consts = mix_forward(
        n1, extras, cols, floats, small_sib, own
    )
    d_res_all, pair, moe_part, *grad_experts, shared, d_res = moe(
        n2,
        scale_note,
        g_all,
        cols,
        eg,
        eg_o,
        eu,
        eu_o,
        ed,
        ed_o,
        extras,
        ids,
        residual,
        scale_own,
        floats,
        own,
    )
    main, bcr, small, block_own, input_own = mix_backward(
        d_res_all, pair, n1, cols, consts, kept, moe_part, shared, residual, d_res, own, floats
    )
    main, bcr, small, block_sib, input_sib = leave(
        main.reshape(16, 96, 768), bcr, small, block_own, input_own
    )
    results = list(
        place(main, bcr, small, block_own, block_sib, input_own, input_sib, *grad_experts)
    )
    for i in (6, 15, 17, 20):
        results[i] = results[i].T
    return tuple(results)


def solution(mesh):
    places = mesh.shape["seq"]
    whole_heads = places == 16 and mesh.shape["head"] == 2
    placed = (
        P("seq", None, None),
        P("seq", None),
        P("seq", None, None),
        P(),
        P("seq", "head"),
        P("seq", "head"),
        P("seq", None),
        P("seq", "head"),
        P(None, "head"),
        P(),
        P("head"),
        P(),
        P("head"),
        P("head"),
        P("head"),
        P("head"),
        P("head", "seq"),
        P(),
        P("seq", None),
        P("seq", "head"),
        P("seq", "head"),
        P("head", "seq"),
        P("seq", None, "head"),
        P("seq", None, "head"),
        P("seq", "head", None),
        P("seq", None, None),
    )
    return jax.shard_map(
        by_heads if whole_heads else on_device,
        mesh=mesh,
        in_specs=placed,
        out_specs=(
            P("seq", None, None),
            P("seq", None, None),
            P(),
            P("seq", "head"),
            P("seq", "head"),
            P("seq", None),
            P("seq", "head"),
            P(None, "head"),
            P(),
            P("head"),
            P(),
            P("head"),
            P("head"),
            P("head"),
            P("head"),
            P("head", "seq"),
            P(),
            P("seq", None),
            P("seq", "head"),
            P("seq", "head"),
            P("head", "seq"),
            P("seq", None, "head"),
            P("seq", None, "head"),
            P("seq", "head", None),
        ),
        check_vma=False,
    )
```

```python
import jax
import jax.numpy as jnp
from jax import lax
from jax.experimental import pallas as pl
from jax.experimental.pallas import tpu as pltpu
from jax.sharding import PartitionSpec as P

KER = 4
INNER = 3072


EPS = 1e-05
HIGH = lax.Precision.HIGHEST


def passed_along(array, axis, by):
    length = lax.axis_size(axis)
    pairs = [(i, i + by) for i in range(length) if 0 <= i + by < length]
    return lax.ppermute(array, axis, pairs)


def entering(array, axis, combine, identity, reverse):
    length, here = (lax.axis_size(axis), lax.axis_index(axis))
    everything = jax.tree.map(
        lambda part, kind: lax.all_gather(part.astype(kind), axis),
        array,
        jax.tree.map(lambda a: jnp.bfloat16 if a.dtype == jnp.float32 else a.dtype, array),
    )
    start = jax.tree.map(
        lambda part, zero: jnp.broadcast_to(jnp.asarray(zero, part.dtype), part.shape),
        array,
        identity,
    )

    def hop(k, before):
        at = length - 1 - k if reverse else k
        reached = at > here if reverse else at < here
        new = combine(
            before, jax.tree.map(lambda part, own: part[at].astype(own.dtype), everything, array)
        )
        return jax.tree.map(lambda a, b: jnp.where(reached, a, b), new, before)

    return lax.fori_loop(0, length, hop, start)


def shortened(array):

    def short(part):
        return part.astype(jnp.bfloat16) if part.dtype == jnp.float32 else part

    return jax.tree.map(short, array)


def conv_apply(conv_ext, docs_ext, weight, conv_bias):
    length_here = conv_ext.shape[0] - (KER - 1)
    running = conv_bias
    for offset in range(KER):
        same_doc = (docs_ext[offset : offset + length_here] == docs_ext[KER - 1 :]).astype(
            jnp.float32
        )
        running = (
            running + weight[offset] * conv_ext[offset : offset + length_here] * same_doc[..., None]
        )
    return jax.nn.silu(running)


def group_parts(x_heads, step_size, b_state, decay_rate, doc_ids, prev_doc):
    log_decay = jnp.cumsum(step_size * decay_rate, axis=0)
    end_keep = (doc_ids == doc_ids[-1:]).astype(jnp.float32)
    weight = jnp.exp(log_decay[-1:] - log_decay) * end_keep[..., None] * step_size
    s_local = jnp.einsum("tsh,tshp,tsn->shpn", weight, x_heads, b_state, precision=HIGH)
    a_total = jnp.exp(log_decay[-1]) * (doc_ids[-1] == prev_doc).astype(jnp.float32)[:, None]
    return (s_local, a_total)


def group_output(x_heads, step_size, b_state, c_state, decay_rate, doc_ids, prev_doc, s_in):
    length_here = x_heads.shape[0]
    log_decay = jnp.cumsum(step_size * decay_rate, axis=0)
    causal = jnp.arange(length_here)[:, None] >= jnp.arange(length_here)[None, :]
    pair_mask = (causal[:, :, None] & (doc_ids[:, None, :] == doc_ids[None, :, :])).astype(
        jnp.float32
    )
    gap_decay = log_decay[:, None] - log_decay[None, :]
    decay_table = (
        jnp.exp(jnp.where(pair_mask[..., None] > 0, gap_decay, 0.0)) * pair_mask[..., None]
    )
    cross_dot = jnp.einsum("tsn,usn->tus", c_state, b_state, precision=HIGH)
    y_intra = jnp.einsum(
        "tush,ush,ushp->tshp",
        decay_table * cross_dot[..., None],
        step_size,
        x_heads,
        precision=HIGH,
    )
    enters = jnp.exp(log_decay) * (doc_ids == prev_doc[None, :]).astype(jnp.float32)[..., None]
    y_inter = jnp.einsum("tsn,shpn->tshp", c_state, s_in, precision=HIGH) * enters[..., None]
    return y_intra + y_inter


def ssm_local(x_heads, step_size, b_state, c_state, decay_rate, s_in, doc_ids, prev_doc):
    y_core = group_output(x_heads, step_size, b_state, c_state, decay_rate, doc_ids, prev_doc, s_in)
    s_local, a_total = group_parts(x_heads, step_size, b_state, decay_rate, doc_ids, prev_doc)
    return (y_core, a_total[..., None, None] * s_in + s_local)


def carry_combine(earlier, later_part):
    return (earlier[0] * later_part[0], later_part[0][..., None, None] * earlier[1] + later_part[1])


def head_total(partial_sum):
    return lax.psum(partial_sum, "head")


def flat_dot(left_side, right_side):
    lead_dims = left_side.shape[:-1]
    product = jnp.dot(
        left_side.reshape(-1, left_side.shape[-1]), right_side, preferred_element_type=jnp.float32
    )
    return product.reshape(lead_dims + (right_side.shape[-1],))


def flat_dot_t(left_side, right_side):
    lead_dims = left_side.shape[:-1]
    product = lax.dot_general(
        left_side.reshape(-1, left_side.shape[-1]),
        right_side,
        (((1,), (1,)), ((), ())),
        preferred_element_type=jnp.float32,
    )
    return product.reshape(lead_dims + (right_side.shape[0],))


def outer_sum(left_side, right_side):
    return lax.dot_general(
        left_side.reshape(-1, left_side.shape[-1]),
        right_side.reshape(-1, right_side.shape[-1]),
        (((0,), (0,)), ((), ())),
        preferred_element_type=jnp.float32,
    )


def silu_slope(values, sigmoid_of):
    return sigmoid_of * (1.0 + values * (1.0 - sigmoid_of))


def norm_back(grad_normed, values, scale_of, gain):
    scaled_grad = grad_normed * gain
    gain_grad = jnp.sum((grad_normed * values * scale_of).reshape(-1, values.shape[-1]), axis=0)
    cube = scale_of * scale_of * scale_of
    value_grad = scale_of * scaled_grad - values * cube * jnp.mean(
        scaled_grad * values, axis=-1, keepdims=True
    )
    return (value_grad, gain_grad)


def on_device(
    hidden_in,
    doc_ids,
    routes,
    norm1_gain,
    w_z,
    w_x,
    w_bc,
    w_dt,
    conv_x,
    conv_bc,
    convb_x,
    convb_bc,
    dt_bias,
    a_log,
    d_skip,
    gnorm_gain,
    w_out,
    norm2_gain,
    router,
    shared_gate,
    shared_up,
    shared_down,
    expert_gate,
    expert_up,
    expert_down,
    cotangent,
):
    block_len, seq_here, width = hidden_in.shape
    top_count = routes.shape[-1]
    heads_here = dt_bias.shape[0]
    inner_here = convb_x.shape[0]
    head_size = inner_here // heads_here
    state_size = convb_bc.shape[0] // 2
    seq_count = lax.axis_size("seq")
    local_experts = expert_gate.shape[0]
    experts_all = local_experts * seq_count
    tok_here = block_len * seq_here
    capacity = 2 * tok_here * top_count // experts_all
    edge_len = KER - 1
    x_float = hidden_in.astype(jnp.float32)
    scale_one = lax.rsqrt(jnp.mean(x_float * x_float, axis=-1, keepdims=True) + EPS)
    normed_one = (x_float * scale_one * norm1_gain).astype(jnp.bfloat16)
    gathered = (
        lax.all_gather(w_z, "seq", axis=0, tiled=True),
        lax.all_gather(w_x, "seq", axis=0, tiled=True),
        lax.all_gather(w_dt, "seq", axis=0, tiled=True),
        lax.all_gather(w_bc, "seq", axis=0, tiled=True),
        lax.all_gather(router, "seq", axis=0, tiled=True),
        lax.all_gather(shared_gate, "seq", axis=0, tiled=True),
        lax.all_gather(shared_up, "seq", axis=0, tiled=True),
        lax.all_gather(w_out, "seq", axis=1, tiled=True),
        lax.all_gather(shared_down, "seq", axis=1, tiled=True),
    )
    full_z, full_x, full_dt, full_bc, full_router, full_sgate, full_sup, full_out, full_sdown = (
        gathered
    )
    gate_z = flat_dot(normed_one, full_z)
    proj_x = flat_dot(normed_one, full_x)
    proj_bc = flat_dot(normed_one, full_bc)
    dt_pre = flat_dot(normed_one, full_dt) + dt_bias
    conv_in = jnp.concatenate([proj_x, proj_bc], axis=-1)
    tail_in, tail_doc = (
        passed_along(conv_in[block_len - edge_len :].astype(jnp.bfloat16), "seq", 1).astype(
            jnp.float32
        ),
        passed_along(
            doc_ids[block_len - edge_len :].astype(jnp.float32).astype(jnp.bfloat16), "seq", 1
        ).astype(jnp.float32),
    )
    conv_ext = jnp.concatenate([tail_in, conv_in], 0)
    docs_ext = jnp.concatenate([tail_doc.astype(jnp.int32), doc_ids], 0)
    conv_weight = jnp.concatenate([conv_x, conv_bc], -1)
    conv_shift = jnp.concatenate([convb_x, convb_bc], -1)
    conv_out = conv_apply(conv_ext, docs_ext, conv_weight, conv_shift)
    x_heads = conv_out[..., :inner_here].reshape(block_len, seq_here, heads_here, head_size)
    b_state = conv_out[..., inner_here : inner_here + state_size]
    c_state = conv_out[..., inner_here + state_size :]
    step_size = jax.nn.softplus(dt_pre)
    decay_rate = -jnp.exp(a_log)
    prev_doc = docs_ext[edge_len - 1]
    s_local, a_total = group_parts(x_heads, step_size, b_state, decay_rate, doc_ids, prev_doc)
    ones_start = jnp.ones_like(a_total)
    zeros_start = jnp.zeros_like(s_local)
    a_before, s_before = entering(
        (a_total, s_local), "seq", carry_combine, (ones_start, zeros_start), False
    )
    y_core = group_output(
        x_heads, step_size, b_state, c_state, decay_rate, doc_ids, prev_doc, s_before
    )
    y_heads = y_core + d_skip[:, None] * x_heads
    y_flat = y_heads.reshape(block_len, seq_here, inner_here)
    gate_sig = jax.nn.sigmoid(gate_z)
    gated = y_flat * gate_z * gate_sig
    square_sum = head_total(jnp.sum(gated * gated, axis=-1, keepdims=True))
    scale_gated = lax.rsqrt(square_sum / INNER + EPS)
    mixed_out = (gated * scale_gated * gnorm_gain).astype(jnp.bfloat16)
    residual = x_float + head_total(flat_dot(mixed_out, full_out))
    scale_two = lax.rsqrt(jnp.mean(residual * residual, axis=-1, keepdims=True) + EPS)
    normed_two = (residual * scale_two * norm2_gain).astype(jnp.bfloat16)
    logits = flat_dot(normed_two, full_router)
    gate_probs = jax.nn.softmax(jnp.take_along_axis(logits, routes, axis=-1), axis=-1)
    share_gate = flat_dot(normed_two, full_sgate)
    share_up = flat_dot(normed_two, full_sup)
    share_sig = jax.nn.sigmoid(share_gate)
    share_act = (share_gate * share_sig * share_up).astype(jnp.bfloat16)
    share_part = flat_dot(share_act, full_sdown)
    slot_total = tok_here * top_count
    route_flat = routes.reshape(slot_total)
    expert_ids = jnp.arange(experts_all, dtype=jnp.int32)
    route_hits = (route_flat[:, None] == expert_ids[None, :]).astype(jnp.int32)
    slot_rank = jnp.sum(jnp.cumsum(route_hits, axis=0) * route_hits, axis=1) - 1
    target = route_flat * capacity + slot_rank
    entry_table = (
        jnp.zeros((experts_all * capacity,), jnp.int32)
        .at[target]
        .set(jnp.arange(slot_total, dtype=jnp.int32) + 1)
    )
    entry_live = entry_table > 0
    entry_slot = jnp.maximum(entry_table - 1, 0)
    entry_token = entry_slot // top_count
    tokens_flat = normed_two.reshape(tok_here, width)
    send_rows = jnp.where(
        entry_live[:, None], tokens_flat[entry_token], jnp.zeros((), jnp.bfloat16)
    ).reshape(experts_all, capacity, width)
    received = lax.all_to_all(send_rows, "seq", split_axis=0, concat_axis=0, tiled=True)
    input_row_block = received.reshape(seq_count, local_experts, received.shape[1], width)
    hid_gate = jnp.einsum(
        "jecd,edf->jecf", input_row_block, expert_gate, preferred_element_type=jnp.float32
    )
    hid_up = jnp.einsum(
        "jecd,edf->jecf", input_row_block, expert_up, preferred_element_type=jnp.float32
    )
    hid_act = (hid_gate * jax.nn.sigmoid(hid_gate) * hid_up).astype(jnp.bfloat16)
    half_out = jnp.einsum(
        "jecf,efd->jecd", hid_act, expert_down, preferred_element_type=jnp.float32
    ).astype(jnp.bfloat16)
    returned_rows = lax.all_to_all(
        half_out.reshape(received.shape), "seq", split_axis=0, concat_axis=0, tiled=True
    )
    kept_shape = (seq_count * local_experts, received.shape[1], hid_gate.shape[-1])
    returned_rows, rows_kept, gate_kept, up_kept = (
        returned_rows,
        received,
        hid_gate.reshape(kept_shape),
        hid_up.reshape(kept_shape),
    )
    slot_rows = returned_rows.reshape(-1, width)[target].reshape(tok_here, top_count, width)
    probs_flat = gate_probs.reshape(tok_here, top_count)
    routed_part = share_part.reshape(tok_here, width)
    for slot_index in range(top_count):
        routed_part = routed_part + probs_flat[:, slot_index, None] * slot_rows[
            :, slot_index
        ].astype(jnp.float32)
    moe_out = head_total(routed_part.reshape(block_len, seq_here, width))
    block_out = residual + moe_out
    gathered = (
        lax.all_gather(w_z, "seq", axis=0, tiled=True),
        lax.all_gather(w_x, "seq", axis=0, tiled=True),
        lax.all_gather(w_dt, "seq", axis=0, tiled=True),
        lax.all_gather(w_bc, "seq", axis=0, tiled=True),
        lax.all_gather(router, "seq", axis=0, tiled=True),
        lax.all_gather(shared_gate, "seq", axis=0, tiled=True),
        lax.all_gather(shared_up, "seq", axis=0, tiled=True),
        lax.all_gather(w_out, "seq", axis=1, tiled=True),
        lax.all_gather(shared_down, "seq", axis=1, tiled=True),
    )
    full_z, full_x, full_dt, full_bc, full_router, full_sgate, full_sup, full_out, full_sdown = (
        gathered
    )
    grad_out = cotangent.astype(jnp.float32)
    grad_flat = grad_out.reshape(tok_here, width)
    entry_prob = jnp.where(entry_live, gate_probs.reshape(-1)[entry_slot], 0.0)
    send_grads = (
        (entry_prob[:, None] * grad_flat[entry_token])
        .astype(jnp.bfloat16)
        .reshape(experts_all, capacity, width)
    )
    recv_grads = lax.all_to_all(send_grads, "seq", split_axis=0, concat_axis=0, tiled=True)
    grads_in = recv_grads.reshape(seq_count, local_experts, capacity, width)
    input_row_block = rows_kept.reshape(seq_count, local_experts, capacity, width)
    hid_gate = gate_kept.reshape(seq_count, local_experts, capacity, -1)
    hid_up = up_kept.reshape(seq_count, local_experts, capacity, -1)
    hid_sig = jax.nn.sigmoid(hid_gate)
    hid_act = (hid_gate * hid_sig * hid_up).astype(jnp.bfloat16)
    d_act = jnp.einsum("jecd,efd->jecf", grads_in, expert_down, preferred_element_type=jnp.float32)
    hidden_up_gradient = (d_act * hid_gate * hid_sig).astype(jnp.bfloat16)
    d_hid_gate = (d_act * hid_up * silu_slope(hid_gate, hid_sig)).astype(jnp.bfloat16)
    grad_edown = jnp.einsum("jecf,jecd->efd", hid_act, grads_in, preferred_element_type=jnp.float32)
    grad_egate = jnp.einsum(
        "uqpy,uqpn->qyn", input_row_block, d_hid_gate, preferred_element_type=jnp.float32
    )
    expert_up_gradient = jnp.einsum(
        "uqpy,uqpn->qyn", input_row_block, hidden_up_gradient, preferred_element_type=jnp.float32
    )
    d_rows = jnp.einsum(
        "jecf,edf->jecd", d_hid_gate, expert_gate, preferred_element_type=jnp.float32
    )
    d_rows = (
        d_rows
        + jnp.einsum(
            "jecf,edf->jecd", hidden_up_gradient, expert_up, preferred_element_type=jnp.float32
        )
    ).astype(jnp.bfloat16)
    back_rows = lax.all_to_all(
        d_rows.reshape(recv_grads.shape), "seq", split_axis=0, concat_axis=0, tiled=True
    )
    d_share_act = flat_dot_t(cotangent, full_sdown)
    d_share_up = (d_share_act * share_gate * share_sig).astype(jnp.bfloat16)
    d_share_gate = (d_share_act * share_up * silu_slope(share_gate, share_sig)).astype(jnp.bfloat16)
    grad_sdown = outer_sum(share_act, cotangent)
    grad_sgate = outer_sum(normed_two, d_share_gate)
    grad_sup = outer_sum(normed_two, d_share_up)
    d_normed_two = (
        flat_dot_t(d_share_gate, full_sgate) + flat_dot_t(d_share_up, full_sup)
    ).reshape(tok_here, width)
    prob_grad = jnp.stack(
        [
            jnp.sum(grad_flat * slot_rows[:, slot_index].astype(jnp.float32), axis=-1)
            for slot_index in range(top_count)
        ],
        axis=-1,
    )
    back_slots = back_rows.reshape(-1, width)[target].reshape(tok_here, top_count, width)
    for slot_index in range(top_count):
        d_normed_two = d_normed_two + back_slots[:, slot_index].astype(jnp.float32)
    d_normed_two, prob_grad = head_total(
        (
            d_normed_two.reshape(block_len, seq_here, width),
            prob_grad.reshape(block_len, seq_here, top_count),
        )
    )
    d_chosen = gate_probs * (prob_grad - jnp.sum(gate_probs * prob_grad, axis=-1, keepdims=True))
    d_logits = jnp.sum(
        d_chosen[..., None] * (routes[..., None] == expert_ids).astype(jnp.float32), axis=-2
    ).astype(jnp.bfloat16)
    grad_router = outer_sum(normed_two, d_logits)
    d_normed_two = d_normed_two + flat_dot_t(d_logits, full_router)
    d_resid_norm, grad_norm2 = norm_back(d_normed_two, residual, scale_two, norm2_gain)
    d_resid = grad_out + d_resid_norm
    d_resid_low = d_resid.astype(jnp.bfloat16)
    d_mixed = flat_dot_t(d_resid_low, full_out)
    grad_out_w = outer_sum(mixed_out, d_resid_low)
    gain_scaled = d_mixed * gnorm_gain
    grad_gnorm = jnp.sum((d_mixed * gated * scale_gated).reshape(-1, inner_here), axis=0)
    cross_sum = head_total(jnp.sum(gain_scaled * gated, axis=-1, keepdims=True))
    d_gated = (
        scale_gated * gain_scaled
        - gated * scale_gated * scale_gated * scale_gated * cross_sum / INNER
    )
    d_y = d_gated * gate_z * gate_sig
    d_gate_z = (d_gated * y_flat * silu_slope(gate_z, gate_sig)).astype(jnp.bfloat16)
    d_y_heads = d_y.reshape(x_heads.shape)
    grad_skip = jnp.sum(d_y_heads * x_heads, axis=(0, 1, 3))
    log_decay = jnp.cumsum(step_size * decay_rate, axis=0)
    enters = jnp.exp(log_decay) * (doc_ids == prev_doc[None, :]).astype(jnp.float32)[..., None]
    g_local = jnp.einsum("tsh,tshp,tsn->shpn", enters, d_y_heads, c_state, precision=HIGH)
    a_after, state_grad = entering(
        (a_total, g_local), "seq", carry_combine, (ones_start, zeros_start), True
    )

    def local_scan(x_part, step_part, b_part, c_part, rate_part, state_part):
        return ssm_local(
            x_part, step_part, b_part, c_part, rate_part, state_part, doc_ids, prev_doc
        )

    _, scan_back = jax.vjp(local_scan, x_heads, step_size, b_state, c_state, decay_rate, s_before)
    d_xh, d_step, d_bstate, d_cstate, d_rate, _ = scan_back((d_y_heads, state_grad))
    d_xh = d_xh + d_skip[:, None] * d_y_heads
    d_bc = head_total(jnp.concatenate([d_bstate, d_cstate], axis=-1))
    d_dt_pre = d_step * jax.nn.sigmoid(dt_pre)
    grad_dtb = jnp.sum(d_dt_pre, axis=(0, 1))
    grad_alog = d_rate * decay_rate
    d_conv_out = jnp.concatenate([d_xh.reshape(block_len, seq_here, inner_here), d_bc], axis=-1)

    def local_conv(ext_part, weight_part, shift_part):
        return conv_apply(ext_part, docs_ext, weight_part, shift_part)

    _, conv_back = jax.vjp(local_conv, conv_ext, conv_weight, conv_shift)
    d_ext, grad_cweight, grad_cshift = conv_back(d_conv_out)
    from_next = passed_along(shortened(d_ext[:edge_len]), "seq", -1)
    d_conv_in = d_ext[edge_len:] + jnp.concatenate(
        [jnp.zeros((block_len - edge_len,) + from_next.shape[1:], jnp.float32), from_next], 0
    )
    d_proj_x = d_conv_in[..., :inner_here].astype(jnp.bfloat16)
    d_proj_bc = d_conv_in[..., inner_here:].astype(jnp.bfloat16)
    d_dt_low = d_dt_pre.astype(jnp.bfloat16)
    grad_wz = outer_sum(normed_one, d_gate_z)
    grad_wx = outer_sum(normed_one, d_proj_x)
    grad_wbc = outer_sum(normed_one, d_proj_bc)
    grad_wdt = outer_sum(normed_one, d_dt_low)
    head_first = jnp.where(lax.axis_index("head") == 0, 1.0, 0.0)
    d_normed_one = (
        flat_dot_t(d_gate_z, full_z) + flat_dot_t(d_proj_x, full_x) + flat_dot_t(d_dt_low, full_dt)
    )
    d_normed_one = head_total(d_normed_one + head_first * flat_dot_t(d_proj_bc, full_bc))
    d_x_norm, grad_norm1 = norm_back(d_normed_one, x_float, scale_one, norm1_gain)
    input_grad = d_resid + d_x_norm
    reduced = (
        lax.psum_scatter(grad_wz, "seq", scatter_dimension=0, tiled=True),
        lax.psum_scatter(grad_wx, "seq", scatter_dimension=0, tiled=True),
        lax.psum_scatter(grad_wdt, "seq", scatter_dimension=0, tiled=True),
        lax.psum_scatter(grad_wbc, "seq", scatter_dimension=0, tiled=True),
        lax.psum_scatter(grad_router, "seq", scatter_dimension=0, tiled=True),
        lax.psum_scatter(grad_sgate, "seq", scatter_dimension=0, tiled=True),
        lax.psum_scatter(grad_sup, "seq", scatter_dimension=0, tiled=True),
        lax.psum_scatter(grad_out_w, "seq", scatter_dimension=1, tiled=True),
        lax.psum_scatter(grad_sdown, "seq", scatter_dimension=1, tiled=True),
    )
    red_z, red_x, red_dt, red_bc, red_router, red_sgate, red_sup, red_out, red_sdown = reduced
    small_sums = lax.psum(
        (
            grad_norm1,
            grad_norm2,
            grad_cweight,
            grad_cshift,
            grad_dtb,
            grad_alog,
            grad_skip,
            grad_gnorm,
        ),
        "seq",
    )
    sum_norm1, sum_norm2, sum_cweight, sum_cshift, sum_dtb, sum_alog, sum_skip, sum_gnorm = (
        small_sums
    )
    return (
        block_out,
        input_grad,
        sum_norm1,
        red_z,
        red_x,
        red_bc,
        red_dt,
        sum_cweight[:, :inner_here],
        sum_cweight[:, inner_here:],
        sum_cshift[:inner_here],
        sum_cshift[inner_here:],
        sum_dtb,
        sum_alog,
        sum_skip,
        sum_gnorm,
        red_out,
        sum_norm2,
        red_router,
        red_sgate,
        red_sup,
        red_sdown,
        grad_egate,
        expert_up_gradient,
        grad_edown,
    )


MESH = pl.DeviceIdType.MESH
VMEM = pltpu.VMEM


def peers():
    here, side = lax.axis_index("seq"), lax.axis_index("head")
    x, y, z = lax.rem(here, 2), lax.rem(here // 2, 2), here // 4
    col = x + 2 * y
    return here, side, z, col, (1 - x) + 2 * y, x + 2 * (1 - y), 3 - col


def layers(z):
    lo, hi = lax.rem(z, 2), z // 2
    return [2 * (1 - hi if k & 2 else hi) + (1 - lo if k & 1 else lo) for k in range(4)]


def call_out(devices):
    barrier = pltpu.get_barrier_semaphore()
    for device in devices:
        pl.semaphore_signal(barrier, inc=1, device_id=device, device_id_type=MESH)
    return len(devices)


def greet(devices):
    pl.semaphore_wait(pltpu.get_barrier_semaphore(), call_out(devices))


class Mail:
    def __init__(self, send, base=0):
        self.send, self.sent, self.base = send, [], base

    def put(self, src, dst, sem, to):
        copy = pltpu.make_async_remote_copy(
            src_ref=src,
            dst_ref=dst,
            send_sem=self.send.at[self.base + len(self.sent)],
            recv_sem=sem,
            device_id=to,
            device_id_type=MESH,
        )
        copy.start()
        self.sent.append(copy)

    def arrived(self, dst, sem):
        pltpu.make_async_remote_copy(
            src_ref=dst,
            dst_ref=dst,
            send_sem=self.send.at[0],
            recv_sem=sem,
            device_id=(0, 0),
            device_id_type=MESH,
        ).wait_recv()

    def finish(self):
        for copy in self.sent:
            copy.wait_send()


def rows_at(ref, start, size, step):
    return ref.at[pl.ds(pl.multiple_of(start, step), size)]


def crossing_lanes(width):
    return width // 3 * 2 if width % 384 == 0 else width


def gather_steps(mail, own_ref, out_ref, recv, recv_half, rows, half=None):
    here, side, z, col, cx, cy, cd = peers()
    zs = layers(z)
    base = 4 * z
    to_x, to_y = (base + cx, side), (base + cy, side)

    def part(place, which, ref=None):
        if half is None:
            width = out_ref.shape[1] // 2
            lane = pl.ds(which * width, width)
            if ref is not None:
                return ref.at[:, lane]
            return out_ref.at[pl.ds(pl.multiple_of(place * rows, 16), rows), lane]
        size = rows - half if which else half
        if ref is not None:
            return ref.at[pl.ds(which * half, size)]
        return rows_at(out_ref, place * rows + which * half, size, 16)

    width = out_ref.shape[1]
    cut = width if half is None else crossing_lanes(width)

    def crossing(place, which, k):
        if k == 0 or cut == width:
            return part(place, which)
        size = rows - half if which else half
        at = pl.ds(pl.multiple_of(place * rows + which * half, 16), size)
        return out_ref.at[at, pl.ds(0, cut)]

    def strip(place):
        at = pl.ds(pl.multiple_of(place * rows, 16), rows)
        return out_ref.at[at, pl.ds(cut, width - cut)]

    def onward(place, k, ref=None):
        for which in (0, 1):
            src = part(place, which, ref)
            mail.put(src, part(place, which), recv.at[6 + 4 * k + which], to_x)
            src = part(place, 1 - which, ref)
            mail.put(src, part(place, 1 - which), recv.at[8 + 4 * k + which], to_y)

    def across(k):
        at = 4 * zs[k] + cd
        mail.arrived(crossing(at, 0, k), recv_half.at[k])
        mail.arrived(crossing(at, 1, k), recv_half.at[4 + k])
        mail.arrived(part(4 * zs[k] + cx, 1), recv.at[7 + 4 * k])
        mail.arrived(part(4 * zs[k] + cy, 0), recv.at[9 + 4 * k])
        if cut == width:
            return
        if k:
            mail.arrived(strip(at), recv_half.at[7 + k])
            return
        for j in (1, 2, 3):
            mail.put(strip(at), strip(at), recv_half.at[7 + j], (4 * zs[j] + col, side))

    onward(here, 0, own_ref)
    for k in (1, 2, 3):
        for which in (0, 1):
            src = part(here, which, own_ref)
            sem = recv.at[2 * (k - 1) + which]
            mail.put(src, part(here, which), sem, (4 * zs[k] + col, side))
    yield
    for k in range(4):
        if k:
            at = 4 * zs[k] + col
            mail.arrived(part(at, 0), recv.at[2 * (k - 1)])
            mail.arrived(part(at, 1), recv.at[2 * (k - 1) + 1])
            onward(at, k)
            yield
        if k == 1:
            across(0)
            yield
        at = 4 * zs[k] + cx
        mail.arrived(part(at, 0), recv.at[6 + 4 * k])
        mail.put(crossing(at, 0, k), crossing(at, 0, k), recv_half.at[k], to_y)
        at = 4 * zs[k] + cy
        mail.arrived(part(at, 1), recv.at[8 + 4 * k])
        mail.put(crossing(at, 1, k), crossing(at, 1, k), recv_half.at[4 + k], to_x)
        yield
        if k > 1:
            across(k - 1)
            yield
    across(3)
    yield


def near(side):
    here, side, z, col, cx, cy, cd = peers()
    zs = layers(z)
    return [(4 * z + cx, side), (4 * z + cy, side)] + [(4 * zs[k] + col, side) for k in (1, 2, 3)]


def note_puts(mail, src_of, notes_out, recv_n):
    here, side = peers()[:2]
    for k in range(1, 16):
        to = lax.rem(here + k, 16)
        mail.put(src_of(to), notes_out.at[here], recv_n.at[here], (to, side))


def note_waits(mail, notes_out, recv_n):
    here = peers()[0]
    for k in range(1, 16):
        place = lax.rem(here + k, 16)
        mail.arrived(notes_out.at[place], recv_n.at[place])


SUM_ORDER = (
    ("far", 3),
    ("joined", 3),
    ("far", 2),
    ("joined", 2),
    ("column", 3),
    ("far", 1),
    ("joined", 1),
    ("column", 2),
    ("far", 0),
    ("column", 1),
    ("joined", 0),
    ("column", 0),
)


def reduce_steps(mail, part_ref, out_ref, got, sums, recv, rows, order=SUM_ORDER):
    here, side, z, col, cx, cy, cd = peers()
    zs = layers(z)
    base = 4 * z
    half = rows // 2
    got_a, got_b, got_x, got_y, got_z, got_d = got
    sum_x, sum_y, sum_z, sum_d = sums
    width = part_ref.shape[1]
    cut = crossing_lanes(width)
    to_x, to_y = (base + cx, side), (base + cy, side)
    f32 = jnp.float32

    def half_of(place, which):
        return rows_at(part_ref, place * rows + which * half, half, half)

    def near_lanes(ref, k):
        return ref.at[k, :, pl.ds(0, cut)]

    def far_lanes(ref):
        return ref.at[0, :, pl.ds(cut, width - cut)]

    def crossing(place, which):
        at = pl.multiple_of(place * rows + which * half, half)
        return part_ref.at[pl.ds(at, half), pl.ds(0, cut)]

    def far(k):
        at = 4 * zs[k] + cd
        mail.put(crossing(at, 0), near_lanes(got_a, k), recv.at[k], to_y)
        mail.put(crossing(at, 1), near_lanes(got_b, k), recv.at[4 + k], to_x)
        if cut == width:
            return
        whole = pl.ds(pl.multiple_of(at * rows, rows), rows)
        if k:
            src = part_ref.at[whole, pl.ds(cut, width - cut)]
            mail.put(src, got_d.at[k - 1], recv.at[26 + k], (4 * zs[k] + col, side))
            return
        for j in (1, 2, 3):
            mail.arrived(got_d.at[j - 1], recv.at[26 + j])
        total = part_ref[whole, cut:width].astype(f32)
        for j in range(3):
            total = total + got_d[j].astype(f32)
        sum_d[0] = total.astype(sum_d.dtype)
        mail.put(sum_d.at[0, pl.ds(0, half)], far_lanes(got_a), recv.at[30], to_y)
        mail.put(sum_d.at[0, pl.ds(half, half)], far_lanes(got_b), recv.at[31], to_x)

    def plain(k):
        mail.put(half_of(4 * zs[k] + cx, 1), got_x.at[k, pl.ds(half, half)], recv.at[12 + k], to_x)
        mail.put(half_of(4 * zs[k] + cy, 0), got_y.at[k, pl.ds(0, half)], recv.at[16 + k], to_y)

    def join(k, at, which, got_ref, sum_ref):
        mine = half_of(at, which)[...]
        mail.arrived(near_lanes(got_ref, k), recv.at[4 * which + k])
        total = mine[:, 0:cut].astype(f32) + got_ref[k, :, 0:cut].astype(f32)
        sum_ref[k, :, 0:cut] = total.astype(sum_ref.dtype)
        if cut == width:
            return
        if k:
            sum_ref[k, :, cut:width] = mine[:, cut:width]
            return
        mail.arrived(far_lanes(got_ref), recv.at[30 + which])
        total = mine[:, cut:width].astype(f32) + got_ref[k, :, cut:width].astype(f32)
        sum_ref[k, :, cut:width] = total.astype(sum_ref.dtype)

    def joined(k):
        join(k, 4 * zs[k] + cx, 0, got_a, sum_x)
        mail.put(sum_x.at[k], got_x.at[k, pl.ds(0, half)], recv.at[8 + k], to_x)
        join(k, 4 * zs[k] + cy, 1, got_b, sum_y)
        mail.put(sum_y.at[k], got_y.at[k, pl.ds(half, half)], recv.at[20 + k], to_y)

    def column(k):
        mail.arrived(got_x.at[k, pl.ds(half, half)], recv.at[12 + k])
        mail.arrived(got_y.at[k, pl.ds(0, half)], recv.at[16 + k])
        mail.arrived(got_x.at[k, pl.ds(0, half)], recv.at[8 + k])
        mail.arrived(got_y.at[k, pl.ds(half, half)], recv.at[20 + k])
        own = part_ref[pl.ds(pl.multiple_of((4 * zs[k] + col) * rows, rows), rows)].astype(f32)
        total = own + got_x[k].astype(f32) + got_y[k].astype(f32)
        if k:
            sum_z[k - 1] = total.astype(sum_z.dtype)
            mail.put(sum_z.at[k - 1], got_z.at[k - 1], recv.at[23 + k], (4 * zs[k] + col, side))
        else:
            out_ref[...] = total

    for turn, k in order:
        if turn == "far":
            far(k)
            plain(k)
        elif turn == "joined":
            joined(k)
        else:
            column(k)
        yield
    for turn, k in order:
        if turn == "column" and k:
            mail.arrived(got_z.at[k - 1], recv.at[23 + k])
            out_ref[...] += got_z[k - 1].astype(f32)


def reduce_scratch(rows, width, kind):
    half = rows // 2
    cut = crossing_lanes(width)
    shapes = [(4, half), (4, half), (4, rows), (4, rows), (3, rows), (3, rows)]
    shapes += [(4, half), (4, half), (3, rows), (1, rows)]
    across = max(width - cut, 128)
    return [
        VMEM(shape + (across if i in (5, 9) else width,), kind) for i, shape in enumerate(shapes)
    ]


def same_side(side, here):
    return [(lax.rem(here + k, 16), side) for k in range(1, 16)]


DMA = pltpu.SemaphoreType.DMA


def remote(src, dst, send, recv, to):
    return pltpu.make_async_remote_copy(
        src_ref=src,
        dst_ref=dst,
        send_sem=send,
        recv_sem=recv,
        device_id=to,
        device_id_type=MESH,
    )


def call(kernel, name, number, outs, scratch, args, spaces=None, limit=60):
    vmem = pl.BlockSpec(memory_space=VMEM)
    hbm = pl.BlockSpec(memory_space=pltpu.HBM)
    ins_far, outs_far = spaces or ((), ())
    args = [
        pltpu.with_memory_space_constraint(array, pltpu.HBM) if i in ins_far else array
        for i, array in enumerate(args)
    ]
    return pl.pallas_call(
        kernel,
        out_shape=tuple(
            pltpu.HBM(*out) if i in outs_far else jax.ShapeDtypeStruct(*out)
            for i, out in enumerate(outs)
        ),
        in_specs=[hbm if i in ins_far else vmem for i in range(len(args))],
        out_specs=tuple(hbm if i in outs_far else vmem for i in range(len(outs))),
        scratch_shapes=scratch,
        compiler_params=pltpu.CompilerParams(
            collective_id=number, has_side_effects=True, vmem_limit_bytes=limit << 20
        ),
        name=name,
    )(*args)


def of_side(ref, side):
    return jnp.where(side == 0, ref[:, 0], ref[:, 1])


def enter_kernel(
    hidden_far,
    cot_far,
    wbc_far,
    router_far,
    wdt_far,
    docs_far,
    routes_far,
    wo_far,
    sd_far,
    wz_far,
    sg_far,
    wx_far,
    su_far,
    convx_far,
    biasx_far,
    gnorm_far,
    bias_far,
    log_far,
    skip_far,
    norm1_far,
    norm2_far,
    convbc_far,
    biasbc_far,
    gate_ref,
    up_ref,
    down_ref,
    all_ref,
    extras_ref,
    extra_ref,
    cols_ref,
    own_ref,
    floats_ref,
    small_other,
    gate_other,
    up_other,
    down_other,
    n1_ref,
    mine_ref,
    misc_ref,
    blocks_ref,
    hidden_ref,
    cot_ref,
    wbc_ref,
    router_ref,
    wdt_ref,
    docs_ref,
    routes_ref,
    wo_ref,
    sd_ref,
    wz_ref,
    sg_ref,
    wx_ref,
    su_ref,
    convx_ref,
    biasx_ref,
    gnorm_ref,
    bias_ref,
    log_ref,
    skip_ref,
    norm1_ref,
    norm2_ref,
    convbc_ref,
    biasbc_ref,
    loaded,
    send,
    recv,
    recv_half,
    recv_m,
    recv_half_m,
    recv_w,
    recv_e,
    recv_s,
    local,
):
    here, side = peers()[:2]
    places = 16
    sibling = (here, 1 - side)
    peer_count = call_out(same_side(side, here) + [sibling])
    far = (wz_far, sg_far, wx_far, su_far, wo_far, sd_far, convx_far, biasx_far, gnorm_far)
    far += (bias_far, log_far, skip_far, norm1_far, norm2_far, convbc_far, biasbc_far)
    far += (hidden_far, cot_far, wbc_far, router_far, wdt_far, docs_far, routes_far)
    close = (wz_ref, sg_ref, wx_ref, su_ref, wo_ref, sd_ref, convx_ref, biasx_ref, gnorm_ref)
    close += (bias_ref, log_ref, skip_ref, norm1_ref, norm2_ref, convbc_ref, biasbc_ref)
    close += (hidden_ref, cot_ref, wbc_ref, router_ref, wdt_ref, docs_ref, routes_ref)
    loads = [pltpu.make_async_copy(*both, loaded.at[i]) for i, both in enumerate(zip(far, close))]
    for load in loads[6:] + loads[:6]:
        load.start()
    floats_ref[...] = jnp.zeros(floats_ref.shape, jnp.float32)
    misc_ref[...] = jnp.zeros(misc_ref.shape, jnp.float32)
    for load in loads[6:]:
        load.wait()
    f32, low = jnp.float32, jnp.bfloat16
    own_ref[0:64] = of_side(hidden_ref, side)
    own_ref[64:128] = of_side(cot_ref, side)
    mine_ref[:, 0:128] = jnp.where(side == 0, wbc_ref[:, 0:128], wbc_ref[:, 128:256])
    misc_ref[0:16, 0:96] = router_ref[...].astype(f32)
    misc_ref[16:40, 0:96] = wdt_ref[...].astype(f32)
    misc_ref[40:41, 0:64] = jnp.where(side == 0, docs_ref[0:1], docs_ref[1:2]).astype(f32)
    misc_ref[41:47, 0:64] = jnp.where(side == 0, routes_ref[0], routes_ref[1]).astype(f32)
    mine_ref[:, 128:256] = misc_ref[...].T[0:96].astype(low)
    floats_ref[0:4] = convx_ref[...]
    floats_ref[4:5] = biasx_ref[...][None, :]
    floats_ref[5:6] = gnorm_ref[...][None, :]
    floats_ref[6:7, 0:24] = bias_ref[...][None, :]
    floats_ref[6:7, 24:48] = log_ref[...][None, :]
    floats_ref[6:7, 48:72] = skip_ref[...][None, :]
    floats_ref[7:8] = norm1_ref[...][None, :]
    floats_ref[8:9] = norm2_ref[...][None, :]
    floats_ref[9:13, 0:256] = convbc_ref[...]
    floats_ref[13:14, 0:256] = biasbc_ref[...][None, :]
    x = own_ref[0:64].astype(jnp.float32)
    scale = lax.rsqrt(jnp.mean(x * x, axis=-1, keepdims=True) + EPS)
    n1_ref[...] = (x * scale * floats_ref[7:8]).astype(jnp.bfloat16)
    pl.semaphore_wait(pltpu.get_barrier_semaphore(), peer_count)
    depth = blocks_ref.shape[1]
    rows, extra = n1_ref.shape[0], mine_ref.shape[0]
    half_here = here // 8
    mail = Mail(send)
    mine = pltpu.make_async_copy(n1_ref, rows_at(all_ref, here * rows, rows, 16), local.at[0])
    mine.start()
    mine_too = pltpu.make_async_copy(
        mine_ref, rows_at(extras_ref, here * extra, extra, 16), local.at[18]
    )
    mine_too.start()

    def strip(place):
        return cols_ref.at[pl.ds(pl.multiple_of(place * depth, 16), depth), pl.ds(0, 768)]

    steps = gather_steps(mail, n1_ref, all_ref, recv, recv_half, rows, rows // 2)
    steps_too = gather_steps(mail, mine_ref, extras_ref, recv_m, recv_half_m, extra)
    next(steps_too)
    next(steps)
    mail.put(floats_ref.at[pl.ds(0, 8)], small_other, recv_s.at[0], sibling)
    for load in loads[:6]:
        load.wait()
    for j in range(8):
        at = 0
        for width, ref in (
            (192, wo_ref),
            (64, sd_ref),
            (192, wz_ref),
            (64, sg_ref),
            (192, wx_ref),
            (64, su_ref),
        ):
            blocks_ref[j, :, at : at + width] = ref[:, width * j : width * (j + 1)]
            at += width
    first = 8 * side + lax.rem(here, 8)
    is_mine = side == half_here
    def send_strip(k):
        to = 8 * side + lax.rem(here + k, 8)
        mail.put(blocks_ref.at[to - 8 * side], strip(here), recv_w.at[here], (to, side))

    send_strip(1)

    def keep():
        return pltpu.make_async_copy(blocks_ref.at[here - 8 * side], strip(here), local.at[1])

    def give():
        block = blocks_ref.at[first - 8 * side]
        return remote(block, strip(here), local.at[1], recv_w.at[here], (first, side))

    @pl.when(is_mine)
    def _():
        keep().start()

    @pl.when(jnp.logical_not(is_mine))
    def _():
        give().start()

    mail.put(gate_ref, gate_other, recv_s.at[1], sibling)
    mail.put(up_ref, up_other, recv_s.at[2], sibling)
    mail.put(down_ref, down_other, recv_s.at[3], sibling)
    def forward(place, k):
        return remote(strip(place), strip(place), local.at[2 + k], recv_w.at[place], sibling)

    def pass_on(k):
        place = lax.rem(here + k, places)
        forward(place, k).wait_recv()

        @pl.when(is_mine)
        def _():
            forward(place, k).start()

    turn = 0
    for _ in steps_too:
        next(steps)
        turn += 1
        if turn < 7:
            send_strip(turn + 1)
        if turn == 6:

            @pl.when(is_mine)
            def _():
                keep().wait()
                forward(here, 0).start()

            @pl.when(jnp.logical_not(is_mine))
            def _():
                forward(here, 0).wait_recv()
                give().wait_send()

    for _ in steps:
        pass
    mine.wait()
    mine_too.wait()
    for place in range(places):
        at = pl.ds(place * extra, extra)
        mail.put(extras_ref.at[at], extra_ref.at[at], recv_e.at[place], sibling)
    for k in range(1, places):
        pass_on(k)

    @pl.when(is_mine)
    def _():
        for k in range(places):
            forward(lax.rem(here + k, places), k).wait_send()

    mail.arrived(small_other, recv_s.at[0])
    mail.arrived(gate_other, recv_s.at[1])
    mail.arrived(up_other, recv_s.at[2])
    mail.arrived(down_other, recv_s.at[3])
    for place in range(places):
        mail.arrived(extra_ref.at[pl.ds(place * extra, extra)], recv_e.at[place])
    cols_ref[:, pl.ds(pl.multiple_of(768 + side * 128, 128), 128)] = extras_ref[:, 0:128]
    cols_ref[:, pl.ds(pl.multiple_of(896 - side * 128, 128), 128)] = extra_ref[:, 0:128]
    is_own = side == half_here
    cols_ref[:, 1024:1152] = jnp.where(is_own, extras_ref[:, 128:256], extra_ref[:, 128:256])
    mail.finish()


def enter(*args):
    low, f32 = jnp.bfloat16, jnp.float32
    return call(
        enter_kernel,
        "enter",
        1,
        (
            ((1024, 1536), low),
            ((1536, 256), low),
            ((1536, 256), low),
            ((1536, 1152), low),
            ((128, 1536), low),
            ((16, 1536), f32),
            ((8, 1536), f32),
            ((1536, 256), low),
            ((1536, 256), low),
            ((256, 1536), low),
        ),
        [
            VMEM((64, 1536), low),
            VMEM((96, 256), low),
            VMEM((128, 128), f32),
            VMEM((8, 96, 768), low),
        ]
        + [VMEM(array.shape, array.dtype) for array in args[:23]]
        + [
            DMA((23,)),
            DMA((90,)),
            DMA((22,)),
            DMA((11,)),
            DMA((22,)),
            DMA((11,)),
            DMA((16,)),
            DMA((16,)),
            DMA((4,)),
            DMA((19,)),
        ],
        args,
        (range(26), (7, 8, 9)),
        limit=12,
    )


FAR_FIRST = (8, 7, 9, 6, 10, 5, 11, 4, 12, 3, 13, 2, 14, 1, 15)


def leave_kernel(
    main_ref,
    bcr_ref,
    small_ref,
    block_ref,
    input_ref,
    main_parts,
    bcr_out,
    small_all,
    block_other,
    input_other,
    got_main,
    got_bcr,
    bcr_part,
    bcr_mine,
    bcr_sib,
    small_got,
    small_sum,
    *refs,
):
    got, sums, refs = refs[:6], refs[6:10], refs[10:]
    send, recv_sib, recv_main, recv_small, recv_pair, cond, r_send, r_recv = refs
    here, side = peers()[:2]
    sibling = (here, 1 - side)
    is_main = side == here // 8
    f32 = jnp.float32
    greet(same_side(side, here) + [sibling])
    mail = Mail(send)
    mail.put(small_ref, small_got, recv_sib.at[1], sibling)

    def give_main():
        return remote(main_ref, got_main, cond.at[0], recv_sib.at[0], sibling)

    def send_on(total, out, sem, slot, k):
        to = lax.rem(here + k, 16)
        return remote(total.at[to], out.at[slot], cond.at[k], sem.at[slot], (to, side))

    slot = lax.rem(here, 8)

    half = bcr_ref.at[:, pl.ds(pl.multiple_of((1 - side) * 128, 128), 128)]
    mail.put(half, got_bcr, recv_sib.at[5], sibling)

    @pl.when(jnp.logical_not(is_main))
    def _():
        give_main().start()

    mail.put(block_ref, block_other, recv_sib.at[3], sibling)
    mail.put(input_ref, input_other, recv_sib.at[4], sibling)
    mail.arrived(small_got, recv_sib.at[1])
    small_sum[...] = small_ref[...] + small_got[...]
    small_all[side, here] = small_sum[side]
    for k in range(1, 16):
        to = lax.rem(here + k, 16)
        mail.put(small_sum.at[side], small_all.at[side, here], recv_small.at[here], (to, side))

    mail.arrived(got_bcr, recv_sib.at[5])
    mine = bcr_ref[:, pl.ds(pl.multiple_of(side * 128, 128), 128)]
    bcr_part[:, 0:128] = (mine.astype(f32) + got_bcr[...].astype(f32)).astype(bcr_part.dtype)
    bcr_part[:, 128:256] = bcr_ref[:, 256:384]
    r_mail = Mail(r_send)
    steps = reduce_steps(r_mail, bcr_part, bcr_mine, got, sums, r_recv, 96)
    next(steps)
    next(steps)

    def hand_back(first, last):
        @pl.when(is_main)
        def _():
            if first == 1:
                give_main().wait_recv()
            for k in FAR_FIRST[first - 1 : last - 1]:
                to = lax.rem(here + k, 16)
                total = main_ref[to].astype(f32) + got_main[to].astype(f32)
                got_main[to] = total.astype(got_main.dtype)
                send_on(got_main, main_parts, recv_main, slot, k).start()
            if last == 16:
                total = main_ref[here].astype(f32) + got_main[here].astype(f32)
                main_parts[slot] = total.astype(main_parts.dtype)

    hand_back(1, 3)
    for j in range(6):
        next(steps)
        hand_back(3 + 2 * j, 5 + 2 * j)
    hand_back(15, 16)
    for _ in steps:
        pass
    mail.put(bcr_mine, bcr_sib, recv_sib.at[2], sibling)
    for k in range(1, 16):
        place = lax.rem(here + k, 16)
        mail.arrived(small_all.at[side, place], recv_small.at[place])
    mail.put(small_all.at[side], small_all.at[side], recv_pair, sibling)
    mail.arrived(small_all.at[1 - side], recv_pair)
    for j in range(8):

        @pl.when(8 * side + j != here)
        def _():
            mail.arrived(main_parts.at[j], recv_main.at[j])

    mail.arrived(bcr_sib, recv_sib.at[2])
    bcr_out[:, pl.ds(pl.multiple_of(side * 128, 128), 128)] = bcr_mine[:, 0:128]
    bcr_out[:, pl.ds(pl.multiple_of((1 - side) * 128, 128), 128)] = bcr_sib[:, 0:128]
    bcr_out[:, 256:384] = bcr_mine[:, 128:256] + bcr_sib[:, 128:256]
    mail.arrived(block_other, recv_sib.at[3])
    mail.arrived(input_other, recv_sib.at[4])

    @pl.when(is_main)
    def _():
        for k in range(1, 16):
            send_on(got_main, main_parts, recv_main, slot, k).wait_send()

    @pl.when(jnp.logical_not(is_main))
    def _():
        give_main().wait_send()

    r_mail.finish()
    mail.finish()


def leave(*args):
    low, f32 = jnp.bfloat16, jnp.float32
    return call(
        leave_kernel,
        "leave",
        5,
        (
            ((8, 96, 768), low),
            ((96, 384), f32),
            ((2, 16, 8, 512), f32),
            ((64, 1536), f32),
            ((64, 1536), f32),
        ),
        [
            VMEM((16, 96, 768), low),
            VMEM((1536, 128), low),
            VMEM((1536, 256), low),
            VMEM((96, 256), f32),
            VMEM((96, 256), f32),
            VMEM((2, 8, 512), f32),
            VMEM((2, 8, 512), f32),
        ]
        + reduce_scratch(96, 256, low)
        + [
            DMA((21,)),
            DMA((6,)),
            DMA((8,)),
            DMA((16,)),
            DMA,
            DMA((16,)),
            DMA((32,)),
            DMA((32,)),
        ],
        args,
        limit=10,
    )


CHUNK = 128
LAYER = 256
HEADW = 64


def mm(left, right, low=True, exact=False):
    return mm_of(left, right, ((1,), (0,)), low, exact)


def mm_nt(left, right, low=True, exact=False):
    return mm_of(left, right, ((1,), (1,)), low, exact)


def mm_tn(left, right, low=True, exact=False):
    return mm_of(left, right, ((0,), (0,)), low, exact)


def mm_of(left, right, dims, low, exact):
    if exact:
        return lax.dot_general(
            left, right, (dims, ((), ())), precision=HIGH, preferred_element_type=jnp.float32
        )
    if low:
        left, right = left.astype(jnp.bfloat16), right.astype(jnp.bfloat16)
    return lax.dot_general(left, right, (dims, ((), ())), preferred_element_type=jnp.float32)


def lanes(shape):
    return lax.broadcasted_iota(jnp.int32, shape, 1)


def by_head(parts, rows):
    lane = lanes((rows, 3 * HEADW))
    return jnp.where(lane < HEADW, parts[0], jnp.where(lane < 2 * HEADW, parts[1], parts[2]))


def spread_heads(array):
    return by_head([array[:, h : h + 1] for h in range(3)], array.shape[0])


def soft_plus(values):
    return jnp.maximum(values, 0.0) + jnp.log1p(jnp.exp(-jnp.abs(values)))


def chunk_tables(step, log_rate, doc_col, doc_row):
    row = lax.broadcasted_iota(jnp.int32, (CHUNK, CHUNK), 0)
    col = lax.broadcasted_iota(jnp.int32, (CHUNK, CHUNK), 1)
    below = (row >= col).astype(jnp.float32)
    logs = mm(below, step * log_rate, exact=True)
    logs_t, step_t = logs.T, step.T
    pair = (row >= col) & (doc_col == doc_row)
    tables = [
        jnp.exp(jnp.where(pair, logs[:, h : h + 1] - logs_t[h : h + 1], -1e9)) for h in range(3)
    ]
    return logs, tables, [step_t[h : h + 1] for h in range(3)]


def as_column(row):
    return jnp.concatenate([row, jnp.zeros((CHUNK - 8, CHUNK), jnp.float32)], 0).T


def as_row(column):
    wide = jnp.broadcast_to(column, (64, CHUNK))
    return jnp.concatenate([wide, jnp.zeros((64, CHUNK), jnp.float32)], 0).T[0:8]


KEPT = dict(z=(0, 192), y=(256, 192), dt=(512, 128), ids=(640, 128), ext=(768, 448), state=(1280, 192))


class Part:
    def __init__(self, ref, lane, width, row=0, height=None):
        self.ref, self.lane, self.width, self.row = ref, lane, width, row
        self.height = ref.shape[0] if height is None else height

    def at_of(self, index):
        rows, cols = index if isinstance(index, tuple) else (index, slice(None))
        if rows is Ellipsis:
            rows = slice(None)
        if isinstance(rows, slice):
            stop = self.height if rows.stop is None else rows.stop
            rows = slice(self.row + (rows.start or 0), self.row + stop)
        stop = self.width if cols.stop is None else cols.stop
        return rows, slice(self.lane + (cols.start or 0), self.lane + stop)

    def __getitem__(self, index):
        return self.ref[self.at_of(index)]

    def __setitem__(self, index, value):
        self.ref[self.at_of(index)] = value


def kept_views(kept_ref):
    return [Part(kept_ref, *KEPT[name]) for name in ("z", "y", "dt", "ids", "ext", "state")]


def const_views(consts_ref):
    return [
        Part(consts_ref, 0, 448, 0, 8),
        Part(consts_ref, 0, 128, 8, 8),
        Part(consts_ref, 128, 192, 8, 8),
    ]


def mix_forward_kernel(
    n1_ref,
    extras_ref,
    cols_ref,
    floats_ref,
    small_other,
    own_ref,
    kept_far,
    g_all_ref,
    n2_ref,
    note_ref,
    res_ref,
    scale_ref,
    ids_out,
    consts_ref,
    part_ref,
    gained_ref,
    notes_ref,
    sum_ref,
    notes_out,
    kept_ref,
    kept_sem,
    *refs,
):
    z_ref, y_ref, dt_ref, ids_ref, ext_ref, state_ref = kept_views(kept_ref)
    taps_ref, head_ref, gain_ref = const_views(consts_ref)
    g_ref = own_ref.at[pl.ds(64, 64)]
    got, sums, refs = refs[:6], refs[6:10], refs[10:]
    send, recv, recv_n, g_send, g_recv, g_recv_half, local = refs
    here, side, z_at = peers()[:3]
    half_here, slot = here // 8, lax.rem(here, 8)
    greet(same_side(side, here))
    low, f32 = jnp.bfloat16, jnp.float32
    mine = pltpu.make_async_copy(g_ref, rows_at(g_all_ref, here * 64, 64, 16), local)
    mine.start()
    g_mail = Mail(g_send)
    g_steps = gather_steps(g_mail, g_ref, g_all_ref, g_recv, g_recv_half, 64, 32)
    next(g_steps)

    small = jnp.where(side == half_here, floats_ref[0:8], small_other[...])
    turned = pltpu.roll(small, lax.rem(1536 - 192 * slot, 1536), 1)
    taps_ref[0:5, 0:256] = floats_ref[9:14, 0:256]
    taps_ref[5:8] = jnp.zeros((3, 448), f32)
    taps_ref[0:5, 256:448] = turned[0:5, 0:192]
    gain_ref[...] = jnp.broadcast_to(turned[5:6, 0:192], (8, 192))
    numbers = pltpu.roll(small[:, 0:128], lax.rem(128 - 3 * slot, 128), 1)[6:7]
    used = lanes((1, 128)) < 3
    head_ref[0:1] = jnp.where(used, numbers, 0.0)
    head_ref[1:2] = jnp.where(used, -jnp.exp(pltpu.roll(numbers, 104, 1)), 0.0)
    head_ref[2:3] = jnp.where(used, pltpu.roll(numbers, 80, 1), 0.0)
    ids_ref[0:8] = jnp.full((8, 128), -1.0, f32)
    ids_ref[1032:1040] = jnp.full((8, 128), -2.0, f32)
    for p in range(16):
        ids_ref[8 + 64 * p : 72 + 64 * p] = extras_ref[96 * p : 96 * p + 64, 128:256].astype(f32)
    ids_out[...] = ids_ref[...]
    notes_ref[...] = jnp.zeros(notes_ref.shape, f32)
    ext_ref[0:8] = jnp.zeros((8, 448), f32)

    @pl.loop(0, 4)
    def _(i):
        at = pl.ds(pl.multiple_of(i * LAYER, LAYER), LAYER)
        shifted = pl.ds(pl.multiple_of(i * LAYER + 8, 8), LAYER)
        rows = n1_ref[at]
        proj = mm(rows, cols_ref[:, 256:1152])
        z_ref[at] = proj[:, 0:192]
        ext_ref[shifted, 0:256] = proj[:, 512:768]
        ext_ref[shifted, 256:448] = proj[:, 256:448]
        dt_ref[at] = pltpu.roll(proj[:, 768:896], 112 - 3 * slot, 1) + head_ref[0:1]

    next(g_steps)
    rate, skip = head_ref[1:2], spread_heads(head_ref[2:3])
    state = jnp.zeros((128, 192), f32)
    ones = jnp.ones((8, 192), f32)
    for c in range(8):
        r = c * CHUNK
        at = pl.ds(r, CHUNK)
        ids = ids_ref[pl.ds(r + 8, CHUNK)]
        doc = ids[:, 40:41]
        pre = conv_pre(taps_ref, ext_ref, ids_ref, r, doc)
        act = pre * jax.nn.sigmoid(pre)
        b, cc, x = act[:, 0:128], act[:, 128:256], act[:, 256:448]
        step = soft_plus(dt_ref[at])
        logs, tables, step_t = chunk_tables(step, rate, doc, ids.T[40:41])
        cross = mm_nt(cc, b)
        stacked = jnp.concatenate([cross * tables[h] * step_t[h] for h in range(3)], 0)
        intra = mm(stacked, x)
        y = by_head([intra[h * CHUNK : (h + 1) * CHUNK] for h in range(3)], CHUNK)
        first, last = chunk_masks(ids_ref, r, doc)
        enters = jnp.exp(logs) * first
        state_ref[at] = state
        y = y + spread_heads(enters) * mm(cc, state) + skip * x
        y_ref[at] = y
        tail = jnp.exp(logs[CHUNK - 1 :] - logs) * last * step
        state = spread_heads(enters[CHUNK - 1 :]) * state + mm_tn(b, spread_heads(tail) * x)
        z = z_ref[at]
        gated = y * z * jax.nn.sigmoid(z)
        gained_ref[at] = (gated * gain_ref[0:1]).astype(low)
        squares = mm_nt(ones, gated * gated, exact=True)
        notes_ref[2 * c, :, 0:64] = squares[:, 0:64]
        notes_ref[2 * c + 1, :, 0:64] = squares[:, 64:128]
        next(g_steps, None)

    keep = pltpu.make_async_copy(kept_ref, kept_far, kept_sem)
    keep.start()
    mail = Mail(send)
    zs = layers(z_at)

    def layer(k):
        at = pl.ds(pl.multiple_of(zs[k] * LAYER, LAYER), LAYER)

        @pl.loop(0, 3)
        def _(i):
            n = pl.ds(pl.multiple_of(i * 512, 512), 512)
            part_ref[at, n] = mm_nt(gained_ref[at], cols_ref[n, 0:192]).astype(low)

    steps = reduce_steps(mail, part_ref, sum_ref, got, sums, recv, 64)
    left = [3, 2, 1, 0]
    for turn in range(13):
        if turn in (0, 2, 5, 8):
            layer(left.pop(0))
        next(steps, None)
        if turn == 4:
            notes_out[here] = notes_ref[here]
            note_puts(mail, lambda to: notes_ref.at[to], notes_out, recv_n)
        if turn > 2:
            next(g_steps, None)
    for _ in g_steps:
        pass
    for _ in steps:
        pass
    note_waits(mail, notes_out, recv_n)
    squares = notes_out[0]
    for j in range(1, 16):
        squares = squares + notes_out[j]
    scale_row = lax.rsqrt(squares / INNER + EPS)
    note_ref[...] = scale_row
    scale = as_column(scale_row)[0:64, 0:1]
    scale_ref[...] = jnp.broadcast_to(scale, (64, 128))
    projected = scale * sum_ref[...]
    res_ref[64:128] = projected
    residual = own_ref[0:64].astype(f32) + projected
    res_ref[0:64] = residual
    scale_two = lax.rsqrt(jnp.mean(residual * residual, axis=-1, keepdims=True) + EPS)
    n2_ref[...] = (residual * scale_two * floats_ref[8:9]).astype(low)
    keep.wait()
    mine.wait()
    g_mail.finish()
    mail.finish()


def conv_pre(taps_ref, ext_ref, ids_ref, r, doc):
    pre = taps_ref[4:5] + taps_ref[3:4] * ext_ref[pl.ds(r + 8, CHUNK)]
    for k in (1, 2, 3):
        same = (ids_ref[pl.ds(r + 8 - k, CHUNK), 40:41] == doc).astype(jnp.float32)
        pre = pre + taps_ref[3 - k : 4 - k] * ext_ref[pl.ds(r + 8 - k, CHUNK)] * same
    return pre


def chunk_masks(ids_ref, r, doc):
    first = (ids_ref[r + 7 : r + 8, 40:41] == doc).astype(jnp.float32)
    last = (ids_ref[r + 7 + CHUNK : r + 8 + CHUNK, 40:41] == doc).astype(jnp.float32)
    return first, last


def mix_forward(*args):
    low, f32 = jnp.bfloat16, jnp.float32
    return call(
        mix_forward_kernel,
        "mix_forward",
        2,
        (
            ((1040, 1536), f32),
            ((1024, 1536), low),
            ((64, 1536), low),
            ((8, 128), f32),
            ((128, 1536), f32),
            ((64, 128), f32),
            ((1040, 128), f32),
            ((16, 512), f32),
        ),
        [
            VMEM((1024, 1536), low),
            VMEM((1024, 192), low),
            VMEM((16, 8, 128), f32),
            VMEM((64, 1536), f32),
            VMEM((16, 8, 128), f32),
            VMEM((1040, 1536), f32),
            DMA,
        ]
        + reduce_scratch(64, 1536, low)
        + [
            DMA((47,)),
            DMA((32,)),
            DMA((16,)),
            DMA((33,)),
            DMA((22,)),
            DMA((11,)),
            DMA,
        ],
        args,
        ((), (0,)),
        limit=24,
    )


def moe_kernel(
    own_ref,
    scale_note_ref,
    g_ref,
    cols_ref,
    eg_far,
    ego_far,
    eu_far,
    euo_far,
    ed_far,
    edo_far,
    extras_ref,
    ids_ref,
    res_ref,
    scale_ref,
    floats_ref,
    mine_ref,
    dres_ref,
    cross_ref,
    moe_ref,
    geg_far,
    geu_far,
    ged_far,
    sg_ref,
    su_ref,
    sd_ref,
    shared_ref,
    dres_own_ref,
    n2_ref,
    act_ref,
    hid_ref,
    probs_ref,
    notes_ref,
    notes_out,
    sum_ref,
    low_ref,
    note_ref,
    og_ref,
    ou_ref,
    od_ref,
    geg_ref,
    geu_ref,
    ged_ref,
    up_ref,
    down_ref,
    both_ref,
    loaded,
    *refs,
):
    got, sums, refs = refs[:6], refs[6:10], refs[10:]
    send, recv, recv_n, d_send, d_recv, d_recv_half, d_recv_n = refs[:7]
    n_send, n_recv, n_recv_half, e_send, e_recv, local = refs[7:]
    loads = [
        pltpu.make_async_copy(far, close, loaded.at[i])
        for i, (far, close) in enumerate(
            (
                (eg_far, up_ref.at[:, pl.ds(0, 256)]),
                (ego_far, up_ref.at[:, pl.ds(256, 256)]),
                (eu_far, up_ref.at[:, pl.ds(640, 256)]),
                (euo_far, up_ref.at[:, pl.ds(896, 256)]),
                (ed_far, down_ref.at[pl.ds(0, 256)]),
                (edo_far, down_ref.at[pl.ds(256, 256)]),
            )
        )
    ]
    for load in loads:
        load.start()
    here, side, z_at = peers()[:3]
    sibling = (here, 1 - side)
    greet(same_side(side, here) + [sibling])
    low, f32 = jnp.bfloat16, jnp.float32
    zs = layers(z_at)
    keep = pltpu.make_async_copy(own_ref, rows_at(n2_ref, here * 64, 64, 16), local.at[1])
    keep.start()
    n_mail = Mail(n_send)
    n_steps = gather_steps(n_mail, own_ref, n2_ref, n_recv, n_recv_half, 64, 32)
    next(n_steps)
    notes_ref[...] = jnp.zeros(notes_ref.shape, f32)
    lane = lanes((LAYER, 128))
    lane640 = lanes((LAYER, 640))
    up_ref[:, 512:640] = cols_ref[:, 384:512]
    up_ref[:, 1152:1280] = cols_ref[:, 640:768]
    for i in range(12):
        n = slice(128 * i, 128 * (i + 1))
        down_ref[512:640, n] = cols_ref[n, 128:256].astype(f32).T.astype(low)
    for load in loads:
        load.wait()

    def layer(k, piece):
        start = pl.multiple_of(zs[k] * LAYER, LAYER)
        at = pl.ds(start, LAYER)
        if piece == 0:
            rows = n2_ref[at]
            logits = mm(rows, extras_ref[:, 128:256])
            ids = ids_ref[pl.ds(pl.multiple_of(start + 8, 8), LAYER)]
            named = jnp.zeros((LAYER, 128), f32)
            for j in range(6):
                named = jnp.where(lane.astype(f32) == ids[:, 41 + j : 42 + j], 1.0, named)
            top = jnp.max(jnp.where(named > 0, logits, -1e30), axis=-1, keepdims=True)
            raised = jnp.exp(jnp.where(named > 0, logits - top, 0.0)) * named
            probs_ref[at] = raised / jnp.sum(raised, axis=-1, keepdims=True)
            both_ref[...] = mm(rows, up_ref[...])
            return
        if piece == 1:
            chosen = jnp.where(lane == here, probs_ref[at], 0.0)
            prob = jnp.sum(chosen, axis=-1, keepdims=True)
            weight = jnp.where(lane640 < 512, prob, jnp.where(lane640 < 576, 0.0, 1.0))
            gate, up = both_ref[:, 0:640], both_ref[:, 640:1280]
            d_act = mm_nt(g_ref[at], down_ref[...])
            sig = jax.nn.sigmoid(gate)
            act = gate * sig * up
            act_ref[at] = (act * weight).astype(low)
            slopes = jnp.sum((act * d_act)[:, 0:512], axis=-1, keepdims=True)
            d_act = d_act * weight
            hid_ref[at, 0:640] = (d_act * up * silu_slope(gate, sig)).astype(low)
            hid_ref[at, 640:1280] = (d_act * gate * sig).astype(low)
            for j in range(4):
                notes_ref[4 * zs[k] + j] = as_row(slopes[64 * j : 64 * (j + 1)])
            return

        @pl.loop(0, 3)
        def _(i):
            n = pl.ds(pl.multiple_of(i * 512, 512), 512)
            moe_ref[at, n] = mm_nt(hid_ref[at], up_ref[n]).astype(low)

    e_mail = Mail(e_send)

    def up_grads(first, last):
        @pl.loop(first, last)
        def _(i):
            n = pl.ds(pl.multiple_of(i * 256, 256), 256)
            total = mm_tn(n2_ref[:, n], hid_ref[...])
            geg_ref[n] = total[:, 0:256]
            og_ref[n] = total[:, 256:512].astype(low)
            shared_ref[n, 0:128] = total[:, 512:640].astype(low)
            geu_ref[n] = total[:, 640:896]
            ou_ref[n] = total[:, 896:1152].astype(low)
            shared_ref[n, 128:256] = total[:, 1152:1280].astype(low)

    def give_up():
        e_mail.put(og_ref, sg_ref, e_recv.at[0], sibling)
        e_mail.put(ou_ref, su_ref, e_recv.at[1], sibling)

    def down_grads():
        od_ref[...] = mm_tn(act_ref[:, 256:512], g_ref[...]).astype(low)
        e_mail.put(od_ref, sd_ref, e_recv.at[2], sibling)
        ged_ref[...] = mm_tn(act_ref[:, 0:256], g_ref[...])

    def shared_down():
        @pl.loop(0, 6)
        def _(i):
            n = pl.ds(pl.multiple_of(i * 256, 256), 256)
            shared_ref[n, 256:384] = mm_tn(g_ref[:, n], act_ref[:, 512:640]).astype(low)

    def moe_part(first, last):
        @pl.loop(first, last)
        def _(i):
            at = pl.ds(pl.multiple_of(i * LAYER, LAYER), LAYER)
            total = mm(act_ref[at], down_ref[...])
            moe_ref[at] = total.astype(low)

    mail = Mail(send)
    steps = reduce_steps(mail, moe_ref, sum_ref, got, sums, recv, 64)

    for _ in range(4):
        next(n_steps)
    keep.wait()
    for j in range(4):
        layer(j, 0)
        next(n_steps, None)
        layer(j, 1)
        next(n_steps, None)
        layer(j, 2)
        next(n_steps, None)
    for turn in range(10):
        next(steps)
        if turn == 4:
            notes_out[here] = notes_ref[here]
            note_puts(mail, lambda to: notes_ref.at[to], notes_out, recv_n)
    up_grads(0, 3)
    next(steps)
    for _ in steps:
        pass
    note_waits(mail, notes_out, recv_n)

    slopes = jnp.concatenate([notes_out[j, 0:1] for j in range(16)], 0)
    slopes = jnp.concatenate([slopes, jnp.zeros((112, 128), f32)], 0).T[0:64]
    own = pl.ds(pl.multiple_of(here * 64, 64), 64)
    probs = probs_ref[own]
    d_logits = probs * (slopes - jnp.sum(probs * slopes, axis=-1, keepdims=True))
    d_logits = d_logits.astype(low)
    dn2 = sum_ref[...] + mm_nt(d_logits, extras_ref[:, 128:256])
    value, gain = norm_step(dn2, res_ref[0:64], floats_ref[8:9])
    dres_own_ref[64:72] = jnp.broadcast_to(gain, (8, 1536))
    d_res = mine_ref[64:128].astype(f32) + value
    dres_own_ref[0:64] = d_res
    low_ref[...] = d_res.astype(low)
    cross = jnp.sum(low_ref[...].astype(f32) * res_ref[64:128], axis=-1, keepdims=True)
    first = lax.broadcasted_iota(jnp.int32, (8, 128), 0) == 0
    note_ref[...] = jnp.where(first, as_row(cross / scale_ref[:, 0:1]), scale_note_ref[...])
    mine = pltpu.make_async_copy(low_ref, rows_at(dres_ref, here * 64, 64, 16), local.at[0])
    mine.start()
    d_mail = Mail(d_send)
    d_steps = gather_steps(d_mail, low_ref, dres_ref, d_recv, d_recv_half, 64, 32)
    next(d_steps)
    cross_ref[here] = note_ref[...]
    note_puts(d_mail, lambda to: note_ref, cross_ref, d_recv_n)
    shared_ref[:, 384:512] = mm_tn(n2_ref[own], d_logits).astype(low)
    next(d_steps)
    mail.finish()
    for i in range(3):
        up_grads(3 + i, 4 + i)
        next(d_steps)
    give_up()
    down_grads()
    next(d_steps)
    stores = [
        pltpu.make_async_copy(geg_ref, geg_far, local.at[2]),
        pltpu.make_async_copy(geu_ref, geu_far, local.at[3]),
        pltpu.make_async_copy(ged_ref, ged_far, local.at[4]),
    ]
    for store in stores:
        store.start()
    for i in range(4):
        moe_part(i, i + 1)
        next(d_steps)
    shared_down()
    for _ in d_steps:
        pass
    e_mail.arrived(sg_ref, e_recv.at[0])
    e_mail.arrived(su_ref, e_recv.at[1])
    e_mail.arrived(sd_ref, e_recv.at[2])
    note_waits(d_mail, cross_ref, d_recv_n)
    mine.wait()
    for store in stores:
        store.wait()
    n_mail.finish()
    e_mail.finish()
    d_mail.finish()


def norm_step(grad, values, gain):
    scale = lax.rsqrt(jnp.mean(values * values, axis=-1, keepdims=True) + EPS)
    gain_grad = jnp.sum(grad * values * scale, axis=0, keepdims=True)
    scaled = grad * gain
    pull = scale * scale * scale * jnp.mean(scaled * values, axis=-1, keepdims=True)
    return scale * scaled - values * pull, gain_grad


def moe(*args):
    low, f32 = jnp.bfloat16, jnp.float32
    return call(
        moe_kernel,
        "moe",
        3,
        (
            ((1024, 1536), low),
            ((16, 8, 128), f32),
            ((1024, 1536), low),
            ((1536, 256), f32),
            ((1536, 256), f32),
            ((256, 1536), f32),
            ((1536, 256), low),
            ((1536, 256), low),
            ((256, 1536), low),
            ((1536, 512), low),
            ((72, 1536), f32),
        ),
        [
            VMEM((1024, 1536), low),
            VMEM((1024, 640), low),
            VMEM((1024, 1280), low),
            VMEM((1024, 128), f32),
            VMEM((16, 8, 128), f32),
            VMEM((16, 8, 128), f32),
            VMEM((64, 1536), f32),
            VMEM((64, 1536), low),
            VMEM((8, 128), f32),
            VMEM((1536, 256), low),
            VMEM((1536, 256), low),
            VMEM((256, 1536), low),
            VMEM((1536, 256), f32),
            VMEM((1536, 256), f32),
            VMEM((256, 1536), f32),
            VMEM((1536, 1280), low),
            VMEM((640, 1536), low),
            VMEM((LAYER, 1280), f32),
            DMA((6,)),
        ]
        + reduce_scratch(64, 1536, low)
        + [
            DMA((47,)),
            DMA((32,)),
            DMA((16,)),
            DMA((48,)),
            DMA((22,)),
            DMA((11,)),
            DMA((16,)),
            DMA((33,)),
            DMA((22,)),
            DMA((11,)),
            DMA((3,)),
            DMA((3,)),
            DMA((5,)),
        ],
        args,
        (range(4, 10), (3, 4, 5, 6, 7, 8)),
        limit=36,
    )


def mix_backward_kernel(
    dres_ref,
    cross_ref,
    n1_far,
    cols_ref,
    consts_ref,
    kept_far,
    moe_ref,
    shared_ref,
    res_ref,
    dres_own_ref,
    own_ref,
    floats_ref,
    main_ref,
    bcr_ref,
    small_ref,
    block_ref,
    input_ref,
    part_ref,
    dm_ref,
    mixed_ref,
    din_ref,
    dpre_ref,
    sum_ref,
    n1_ref,
    kept_ref,
    loaded,
    *refs,
):
    got, sums, refs = refs[:6], refs[6:10], refs[10:]
    b_got, b_sums, refs = refs[:6], refs[6:10], refs[10:]
    send, recv, b_send, b_recv = refs
    loads = (
        pltpu.make_async_copy(kept_far, kept_ref, loaded.at[0]),
        pltpu.make_async_copy(n1_far, n1_ref, loaded.at[1]),
    )
    for load in loads:
        load.start()
    z_ref, y_ref, dt_ref, ids_ref, ext_ref, state_ref = kept_views(kept_ref)
    taps_ref, head_ref, gain_ref = const_views(consts_ref)
    here, side, z_at = peers()[:3]
    half_here, slot = here // 8, lax.rem(here, 8)
    greet(near(side))
    low, f32 = jnp.bfloat16, jnp.float32
    zs = layers(z_at)
    b_mail = Mail(b_send)
    order = [("far", 3), ("far", 2), ("joined", 3), ("far", 1), ("joined", 2), ("column", 3)]
    order += [("far", 0), ("joined", 1), ("column", 2), ("joined", 0), ("column", 1), ("column", 0)]
    b_steps = reduce_steps(b_mail, moe_ref, block_ref, b_got, b_sums, b_recv, 64, order)
    next(b_steps)

    @pl.loop(0, 4)
    def _(i):
        at = pl.ds(pl.multiple_of(i * LAYER, LAYER), LAYER)
        dm_ref[at] = mm(dres_ref[at], cols_ref[:, 0:192])

    next(b_steps)
    loads[0].wait()
    rate, skip = head_ref[1:2], spread_heads(head_ref[2:3])
    onehot = (
        lax.broadcasted_iota(jnp.int32, (192, 128), 0) // HEADW
        == lax.broadcasted_iota(jnp.int32, (192, 128), 1)
    ).astype(f32)
    row = lax.broadcasted_iota(jnp.int32, (CHUNK, CHUNK), 0)
    lane = lanes((CHUNK, CHUNK))
    above = (row <= lane).astype(f32)
    lane192 = lanes((CHUNK, 192))
    masks = [((lane192 // HEADW) == h).astype(f32) for h in range(3)]
    d_state = jnp.zeros((128, 192), f32)
    g_gain = jnp.zeros((1, 192), f32)
    g_skip = jnp.zeros((1, 192), f32)
    g_rate = jnp.zeros((1, 128), f32)
    g_dt = jnp.zeros((1, 128), f32)
    g_taps = [jnp.zeros((1, 448), f32) for _ in range(5)]
    dpre_ref[0:8] = jnp.zeros((8, 448), f32)
    din_ref[:, 128:256] = jnp.zeros((1024, 128), low)
    din_ref[:, 384:512] = jnp.zeros((1024, 128), low)
    mixed_ref[:, 128:256] = jnp.zeros((1024, 128), low)
    for c in range(7, -1, -1):
        r = c * CHUNK
        at = pl.ds(r, CHUNK)
        ids = ids_ref[pl.ds(r + 8, CHUNK)]
        doc = ids[:, 40:41]
        noted = jnp.concatenate([cross_ref[2 * c, :, 0:64], cross_ref[2 * c + 1, :, 0:64]], 1)
        noted = as_column(noted)
        scale = noted[:, 1:2]
        pull = scale * scale * scale * noted[:, 0:1] / INNER
        z, y, dm, gain = z_ref[at], y_ref[at], dm_ref[at], gain_ref[0:1]
        sig = jax.nn.sigmoid(z)
        gated = y * z * sig
        scaled = gated * scale
        mixed_ref[at, 0:192] = (scaled * gain).astype(low)
        g_gain = g_gain + jnp.sum(dm * scaled, axis=0, keepdims=True)
        d_gated = scale * gain * dm - gated * pull
        d_y = d_gated * z * sig
        din_ref[at, 0:192] = (d_gated * y * silu_slope(z, sig)).astype(low)
        pre = conv_pre(taps_ref, ext_ref, ids_ref, r, doc)
        pre_sig = jax.nn.sigmoid(pre)
        act = pre * pre_sig
        b, cc, x = act[:, 0:128], act[:, 128:256], act[:, 256:448]
        g_skip = g_skip + jnp.sum(d_y * x, axis=0, keepdims=True)
        dt = dt_ref[at]
        step = soft_plus(dt)
        logs, tables, step_t = chunk_tables(step, rate, doc, ids.T[40:41])
        cross = mm_nt(cc, b)
        decays = [tables[h] * step_t[h] for h in range(3)]
        stacked = jnp.concatenate([cross * decays[h] for h in range(3)], 0)
        d_ys = jnp.concatenate([d_y * masks[h] for h in range(3)], 0)
        d_stack = mm_nt(d_ys, x)
        d_x = skip * d_y + mm_tn(stacked, d_ys)
        state = state_ref[at]
        first, last = chunk_masks(ids_ref, r, doc)
        enters = jnp.exp(logs) * first
        d_in_y = spread_heads(enters) * d_y
        from_state = mm(cc, state)
        tail_w = jnp.exp(logs[CHUNK - 1 :] - logs) * last
        tail = tail_w * step
        tail_x = spread_heads(tail)
        to_state = mm(b, d_state)
        d_x = d_x + tail_x * to_state
        kept = enters[CHUNK - 1 :]
        d_kept = jnp.sum(d_state * state, axis=0, keepdims=True)
        folded = mm(
            jnp.concatenate(
                [d_y * from_state, x * to_state, jnp.broadcast_to(d_kept, (8, 192))], 0
            ),
            onehot,
            exact=True,
        )
        d_enters, d_tail = folded[:CHUNK], folded[CHUNK : 2 * CHUNK]
        d_kept = folded[2 * CHUNK : 2 * CHUNK + 1]
        d_cross = jnp.zeros((CHUNK, CHUNK), f32)
        row_sums = jnp.zeros((CHUNK, CHUNK), f32)
        col_sums = []
        for h in range(3):
            d_a = d_stack[h * CHUNK : (h + 1) * CHUNK]
            d_cross = d_cross + d_a * decays[h]
            plain = d_a * cross * tables[h]
            col_sums.append(jnp.sum(plain, axis=0, keepdims=True))
            total = jnp.sum(plain * step_t[h], axis=1, keepdims=True)
            row_sums = jnp.where(lane == h, total, row_sums)
        col_sums = as_column(jnp.concatenate(col_sums + [jnp.zeros((5, CHUNK), f32)], 0))
        d_c = mm(d_cross, b) + mm_nt(d_in_y, state)
        d_b = mm_tn(d_cross, cc) + mm_nt(tail_x * x, d_state)
        pulled = d_tail * tail
        d_logs = row_sums - step * col_sums + d_enters * enters - pulled
        d_last = jnp.sum(pulled, axis=0, keepdims=True) + d_kept * kept
        d_logs = d_logs + jnp.where(row == CHUNK - 1, d_last, 0.0)
        d_l = mm(above, d_logs, exact=True)
        d_step = col_sums + d_tail * tail_w + d_l * rate
        g_rate = g_rate + jnp.sum(d_l * step, axis=0, keepdims=True)
        d_dt = jnp.where(lane < 3, d_step * jax.nn.sigmoid(dt), 0.0)
        g_dt = g_dt + jnp.sum(d_dt, axis=0, keepdims=True)
        din_ref[at, 768:896] = pltpu.roll(d_dt, 16 + 3 * slot, 1).astype(low)
        d_state = spread_heads(kept) * d_state + mm_tn(cc, d_in_y)
        d_pre = jnp.concatenate([d_b, d_c, d_x], 1) * silu_slope(pre, pre_sig)
        dpre_ref[CHUNK : CHUNK + 8] = dpre_ref[0:8]
        dpre_ref[0:CHUNK] = d_pre
        g_taps[4] = g_taps[4] + jnp.sum(d_pre, axis=0, keepdims=True)
        g_taps[3] = g_taps[3] + jnp.sum(d_pre * ext_ref[pl.ds(r + 8, CHUNK)], axis=0, keepdims=True)
        d_ext = taps_ref[3:4] * d_pre
        for k in (1, 2, 3):
            same = (ids_ref[pl.ds(r + 8 - k, CHUNK), 40:41] == doc).astype(f32)
            g_taps[3 - k] = g_taps[3 - k] + jnp.sum(
                d_pre * same * ext_ref[pl.ds(r + 8 - k, CHUNK)], axis=0, keepdims=True
            )
            same = (ids_ref[pl.ds(r + 8 + k, CHUNK), 40:41] == doc).astype(f32)
            d_ext = d_ext + taps_ref[3 - k : 4 - k] * (dpre_ref[k : k + CHUNK] * same)
        din_ref[at, 512:768] = d_ext[:, 0:256].astype(low)
        din_ref[at, 256:448] = d_ext[:, 256:448].astype(low)
        next(b_steps, None)
    loads[1].wait()
    small_ref[...] = jnp.zeros((2, 8, 512), f32)
    for k in range(5):
        small_ref[1, k : k + 1, 0:448] = g_taps[k]
    small_ref[1, 5:6, 0:192] = g_gain
    small_ref[1, 5:6, 256:448] = g_skip
    small_ref[1, 6:7, 0:128] = g_dt
    small_ref[1, 6:7, 256:384] = g_rate * rate

    def layer(k):
        at = pl.ds(pl.multiple_of(zs[k] * LAYER, LAYER), LAYER)

        @pl.loop(0, 3)
        def _(i):
            n = pl.ds(pl.multiple_of(i * 512, 512), 512)
            part_ref[at, n] = mm_nt(din_ref[at], cols_ref[n, 256:1152]).astype(low)

    moved = 24 * half_here

    def grads(first, last):
        @pl.loop(first, last)
        def _(i):
            n = pl.ds(pl.multiple_of(i * 256, 256), 256)
            total = mm_tn(n1_ref[:, n], din_ref[...])
            out = mm_tn(dres_ref[:, n], mixed_ref[...])
            main_ref[n, 0:128] = out[:, 0:128].astype(low)
            main_ref[n, 128:256] = out[:, 128:256].astype(low) + shared_ref[n, 256:384]
            main_ref[n, 256:384] = total[:, 0:128].astype(low)
            main_ref[n, 384:512] = total[:, 128:256].astype(low) + shared_ref[n, 0:128]
            main_ref[n, 512:640] = total[:, 256:384].astype(low)
            main_ref[n, 640:768] = total[:, 384:512].astype(low) + shared_ref[n, 128:256]
            bcr_ref[n, 0:256] = total[:, 512:768].astype(low)
            steps_part = pltpu.roll(total[:, 768:896], moved, 1)
            bcr_ref[n, 256:384] = (steps_part + shared_ref[n, 384:512].astype(f32)).astype(low)

    mail = Mail(send)
    steps = reduce_steps(mail, part_ref, sum_ref, got, sums, recv, 64, order)
    left = [3, 2, 1, 0]
    for turn in range(13):
        if turn in (0, 1, 3, 6):
            layer(left.pop(0))
        next(steps, None)
        next(b_steps, None)
        if turn in (7, 8, 9):
            grads(2 * (turn - 7), 2 * (turn - 6))
    for _ in b_steps:
        pass
    block_ref[...] += res_ref[0:64]
    for _ in steps:
        pass
    value, gain = norm_step(sum_ref[...], own_ref[0:64].astype(f32), floats_ref[7:8])
    input_ref[...] = dres_own_ref[0:64] + value
    for i in range(4):
        small_ref[0, i : i + 1, 0:384] = gain[:, 384 * i : 384 * (i + 1)]
        small_ref[0, 4 + i : 5 + i, 0:384] = dres_own_ref[64:65, 384 * i : 384 * (i + 1)]
    b_mail.finish()
    mail.finish()


def mix_backward(*args):
    low, f32 = jnp.bfloat16, jnp.float32
    return call(
        mix_backward_kernel,
        "mix_backward",
        4,
        (
            ((1536, 768), low),
            ((1536, 384), low),
            ((2, 8, 512), f32),
            ((64, 1536), f32),
            ((64, 1536), f32),
        ),
        [
            VMEM((1024, 1536), low),
            VMEM((1024, 192), f32),
            VMEM((1024, 256), low),
            VMEM((1024, 896), low),
            VMEM((CHUNK + 8, 448), f32),
            VMEM((64, 1536), f32),
            VMEM((1024, 1536), low),
            VMEM((1040, 1536), f32),
            DMA((2,)),
        ]
        + reduce_scratch(64, 1536, low)
        + reduce_scratch(64, 1536, low)
        + [DMA((32,)), DMA((32,)), DMA((32,)), DMA((32,))],
        args,
        ((2, 5), ()),
        limit=34,
    )


def place_kernel(
    main_ref,
    bcr_ref,
    small_ref,
    block_own,
    block_other,
    input_own,
    input_other,
    geg_ref,
    geu_ref,
    ged_ref,
    sg_ref,
    su_ref,
    sd_ref,
    block_out,
    input_out,
    norm1_out,
    wz_out,
    wx_out,
    wbc_out,
    wdt_out,
    convx_out,
    convbc_out,
    biasx_out,
    biasbc_out,
    dt_out,
    log_out,
    skip_out,
    gnorm_out,
    wout_out,
    norm2_out,
    router_out,
    sgate_out,
    sup_out,
    sdown_out,
    eg_out,
    eu_out,
    ed_out,
    biasx_row,
    gnorm_row,
    heads_row,
):
    side = lax.axis_index("head")
    f32 = jnp.float32
    for own, other, out in (
        (block_own, block_other, block_out),
        (input_own, input_other, input_out),
    ):
        out[:, 0] = jnp.where(side == 0, own[...], other[...])
        out[:, 1] = jnp.where(side == 0, other[...], own[...])
    norms = small_ref[0, 0]
    taps = small_ref[1, 0, :, 0:256]
    for j in range(1, 16):
        norms = norms + small_ref[0, j]
        taps = taps + small_ref[1, j, :, 0:256]
    for i in range(4):
        norm1_out[384 * i : 384 * (i + 1)] = norms[i, 0:384]
        norm2_out[384 * i : 384 * (i + 1)] = norms[4 + i, 0:384]
    convbc_out[...] = taps[0:4]
    biasbc_out[...] = taps[4]
    wbc_out[...] = bcr_ref[:, 0:256]
    turned = jnp.concatenate([bcr_ref[:, 256:384], jnp.zeros((32, 128), f32)], 0).T
    router_out[...] = turned[0:16, 0:96]
    wdt_out[...] = jnp.where(side == 0, turned[16:40, 0:96], turned[40:64, 0:96])
    onehot = (
        lax.broadcasted_iota(jnp.int32, (192, 128), 0) // HEADW
        == lax.broadcasted_iota(jnp.int32, (192, 128), 1)
    ).astype(f32)
    for j in range(8):
        place = 8 * side + j
        wide, narrow = slice(192 * j, 192 * (j + 1)), slice(64 * j, 64 * (j + 1))
        convx_out[:, wide] = small_ref[1, place, 0:4, 256:448]
        biasx_row[:, wide] = small_ref[1, place, 4:5, 256:448]
        gnorm_row[:, wide] = small_ref[1, place, 5:6, 0:192]
        skips = jnp.broadcast_to(small_ref[1, place, 5:6, 256:448], (8, 192))
        heads_row[2:3, 3 * j : 3 * j + 3] = mm(skips, onehot, exact=True)[0:1, 0:3]
        heads_row[0:1, 3 * j : 3 * j + 3] = small_ref[1, place, 6:7, 0:3]
        heads_row[1:2, 3 * j : 3 * j + 3] = small_ref[1, place, 6:7, 256:259]
        part = main_ref[j].astype(f32)
        wz_out[:, wide] = part[:, 256:448]
        sgate_out[:, narrow] = part[:, 448:512]
        wx_out[:, wide] = part[:, 512:704]
        sup_out[:, narrow] = part[:, 704:768]
        wout_out[:, wide] = part[:, 0:192]
        sdown_out[:, narrow] = part[:, 192:256]
    biasx_out[...] = biasx_row[0]
    gnorm_out[...] = gnorm_row[0]
    dt_out[...] = heads_row[0, 0:24]
    log_out[...] = heads_row[1, 0:24]
    skip_out[...] = heads_row[2, 0:24]
    eg_out[0] = geg_ref[...] + sg_ref[...].astype(f32)
    eu_out[0] = geu_ref[...] + su_ref[...].astype(f32)
    ed_out[0] = ged_ref[...] + sd_ref[...].astype(f32)


def place(*args):
    shapes = (
        (64, 2, 1536),
        (64, 2, 1536),
        (1536,),
        (96, 1536),
        (96, 1536),
        (96, 256),
        (24, 96),
        (4, 1536),
        (4, 256),
        (1536,),
        (256,),
        (24,),
        (24,),
        (24,),
        (1536,),
        (96, 1536),
        (1536,),
        (16, 96),
        (96, 512),
        (96, 512),
        (96, 512),
        (1, 1536, 256),
        (1, 1536, 256),
        (1, 256, 1536),
    )
    vmem = pl.BlockSpec(memory_space=VMEM)
    return pl.pallas_call(
        place_kernel,
        out_shape=tuple(jax.ShapeDtypeStruct(shape, jnp.float32) for shape in shapes),
        in_specs=[vmem] * len(args),
        out_specs=(vmem,) * len(shapes),
        scratch_shapes=[
            VMEM((1, 1536), jnp.float32),
            VMEM((1, 1536), jnp.float32),
            VMEM((8, 128), jnp.float32),
        ],
        compiler_params=pltpu.CompilerParams(vmem_limit_bytes=48 << 20),
        name="place",
    )(*args)


def by_heads(
    hidden_in,
    doc_ids,
    routes,
    norm1_gain,
    w_z,
    w_x,
    w_bc,
    w_dt,
    conv_x,
    conv_bc,
    convb_x,
    convb_bc,
    dt_bias,
    a_log,
    d_skip,
    gnorm_gain,
    w_out,
    norm2_gain,
    router,
    shared_gate,
    shared_up,
    shared_down,
    expert_gate,
    expert_up,
    expert_down,
    cotangent,
):
    eg, eu, ed = expert_gate[0], expert_up[0], expert_down[0]
    n1, extras, _, cols, own, floats, small_sib, eg_o, eu_o, ed_o = enter(
        hidden_in,
        cotangent,
        w_bc,
        router.T,
        w_dt.T,
        doc_ids.T,
        routes.transpose(1, 2, 0),
        w_out.T,
        shared_down.T,
        w_z,
        shared_gate,
        w_x,
        shared_up,
        conv_x,
        convb_x,
        gnorm_gain,
        dt_bias,
        a_log,
        d_skip,
        norm1_gain,
        norm2_gain,
        conv_bc,
        convb_bc,
        eg,
        eu,
        ed,
    )
    kept, g_all, n2, scale_note, residual, scale_own, ids, consts = mix_forward(
        n1, extras, cols, floats, small_sib, own
    )
    d_res_all, pair, moe_part, *grad_experts, shared, d_res = moe(
        n2,
        scale_note,
        g_all,
        cols,
        eg,
        eg_o,
        eu,
        eu_o,
        ed,
        ed_o,
        extras,
        ids,
        residual,
        scale_own,
        floats,
        own,
    )
    main, bcr, small, block_own, input_own = mix_backward(
        d_res_all, pair, n1, cols, consts, kept, moe_part, shared, residual, d_res, own, floats
    )
    main, bcr, small, block_sib, input_sib = leave(
        main.reshape(16, 96, 768), bcr, small, block_own, input_own
    )
    results = list(
        place(main, bcr, small, block_own, block_sib, input_own, input_sib, *grad_experts)
    )
    for i in (6, 15, 17, 20):
        results[i] = results[i].T
    return tuple(results)


def solution(mesh):
    places = mesh.shape["seq"]
    whole_heads = places == 16 and mesh.shape["head"] == 2
    placed = (
        P("seq", None, None),
        P("seq", None),
        P("seq", None, None),
        P(),
        P("seq", "head"),
        P("seq", "head"),
        P("seq", None),
        P("seq", "head"),
        P(None, "head"),
        P(),
        P("head"),
        P(),
        P("head"),
        P("head"),
        P("head"),
        P("head"),
        P("head", "seq"),
        P(),
        P("seq", None),
        P("seq", "head"),
        P("seq", "head"),
        P("head", "seq"),
        P("seq", None, "head"),
        P("seq", None, "head"),
        P("seq", "head", None),
        P("seq", None, None),
    )
    return jax.shard_map(
        by_heads if whole_heads else on_device,
        mesh=mesh,
        in_specs=placed,
        out_specs=(
            P("seq", None, None),
            P("seq", None, None),
            P(),
            P("seq", "head"),
            P("seq", "head"),
            P("seq", None),
            P("seq", "head"),
            P(None, "head"),
            P(),
            P("head"),
            P(),
            P("head"),
            P("head"),
            P("head"),
            P("head"),
            P("head", "seq"),
            P(),
            P("seq", None),
            P("seq", "head"),
            P("seq", "head"),
            P("head", "seq"),
            P("seq", None, "head"),
            P("seq", None, "head"),
            P("seq", "head", None),
        ),
        check_vma=False,
    )
```

```python
import jax
import jax.numpy as jnp
from jax import lax
from jax.experimental import pallas as pl
from jax.experimental.pallas import tpu as pltpu
from jax.sharding import PartitionSpec as P

KER = 4
INNER = 3072


EPS = 1e-05
HIGH = lax.Precision.HIGHEST


def passed_along(array, axis, by):
    length = lax.axis_size(axis)
    pairs = [(i, i + by) for i in range(length) if 0 <= i + by < length]
    return lax.ppermute(array, axis, pairs)


def entering(array, axis, combine, identity, reverse):
    length, here = (lax.axis_size(axis), lax.axis_index(axis))
    everything = jax.tree.map(
        lambda part, kind: lax.all_gather(part.astype(kind), axis),
        array,
        jax.tree.map(lambda a: jnp.bfloat16 if a.dtype == jnp.float32 else a.dtype, array),
    )
    start = jax.tree.map(
        lambda part, zero: jnp.broadcast_to(jnp.asarray(zero, part.dtype), part.shape),
        array,
        identity,
    )

    def hop(k, before):
        at = length - 1 - k if reverse else k
        reached = at > here if reverse else at < here
        new = combine(
            before, jax.tree.map(lambda part, own: part[at].astype(own.dtype), everything, array)
        )
        return jax.tree.map(lambda a, b: jnp.where(reached, a, b), new, before)

    return lax.fori_loop(0, length, hop, start)


def shortened(array):

    def short(part):
        return part.astype(jnp.bfloat16) if part.dtype == jnp.float32 else part

    return jax.tree.map(short, array)


def conv_apply(conv_ext, docs_ext, weight, conv_bias):
    length_here = conv_ext.shape[0] - (KER - 1)
    running = conv_bias
    for offset in range(KER):
        same_doc = (docs_ext[offset : offset + length_here] == docs_ext[KER - 1 :]).astype(
            jnp.float32
        )
        running = (
            running + weight[offset] * conv_ext[offset : offset + length_here] * same_doc[..., None]
        )
    return jax.nn.silu(running)


def group_parts(x_heads, step_size, b_state, decay_rate, doc_ids, prev_doc):
    log_decay = jnp.cumsum(step_size * decay_rate, axis=0)
    end_keep = (doc_ids == doc_ids[-1:]).astype(jnp.float32)
    weight = jnp.exp(log_decay[-1:] - log_decay) * end_keep[..., None] * step_size
    s_local = jnp.einsum("tsh,tshp,tsn->shpn", weight, x_heads, b_state, precision=HIGH)
    a_total = jnp.exp(log_decay[-1]) * (doc_ids[-1] == prev_doc).astype(jnp.float32)[:, None]
    return (s_local, a_total)


def group_output(x_heads, step_size, b_state, c_state, decay_rate, doc_ids, prev_doc, s_in):
    length_here = x_heads.shape[0]
    log_decay = jnp.cumsum(step_size * decay_rate, axis=0)
    causal = jnp.arange(length_here)[:, None] >= jnp.arange(length_here)[None, :]
    pair_mask = (causal[:, :, None] & (doc_ids[:, None, :] == doc_ids[None, :, :])).astype(
        jnp.float32
    )
    gap_decay = log_decay[:, None] - log_decay[None, :]
    decay_table = (
        jnp.exp(jnp.where(pair_mask[..., None] > 0, gap_decay, 0.0)) * pair_mask[..., None]
    )
    cross_dot = jnp.einsum("tsn,usn->tus", c_state, b_state, precision=HIGH)
    y_intra = jnp.einsum(
        "tush,ush,ushp->tshp",
        decay_table * cross_dot[..., None],
        step_size,
        x_heads,
        precision=HIGH,
    )
    enters = jnp.exp(log_decay) * (doc_ids == prev_doc[None, :]).astype(jnp.float32)[..., None]
    y_inter = jnp.einsum("tsn,shpn->tshp", c_state, s_in, precision=HIGH) * enters[..., None]
    return y_intra + y_inter


def ssm_local(x_heads, step_size, b_state, c_state, decay_rate, s_in, doc_ids, prev_doc):
    y_core = group_output(x_heads, step_size, b_state, c_state, decay_rate, doc_ids, prev_doc, s_in)
    s_local, a_total = group_parts(x_heads, step_size, b_state, decay_rate, doc_ids, prev_doc)
    return (y_core, a_total[..., None, None] * s_in + s_local)


def carry_combine(earlier, later_part):
    return (earlier[0] * later_part[0], later_part[0][..., None, None] * earlier[1] + later_part[1])


def head_total(partial_sum):
    return lax.psum(partial_sum, "head")


def flat_dot(left_side, right_side):
    lead_dims = left_side.shape[:-1]
    product = jnp.dot(
        left_side.reshape(-1, left_side.shape[-1]), right_side, preferred_element_type=jnp.float32
    )
    return product.reshape(lead_dims + (right_side.shape[-1],))


def flat_dot_t(left_side, right_side):
    lead_dims = left_side.shape[:-1]
    product = lax.dot_general(
        left_side.reshape(-1, left_side.shape[-1]),
        right_side,
        (((1,), (1,)), ((), ())),
        preferred_element_type=jnp.float32,
    )
    return product.reshape(lead_dims + (right_side.shape[0],))


def outer_sum(left_side, right_side):
    return lax.dot_general(
        left_side.reshape(-1, left_side.shape[-1]),
        right_side.reshape(-1, right_side.shape[-1]),
        (((0,), (0,)), ((), ())),
        preferred_element_type=jnp.float32,
    )


def silu_slope(values, sigmoid_of):
    return sigmoid_of * (1.0 + values * (1.0 - sigmoid_of))


def norm_back(grad_normed, values, scale_of, gain):
    scaled_grad = grad_normed * gain
    gain_grad = jnp.sum((grad_normed * values * scale_of).reshape(-1, values.shape[-1]), axis=0)
    cube = scale_of * scale_of * scale_of
    value_grad = scale_of * scaled_grad - values * cube * jnp.mean(
        scaled_grad * values, axis=-1, keepdims=True
    )
    return (value_grad, gain_grad)


def on_device(
    hidden_in,
    doc_ids,
    routes,
    norm1_gain,
    w_z,
    w_x,
    w_bc,
    w_dt,
    conv_x,
    conv_bc,
    convb_x,
    convb_bc,
    dt_bias,
    a_log,
    d_skip,
    gnorm_gain,
    w_out,
    norm2_gain,
    router,
    shared_gate,
    shared_up,
    shared_down,
    expert_gate,
    expert_up,
    expert_down,
    cotangent,
):
    block_len, seq_here, width = hidden_in.shape
    top_count = routes.shape[-1]
    heads_here = dt_bias.shape[0]
    inner_here = convb_x.shape[0]
    head_size = inner_here // heads_here
    state_size = convb_bc.shape[0] // 2
    seq_count = lax.axis_size("seq")
    local_experts = expert_gate.shape[0]
    experts_all = local_experts * seq_count
    tok_here = block_len * seq_here
    capacity = 2 * tok_here * top_count // experts_all
    edge_len = KER - 1
    x_float = hidden_in.astype(jnp.float32)
    scale_one = lax.rsqrt(jnp.mean(x_float * x_float, axis=-1, keepdims=True) + EPS)
    normed_one = (x_float * scale_one * norm1_gain).astype(jnp.bfloat16)
    gathered = (
        lax.all_gather(w_z, "seq", axis=0, tiled=True),
        lax.all_gather(w_x, "seq", axis=0, tiled=True),
        lax.all_gather(w_dt, "seq", axis=0, tiled=True),
        lax.all_gather(w_bc, "seq", axis=0, tiled=True),
        lax.all_gather(router, "seq", axis=0, tiled=True),
        lax.all_gather(shared_gate, "seq", axis=0, tiled=True),
        lax.all_gather(shared_up, "seq", axis=0, tiled=True),
        lax.all_gather(w_out, "seq", axis=1, tiled=True),
        lax.all_gather(shared_down, "seq", axis=1, tiled=True),
    )
    full_z, full_x, full_dt, full_bc, full_router, full_sgate, full_sup, full_out, full_sdown = (
        gathered
    )
    gate_z = flat_dot(normed_one, full_z)
    proj_x = flat_dot(normed_one, full_x)
    proj_bc = flat_dot(normed_one, full_bc)
    dt_pre = flat_dot(normed_one, full_dt) + dt_bias
    conv_in = jnp.concatenate([proj_x, proj_bc], axis=-1)
    tail_in, tail_doc = (
        passed_along(conv_in[block_len - edge_len :].astype(jnp.bfloat16), "seq", 1).astype(
            jnp.float32
        ),
        passed_along(
            doc_ids[block_len - edge_len :].astype(jnp.float32).astype(jnp.bfloat16), "seq", 1
        ).astype(jnp.float32),
    )
    conv_ext = jnp.concatenate([tail_in, conv_in], 0)
    docs_ext = jnp.concatenate([tail_doc.astype(jnp.int32), doc_ids], 0)
    conv_weight = jnp.concatenate([conv_x, conv_bc], -1)
    conv_shift = jnp.concatenate([convb_x, convb_bc], -1)
    conv_out = conv_apply(conv_ext, docs_ext, conv_weight, conv_shift)
    x_heads = conv_out[..., :inner_here].reshape(block_len, seq_here, heads_here, head_size)
    b_state = conv_out[..., inner_here : inner_here + state_size]
    c_state = conv_out[..., inner_here + state_size :]
    step_size = jax.nn.softplus(dt_pre)
    decay_rate = -jnp.exp(a_log)
    prev_doc = docs_ext[edge_len - 1]
    s_local, a_total = group_parts(x_heads, step_size, b_state, decay_rate, doc_ids, prev_doc)
    ones_start = jnp.ones_like(a_total)
    zeros_start = jnp.zeros_like(s_local)
    a_before, s_before = entering(
        (a_total, s_local), "seq", carry_combine, (ones_start, zeros_start), False
    )
    y_core = group_output(
        x_heads, step_size, b_state, c_state, decay_rate, doc_ids, prev_doc, s_before
    )
    y_heads = y_core + d_skip[:, None] * x_heads
    y_flat = y_heads.reshape(block_len, seq_here, inner_here)
    gate_sig = jax.nn.sigmoid(gate_z)
    gated = y_flat * gate_z * gate_sig
    square_sum = head_total(jnp.sum(gated * gated, axis=-1, keepdims=True))
    scale_gated = lax.rsqrt(square_sum / INNER + EPS)
    mixed_out = (gated * scale_gated * gnorm_gain).astype(jnp.bfloat16)
    residual = x_float + head_total(flat_dot(mixed_out, full_out))
    scale_two = lax.rsqrt(jnp.mean(residual * residual, axis=-1, keepdims=True) + EPS)
    normed_two = (residual * scale_two * norm2_gain).astype(jnp.bfloat16)
    logits = flat_dot(normed_two, full_router)
    gate_probs = jax.nn.softmax(jnp.take_along_axis(logits, routes, axis=-1), axis=-1)
    share_gate = flat_dot(normed_two, full_sgate)
    share_up = flat_dot(normed_two, full_sup)
    share_sig = jax.nn.sigmoid(share_gate)
    share_act = (share_gate * share_sig * share_up).astype(jnp.bfloat16)
    share_part = flat_dot(share_act, full_sdown)
    slot_total = tok_here * top_count
    route_flat = routes.reshape(slot_total)
    expert_ids = jnp.arange(experts_all, dtype=jnp.int32)
    route_hits = (route_flat[:, None] == expert_ids[None, :]).astype(jnp.int32)
    slot_rank = jnp.sum(jnp.cumsum(route_hits, axis=0) * route_hits, axis=1) - 1
    target = route_flat * capacity + slot_rank
    entry_table = (
        jnp.zeros((experts_all * capacity,), jnp.int32)
        .at[target]
        .set(jnp.arange(slot_total, dtype=jnp.int32) + 1)
    )
    entry_live = entry_table > 0
    entry_slot = jnp.maximum(entry_table - 1, 0)
    entry_token = entry_slot // top_count
    tokens_flat = normed_two.reshape(tok_here, width)
    send_rows = jnp.where(
        entry_live[:, None], tokens_flat[entry_token], jnp.zeros((), jnp.bfloat16)
    ).reshape(experts_all, capacity, width)
    received = lax.all_to_all(send_rows, "seq", split_axis=0, concat_axis=0, tiled=True)
    input_row_block = received.reshape(seq_count, local_experts, received.shape[1], width)
    hid_gate = jnp.einsum(
        "jecd,edf->jecf", input_row_block, expert_gate, preferred_element_type=jnp.float32
    )
    hid_up = jnp.einsum(
        "jecd,edf->jecf", input_row_block, expert_up, preferred_element_type=jnp.float32
    )
    hid_act = (hid_gate * jax.nn.sigmoid(hid_gate) * hid_up).astype(jnp.bfloat16)
    half_out = jnp.einsum(
        "jecf,efd->jecd", hid_act, expert_down, preferred_element_type=jnp.float32
    ).astype(jnp.bfloat16)
    returned_rows = lax.all_to_all(
        half_out.reshape(received.shape), "seq", split_axis=0, concat_axis=0, tiled=True
    )
    kept_shape = (seq_count * local_experts, received.shape[1], hid_gate.shape[-1])
    returned_rows, rows_kept, gate_kept, up_kept = (
        returned_rows,
        received,
        hid_gate.reshape(kept_shape),
        hid_up.reshape(kept_shape),
    )
    slot_rows = returned_rows.reshape(-1, width)[target].reshape(tok_here, top_count, width)
    probs_flat = gate_probs.reshape(tok_here, top_count)
    routed_part = share_part.reshape(tok_here, width)
    for slot_index in range(top_count):
        routed_part = routed_part + probs_flat[:, slot_index, None] * slot_rows[
            :, slot_index
        ].astype(jnp.float32)
    moe_out = head_total(routed_part.reshape(block_len, seq_here, width))
    block_out = residual + moe_out
    gathered = (
        lax.all_gather(w_z, "seq", axis=0, tiled=True),
        lax.all_gather(w_x, "seq", axis=0, tiled=True),
        lax.all_gather(w_dt, "seq", axis=0, tiled=True),
        lax.all_gather(w_bc, "seq", axis=0, tiled=True),
        lax.all_gather(router, "seq", axis=0, tiled=True),
        lax.all_gather(shared_gate, "seq", axis=0, tiled=True),
        lax.all_gather(shared_up, "seq", axis=0, tiled=True),
        lax.all_gather(w_out, "seq", axis=1, tiled=True),
        lax.all_gather(shared_down, "seq", axis=1, tiled=True),
    )
    full_z, full_x, full_dt, full_bc, full_router, full_sgate, full_sup, full_out, full_sdown = (
        gathered
    )
    grad_out = cotangent.astype(jnp.float32)
    grad_flat = grad_out.reshape(tok_here, width)
    entry_prob = jnp.where(entry_live, gate_probs.reshape(-1)[entry_slot], 0.0)
    send_grads = (
        (entry_prob[:, None] * grad_flat[entry_token])
        .astype(jnp.bfloat16)
        .reshape(experts_all, capacity, width)
    )
    recv_grads = lax.all_to_all(send_grads, "seq", split_axis=0, concat_axis=0, tiled=True)
    grads_in = recv_grads.reshape(seq_count, local_experts, capacity, width)
    input_row_block = rows_kept.reshape(seq_count, local_experts, capacity, width)
    hid_gate = gate_kept.reshape(seq_count, local_experts, capacity, -1)
    hid_up = up_kept.reshape(seq_count, local_experts, capacity, -1)
    hid_sig = jax.nn.sigmoid(hid_gate)
    hid_act = (hid_gate * hid_sig * hid_up).astype(jnp.bfloat16)
    d_act = jnp.einsum("jecd,efd->jecf", grads_in, expert_down, preferred_element_type=jnp.float32)
    hidden_up_gradient = (d_act * hid_gate * hid_sig).astype(jnp.bfloat16)
    d_hid_gate = (d_act * hid_up * silu_slope(hid_gate, hid_sig)).astype(jnp.bfloat16)
    grad_edown = jnp.einsum("jecf,jecd->efd", hid_act, grads_in, preferred_element_type=jnp.float32)
    grad_egate = jnp.einsum(
        "uqpy,uqpn->qyn", input_row_block, d_hid_gate, preferred_element_type=jnp.float32
    )
    expert_up_gradient = jnp.einsum(
        "uqpy,uqpn->qyn", input_row_block, hidden_up_gradient, preferred_element_type=jnp.float32
    )
    d_rows = jnp.einsum(
        "jecf,edf->jecd", d_hid_gate, expert_gate, preferred_element_type=jnp.float32
    )
    d_rows = (
        d_rows
        + jnp.einsum(
            "jecf,edf->jecd", hidden_up_gradient, expert_up, preferred_element_type=jnp.float32
        )
    ).astype(jnp.bfloat16)
    back_rows = lax.all_to_all(
        d_rows.reshape(recv_grads.shape), "seq", split_axis=0, concat_axis=0, tiled=True
    )
    d_share_act = flat_dot_t(cotangent, full_sdown)
    d_share_up = (d_share_act * share_gate * share_sig).astype(jnp.bfloat16)
    d_share_gate = (d_share_act * share_up * silu_slope(share_gate, share_sig)).astype(jnp.bfloat16)
    grad_sdown = outer_sum(share_act, cotangent)
    grad_sgate = outer_sum(normed_two, d_share_gate)
    grad_sup = outer_sum(normed_two, d_share_up)
    d_normed_two = (
        flat_dot_t(d_share_gate, full_sgate) + flat_dot_t(d_share_up, full_sup)
    ).reshape(tok_here, width)
    prob_grad = jnp.stack(
        [
            jnp.sum(grad_flat * slot_rows[:, slot_index].astype(jnp.float32), axis=-1)
            for slot_index in range(top_count)
        ],
        axis=-1,
    )
    back_slots = back_rows.reshape(-1, width)[target].reshape(tok_here, top_count, width)
    for slot_index in range(top_count):
        d_normed_two = d_normed_two + back_slots[:, slot_index].astype(jnp.float32)
    d_normed_two, prob_grad = head_total(
        (
            d_normed_two.reshape(block_len, seq_here, width),
            prob_grad.reshape(block_len, seq_here, top_count),
        )
    )
    d_chosen = gate_probs * (prob_grad - jnp.sum(gate_probs * prob_grad, axis=-1, keepdims=True))
    d_logits = jnp.sum(
        d_chosen[..., None] * (routes[..., None] == expert_ids).astype(jnp.float32), axis=-2
    ).astype(jnp.bfloat16)
    grad_router = outer_sum(normed_two, d_logits)
    d_normed_two = d_normed_two + flat_dot_t(d_logits, full_router)
    d_resid_norm, grad_norm2 = norm_back(d_normed_two, residual, scale_two, norm2_gain)
    d_resid = grad_out + d_resid_norm
    d_resid_low = d_resid.astype(jnp.bfloat16)
    d_mixed = flat_dot_t(d_resid_low, full_out)
    grad_out_w = outer_sum(mixed_out, d_resid_low)
    gain_scaled = d_mixed * gnorm_gain
    grad_gnorm = jnp.sum((d_mixed * gated * scale_gated).reshape(-1, inner_here), axis=0)
    cross_sum = head_total(jnp.sum(gain_scaled * gated, axis=-1, keepdims=True))
    d_gated = (
        scale_gated * gain_scaled
        - gated * scale_gated * scale_gated * scale_gated * cross_sum / INNER
    )
    d_y = d_gated * gate_z * gate_sig
    d_gate_z = (d_gated * y_flat * silu_slope(gate_z, gate_sig)).astype(jnp.bfloat16)
    d_y_heads = d_y.reshape(x_heads.shape)
    grad_skip = jnp.sum(d_y_heads * x_heads, axis=(0, 1, 3))
    log_decay = jnp.cumsum(step_size * decay_rate, axis=0)
    enters = jnp.exp(log_decay) * (doc_ids == prev_doc[None, :]).astype(jnp.float32)[..., None]
    g_local = jnp.einsum("tsh,tshp,tsn->shpn", enters, d_y_heads, c_state, precision=HIGH)
    a_after, state_grad = entering(
        (a_total, g_local), "seq", carry_combine, (ones_start, zeros_start), True
    )

    def local_scan(x_part, step_part, b_part, c_part, rate_part, state_part):
        return ssm_local(
            x_part, step_part, b_part, c_part, rate_part, state_part, doc_ids, prev_doc
        )

    _, scan_back = jax.vjp(local_scan, x_heads, step_size, b_state, c_state, decay_rate, s_before)
    d_xh, d_step, d_bstate, d_cstate, d_rate, _ = scan_back((d_y_heads, state_grad))
    d_xh = d_xh + d_skip[:, None] * d_y_heads
    d_bc = head_total(jnp.concatenate([d_bstate, d_cstate], axis=-1))
    d_dt_pre = d_step * jax.nn.sigmoid(dt_pre)
    grad_dtb = jnp.sum(d_dt_pre, axis=(0, 1))
    grad_alog = d_rate * decay_rate
    d_conv_out = jnp.concatenate([d_xh.reshape(block_len, seq_here, inner_here), d_bc], axis=-1)

    def local_conv(ext_part, weight_part, shift_part):
        return conv_apply(ext_part, docs_ext, weight_part, shift_part)

    _, conv_back = jax.vjp(local_conv, conv_ext, conv_weight, conv_shift)
    d_ext, grad_cweight, grad_cshift = conv_back(d_conv_out)
    from_next = passed_along(shortened(d_ext[:edge_len]), "seq", -1)
    d_conv_in = d_ext[edge_len:] + jnp.concatenate(
        [jnp.zeros((block_len - edge_len,) + from_next.shape[1:], jnp.float32), from_next], 0
    )
    d_proj_x = d_conv_in[..., :inner_here].astype(jnp.bfloat16)
    d_proj_bc = d_conv_in[..., inner_here:].astype(jnp.bfloat16)
    d_dt_low = d_dt_pre.astype(jnp.bfloat16)
    grad_wz = outer_sum(normed_one, d_gate_z)
    grad_wx = outer_sum(normed_one, d_proj_x)
    grad_wbc = outer_sum(normed_one, d_proj_bc)
    grad_wdt = outer_sum(normed_one, d_dt_low)
    head_first = jnp.where(lax.axis_index("head") == 0, 1.0, 0.0)
    d_normed_one = (
        flat_dot_t(d_gate_z, full_z) + flat_dot_t(d_proj_x, full_x) + flat_dot_t(d_dt_low, full_dt)
    )
    d_normed_one = head_total(d_normed_one + head_first * flat_dot_t(d_proj_bc, full_bc))
    d_x_norm, grad_norm1 = norm_back(d_normed_one, x_float, scale_one, norm1_gain)
    input_grad = d_resid + d_x_norm
    reduced = (
        lax.psum_scatter(grad_wz, "seq", scatter_dimension=0, tiled=True),
        lax.psum_scatter(grad_wx, "seq", scatter_dimension=0, tiled=True),
        lax.psum_scatter(grad_wdt, "seq", scatter_dimension=0, tiled=True),
        lax.psum_scatter(grad_wbc, "seq", scatter_dimension=0, tiled=True),
        lax.psum_scatter(grad_router, "seq", scatter_dimension=0, tiled=True),
        lax.psum_scatter(grad_sgate, "seq", scatter_dimension=0, tiled=True),
        lax.psum_scatter(grad_sup, "seq", scatter_dimension=0, tiled=True),
        lax.psum_scatter(grad_out_w, "seq", scatter_dimension=1, tiled=True),
        lax.psum_scatter(grad_sdown, "seq", scatter_dimension=1, tiled=True),
    )
    red_z, red_x, red_dt, red_bc, red_router, red_sgate, red_sup, red_out, red_sdown = reduced
    small_sums = lax.psum(
        (
            grad_norm1,
            grad_norm2,
            grad_cweight,
            grad_cshift,
            grad_dtb,
            grad_alog,
            grad_skip,
            grad_gnorm,
        ),
        "seq",
    )
    sum_norm1, sum_norm2, sum_cweight, sum_cshift, sum_dtb, sum_alog, sum_skip, sum_gnorm = (
        small_sums
    )
    return (
        block_out,
        input_grad,
        sum_norm1,
        red_z,
        red_x,
        red_bc,
        red_dt,
        sum_cweight[:, :inner_here],
        sum_cweight[:, inner_here:],
        sum_cshift[:inner_here],
        sum_cshift[inner_here:],
        sum_dtb,
        sum_alog,
        sum_skip,
        sum_gnorm,
        red_out,
        sum_norm2,
        red_router,
        red_sgate,
        red_sup,
        red_sdown,
        grad_egate,
        expert_up_gradient,
        grad_edown,
    )


MESH = pl.DeviceIdType.MESH
VMEM = pltpu.VMEM


def peers():
    here, side = lax.axis_index("seq"), lax.axis_index("head")
    x, y, z = lax.rem(here, 2), lax.rem(here // 2, 2), here // 4
    col = x + 2 * y
    return here, side, z, col, (1 - x) + 2 * y, x + 2 * (1 - y), 3 - col


def layers(z):
    lo, hi = lax.rem(z, 2), z // 2
    return [2 * (1 - hi if k & 2 else hi) + (1 - lo if k & 1 else lo) for k in range(4)]


def call_out(devices):
    barrier = pltpu.get_barrier_semaphore()
    for device in devices:
        pl.semaphore_signal(barrier, inc=1, device_id=device, device_id_type=MESH)
    return len(devices)


def greet(devices):
    pl.semaphore_wait(pltpu.get_barrier_semaphore(), call_out(devices))


class Mail:
    def __init__(self, send, base=0):
        self.send, self.sent, self.base = send, [], base

    def put(self, src, dst, sem, to):
        copy = pltpu.make_async_remote_copy(
            src_ref=src,
            dst_ref=dst,
            send_sem=self.send.at[self.base + len(self.sent)],
            recv_sem=sem,
            device_id=to,
            device_id_type=MESH,
        )
        copy.start()
        self.sent.append(copy)

    def arrived(self, dst, sem):
        pltpu.make_async_remote_copy(
            src_ref=dst,
            dst_ref=dst,
            send_sem=self.send.at[0],
            recv_sem=sem,
            device_id=(0, 0),
            device_id_type=MESH,
        ).wait_recv()

    def finish(self):
        for copy in self.sent:
            copy.wait_send()


def rows_at(ref, start, size, step):
    return ref.at[pl.ds(pl.multiple_of(start, step), size)]


def crossing_lanes(width):
    return width // 3 * 2 if width % 384 == 0 else width


def gather_steps(mail, own_ref, out_ref, recv, recv_half, rows, half=None):
    here, side, z, col, cx, cy, cd = peers()
    zs = layers(z)
    base = 4 * z
    to_x, to_y = (base + cx, side), (base + cy, side)

    def part(place, which, ref=None):
        if half is None:
            width = out_ref.shape[1] // 2
            lane = pl.ds(which * width, width)
            if ref is not None:
                return ref.at[:, lane]
            return out_ref.at[pl.ds(pl.multiple_of(place * rows, 16), rows), lane]
        size = rows - half if which else half
        if ref is not None:
            return ref.at[pl.ds(which * half, size)]
        return rows_at(out_ref, place * rows + which * half, size, 16)

    width = out_ref.shape[1]
    cut = width if half is None else crossing_lanes(width)

    def crossing(place, which, k):
        if k == 0 or cut == width:
            return part(place, which)
        size = rows - half if which else half
        at = pl.ds(pl.multiple_of(place * rows + which * half, 16), size)
        return out_ref.at[at, pl.ds(0, cut)]

    def strip(place):
        at = pl.ds(pl.multiple_of(place * rows, 16), rows)
        return out_ref.at[at, pl.ds(cut, width - cut)]

    def onward(place, k, ref=None):
        for which in (0, 1):
            src = part(place, which, ref)
            mail.put(src, part(place, which), recv.at[6 + 4 * k + which], to_x)
            src = part(place, 1 - which, ref)
            mail.put(src, part(place, 1 - which), recv.at[8 + 4 * k + which], to_y)

    def across(k):
        at = 4 * zs[k] + cd
        mail.arrived(crossing(at, 0, k), recv_half.at[k])
        mail.arrived(crossing(at, 1, k), recv_half.at[4 + k])
        mail.arrived(part(4 * zs[k] + cx, 1), recv.at[7 + 4 * k])
        mail.arrived(part(4 * zs[k] + cy, 0), recv.at[9 + 4 * k])
        if cut == width:
            return
        if k:
            mail.arrived(strip(at), recv_half.at[7 + k])
            return
        for j in (1, 2, 3):
            mail.put(strip(at), strip(at), recv_half.at[7 + j], (4 * zs[j] + col, side))

    onward(here, 0, own_ref)
    for k in (1, 2, 3):
        for which in (0, 1):
            src = part(here, which, own_ref)
            sem = recv.at[2 * (k - 1) + which]
            mail.put(src, part(here, which), sem, (4 * zs[k] + col, side))
    yield
    for k in range(4):
        if k:
            at = 4 * zs[k] + col
            mail.arrived(part(at, 0), recv.at[2 * (k - 1)])
            mail.arrived(part(at, 1), recv.at[2 * (k - 1) + 1])
            onward(at, k)
            yield
        if k == 1:
            across(0)
            yield
        at = 4 * zs[k] + cx
        mail.arrived(part(at, 0), recv.at[6 + 4 * k])
        mail.put(crossing(at, 0, k), crossing(at, 0, k), recv_half.at[k], to_y)
        at = 4 * zs[k] + cy
        mail.arrived(part(at, 1), recv.at[8 + 4 * k])
        mail.put(crossing(at, 1, k), crossing(at, 1, k), recv_half.at[4 + k], to_x)
        yield
        if k > 1:
            across(k - 1)
            yield
    across(3)
    yield


def near(side):
    here, side, z, col, cx, cy, cd = peers()
    zs = layers(z)
    return [(4 * z + cx, side), (4 * z + cy, side)] + [(4 * zs[k] + col, side) for k in (1, 2, 3)]


def note_puts(mail, src_of, notes_out, recv_n):
    here, side = peers()[:2]
    for k in range(1, 16):
        to = lax.rem(here + k, 16)
        mail.put(src_of(to), notes_out.at[here], recv_n.at[here], (to, side))


def note_waits(mail, notes_out, recv_n):
    here = peers()[0]
    for k in range(1, 16):
        place = lax.rem(here + k, 16)
        mail.arrived(notes_out.at[place], recv_n.at[place])


SUM_ORDER = (
    ("far", 3),
    ("joined", 3),
    ("far", 2),
    ("joined", 2),
    ("column", 3),
    ("far", 1),
    ("joined", 1),
    ("column", 2),
    ("far", 0),
    ("column", 1),
    ("joined", 0),
    ("column", 0),
)


def reduce_steps(mail, part_ref, out_ref, got, sums, recv, rows, order=SUM_ORDER):
    here, side, z, col, cx, cy, cd = peers()
    zs = layers(z)
    base = 4 * z
    half = rows // 2
    got_a, got_b, got_x, got_y, got_z, got_d = got
    sum_x, sum_y, sum_z, sum_d = sums
    width = part_ref.shape[1]
    cut = crossing_lanes(width)
    to_x, to_y = (base + cx, side), (base + cy, side)
    f32 = jnp.float32

    def half_of(place, which):
        return rows_at(part_ref, place * rows + which * half, half, half)

    def near_lanes(ref, k):
        return ref.at[k, :, pl.ds(0, cut)]

    def far_lanes(ref):
        return ref.at[0, :, pl.ds(cut, width - cut)]

    def crossing(place, which):
        at = pl.multiple_of(place * rows + which * half, half)
        return part_ref.at[pl.ds(at, half), pl.ds(0, cut)]

    def far(k):
        at = 4 * zs[k] + cd
        mail.put(crossing(at, 0), near_lanes(got_a, k), recv.at[k], to_y)
        mail.put(crossing(at, 1), near_lanes(got_b, k), recv.at[4 + k], to_x)
        if cut == width:
            return
        whole = pl.ds(pl.multiple_of(at * rows, rows), rows)
        if k:
            src = part_ref.at[whole, pl.ds(cut, width - cut)]
            mail.put(src, got_d.at[k - 1], recv.at[26 + k], (4 * zs[k] + col, side))
            return
        for j in (1, 2, 3):
            mail.arrived(got_d.at[j - 1], recv.at[26 + j])
        total = part_ref[whole, cut:width].astype(f32)
        for j in range(3):
            total = total + got_d[j].astype(f32)
        sum_d[0] = total.astype(sum_d.dtype)
        mail.put(sum_d.at[0, pl.ds(0, half)], far_lanes(got_a), recv.at[30], to_y)
        mail.put(sum_d.at[0, pl.ds(half, half)], far_lanes(got_b), recv.at[31], to_x)

    def plain(k):
        mail.put(half_of(4 * zs[k] + cx, 1), got_x.at[k, pl.ds(half, half)], recv.at[12 + k], to_x)
        mail.put(half_of(4 * zs[k] + cy, 0), got_y.at[k, pl.ds(0, half)], recv.at[16 + k], to_y)

    def join(k, at, which, got_ref, sum_ref):
        mine = half_of(at, which)[...]
        mail.arrived(near_lanes(got_ref, k), recv.at[4 * which + k])
        total = mine[:, 0:cut].astype(f32) + got_ref[k, :, 0:cut].astype(f32)
        sum_ref[k, :, 0:cut] = total.astype(sum_ref.dtype)
        if cut == width:
            return
        if k:
            sum_ref[k, :, cut:width] = mine[:, cut:width]
            return
        mail.arrived(far_lanes(got_ref), recv.at[30 + which])
        total = mine[:, cut:width].astype(f32) + got_ref[k, :, cut:width].astype(f32)
        sum_ref[k, :, cut:width] = total.astype(sum_ref.dtype)

    def joined(k):
        join(k, 4 * zs[k] + cx, 0, got_a, sum_x)
        mail.put(sum_x.at[k], got_x.at[k, pl.ds(0, half)], recv.at[8 + k], to_x)
        join(k, 4 * zs[k] + cy, 1, got_b, sum_y)
        mail.put(sum_y.at[k], got_y.at[k, pl.ds(half, half)], recv.at[20 + k], to_y)

    def column(k):
        mail.arrived(got_x.at[k, pl.ds(half, half)], recv.at[12 + k])
        mail.arrived(got_y.at[k, pl.ds(0, half)], recv.at[16 + k])
        mail.arrived(got_x.at[k, pl.ds(0, half)], recv.at[8 + k])
        mail.arrived(got_y.at[k, pl.ds(half, half)], recv.at[20 + k])
        own = part_ref[pl.ds(pl.multiple_of((4 * zs[k] + col) * rows, rows), rows)].astype(f32)
        total = own + got_x[k].astype(f32) + got_y[k].astype(f32)
        if k:
            sum_z[k - 1] = total.astype(sum_z.dtype)
            mail.put(sum_z.at[k - 1], got_z.at[k - 1], recv.at[23 + k], (4 * zs[k] + col, side))
        else:
            out_ref[...] = total

    for turn, k in order:
        if turn == "far":
            far(k)
            plain(k)
        elif turn == "joined":
            joined(k)
        else:
            column(k)
        yield
    for turn, k in order:
        if turn == "column" and k:
            mail.arrived(got_z.at[k - 1], recv.at[23 + k])
            out_ref[...] += got_z[k - 1].astype(f32)


def reduce_scratch(rows, width, kind):
    half = rows // 2
    cut = crossing_lanes(width)
    shapes = [(4, half), (4, half), (4, rows), (4, rows), (3, rows), (3, rows)]
    shapes += [(4, half), (4, half), (3, rows), (1, rows)]
    across = max(width - cut, 128)
    return [
        VMEM(shape + (across if i in (5, 9) else width,), kind) for i, shape in enumerate(shapes)
    ]


def same_side(side, here):
    return [(lax.rem(here + k, 16), side) for k in range(1, 16)]


DMA = pltpu.SemaphoreType.DMA


def remote(src, dst, send, recv, to):
    return pltpu.make_async_remote_copy(
        src_ref=src,
        dst_ref=dst,
        send_sem=send,
        recv_sem=recv,
        device_id=to,
        device_id_type=MESH,
    )


def call(kernel, name, number, outs, scratch, args, spaces=None, limit=60):
    vmem = pl.BlockSpec(memory_space=VMEM)
    hbm = pl.BlockSpec(memory_space=pltpu.HBM)
    ins_far, outs_far = spaces or ((), ())
    args = [
        pltpu.with_memory_space_constraint(array, pltpu.HBM) if i in ins_far else array
        for i, array in enumerate(args)
    ]
    return pl.pallas_call(
        kernel,
        out_shape=tuple(
            pltpu.HBM(*out) if i in outs_far else jax.ShapeDtypeStruct(*out)
            for i, out in enumerate(outs)
        ),
        in_specs=[hbm if i in ins_far else vmem for i in range(len(args))],
        out_specs=tuple(hbm if i in outs_far else vmem for i in range(len(outs))),
        scratch_shapes=scratch,
        compiler_params=pltpu.CompilerParams(
            collective_id=number, has_side_effects=True, vmem_limit_bytes=limit << 20
        ),
        name=name,
    )(*args)


def of_side(ref, side):
    return jnp.where(side == 0, ref[:, 0], ref[:, 1])


def enter_kernel(
    hidden_far,
    cot_far,
    wbc_far,
    router_far,
    wdt_far,
    docs_far,
    routes_far,
    wo_far,
    sd_far,
    wz_far,
    sg_far,
    wx_far,
    su_far,
    convx_far,
    biasx_far,
    gnorm_far,
    bias_far,
    log_far,
    skip_far,
    norm1_far,
    norm2_far,
    convbc_far,
    biasbc_far,
    gate_ref,
    up_ref,
    down_ref,
    all_ref,
    extras_ref,
    extra_ref,
    cols_ref,
    own_ref,
    floats_ref,
    small_other,
    gate_other,
    up_other,
    down_other,
    n1_ref,
    mine_ref,
    misc_ref,
    blocks_ref,
    hidden_ref,
    cot_ref,
    wbc_ref,
    router_ref,
    wdt_ref,
    docs_ref,
    routes_ref,
    wo_ref,
    sd_ref,
    wz_ref,
    sg_ref,
    wx_ref,
    su_ref,
    convx_ref,
    biasx_ref,
    gnorm_ref,
    bias_ref,
    log_ref,
    skip_ref,
    norm1_ref,
    norm2_ref,
    convbc_ref,
    biasbc_ref,
    loaded,
    send,
    recv,
    recv_half,
    recv_m,
    recv_half_m,
    recv_w,
    recv_e,
    recv_s,
    local,
):
    here, side = peers()[:2]
    places = 16
    sibling = (here, 1 - side)
    peer_count = call_out(same_side(side, here) + [sibling])
    far = (wz_far, sg_far, wx_far, su_far, wo_far, sd_far, convx_far, biasx_far, gnorm_far)
    far += (bias_far, log_far, skip_far, norm1_far, norm2_far, convbc_far, biasbc_far)
    far += (hidden_far, cot_far, wbc_far, router_far, wdt_far, docs_far, routes_far)
    close = (wz_ref, sg_ref, wx_ref, su_ref, wo_ref, sd_ref, convx_ref, biasx_ref, gnorm_ref)
    close += (bias_ref, log_ref, skip_ref, norm1_ref, norm2_ref, convbc_ref, biasbc_ref)
    close += (hidden_ref, cot_ref, wbc_ref, router_ref, wdt_ref, docs_ref, routes_ref)
    loads = [pltpu.make_async_copy(*both, loaded.at[i]) for i, both in enumerate(zip(far, close))]
    for load in loads[6:] + loads[:6]:
        load.start()
    floats_ref[...] = jnp.zeros(floats_ref.shape, jnp.float32)
    misc_ref[...] = jnp.zeros(misc_ref.shape, jnp.float32)
    for load in loads[6:]:
        load.wait()
    f32, low = jnp.float32, jnp.bfloat16
    own_ref[0:64] = of_side(hidden_ref, side)
    own_ref[64:128] = of_side(cot_ref, side)
    mine_ref[:, 0:128] = jnp.where(side == 0, wbc_ref[:, 0:128], wbc_ref[:, 128:256])
    misc_ref[0:16, 0:96] = router_ref[...].astype(f32)
    misc_ref[16:40, 0:96] = wdt_ref[...].astype(f32)
    misc_ref[40:41, 0:64] = jnp.where(side == 0, docs_ref[0:1], docs_ref[1:2]).astype(f32)
    misc_ref[41:47, 0:64] = jnp.where(side == 0, routes_ref[0], routes_ref[1]).astype(f32)
    mine_ref[:, 128:256] = misc_ref[...].T[0:96].astype(low)
    floats_ref[0:4] = convx_ref[...]
    floats_ref[4:5] = biasx_ref[...][None, :]
    floats_ref[5:6] = gnorm_ref[...][None, :]
    floats_ref[6:7, 0:24] = bias_ref[...][None, :]
    floats_ref[6:7, 24:48] = log_ref[...][None, :]
    floats_ref[6:7, 48:72] = skip_ref[...][None, :]
    floats_ref[7:8] = norm1_ref[...][None, :]
    floats_ref[8:9] = norm2_ref[...][None, :]
    floats_ref[9:13, 0:256] = convbc_ref[...]
    floats_ref[13:14, 0:256] = biasbc_ref[...][None, :]
    x = own_ref[0:64].astype(jnp.float32)
    scale = lax.rsqrt(jnp.mean(x * x, axis=-1, keepdims=True) + EPS)
    n1_ref[...] = (x * scale * floats_ref[7:8]).astype(jnp.bfloat16)
    pl.semaphore_wait(pltpu.get_barrier_semaphore(), peer_count)
    depth = blocks_ref.shape[1]
    rows, extra = n1_ref.shape[0], mine_ref.shape[0]
    half_here = here // 8
    mail = Mail(send)
    mine = pltpu.make_async_copy(n1_ref, rows_at(all_ref, here * rows, rows, 16), local.at[0])
    mine.start()
    mine_too = pltpu.make_async_copy(
        mine_ref, rows_at(extras_ref, here * extra, extra, 16), local.at[18]
    )
    mine_too.start()

    def strip(place):
        return cols_ref.at[pl.ds(pl.multiple_of(place * depth, 16), depth), pl.ds(0, 768)]

    steps = gather_steps(mail, n1_ref, all_ref, recv, recv_half, rows, rows // 2)
    steps_too = gather_steps(mail, mine_ref, extras_ref, recv_m, recv_half_m, extra)
    next(steps_too)
    next(steps)
    mail.put(floats_ref.at[pl.ds(0, 8)], small_other, recv_s.at[0], sibling)
    for load in loads[:6]:
        load.wait()
    for j in range(8):
        at = 0
        for width, ref in (
            (192, wo_ref),
            (64, sd_ref),
            (192, wz_ref),
            (64, sg_ref),
            (192, wx_ref),
            (64, su_ref),
        ):
            blocks_ref[j, :, at : at + width] = ref[:, width * j : width * (j + 1)]
            at += width
    first = 8 * side + lax.rem(here, 8)
    is_mine = side == half_here
    def send_strip(k):
        to = 8 * side + lax.rem(here + k, 8)
        mail.put(blocks_ref.at[to - 8 * side], strip(here), recv_w.at[here], (to, side))

    send_strip(1)

    def keep():
        return pltpu.make_async_copy(blocks_ref.at[here - 8 * side], strip(here), local.at[1])

    def give():
        block = blocks_ref.at[first - 8 * side]
        return remote(block, strip(here), local.at[1], recv_w.at[here], (first, side))

    @pl.when(is_mine)
    def _():
        keep().start()

    @pl.when(jnp.logical_not(is_mine))
    def _():
        give().start()

    mail.put(gate_ref, gate_other, recv_s.at[1], sibling)
    mail.put(up_ref, up_other, recv_s.at[2], sibling)
    mail.put(down_ref, down_other, recv_s.at[3], sibling)
    def forward(place, k):
        return remote(strip(place), strip(place), local.at[2 + k], recv_w.at[place], sibling)

    def pass_on(k):
        place = lax.rem(here + k, places)
        forward(place, k).wait_recv()

        @pl.when(is_mine)
        def _():
            forward(place, k).start()

    turn = 0
    for _ in steps_too:
        next(steps)
        turn += 1
        if turn < 7:
            send_strip(turn + 1)
        if turn == 6:

            @pl.when(is_mine)
            def _():
                keep().wait()
                forward(here, 0).start()

            @pl.when(jnp.logical_not(is_mine))
            def _():
                forward(here, 0).wait_recv()
                give().wait_send()

    for _ in steps:
        pass
    mine.wait()
    mine_too.wait()
    for place in range(places):
        at = pl.ds(place * extra, extra)
        mail.put(extras_ref.at[at], extra_ref.at[at], recv_e.at[place], sibling)
    for k in range(1, places):
        pass_on(k)

    @pl.when(is_mine)
    def _():
        for k in range(places):
            forward(lax.rem(here + k, places), k).wait_send()

    mail.arrived(small_other, recv_s.at[0])
    mail.arrived(gate_other, recv_s.at[1])
    mail.arrived(up_other, recv_s.at[2])
    mail.arrived(down_other, recv_s.at[3])
    for place in range(places):
        mail.arrived(extra_ref.at[pl.ds(place * extra, extra)], recv_e.at[place])
    cols_ref[:, pl.ds(pl.multiple_of(768 + side * 128, 128), 128)] = extras_ref[:, 0:128]
    cols_ref[:, pl.ds(pl.multiple_of(896 - side * 128, 128), 128)] = extra_ref[:, 0:128]
    is_own = side == half_here
    cols_ref[:, 1024:1152] = jnp.where(is_own, extras_ref[:, 128:256], extra_ref[:, 128:256])
    mail.finish()


def enter(*args):
    low, f32 = jnp.bfloat16, jnp.float32
    return call(
        enter_kernel,
        "enter",
        1,
        (
            ((1024, 1536), low),
            ((1536, 256), low),
            ((1536, 256), low),
            ((1536, 1152), low),
            ((128, 1536), low),
            ((16, 1536), f32),
            ((8, 1536), f32),
            ((1536, 256), low),
            ((1536, 256), low),
            ((256, 1536), low),
        ),
        [
            VMEM((64, 1536), low),
            VMEM((96, 256), low),
            VMEM((128, 128), f32),
            VMEM((8, 96, 768), low),
        ]
        + [VMEM(array.shape, array.dtype) for array in args[:23]]
        + [
            DMA((23,)),
            DMA((90,)),
            DMA((22,)),
            DMA((11,)),
            DMA((22,)),
            DMA((11,)),
            DMA((16,)),
            DMA((16,)),
            DMA((4,)),
            DMA((19,)),
        ],
        args,
        (range(26), (7, 8, 9)),
        limit=12,
    )


FAR_FIRST = (8, 7, 9, 6, 10, 5, 11, 4, 12, 3, 13, 2, 14, 1, 15)


def leave_kernel(
    main_ref,
    bcr_ref,
    small_ref,
    block_ref,
    input_ref,
    main_parts,
    bcr_out,
    small_all,
    block_other,
    input_other,
    got_main,
    got_bcr,
    bcr_part,
    bcr_mine,
    bcr_sib,
    small_got,
    small_sum,
    *refs,
):
    got, sums, refs = refs[:6], refs[6:10], refs[10:]
    send, recv_sib, recv_main, recv_small, recv_pair, cond, r_send, r_recv = refs
    here, side = peers()[:2]
    sibling = (here, 1 - side)
    is_main = side == here // 8
    f32 = jnp.float32
    greet(same_side(side, here) + [sibling])
    mail = Mail(send)
    mail.put(small_ref, small_got, recv_sib.at[1], sibling)

    def give_main():
        return remote(main_ref, got_main, cond.at[0], recv_sib.at[0], sibling)

    def send_on(total, out, sem, slot, k):
        to = lax.rem(here + k, 16)
        return remote(total.at[to], out.at[slot], cond.at[k], sem.at[slot], (to, side))

    slot = lax.rem(here, 8)

    half = bcr_ref.at[:, pl.ds(pl.multiple_of((1 - side) * 128, 128), 128)]
    mail.put(half, got_bcr, recv_sib.at[5], sibling)

    @pl.when(jnp.logical_not(is_main))
    def _():
        give_main().start()

    mail.put(block_ref, block_other, recv_sib.at[3], sibling)
    mail.put(input_ref, input_other, recv_sib.at[4], sibling)
    mail.arrived(small_got, recv_sib.at[1])
    small_sum[...] = small_ref[...] + small_got[...]
    small_all[side, here] = small_sum[side]
    for k in range(1, 16):
        to = lax.rem(here + k, 16)
        mail.put(small_sum.at[side], small_all.at[side, here], recv_small.at[here], (to, side))

    mail.arrived(got_bcr, recv_sib.at[5])
    mine = bcr_ref[:, pl.ds(pl.multiple_of(side * 128, 128), 128)]
    bcr_part[:, 0:128] = (mine.astype(f32) + got_bcr[...].astype(f32)).astype(bcr_part.dtype)
    bcr_part[:, 128:256] = bcr_ref[:, 256:384]
    r_mail = Mail(r_send)
    steps = reduce_steps(r_mail, bcr_part, bcr_mine, got, sums, r_recv, 96)
    next(steps)
    next(steps)

    def hand_back(first, last):
        @pl.when(is_main)
        def _():
            if first == 1:
                give_main().wait_recv()
            for k in FAR_FIRST[first - 1 : last - 1]:
                to = lax.rem(here + k, 16)
                total = main_ref[to].astype(f32) + got_main[to].astype(f32)
                got_main[to] = total.astype(got_main.dtype)
                send_on(got_main, main_parts, recv_main, slot, k).start()
            if last == 16:
                total = main_ref[here].astype(f32) + got_main[here].astype(f32)
                main_parts[slot] = total.astype(main_parts.dtype)

    hand_back(1, 3)
    for j in range(6):
        next(steps)
        hand_back(3 + 2 * j, 5 + 2 * j)
    hand_back(15, 16)
    for _ in steps:
        pass
    mail.put(bcr_mine, bcr_sib, recv_sib.at[2], sibling)
    for k in range(1, 16):
        place = lax.rem(here + k, 16)
        mail.arrived(small_all.at[side, place], recv_small.at[place])
    mail.put(small_all.at[side], small_all.at[side], recv_pair, sibling)
    mail.arrived(small_all.at[1 - side], recv_pair)
    for j in range(8):

        @pl.when(8 * side + j != here)
        def _():
            mail.arrived(main_parts.at[j], recv_main.at[j])

    mail.arrived(bcr_sib, recv_sib.at[2])
    bcr_out[:, pl.ds(pl.multiple_of(side * 128, 128), 128)] = bcr_mine[:, 0:128]
    bcr_out[:, pl.ds(pl.multiple_of((1 - side) * 128, 128), 128)] = bcr_sib[:, 0:128]
    bcr_out[:, 256:384] = bcr_mine[:, 128:256] + bcr_sib[:, 128:256]
    mail.arrived(block_other, recv_sib.at[3])
    mail.arrived(input_other, recv_sib.at[4])

    @pl.when(is_main)
    def _():
        for k in range(1, 16):
            send_on(got_main, main_parts, recv_main, slot, k).wait_send()

    @pl.when(jnp.logical_not(is_main))
    def _():
        give_main().wait_send()

    r_mail.finish()
    mail.finish()


def leave(*args):
    low, f32 = jnp.bfloat16, jnp.float32
    return call(
        leave_kernel,
        "leave",
        5,
        (
            ((8, 96, 768), low),
            ((96, 384), f32),
            ((2, 16, 8, 512), f32),
            ((64, 1536), f32),
            ((64, 1536), f32),
        ),
        [
            VMEM((16, 96, 768), low),
            VMEM((1536, 128), low),
            VMEM((1536, 256), low),
            VMEM((96, 256), f32),
            VMEM((96, 256), f32),
            VMEM((2, 8, 512), f32),
            VMEM((2, 8, 512), f32),
        ]
        + reduce_scratch(96, 256, low)
        + [
            DMA((21,)),
            DMA((6,)),
            DMA((8,)),
            DMA((16,)),
            DMA,
            DMA((16,)),
            DMA((32,)),
            DMA((32,)),
        ],
        args,
        limit=10,
    )


CHUNK = 128
LAYER = 256
HEADW = 64


def mm(left, right, low=True, exact=False):
    return mm_of(left, right, ((1,), (0,)), low, exact)


def mm_nt(left, right, low=True, exact=False):
    return mm_of(left, right, ((1,), (1,)), low, exact)


def mm_tn(left, right, low=True, exact=False):
    return mm_of(left, right, ((0,), (0,)), low, exact)


def mm_of(left, right, dims, low, exact):
    if exact:
        return lax.dot_general(
            left, right, (dims, ((), ())), precision=HIGH, preferred_element_type=jnp.float32
        )
    if low:
        left, right = left.astype(jnp.bfloat16), right.astype(jnp.bfloat16)
    return lax.dot_general(left, right, (dims, ((), ())), preferred_element_type=jnp.float32)


def lanes(shape):
    return lax.broadcasted_iota(jnp.int32, shape, 1)


def by_head(parts, rows):
    lane = lanes((rows, 3 * HEADW))
    return jnp.where(lane < HEADW, parts[0], jnp.where(lane < 2 * HEADW, parts[1], parts[2]))


def spread_heads(array):
    return by_head([array[:, h : h + 1] for h in range(3)], array.shape[0])


def soft_plus(values):
    return jnp.maximum(values, 0.0) + jnp.log1p(jnp.exp(-jnp.abs(values)))


def chunk_tables(step, log_rate, doc_col, doc_row):
    row = lax.broadcasted_iota(jnp.int32, (CHUNK, CHUNK), 0)
    col = lax.broadcasted_iota(jnp.int32, (CHUNK, CHUNK), 1)
    below = (row >= col).astype(jnp.float32)
    logs = mm(below, step * log_rate, exact=True)
    logs_t, step_t = logs.T, step.T
    pair = (row >= col) & (doc_col == doc_row)
    tables = [
        jnp.exp(jnp.where(pair, logs[:, h : h + 1] - logs_t[h : h + 1], -1e9)) for h in range(3)
    ]
    return logs, tables, [step_t[h : h + 1] for h in range(3)]


def as_column(row):
    return jnp.concatenate([row, jnp.zeros((CHUNK - 8, CHUNK), jnp.float32)], 0).T


def as_row(column):
    wide = jnp.broadcast_to(column, (64, CHUNK))
    return jnp.concatenate([wide, jnp.zeros((64, CHUNK), jnp.float32)], 0).T[0:8]


KEPT = dict(z=(0, 192), y=(256, 192), dt=(512, 128), ids=(640, 128), ext=(768, 448), state=(1280, 192))


class Part:
    def __init__(self, ref, lane, width, row=0, height=None):
        self.ref, self.lane, self.width, self.row = ref, lane, width, row
        self.height = ref.shape[0] if height is None else height

    def at_of(self, index):
        rows, cols = index if isinstance(index, tuple) else (index, slice(None))
        if rows is Ellipsis:
            rows = slice(None)
        if isinstance(rows, slice):
            stop = self.height if rows.stop is None else rows.stop
            rows = slice(self.row + (rows.start or 0), self.row + stop)
        stop = self.width if cols.stop is None else cols.stop
        return rows, slice(self.lane + (cols.start or 0), self.lane + stop)

    def __getitem__(self, index):
        return self.ref[self.at_of(index)]

    def __setitem__(self, index, value):
        self.ref[self.at_of(index)] = value


def kept_views(kept_ref):
    return [Part(kept_ref, *KEPT[name]) for name in ("z", "y", "dt", "ids", "ext", "state")]


def const_views(consts_ref):
    return [
        Part(consts_ref, 0, 448, 0, 8),
        Part(consts_ref, 0, 128, 8, 8),
        Part(consts_ref, 128, 192, 8, 8),
    ]


def mix_forward_kernel(
    n1_ref,
    extras_ref,
    cols_ref,
    floats_ref,
    small_other,
    own_ref,
    kept_far,
    g_all_ref,
    n2_ref,
    note_ref,
    res_ref,
    scale_ref,
    ids_out,
    consts_ref,
    part_ref,
    gained_ref,
    notes_ref,
    sum_ref,
    notes_out,
    kept_ref,
    kept_sem,
    *refs,
):
    z_ref, y_ref, dt_ref, ids_ref, ext_ref, state_ref = kept_views(kept_ref)
    taps_ref, head_ref, gain_ref = const_views(consts_ref)
    g_ref = own_ref.at[pl.ds(64, 64)]
    got, sums, refs = refs[:6], refs[6:10], refs[10:]
    send, recv, recv_n, g_send, g_recv, g_recv_half, local = refs
    here, side, z_at = peers()[:3]
    half_here, slot = here // 8, lax.rem(here, 8)
    greet(same_side(side, here))
    low, f32 = jnp.bfloat16, jnp.float32
    mine = pltpu.make_async_copy(g_ref, rows_at(g_all_ref, here * 64, 64, 16), local)
    mine.start()
    g_mail = Mail(g_send)
    g_steps = gather_steps(g_mail, g_ref, g_all_ref, g_recv, g_recv_half, 64, 32)
    next(g_steps)

    small = jnp.where(side == half_here, floats_ref[0:8], small_other[...])
    turned = pltpu.roll(small, lax.rem(1536 - 192 * slot, 1536), 1)
    taps_ref[0:5, 0:256] = floats_ref[9:14, 0:256]
    taps_ref[5:8] = jnp.zeros((3, 448), f32)
    taps_ref[0:5, 256:448] = turned[0:5, 0:192]
    gain_ref[...] = jnp.broadcast_to(turned[5:6, 0:192], (8, 192))
    numbers = pltpu.roll(small[:, 0:128], lax.rem(128 - 3 * slot, 128), 1)[6:7]
    used = lanes((1, 128)) < 3
    head_ref[0:1] = jnp.where(used, numbers, 0.0)
    head_ref[1:2] = jnp.where(used, -jnp.exp(pltpu.roll(numbers, 104, 1)), 0.0)
    head_ref[2:3] = jnp.where(used, pltpu.roll(numbers, 80, 1), 0.0)
    ids_ref[0:8] = jnp.full((8, 128), -1.0, f32)
    ids_ref[1032:1040] = jnp.full((8, 128), -2.0, f32)
    for p in range(16):
        ids_ref[8 + 64 * p : 72 + 64 * p] = extras_ref[96 * p : 96 * p + 64, 128:256].astype(f32)
    ids_out[...] = ids_ref[...]
    notes_ref[...] = jnp.zeros(notes_ref.shape, f32)
    ext_ref[0:8] = jnp.zeros((8, 448), f32)

    @pl.loop(0, 4)
    def _(i):
        at = pl.ds(pl.multiple_of(i * LAYER, LAYER), LAYER)
        shifted = pl.ds(pl.multiple_of(i * LAYER + 8, 8), LAYER)
        rows = n1_ref[at]
        proj = mm(rows, cols_ref[:, 256:1152])
        z_ref[at] = proj[:, 0:192]
        ext_ref[shifted, 0:256] = proj[:, 512:768]
        ext_ref[shifted, 256:448] = proj[:, 256:448]
        dt_ref[at] = pltpu.roll(proj[:, 768:896], 112 - 3 * slot, 1) + head_ref[0:1]

    next(g_steps)
    rate, skip = head_ref[1:2], spread_heads(head_ref[2:3])
    state = jnp.zeros((128, 192), f32)
    ones = jnp.ones((8, 192), f32)
    for c in range(8):
        r = c * CHUNK
        at = pl.ds(r, CHUNK)
        ids = ids_ref[pl.ds(r + 8, CHUNK)]
        doc = ids[:, 40:41]
        pre = conv_pre(taps_ref, ext_ref, ids_ref, r, doc)
        act = pre * jax.nn.sigmoid(pre)
        b, cc, x = act[:, 0:128], act[:, 128:256], act[:, 256:448]
        step = soft_plus(dt_ref[at])
        logs, tables, step_t = chunk_tables(step, rate, doc, ids.T[40:41])
        cross = mm_nt(cc, b)
        stacked = jnp.concatenate([cross * tables[h] * step_t[h] for h in range(3)], 0)
        intra = mm(stacked, x)
        y = by_head([intra[h * CHUNK : (h + 1) * CHUNK] for h in range(3)], CHUNK)
        first, last = chunk_masks(ids_ref, r, doc)
        enters = jnp.exp(logs) * first
        state_ref[at] = state
        y = y + spread_heads(enters) * mm(cc, state) + skip * x
        y_ref[at] = y
        tail = jnp.exp(logs[CHUNK - 1 :] - logs) * last * step
        state = spread_heads(enters[CHUNK - 1 :]) * state + mm_tn(b, spread_heads(tail) * x)
        z = z_ref[at]
        gated = y * z * jax.nn.sigmoid(z)
        gained_ref[at] = (gated * gain_ref[0:1]).astype(low)
        squares = mm_nt(ones, gated * gated, exact=True)
        notes_ref[2 * c, :, 0:64] = squares[:, 0:64]
        notes_ref[2 * c + 1, :, 0:64] = squares[:, 64:128]
        next(g_steps, None)

    keep = pltpu.make_async_copy(kept_ref, kept_far, kept_sem)
    keep.start()
    mail = Mail(send)
    zs = layers(z_at)

    def layer(k):
        at = pl.ds(pl.multiple_of(zs[k] * LAYER, LAYER), LAYER)

        @pl.loop(0, 3)
        def _(i):
            n = pl.ds(pl.multiple_of(i * 512, 512), 512)
            part_ref[at, n] = mm_nt(gained_ref[at], cols_ref[n, 0:192]).astype(low)

    steps = reduce_steps(mail, part_ref, sum_ref, got, sums, recv, 64)
    left = [3, 2, 1, 0]
    for turn in range(13):
        if turn in (0, 2, 5, 8):
            layer(left.pop(0))
        next(steps, None)
        if turn == 4:
            notes_out[here] = notes_ref[here]
            note_puts(mail, lambda to: notes_ref.at[to], notes_out, recv_n)
        if turn > 2:
            next(g_steps, None)
    for _ in g_steps:
        pass
    for _ in steps:
        pass
    note_waits(mail, notes_out, recv_n)
    squares = notes_out[0]
    for j in range(1, 16):
        squares = squares + notes_out[j]
    scale_row = lax.rsqrt(squares / INNER + EPS)
    note_ref[...] = scale_row
    scale = as_column(scale_row)[0:64, 0:1]
    scale_ref[...] = jnp.broadcast_to(scale, (64, 128))
    projected = scale * sum_ref[...]
    res_ref[64:128] = projected
    residual = own_ref[0:64].astype(f32) + projected
    res_ref[0:64] = residual
    scale_two = lax.rsqrt(jnp.mean(residual * residual, axis=-1, keepdims=True) + EPS)
    n2_ref[...] = (residual * scale_two * floats_ref[8:9]).astype(low)
    keep.wait()
    mine.wait()
    g_mail.finish()
    mail.finish()


def conv_pre(taps_ref, ext_ref, ids_ref, r, doc):
    pre = taps_ref[4:5] + taps_ref[3:4] * ext_ref[pl.ds(r + 8, CHUNK)]
    for k in (1, 2, 3):
        same = (ids_ref[pl.ds(r + 8 - k, CHUNK), 40:41] == doc).astype(jnp.float32)
        pre = pre + taps_ref[3 - k : 4 - k] * ext_ref[pl.ds(r + 8 - k, CHUNK)] * same
    return pre


def chunk_masks(ids_ref, r, doc):
    first = (ids_ref[r + 7 : r + 8, 40:41] == doc).astype(jnp.float32)
    last = (ids_ref[r + 7 + CHUNK : r + 8 + CHUNK, 40:41] == doc).astype(jnp.float32)
    return first, last


def mix_forward(*args):
    low, f32 = jnp.bfloat16, jnp.float32
    return call(
        mix_forward_kernel,
        "mix_forward",
        2,
        (
            ((1040, 1536), f32),
            ((1024, 1536), low),
            ((64, 1536), low),
            ((8, 128), f32),
            ((128, 1536), f32),
            ((64, 128), f32),
            ((1040, 128), f32),
            ((16, 512), f32),
        ),
        [
            VMEM((1024, 1536), low),
            VMEM((1024, 192), low),
            VMEM((16, 8, 128), f32),
            VMEM((64, 1536), f32),
            VMEM((16, 8, 128), f32),
            VMEM((1040, 1536), f32),
            DMA,
        ]
        + reduce_scratch(64, 1536, low)
        + [
            DMA((47,)),
            DMA((32,)),
            DMA((16,)),
            DMA((33,)),
            DMA((22,)),
            DMA((11,)),
            DMA,
        ],
        args,
        ((), (0,)),
        limit=24,
    )


def moe_kernel(
    own_ref,
    scale_note_ref,
    g_ref,
    cols_ref,
    eg_far,
    ego_far,
    eu_far,
    euo_far,
    ed_far,
    edo_far,
    extras_ref,
    ids_ref,
    res_ref,
    scale_ref,
    floats_ref,
    mine_ref,
    dres_ref,
    cross_ref,
    moe_ref,
    geg_far,
    geu_far,
    ged_far,
    sg_ref,
    su_ref,
    sd_ref,
    shared_ref,
    dres_own_ref,
    n2_ref,
    act_ref,
    hid_ref,
    probs_ref,
    notes_ref,
    notes_out,
    sum_ref,
    low_ref,
    note_ref,
    og_ref,
    ou_ref,
    od_ref,
    geg_ref,
    geu_ref,
    ged_ref,
    up_ref,
    down_ref,
    both_ref,
    loaded,
    *refs,
):
    got, sums, refs = refs[:6], refs[6:10], refs[10:]
    send, recv, recv_n, d_send, d_recv, d_recv_half, d_recv_n = refs[:7]
    n_send, n_recv, n_recv_half, e_send, e_recv, local = refs[7:]
    loads = [
        pltpu.make_async_copy(far, close, loaded.at[i])
        for i, (far, close) in enumerate(
            (
                (eg_far, up_ref.at[:, pl.ds(0, 256)]),
                (ego_far, up_ref.at[:, pl.ds(256, 256)]),
                (eu_far, up_ref.at[:, pl.ds(640, 256)]),
                (euo_far, up_ref.at[:, pl.ds(896, 256)]),
                (ed_far, down_ref.at[pl.ds(0, 256)]),
                (edo_far, down_ref.at[pl.ds(256, 256)]),
            )
        )
    ]
    for load in loads:
        load.start()
    here, side, z_at = peers()[:3]
    sibling = (here, 1 - side)
    greet(same_side(side, here) + [sibling])
    low, f32 = jnp.bfloat16, jnp.float32
    zs = layers(z_at)
    keep = pltpu.make_async_copy(own_ref, rows_at(n2_ref, here * 64, 64, 16), local.at[1])
    keep.start()
    n_mail = Mail(n_send)
    n_steps = gather_steps(n_mail, own_ref, n2_ref, n_recv, n_recv_half, 64, 32)
    next(n_steps)
    notes_ref[...] = jnp.zeros(notes_ref.shape, f32)
    lane = lanes((LAYER, 128))
    lane640 = lanes((LAYER, 640))
    up_ref[:, 512:640] = cols_ref[:, 384:512]
    up_ref[:, 1152:1280] = cols_ref[:, 640:768]
    for i in range(12):
        n = slice(128 * i, 128 * (i + 1))
        down_ref[512:640, n] = cols_ref[n, 128:256].astype(f32).T.astype(low)
    for load in loads:
        load.wait()

    def layer(k, piece):
        start = pl.multiple_of(zs[k] * LAYER, LAYER)
        at = pl.ds(start, LAYER)
        if piece == 0:
            rows = n2_ref[at]
            logits = mm(rows, extras_ref[:, 128:256])
            ids = ids_ref[pl.ds(pl.multiple_of(start + 8, 8), LAYER)]
            named = jnp.zeros((LAYER, 128), f32)
            for j in range(6):
                named = jnp.where(lane.astype(f32) == ids[:, 41 + j : 42 + j], 1.0, named)
            top = jnp.max(jnp.where(named > 0, logits, -1e30), axis=-1, keepdims=True)
            raised = jnp.exp(jnp.where(named > 0, logits - top, 0.0)) * named
            probs_ref[at] = raised / jnp.sum(raised, axis=-1, keepdims=True)
            both_ref[...] = mm(rows, up_ref[...])
            return
        if piece == 1:
            chosen = jnp.where(lane == here, probs_ref[at], 0.0)
            prob = jnp.sum(chosen, axis=-1, keepdims=True)
            weight = jnp.where(lane640 < 512, prob, jnp.where(lane640 < 576, 0.0, 1.0))
            gate, up = both_ref[:, 0:640], both_ref[:, 640:1280]
            d_act = mm_nt(g_ref[at], down_ref[...])
            sig = jax.nn.sigmoid(gate)
            act = gate * sig * up
            act_ref[at] = (act * weight).astype(low)
            slopes = jnp.sum((act * d_act)[:, 0:512], axis=-1, keepdims=True)
            d_act = d_act * weight
            hid_ref[at, 0:640] = (d_act * up * silu_slope(gate, sig)).astype(low)
            hid_ref[at, 640:1280] = (d_act * gate * sig).astype(low)
            for j in range(4):
                notes_ref[4 * zs[k] + j] = as_row(slopes[64 * j : 64 * (j + 1)])
            return

        @pl.loop(0, 3)
        def _(i):
            n = pl.ds(pl.multiple_of(i * 512, 512), 512)
            moe_ref[at, n] = mm_nt(hid_ref[at], up_ref[n]).astype(low)

    e_mail = Mail(e_send)

    def up_grads(first, last):
        @pl.loop(first, last)
        def _(i):
            n = pl.ds(pl.multiple_of(i * 256, 256), 256)
            total = mm_tn(n2_ref[:, n], hid_ref[...])
            geg_ref[n] = total[:, 0:256]
            og_ref[n] = total[:, 256:512].astype(low)
            shared_ref[n, 0:128] = total[:, 512:640].astype(low)
            geu_ref[n] = total[:, 640:896]
            ou_ref[n] = total[:, 896:1152].astype(low)
            shared_ref[n, 128:256] = total[:, 1152:1280].astype(low)

    def give_up():
        e_mail.put(og_ref, sg_ref, e_recv.at[0], sibling)
        e_mail.put(ou_ref, su_ref, e_recv.at[1], sibling)

    def down_grads():
        od_ref[...] = mm_tn(act_ref[:, 256:512], g_ref[...]).astype(low)
        e_mail.put(od_ref, sd_ref, e_recv.at[2], sibling)
        ged_ref[...] = mm_tn(act_ref[:, 0:256], g_ref[...])

    def shared_down():
        @pl.loop(0, 6)
        def _(i):
            n = pl.ds(pl.multiple_of(i * 256, 256), 256)
            shared_ref[n, 256:384] = mm_tn(g_ref[:, n], act_ref[:, 512:640]).astype(low)

    def moe_part(first, last):
        @pl.loop(first, last)
        def _(i):
            at = pl.ds(pl.multiple_of(i * LAYER, LAYER), LAYER)
            total = mm(act_ref[at], down_ref[...])
            moe_ref[at] = total.astype(low)

    mail = Mail(send)
    steps = reduce_steps(mail, moe_ref, sum_ref, got, sums, recv, 64)

    for _ in range(4):
        next(n_steps)
    keep.wait()
    for j in range(4):
        layer(j, 0)
        next(n_steps, None)
        layer(j, 1)
        next(n_steps, None)
        layer(j, 2)
        next(n_steps, None)
    for turn in range(10):
        next(steps)
        if turn == 4:
            notes_out[here] = notes_ref[here]
            note_puts(mail, lambda to: notes_ref.at[to], notes_out, recv_n)
    up_grads(0, 3)
    next(steps)
    for _ in steps:
        pass
    note_waits(mail, notes_out, recv_n)

    slopes = jnp.concatenate([notes_out[j, 0:1] for j in range(16)], 0)
    slopes = jnp.concatenate([slopes, jnp.zeros((112, 128), f32)], 0).T[0:64]
    own = pl.ds(pl.multiple_of(here * 64, 64), 64)
    probs = probs_ref[own]
    d_logits = probs * (slopes - jnp.sum(probs * slopes, axis=-1, keepdims=True))
    d_logits = d_logits.astype(low)
    dn2 = sum_ref[...] + mm_nt(d_logits, extras_ref[:, 128:256])
    value, gain = norm_step(dn2, res_ref[0:64], floats_ref[8:9])
    dres_own_ref[64:72] = jnp.broadcast_to(gain, (8, 1536))
    d_res = mine_ref[64:128].astype(f32) + value
    dres_own_ref[0:64] = d_res
    low_ref[...] = d_res.astype(low)
    cross = jnp.sum(low_ref[...].astype(f32) * res_ref[64:128], axis=-1, keepdims=True)
    first = lax.broadcasted_iota(jnp.int32, (8, 128), 0) == 0
    note_ref[...] = jnp.where(first, as_row(cross / scale_ref[:, 0:1]), scale_note_ref[...])
    mine = pltpu.make_async_copy(low_ref, rows_at(dres_ref, here * 64, 64, 16), local.at[0])
    mine.start()
    d_mail = Mail(d_send)
    d_steps = gather_steps(d_mail, low_ref, dres_ref, d_recv, d_recv_half, 64, 32)
    next(d_steps)
    cross_ref[here] = note_ref[...]
    note_puts(d_mail, lambda to: note_ref, cross_ref, d_recv_n)
    shared_ref[:, 384:512] = mm_tn(n2_ref[own], d_logits).astype(low)
    next(d_steps)
    mail.finish()
    for i in range(3):
        up_grads(3 + i, 4 + i)
        next(d_steps)
    give_up()
    down_grads()
    next(d_steps)
    stores = [
        pltpu.make_async_copy(geg_ref, geg_far, local.at[2]),
        pltpu.make_async_copy(geu_ref, geu_far, local.at[3]),
        pltpu.make_async_copy(ged_ref, ged_far, local.at[4]),
    ]
    for store in stores:
        store.start()
    for i in range(4):
        moe_part(i, i + 1)
        next(d_steps)
    shared_down()
    for _ in d_steps:
        pass
    e_mail.arrived(sg_ref, e_recv.at[0])
    e_mail.arrived(su_ref, e_recv.at[1])
    e_mail.arrived(sd_ref, e_recv.at[2])
    note_waits(d_mail, cross_ref, d_recv_n)
    mine.wait()
    for store in stores:
        store.wait()
    n_mail.finish()
    e_mail.finish()
    d_mail.finish()


def norm_step(grad, values, gain):
    scale = lax.rsqrt(jnp.mean(values * values, axis=-1, keepdims=True) + EPS)
    gain_grad = jnp.sum(grad * values * scale, axis=0, keepdims=True)
    scaled = grad * gain
    pull = scale * scale * scale * jnp.mean(scaled * values, axis=-1, keepdims=True)
    return scale * scaled - values * pull, gain_grad


def moe(*args):
    low, f32 = jnp.bfloat16, jnp.float32
    return call(
        moe_kernel,
        "moe",
        3,
        (
            ((1024, 1536), low),
            ((16, 8, 128), f32),
            ((1024, 1536), low),
            ((1536, 256), f32),
            ((1536, 256), f32),
            ((256, 1536), f32),
            ((1536, 256), low),
            ((1536, 256), low),
            ((256, 1536), low),
            ((1536, 512), low),
            ((72, 1536), f32),
        ),
        [
            VMEM((1024, 1536), low),
            VMEM((1024, 640), low),
            VMEM((1024, 1280), low),
            VMEM((1024, 128), f32),
            VMEM((16, 8, 128), f32),
            VMEM((16, 8, 128), f32),
            VMEM((64, 1536), f32),
            VMEM((64, 1536), low),
            VMEM((8, 128), f32),
            VMEM((1536, 256), low),
            VMEM((1536, 256), low),
            VMEM((256, 1536), low),
            VMEM((1536, 256), f32),
            VMEM((1536, 256), f32),
            VMEM((256, 1536), f32),
            VMEM((1536, 1280), low),
            VMEM((640, 1536), low),
            VMEM((LAYER, 1280), f32),
            DMA((6,)),
        ]
        + reduce_scratch(64, 1536, low)
        + [
            DMA((47,)),
            DMA((32,)),
            DMA((16,)),
            DMA((48,)),
            DMA((22,)),
            DMA((11,)),
            DMA((16,)),
            DMA((33,)),
            DMA((22,)),
            DMA((11,)),
            DMA((3,)),
            DMA((3,)),
            DMA((5,)),
        ],
        args,
        (range(4, 10), (3, 4, 5, 6, 7, 8)),
        limit=36,
    )


def mix_backward_kernel(
    dres_ref,
    cross_ref,
    n1_far,
    cols_ref,
    consts_ref,
    kept_far,
    moe_ref,
    shared_ref,
    res_ref,
    dres_own_ref,
    own_ref,
    floats_ref,
    main_ref,
    bcr_ref,
    small_ref,
    block_ref,
    input_ref,
    part_ref,
    dm_ref,
    mixed_ref,
    din_ref,
    dpre_ref,
    sum_ref,
    n1_ref,
    kept_ref,
    loaded,
    *refs,
):
    got, sums, refs = refs[:6], refs[6:10], refs[10:]
    b_got, b_sums, refs = refs[:6], refs[6:10], refs[10:]
    send, recv, b_send, b_recv = refs
    loads = (
        pltpu.make_async_copy(kept_far, kept_ref, loaded.at[0]),
        pltpu.make_async_copy(n1_far, n1_ref, loaded.at[1]),
    )
    for load in loads:
        load.start()
    z_ref, y_ref, dt_ref, ids_ref, ext_ref, state_ref = kept_views(kept_ref)
    taps_ref, head_ref, gain_ref = const_views(consts_ref)
    here, side, z_at = peers()[:3]
    half_here, slot = here // 8, lax.rem(here, 8)
    greet(near(side))
    low, f32 = jnp.bfloat16, jnp.float32
    zs = layers(z_at)
    b_mail = Mail(b_send)
    order = [("far", 3), ("far", 2), ("joined", 3), ("far", 1), ("joined", 2), ("column", 3)]
    order += [("far", 0), ("joined", 1), ("column", 2), ("joined", 0), ("column", 1), ("column", 0)]
    b_steps = reduce_steps(b_mail, moe_ref, block_ref, b_got, b_sums, b_recv, 64, order)
    next(b_steps)

    @pl.loop(0, 4)
    def _(i):
        at = pl.ds(pl.multiple_of(i * LAYER, LAYER), LAYER)
        dm_ref[at] = mm(dres_ref[at], cols_ref[:, 0:192])

    next(b_steps)
    loads[0].wait()
    rate, skip = head_ref[1:2], spread_heads(head_ref[2:3])
    onehot = (
        lax.broadcasted_iota(jnp.int32, (192, 128), 0) // HEADW
        == lax.broadcasted_iota(jnp.int32, (192, 128), 1)
    ).astype(f32)
    row = lax.broadcasted_iota(jnp.int32, (CHUNK, CHUNK), 0)
    lane = lanes((CHUNK, CHUNK))
    above = (row <= lane).astype(f32)
    lane192 = lanes((CHUNK, 192))
    masks = [((lane192 // HEADW) == h).astype(f32) for h in range(3)]
    d_state = jnp.zeros((128, 192), f32)
    g_gain = jnp.zeros((1, 192), f32)
    g_skip = jnp.zeros((1, 192), f32)
    g_rate = jnp.zeros((1, 128), f32)
    g_dt = jnp.zeros((1, 128), f32)
    g_taps = [jnp.zeros((1, 448), f32) for _ in range(5)]
    dpre_ref[0:8] = jnp.zeros((8, 448), f32)
    din_ref[:, 128:256] = jnp.zeros((1024, 128), low)
    din_ref[:, 384:512] = jnp.zeros((1024, 128), low)
    mixed_ref[:, 128:256] = jnp.zeros((1024, 128), low)
    for c in range(7, -1, -1):
        r = c * CHUNK
        at = pl.ds(r, CHUNK)
        ids = ids_ref[pl.ds(r + 8, CHUNK)]
        doc = ids[:, 40:41]
        noted = jnp.concatenate([cross_ref[2 * c, :, 0:64], cross_ref[2 * c + 1, :, 0:64]], 1)
        noted = as_column(noted)
        scale = noted[:, 1:2]
        pull = scale * scale * scale * noted[:, 0:1] / INNER
        z, y, dm, gain = z_ref[at], y_ref[at], dm_ref[at], gain_ref[0:1]
        sig = jax.nn.sigmoid(z)
        gated = y * z * sig
        scaled = gated * scale
        mixed_ref[at, 0:192] = (scaled * gain).astype(low)
        g_gain = g_gain + jnp.sum(dm * scaled, axis=0, keepdims=True)
        d_gated = scale * gain * dm - gated * pull
        d_y = d_gated * z * sig
        din_ref[at, 0:192] = (d_gated * y * silu_slope(z, sig)).astype(low)
        pre = conv_pre(taps_ref, ext_ref, ids_ref, r, doc)
        pre_sig = jax.nn.sigmoid(pre)
        act = pre * pre_sig
        b, cc, x = act[:, 0:128], act[:, 128:256], act[:, 256:448]
        g_skip = g_skip + jnp.sum(d_y * x, axis=0, keepdims=True)
        dt = dt_ref[at]
        step = soft_plus(dt)
        logs, tables, step_t = chunk_tables(step, rate, doc, ids.T[40:41])
        cross = mm_nt(cc, b)
        decays = [tables[h] * step_t[h] for h in range(3)]
        stacked = jnp.concatenate([cross * decays[h] for h in range(3)], 0)
        d_ys = jnp.concatenate([d_y * masks[h] for h in range(3)], 0)
        d_stack = mm_nt(d_ys, x)
        d_x = skip * d_y + mm_tn(stacked, d_ys)
        state = state_ref[at]
        first, last = chunk_masks(ids_ref, r, doc)
        enters = jnp.exp(logs) * first
        d_in_y = spread_heads(enters) * d_y
        from_state = mm(cc, state)
        tail_w = jnp.exp(logs[CHUNK - 1 :] - logs) * last
        tail = tail_w * step
        tail_x = spread_heads(tail)
        to_state = mm(b, d_state)
        d_x = d_x + tail_x * to_state
        kept = enters[CHUNK - 1 :]
        d_kept = jnp.sum(d_state * state, axis=0, keepdims=True)
        folded = mm(
            jnp.concatenate(
                [d_y * from_state, x * to_state, jnp.broadcast_to(d_kept, (8, 192))], 0
            ),
            onehot,
            exact=True,
        )
        d_enters, d_tail = folded[:CHUNK], folded[CHUNK : 2 * CHUNK]
        d_kept = folded[2 * CHUNK : 2 * CHUNK + 1]
        d_cross = jnp.zeros((CHUNK, CHUNK), f32)
        row_sums = jnp.zeros((CHUNK, CHUNK), f32)
        col_sums = []
        for h in range(3):
            d_a = d_stack[h * CHUNK : (h + 1) * CHUNK]
            d_cross = d_cross + d_a * decays[h]
            plain = d_a * cross * tables[h]
            col_sums.append(jnp.sum(plain, axis=0, keepdims=True))
            total = jnp.sum(plain * step_t[h], axis=1, keepdims=True)
            row_sums = jnp.where(lane == h, total, row_sums)
        col_sums = as_column(jnp.concatenate(col_sums + [jnp.zeros((5, CHUNK), f32)], 0))
        d_c = mm(d_cross, b) + mm_nt(d_in_y, state)
        d_b = mm_tn(d_cross, cc) + mm_nt(tail_x * x, d_state)
        pulled = d_tail * tail
        d_logs = row_sums - step * col_sums + d_enters * enters - pulled
        d_last = jnp.sum(pulled, axis=0, keepdims=True) + d_kept * kept
        d_logs = d_logs + jnp.where(row == CHUNK - 1, d_last, 0.0)
        d_l = mm(above, d_logs, exact=True)
        d_step = col_sums + d_tail * tail_w + d_l * rate
        g_rate = g_rate + jnp.sum(d_l * step, axis=0, keepdims=True)
        d_dt = jnp.where(lane < 3, d_step * jax.nn.sigmoid(dt), 0.0)
        g_dt = g_dt + jnp.sum(d_dt, axis=0, keepdims=True)
        din_ref[at, 768:896] = pltpu.roll(d_dt, 16 + 3 * slot, 1).astype(low)
        d_state = spread_heads(kept) * d_state + mm_tn(cc, d_in_y)
        d_pre = jnp.concatenate([d_b, d_c, d_x], 1) * silu_slope(pre, pre_sig)
        dpre_ref[CHUNK : CHUNK + 8] = dpre_ref[0:8]
        dpre_ref[0:CHUNK] = d_pre
        g_taps[4] = g_taps[4] + jnp.sum(d_pre, axis=0, keepdims=True)
        g_taps[3] = g_taps[3] + jnp.sum(d_pre * ext_ref[pl.ds(r + 8, CHUNK)], axis=0, keepdims=True)
        d_ext = taps_ref[3:4] * d_pre
        for k in (1, 2, 3):
            same = (ids_ref[pl.ds(r + 8 - k, CHUNK), 40:41] == doc).astype(f32)
            g_taps[3 - k] = g_taps[3 - k] + jnp.sum(
                d_pre * same * ext_ref[pl.ds(r + 8 - k, CHUNK)], axis=0, keepdims=True
            )
            same = (ids_ref[pl.ds(r + 8 + k, CHUNK), 40:41] == doc).astype(f32)
            d_ext = d_ext + taps_ref[3 - k : 4 - k] * (dpre_ref[k : k + CHUNK] * same)
        din_ref[at, 512:768] = d_ext[:, 0:256].astype(low)
        din_ref[at, 256:448] = d_ext[:, 256:448].astype(low)
        next(b_steps, None)
    loads[1].wait()
    small_ref[...] = jnp.zeros((2, 8, 512), f32)
    for k in range(5):
        small_ref[1, k : k + 1, 0:448] = g_taps[k]
    small_ref[1, 5:6, 0:192] = g_gain
    small_ref[1, 5:6, 256:448] = g_skip
    small_ref[1, 6:7, 0:128] = g_dt
    small_ref[1, 6:7, 256:384] = g_rate * rate

    def layer(k):
        at = pl.ds(pl.multiple_of(zs[k] * LAYER, LAYER), LAYER)

        @pl.loop(0, 3)
        def _(i):
            n = pl.ds(pl.multiple_of(i * 512, 512), 512)
            part_ref[at, n] = mm_nt(din_ref[at], cols_ref[n, 256:1152]).astype(low)

    moved = 24 * half_here

    def grads(first, last):
        @pl.loop(first, last)
        def _(i):
            n = pl.ds(pl.multiple_of(i * 256, 256), 256)
            total = mm_tn(n1_ref[:, n], din_ref[...])
            out = mm_tn(dres_ref[:, n], mixed_ref[...])
            main_ref[n, 0:128] = out[:, 0:128].astype(low)
            main_ref[n, 128:256] = out[:, 128:256].astype(low) + shared_ref[n, 256:384]
            main_ref[n, 256:384] = total[:, 0:128].astype(low)
            main_ref[n, 384:512] = total[:, 128:256].astype(low) + shared_ref[n, 0:128]
            main_ref[n, 512:640] = total[:, 256:384].astype(low)
            main_ref[n, 640:768] = total[:, 384:512].astype(low) + shared_ref[n, 128:256]
            bcr_ref[n, 0:256] = total[:, 512:768].astype(low)
            steps_part = pltpu.roll(total[:, 768:896], moved, 1)
            bcr_ref[n, 256:384] = (steps_part + shared_ref[n, 384:512].astype(f32)).astype(low)

    mail = Mail(send)
    steps = reduce_steps(mail, part_ref, sum_ref, got, sums, recv, 64, order)
    left = [3, 2, 1, 0]
    for turn in range(13):
        if turn in (0, 1, 3, 6):
            layer(left.pop(0))
        next(steps, None)
        next(b_steps, None)
        if turn in (7, 8, 9):
            grads(2 * (turn - 7), 2 * (turn - 6))
    for _ in b_steps:
        pass
    block_ref[...] += res_ref[0:64]
    for _ in steps:
        pass
    value, gain = norm_step(sum_ref[...], own_ref[0:64].astype(f32), floats_ref[7:8])
    input_ref[...] = dres_own_ref[0:64] + value
    for i in range(4):
        small_ref[0, i : i + 1, 0:384] = gain[:, 384 * i : 384 * (i + 1)]
        small_ref[0, 4 + i : 5 + i, 0:384] = dres_own_ref[64:65, 384 * i : 384 * (i + 1)]
    b_mail.finish()
    mail.finish()


def mix_backward(*args):
    low, f32 = jnp.bfloat16, jnp.float32
    return call(
        mix_backward_kernel,
        "mix_backward",
        4,
        (
            ((1536, 768), low),
            ((1536, 384), low),
            ((2, 8, 512), f32),
            ((64, 1536), f32),
            ((64, 1536), f32),
        ),
        [
            VMEM((1024, 1536), low),
            VMEM((1024, 192), f32),
            VMEM((1024, 256), low),
            VMEM((1024, 896), low),
            VMEM((CHUNK + 8, 448), f32),
            VMEM((64, 1536), f32),
            VMEM((1024, 1536), low),
            VMEM((1040, 1536), f32),
            DMA((2,)),
        ]
        + reduce_scratch(64, 1536, low)
        + reduce_scratch(64, 1536, low)
        + [DMA((32,)), DMA((32,)), DMA((32,)), DMA((32,))],
        args,
        ((2, 5), ()),
        limit=34,
    )


def place_kernel(
    main_ref,
    bcr_ref,
    small_ref,
    block_own,
    block_other,
    input_own,
    input_other,
    geg_ref,
    geu_ref,
    ged_ref,
    sg_ref,
    su_ref,
    sd_ref,
    block_out,
    input_out,
    norm1_out,
    wz_out,
    wx_out,
    wbc_out,
    wdt_out,
    convx_out,
    convbc_out,
    biasx_out,
    biasbc_out,
    dt_out,
    log_out,
    skip_out,
    gnorm_out,
    wout_out,
    norm2_out,
    router_out,
    sgate_out,
    sup_out,
    sdown_out,
    eg_out,
    eu_out,
    ed_out,
    biasx_row,
    gnorm_row,
    heads_row,
):
    side = lax.axis_index("head")
    f32 = jnp.float32
    for own, other, out in (
        (block_own, block_other, block_out),
        (input_own, input_other, input_out),
    ):
        out[:, 0] = jnp.where(side == 0, own[...], other[...])
        out[:, 1] = jnp.where(side == 0, other[...], own[...])
    norms = small_ref[0, 0]
    taps = small_ref[1, 0, :, 0:256]
    for j in range(1, 16):
        norms = norms + small_ref[0, j]
        taps = taps + small_ref[1, j, :, 0:256]
    for i in range(4):
        norm1_out[384 * i : 384 * (i + 1)] = norms[i, 0:384]
        norm2_out[384 * i : 384 * (i + 1)] = norms[4 + i, 0:384]
    convbc_out[...] = taps[0:4]
    biasbc_out[...] = taps[4]
    wbc_out[...] = bcr_ref[:, 0:256]
    turned = jnp.concatenate([bcr_ref[:, 256:384], jnp.zeros((32, 128), f32)], 0).T
    router_out[...] = turned[0:16, 0:96]
    wdt_out[...] = jnp.where(side == 0, turned[16:40, 0:96], turned[40:64, 0:96])
    onehot = (
        lax.broadcasted_iota(jnp.int32, (192, 128), 0) // HEADW
        == lax.broadcasted_iota(jnp.int32, (192, 128), 1)
    ).astype(f32)
    for j in range(8):
        place = 8 * side + j
        wide, narrow = slice(192 * j, 192 * (j + 1)), slice(64 * j, 64 * (j + 1))
        convx_out[:, wide] = small_ref[1, place, 0:4, 256:448]
        biasx_row[:, wide] = small_ref[1, place, 4:5, 256:448]
        gnorm_row[:, wide] = small_ref[1, place, 5:6, 0:192]
        skips = jnp.broadcast_to(small_ref[1, place, 5:6, 256:448], (8, 192))
        heads_row[2:3, 3 * j : 3 * j + 3] = mm(skips, onehot, exact=True)[0:1, 0:3]
        heads_row[0:1, 3 * j : 3 * j + 3] = small_ref[1, place, 6:7, 0:3]
        heads_row[1:2, 3 * j : 3 * j + 3] = small_ref[1, place, 6:7, 256:259]
        part = main_ref[j].astype(f32)
        wz_out[:, wide] = part[:, 256:448]
        sgate_out[:, narrow] = part[:, 448:512]
        wx_out[:, wide] = part[:, 512:704]
        sup_out[:, narrow] = part[:, 704:768]
        wout_out[:, wide] = part[:, 0:192]
        sdown_out[:, narrow] = part[:, 192:256]
    biasx_out[...] = biasx_row[0]
    gnorm_out[...] = gnorm_row[0]
    dt_out[...] = heads_row[0, 0:24]
    log_out[...] = heads_row[1, 0:24]
    skip_out[...] = heads_row[2, 0:24]
    eg_out[0] = geg_ref[...] + sg_ref[...].astype(f32)
    eu_out[0] = geu_ref[...] + su_ref[...].astype(f32)
    ed_out[0] = ged_ref[...] + sd_ref[...].astype(f32)


def place(*args):
    shapes = (
        (64, 2, 1536),
        (64, 2, 1536),
        (1536,),
        (96, 1536),
        (96, 1536),
        (96, 256),
        (24, 96),
        (4, 1536),
        (4, 256),
        (1536,),
        (256,),
        (24,),
        (24,),
        (24,),
        (1536,),
        (96, 1536),
        (1536,),
        (16, 96),
        (96, 512),
        (96, 512),
        (96, 512),
        (1, 1536, 256),
        (1, 1536, 256),
        (1, 256, 1536),
    )
    vmem = pl.BlockSpec(memory_space=VMEM)
    return pl.pallas_call(
        place_kernel,
        out_shape=tuple(jax.ShapeDtypeStruct(shape, jnp.float32) for shape in shapes),
        in_specs=[vmem] * len(args),
        out_specs=(vmem,) * len(shapes),
        scratch_shapes=[
            VMEM((1, 1536), jnp.float32),
            VMEM((1, 1536), jnp.float32),
            VMEM((8, 128), jnp.float32),
        ],
        compiler_params=pltpu.CompilerParams(vmem_limit_bytes=22 << 20),
        name="place",
    )(*args)


def by_heads(
    hidden_in,
    doc_ids,
    routes,
    norm1_gain,
    w_z,
    w_x,
    w_bc,
    w_dt,
    conv_x,
    conv_bc,
    convb_x,
    convb_bc,
    dt_bias,
    a_log,
    d_skip,
    gnorm_gain,
    w_out,
    norm2_gain,
    router,
    shared_gate,
    shared_up,
    shared_down,
    expert_gate,
    expert_up,
    expert_down,
    cotangent,
):
    eg, eu, ed = expert_gate[0], expert_up[0], expert_down[0]
    n1, extras, _, cols, own, floats, small_sib, eg_o, eu_o, ed_o = enter(
        hidden_in,
        cotangent,
        w_bc,
        router.T,
        w_dt.T,
        doc_ids.T,
        routes.transpose(1, 2, 0),
        w_out.T,
        shared_down.T,
        w_z,
        shared_gate,
        w_x,
        shared_up,
        conv_x,
        convb_x,
        gnorm_gain,
        dt_bias,
        a_log,
        d_skip,
        norm1_gain,
        norm2_gain,
        conv_bc,
        convb_bc,
        eg,
        eu,
        ed,
    )
    kept, g_all, n2, scale_note, residual, scale_own, ids, consts = mix_forward(
        n1, extras, cols, floats, small_sib, own
    )
    d_res_all, pair, moe_part, *grad_experts, shared, d_res = moe(
        n2,
        scale_note,
        g_all,
        cols,
        eg,
        eg_o,
        eu,
        eu_o,
        ed,
        ed_o,
        extras,
        ids,
        residual,
        scale_own,
        floats,
        own,
    )
    main, bcr, small, block_own, input_own = mix_backward(
        d_res_all, pair, n1, cols, consts, kept, moe_part, shared, residual, d_res, own, floats
    )
    main, bcr, small, block_sib, input_sib = leave(
        main.reshape(16, 96, 768), bcr, small, block_own, input_own
    )
    results = list(
        place(main, bcr, small, block_own, block_sib, input_own, input_sib, *grad_experts)
    )
    for i in (6, 15, 17, 20):
        results[i] = results[i].T
    return tuple(results)


def solution(mesh):
    places = mesh.shape["seq"]
    whole_heads = places == 16 and mesh.shape["head"] == 2
    placed = (
        P("seq", None, None),
        P("seq", None),
        P("seq", None, None),
        P(),
        P("seq", "head"),
        P("seq", "head"),
        P("seq", None),
        P("seq", "head"),
        P(None, "head"),
        P(),
        P("head"),
        P(),
        P("head"),
        P("head"),
        P("head"),
        P("head"),
        P("head", "seq"),
        P(),
        P("seq", None),
        P("seq", "head"),
        P("seq", "head"),
        P("head", "seq"),
        P("seq", None, "head"),
        P("seq", None, "head"),
        P("seq", "head", None),
        P("seq", None, None),
    )
    return jax.shard_map(
        by_heads if whole_heads else on_device,
        mesh=mesh,
        in_specs=placed,
        out_specs=(
            P("seq", None, None),
            P("seq", None, None),
            P(),
            P("seq", "head"),
            P("seq", "head"),
            P("seq", None),
            P("seq", "head"),
            P(None, "head"),
            P(),
            P("head"),
            P(),
            P("head"),
            P("head"),
            P("head"),
            P("head"),
            P("head", "seq"),
            P(),
            P("seq", None),
            P("seq", "head"),
            P("seq", "head"),
            P("head", "seq"),
            P("seq", None, "head"),
            P("seq", None, "head"),
            P("seq", "head", None),
        ),
        check_vma=False,
    )
```
